32 devices in a mesh: row: 2 (over x), seq: 16 (over z, y, core).
Axes of the slice: x: 2, y: 2, z: 4, core: 2. Of those that a mesh axis runs over, the one named last changes fastest.
Arguments:
- inputs: bfloat16 [2, 16384, 768], P('row', 'seq'), may hold values from -4 to 4
- doc_lengths: int32 [2, 4], P('row'), may hold values from 64 to 15916, as said below
- w_qkv: bfloat16 [768, 2304], replicated, may hold values from -0.21875 to 0.21875
- bias_q: float32 [768], replicated, may hold values from -2.5 to 2.5
- bias_v: float32 [768], replicated, may hold values from -2.5 to 2.5
- conv_taps: float32 [12, 33], replicated, may hold values from -2.5 to 2.5
- w_out: bfloat16 [768, 768], replicated, may hold values from -0.21875 to 0.21875
- bias_out: float32 [768], replicated, may hold values from -1.5 to 1.5
- norm1_gain: float32 [768], replicated, may hold values from 0.25 to 1.75
- norm1_bias: float32 [768], replicated, may hold values from -1.5 to 1.5
- w_up: bfloat16 [768, 3072], replicated, may hold values from -0.21875 to 0.21875
- bias_up: float32 [3072], replicated, may hold values from -2.5 to 2.5
- w_down: bfloat16 [3072, 768], replicated, may hold values from -0.109375 to 0.109375
- bias_down: float32 [768], replicated, may hold values from -1.5 to 1.5
- norm2_gain: float32 [768], replicated, may hold values from 0.25 to 1.75
- norm2_bias: float32 [768], replicated, may hold values from -1.5 to 1.5
- cotangent: bfloat16 [2, 16384, 768], P('row', 'seq'), may hold values from -6 to 6
Outputs:
- result: float32 [2, 16384, 768], P('row', 'seq')
- grad_input: float32 [2, 16384, 768], P('row', 'seq')
- grad_w_qkv: float32 [768, 2304], replicated
- grad_bias_q: float32 [768], replicated
- grad_bias_v: float32 [768], replicated
- grad_conv_taps: float32 [12, 33], replicated
- grad_w_out: float32 [768, 768], replicated
- grad_bias_out: float32 [768], replicated
- grad_norm1_gain: float32 [768], replicated
- grad_norm1_bias: float32 [768], replicated
- grad_w_up: float32 [768, 3072], replicated
- grad_bias_up: float32 [3072], replicated
- grad_w_down: float32 [3072, 768], replicated
- grad_bias_down: float32 [768], replicated
- grad_norm2_gain: float32 [768], replicated
- grad_norm2_bias: float32 [768], replicated
The draws below stay inside these ranges and needn't reach their ends.
Inputs may be any that keep to these rules, and one draw needn't show every extreme that they name: `doc_lengths`: each row holds 4 documents laid end to end in the order of its tokens; their lengths sum to 16384. In every row one document has exactly the least length and one exactly the largest.
All inputs are finite; a program needn't handle non-finite values.
Results may differ from the reference program's by a relative error of at most 0.039.
Values may be sent and summed in bfloat16 or wider, within the bound.
No kernel may reach another device: no remote copies, remote signals or barrier semaphores. Data moves between devices by JAX's collectives and lax.ppermute only.
A program may use at most 576 MiB of HBM per device.

```python
import math
import jax
import jax.numpy as jnp
from jax import lax

D = 768
HEADS = 12
FF = 3072
LAND = 64
DOCS = 4
TAPS = 33
NS_ITERS = 6
TOK_DEV = 1024
ROWS = 2
ROW_LEN = 16384


def row_lengths(key):
    key = jax.random.fold_in(key, 23)
    long_key, zero_key, extra_key = jax.random.split(key, 3)
    spread = (TOK_DEV - (DOCS - 1) * LAND) // (DOCS - 1)
    half = spread // 2
    share = half // max(DOCS - 3, 1)
    doc_number = jnp.arange(DOCS, dtype=jnp.int32)[None, :]
    long_at = jax.random.randint(long_key, (ROWS, 1), 0, DOCS)
    zero_at = (long_at + 1 + jax.random.randint(zero_key, (ROWS, 1), 0, DOCS - 1)) % DOCS
    middle = (doc_number != long_at) & (doc_number != zero_at)
    last_middle = jnp.max(jnp.where(middle, doc_number, -1), axis=1, keepdims=True)
    free_middle = middle & (doc_number != last_middle)
    wobble = jnp.where(free_middle, jax.random.randint(extra_key, (ROWS, DOCS), 0, share + 1), 0)
    wobble_sum = jnp.sum(wobble, axis=1, keepdims=True)
    extra = jnp.where(free_middle, half + wobble, 0)
    extra = jnp.where(middle & (doc_number == last_middle), half - wobble_sum, extra)
    short_len = LAND + extra
    rest_len = jnp.sum(jnp.where(doc_number == long_at, 0, short_len), axis=1, keepdims=True)
    return jnp.where(doc_number == long_at, ROW_LEN - rest_len, short_len).astype(jnp.int32)


def pick_rows(table, marks):
    return table[marks]


def draw_inputs(key, part):
    lengths = row_lengths(key)
    key = jax.random.fold_in(key, 11)
    noise_key, freq_key, phase_key, scale_key, mark_key = jax.random.split(key, 5)
    noise_vals = jnp.clip(jax.random.normal(noise_key, (ROWS, ROW_LEN, D), jnp.float32), -2.5, 2.5)
    frequency = jax.random.randint(freq_key, (ROWS, 1, D), 1, LAND // 2 + 1).astype(jnp.float32)
    phase_off = jax.random.uniform(phase_key, (ROWS, 1, D), jnp.float32, -3.14159, 3.14159)
    amplitude = jax.random.uniform(scale_key, (ROWS, 1, D), jnp.float32, 0.5, 1.0)
    position = jnp.arange(ROW_LEN, dtype=jnp.float32)[None, :, None] / ROW_LEN
    smooth = amplitude * jnp.cos(6.283185307 * frequency * position + phase_off)
    doc_ends = jnp.cumsum(lengths, axis=1).astype(jnp.int32)
    doc_starts = (doc_ends - lengths).astype(jnp.int32)
    places = jnp.arange(ROW_LEN, dtype=jnp.int32)[None, :, None]
    inside = ((places >= doc_starts[:, None, :]) & (places < doc_ends[:, None, :])).astype(jnp.int32)
    doc_number = jnp.arange(DOCS, dtype=jnp.int32)[None, None, :]
    doc_index = jnp.sum(inside * doc_number, axis=2)
    doc_start = jnp.sum(inside * doc_starts[:, None, :], axis=2)
    doc_length = jnp.maximum(jnp.sum(inside * lengths[:, None, :], axis=2), 1)
    marks = (doc_index * LAND + (places[:, :, 0] - doc_start) * LAND // doc_length).astype(jnp.int32)
    table = 0.7 * jnp.clip(jax.random.normal(mark_key, (ROWS, DOCS * LAND, D), jnp.float32), -2.5, 2.5)
    landmark_part = jax.vmap(pick_rows)(table, marks)
    return jnp.clip(noise_vals + smooth + landmark_part, -4.0, 4.0).astype(jnp.bfloat16)


def draw_doc_lengths(key, part):
    return row_lengths(key)


def levels(stream_key, dims, pieces, low, largest):
    loudness, own = 1.0, jax.random.fold_in(stream_key, 6)
    for dim, blocks in pieces:
        steps = jnp.exp(jax.random.uniform(jax.random.fold_in(own, dim), (blocks,), jnp.float32, low / len(pieces), largest / len(pieces)))
        loudness = loudness * jnp.repeat(steps, dims[dim] // blocks).reshape([-1 if axis == dim else 1 for axis in range(len(dims))])
    return loudness


def gaussian(stream_key, extent, width, reach, cuts=(), kind=jnp.bfloat16):
    array = jax.random.normal(stream_key, extent, jnp.float32) * width
    if len(cuts) > 0:
        array = levels(stream_key, extent, cuts, -0.22, 0.18) * array
    return jnp.clip(array, min=-reach, max=reach).astype(kind)


def setup_inputs(seed: int = 0) -> dict:
    arg_keys = jax.random.split(jax.random.key(seed), 18)
    inputs = draw_inputs(jax.random.fold_in(arg_keys[17], 71), 0)
    doc_lengths = draw_doc_lengths(jax.random.fold_in(arg_keys[17], 71), 0)
    w_qkv = gaussian(arg_keys[2], (D, 3 * D), D ** -0.5, 0.21875)
    bias_q = gaussian(arg_keys[3], (D,), 0.5, 2.5, (), jnp.float32)
    bias_v = gaussian(arg_keys[4], (D,), 0.5, 2.5, (), jnp.float32)
    conv_taps = gaussian(arg_keys[5], (HEADS, TAPS), 0.5, 2.5, (), jnp.float32)
    w_out = gaussian(arg_keys[6], (D, D), D ** -0.5, 0.21875)
    bias_out = gaussian(arg_keys[7], (D,), 0.3, 1.5, (), jnp.float32)
    norm1_gain = jnp.clip(1.0 + 0.15 * jax.random.normal(arg_keys[8], (D,), jnp.float32), 0.25, 1.75)
    norm1_bias = gaussian(arg_keys[9], (D,), 0.3, 1.5, (), jnp.float32)
    w_up = gaussian(arg_keys[10], (D, FF), D ** -0.5, 0.21875)
    bias_up = gaussian(arg_keys[11], (FF,), 0.5, 2.5, (), jnp.float32)
    w_down = gaussian(arg_keys[12], (FF, D), FF ** -0.5, 0.109375)
    bias_down = gaussian(arg_keys[13], (D,), 0.3, 1.5, (), jnp.float32)
    norm2_gain = jnp.clip(1.0 + 0.15 * jax.random.normal(arg_keys[14], (D,), jnp.float32), 0.25, 1.75)
    norm2_bias = gaussian(arg_keys[15], (D,), 0.3, 1.5, (), jnp.float32)
    cotangent = gaussian(arg_keys[16], (ROWS, ROW_LEN, D), 1.0, 6.0, ((0, 2), (1, 16)))
    return {"inputs": inputs, "doc_lengths": doc_lengths, "w_qkv": w_qkv, "bias_q": bias_q, "bias_v": bias_v, "conv_taps": conv_taps, "w_out": w_out, "bias_out": bias_out, "norm1_gain": norm1_gain, "norm1_bias": norm1_bias, "w_up": w_up, "bias_up": bias_up, "w_down": w_down, "bias_down": bias_down, "norm2_gain": norm2_gain, "norm2_bias": norm2_bias, "cotangent": cotangent}


PRECISE = lax.Precision.HIGHEST
NEGATIVE = -1e+30

@jax.custom_vjp
def low(v):
    return lax.optimization_barrier(v.astype(jnp.bfloat16)).astype(jnp.float32)

@jax.custom_vjp
def low_back(v):
    return v

def low_keep(v):
    return (low(v), None)

def low_pass(kept, grad):
    return (grad,)

def back_keep(v):
    return (v, None)

def back_low(kept, grad):
    return (low(grad),)
low.defvjp(low_keep, low_pass)
low_back.defvjp(back_keep, back_low)

def locate(places, lengths):
    doc_ends = jnp.cumsum(lengths).astype(jnp.int32)
    doc_starts = (doc_ends - lengths).astype(jnp.int32)
    inside = ((places[:, None] >= doc_starts[None, :]) & (places[:, None] < doc_ends[None, :])).astype(jnp.int32)
    doc_number = jnp.arange(lengths.shape[0], dtype=jnp.int32)
    doc_index = lax.optimization_barrier(jnp.sum(inside * doc_number[None, :], axis=1)).astype(jnp.int32)
    doc_start = lax.optimization_barrier(jnp.sum(inside * doc_starts[None, :], axis=1)).astype(jnp.int32)
    doc_length = jnp.maximum(lax.optimization_barrier(jnp.sum(inside * lengths[None, :], axis=1)), 1).astype(jnp.int32)
    segment = (places - doc_start) * LAND // doc_length
    inside_row = lax.optimization_barrier(jnp.sum(inside, axis=1)) > 0
    return (doc_index, (doc_index * LAND + segment).astype(jnp.int32), inside_row)

def gelu_tanh(upper):
    return 0.5 * upper * (1.0 + jnp.tanh(0.7978845608028654 * (upper + 0.044715 * upper * upper * upper)))

def layer_norm(residual, gain, shift):
    row_mean = lax.optimization_barrier(jnp.mean(residual, axis=-1, keepdims=True))
    centered = residual - row_mean
    row_var = lax.optimization_barrier(jnp.mean(centered * centered, axis=-1, keepdims=True))
    return centered * lax.rsqrt(row_var + 1e-05) * gain + shift

def softmax_rows(scores, allowed):
    scores = jnp.where(allowed, scores, NEGATIVE)
    row_max = lax.optimization_barrier(jnp.max(scores, axis=-1, keepdims=True))
    weights = jnp.where(allowed, jnp.exp(scores - row_max), 0.0)
    return weights / lax.optimization_barrier(jnp.sum(weights, axis=-1, keepdims=True))

def pinv_kernel(mark_q, mark_k, head_count):
    mark_count, model_width = mark_q.shape
    head_size = model_width // head_count
    docs_here = mark_count // LAND
    score_scale = 1.0 / math.sqrt(head_size)
    queries = mark_q.reshape(docs_here, LAND, head_count, head_size)
    key_rows = mark_k.reshape(docs_here, LAND, head_count, head_size)
    scores = jnp.einsum('aihe,ajhe->ahij', queries, key_rows, precision=PRECISE) * score_scale
    row_max = lax.optimization_barrier(jnp.max(scores, axis=-1, keepdims=True))
    weights = jnp.exp(scores - row_max)
    kernel = weights / lax.optimization_barrier(jnp.sum(weights, axis=-1, keepdims=True))
    column_max = lax.optimization_barrier(jnp.max(lax.optimization_barrier(jnp.sum(kernel, axis=2)), axis=-1))
    inverse = jnp.swapaxes(kernel, -1, -2) / column_max[..., None, None]
    identity = jnp.eye(LAND, dtype=jnp.float32)
    for sweep in range(NS_ITERS):
        product = jnp.matmul(kernel, inverse, precision=PRECISE)
        bracket = 7.0 * identity - product
        bracket = 15.0 * identity - jnp.matmul(product, bracket, precision=PRECISE)
        bracket = 13.0 * identity - jnp.matmul(product, bracket, precision=PRECISE)
        inverse = 0.25 * jnp.matmul(inverse, bracket, precision=PRECISE)
    return inverse

def landmark_mix(inverse, numer, total):
    head_count, mark_count, head_size = numer.shape
    docs_here = mark_count // LAND
    averaged = (numer / total[..., None]).reshape(head_count, docs_here, LAND, head_size)
    mixed_marks = jnp.einsum('ahij,haje->aihe', inverse, averaged, precision=PRECISE)
    return mixed_marks.reshape(mark_count, head_count * head_size)

def forward_row(row_inputs, lengths, params):
    w_qkv, bias_q, bias_v, conv_taps, w_out, bias_out, norm1_gain, norm1_bias, w_up, bias_up, w_down, bias_down, norm2_gain, norm2_bias = params
    tok_count, model_width = row_inputs.shape
    head_count, tap_count = conv_taps.shape
    head_size = model_width // head_count
    radius = (tap_count - 1) // 2
    mark_count = lengths.shape[0] * LAND
    score_scale = 1.0 / math.sqrt(head_size)
    places = jnp.arange(tok_count, dtype=jnp.int32)
    tok_doc, tok_mark, tok_inside = locate(places, lengths)
    mark_ids = jnp.arange(mark_count, dtype=jnp.int32)
    mark_doc = mark_ids // LAND
    projected = jnp.dot(row_inputs, w_qkv, precision=PRECISE)
    queries = low(low_back(projected[:, :model_width] + bias_q))
    key_rows = low(low_back(projected[:, model_width:2 * model_width]))
    values = low(low_back(projected[:, 2 * model_width:] + bias_v))
    onehot = (tok_mark[:, None] == mark_ids[None, :]).astype(jnp.float32)
    counts = lax.optimization_barrier(jnp.sum(onehot, axis=0))
    mark_q = low(jnp.dot(onehot.T, queries, precision=PRECISE) / counts[:, None])
    mark_k = low(jnp.dot(onehot.T, key_rows, precision=PRECISE) / counts[:, None])
    inverse = pinv_kernel(mark_q, mark_k, head_count)
    allowed_three = mark_doc[:, None] == tok_doc[None, :]
    heads_mq = mark_q.reshape(mark_count, head_count, head_size).transpose(1, 0, 2)
    heads_k = key_rows.reshape(tok_count, head_count, head_size).transpose(1, 0, 2)
    heads_v = values.reshape(tok_count, head_count, head_size).transpose(1, 0, 2)

    def landmark_head(operands):
        mark_rows, key_part, value_part = operands
        scores = low_back(jnp.dot(mark_rows, key_part.T, precision=PRECISE) * score_scale)
        scores = jnp.where(allowed_three, scores, NEGATIVE)
        row_max = lax.optimization_barrier(jnp.max(scores, axis=-1, keepdims=True))
        weights = jnp.where(allowed_three, jnp.exp(scores - row_max), 0.0)
        numer = low_back(jnp.dot(low(weights), value_part, precision=PRECISE))
        return (numer, lax.optimization_barrier(jnp.sum(weights, axis=-1)))
    numer, total = lax.map(jax.checkpoint(landmark_head), (heads_mq, heads_k, heads_v))
    mixed_marks = landmark_mix(inverse, numer, total)
    allowed_one = tok_doc[:, None] == mark_doc[None, :]
    heads_q = queries.reshape(tok_count, head_count, head_size).transpose(1, 0, 2)
    heads_mk = mark_k.reshape(mark_count, head_count, head_size).transpose(1, 0, 2)
    heads_mix = mixed_marks.reshape(mark_count, head_count, head_size).transpose(1, 0, 2)

    def token_head(operands):
        query_part, mark_part, mix_part = operands
        scores = low_back(jnp.dot(query_part, mark_part.T, precision=PRECISE) * score_scale)
        return jnp.dot(softmax_rows(scores, allowed_one), mix_part, precision=PRECISE)
    nystrom = lax.map(jax.checkpoint(token_head), (heads_q, heads_mk, heads_mix))
    nystrom = nystrom.transpose(1, 0, 2).reshape(tok_count, model_width)
    padded = jnp.pad(values, ((radius, radius), (0, 0)))
    ext_places = jnp.arange(tok_count + 2 * radius, dtype=jnp.int32) - radius
    ext_doc, ext_mark, ext_inside = locate(ext_places, lengths)
    tap_columns = jnp.repeat(conv_taps.T, head_size, axis=1)
    convolved = jnp.zeros((tok_count, model_width), jnp.float32)
    for offset in range(tap_count):
        keep_mask = (ext_doc[offset:offset + tok_count] == tok_doc) & ext_inside[offset:offset + tok_count]
        convolved = convolved + jnp.where(keep_mask[:, None], padded[offset:offset + tok_count] * tap_columns[offset][None, :], 0.0)
    mixed = low(low_back(nystrom + convolved))
    attended = low_back(jnp.dot(mixed, w_out, precision=PRECISE) + bias_out)
    hidden_one = layer_norm(row_inputs + attended, norm1_gain, norm1_bias)
    upper = low_back(jnp.dot(low(hidden_one), w_up, precision=PRECISE) + bias_up)
    active = low(gelu_tanh(upper))
    lowered = low_back(jnp.dot(active, w_down, precision=PRECISE) + bias_down)
    return layer_norm(hidden_one + lowered, norm2_gain, norm2_bias)

def reference(inputs, doc_lengths, w_qkv, bias_q, bias_v, conv_taps, w_out, bias_out, norm1_gain, norm1_bias, w_up, bias_up, w_down, bias_down, norm2_gain, norm2_bias, cotangent):
    params = tuple((weight.astype(jnp.float32) for weight in (w_qkv, bias_q, bias_v, conv_taps, w_out, bias_out, norm1_gain, norm1_bias, w_up, bias_up, w_down, bias_down, norm2_gain, norm2_bias)))

    def row_step(summed, operands):
        row_inputs, lengths, row_cot = operands

        def row_forward(row_in, weights):
            return forward_row(row_in, lengths, weights)
        row_out, pullback = jax.vjp(row_forward, row_inputs.astype(jnp.float32), params)
        grad_row, grad_params = pullback(row_cot.astype(jnp.float32))
        summed = tuple((earlier + later for earlier, later in zip(summed, grad_params)))
        return (summed, (row_out, grad_row))
    zero_sums = tuple((jnp.zeros(weight.shape, jnp.float32) for weight in params))
    summed, outputs = lax.scan(row_step, zero_sums, (inputs, doc_lengths, cotangent))
    return (outputs[0], outputs[1], summed[0], summed[1], summed[2], summed[3], summed[4], summed[5], summed[6], summed[7], summed[8], summed[9], summed[10], summed[11], summed[12], summed[13])
```

```python
import math

import jax
import jax.numpy as jnp
from jax import lax
from jax.sharding import PartitionSpec as P

LAND = 64
NS_ITERS = 6
HIGH = lax.Precision.HIGHEST
NEGATIVE = -1e30
BF = jnp.bfloat16
F32 = jnp.float32

T_X = BF
T_NUM = BF
T_MIX = BF
T_GMIX = BF
T_GNUM = BF
T_Y = BF
T_W = BF
P_MIX = lax.Precision.DEFAULT


def swap(array, axis, bit):
    count = lax.axis_size(axis)
    return lax.ppermute(array, axis, [(i, i ^ bit) for i in range(count)])


def add_parts(parts):
    total = parts[0].astype(F32)
    for part in parts[1:]:
        total = total + part.astype(F32)
    return total


def scatter_blocks(blocks, join, kind):
    count = lax.axis_size("seq")
    me = lax.axis_index("seq")
    core, chip = me % 2, me // 2
    pairs = blocks.reshape((count // 2, 2) + blocks.shape[1:])
    mine = lax.dynamic_index_in_dim(pairs, core, 1, keepdims=False)
    other = lax.dynamic_index_in_dim(pairs, 1 - core, 1, keepdims=False)
    held = join([mine, swap(other.astype(kind), "seq", 1)]).astype(kind)
    parts = [lax.dynamic_index_in_dim(held, chip, 0, keepdims=False)]
    for step in range(1, count // 2):
        part = lax.dynamic_index_in_dim(held, chip ^ step, 0, keepdims=False)
        parts.append(swap(part, "seq", 2 * step))
    return join(parts)


def gather_blocks(block):
    count = lax.axis_size("seq")
    me = lax.axis_index("seq")
    core, chip = me % 2, me // 2
    held = jnp.zeros((count // 2,) + block.shape, block.dtype)
    held = lax.dynamic_update_index_in_dim(held, block, chip, 0)
    for step in range(1, count // 2):
        held = lax.dynamic_update_index_in_dim(
            held, swap(block, "seq", 2 * step), chip ^ step, 0
        )
    other = swap(held, "seq", 1)
    first = jnp.where(core == 0, held, other)
    second = jnp.where(core == 0, other, held)
    return jnp.stack([first, second], axis=1).reshape((count,) + block.shape)


def stages(first):
    seq_bits = [("seq", 1 << i) for i in range(1, lax.axis_size("seq").bit_length() - 1)]
    row_bits = [("row", 1 << i) for i in range(lax.axis_size("row").bit_length() - 1)]
    rest = row_bits + seq_bits if first == "row" else seq_bits[:1] + row_bits + seq_bits[1:]
    return [("seq", 1)] + rest


def all_sum(array, first):
    plan = stages(first)
    held = array
    for axis, bit in plan:
        half = held.shape[0] // 2
        side = (lax.axis_index(axis) // bit) % 2
        mine = lax.dynamic_slice_in_dim(held, side * half, half, 0)
        other = lax.dynamic_slice_in_dim(held, (1 - side) * half, half, 0)
        held = mine.astype(F32) + swap(other.astype(T_W), axis, bit).astype(F32)
        held = held.astype(T_W)
    for axis, bit in reversed(plan):
        half = held.shape[0]
        side = (lax.axis_index(axis) // bit) % 2
        other = swap(held, axis, bit)
        held = jnp.where(
            side == 0,
            jnp.concatenate([held, other], 0),
            jnp.concatenate([other, held], 0),
        )
    return held.astype(F32)


def small_sum(array):
    for axis, bit in stages("row"):
        array = array + swap(array, axis, bit)
    return array


def extended(cells, width):
    count = lax.axis_size("seq")
    head = cells[:width]
    tail = cells[-width:]
    return jnp.concatenate(
        [
            lax.ppermute(tail, "seq", [(i, i + 1) for i in range(count - 1)]),
            cells,
            lax.ppermute(head, "seq", [(i + 1, i) for i in range(count - 1)]),
        ],
        axis=0,
    )


def locate(places, lengths):
    doc_ends = jnp.cumsum(lengths)
    doc_starts = doc_ends - lengths
    inside = (
        (places[:, None] >= doc_starts[None, :]) & (places[:, None] < doc_ends[None, :])
    ).astype(jnp.int32)
    doc_number = jnp.arange(lengths.shape[0], dtype=jnp.int32)
    doc_index = jnp.sum(inside * doc_number[None, :], axis=1)
    doc_start = jnp.sum(inside * doc_starts[None, :], axis=1)
    doc_length = jnp.maximum(jnp.sum(inside * lengths[None, :], axis=1), 1)
    segment = (places - doc_start) * LAND // doc_length
    inside_row = jnp.sum(inside, axis=1) > 0
    return (doc_index, doc_index * LAND + segment, inside_row)


def gelu_both(upper):
    tangent = jnp.tanh(0.7978845608028654 * (upper + 0.044715 * upper * upper * upper))
    inner_slope = 0.7978845608028654 * (1.0 + 3.0 * 0.044715 * upper * upper)
    active = 0.5 * upper * (1.0 + tangent)
    slope = 0.5 * (1.0 + tangent) + 0.5 * upper * (1.0 - tangent * tangent) * inner_slope
    return active, slope


def normalize(residual):
    row_mean = jnp.mean(residual, axis=-1, keepdims=True)
    centered = residual - row_mean
    row_var = jnp.mean(centered * centered, axis=-1, keepdims=True)
    inverse_dev = lax.rsqrt(row_var + 1e-05)
    return (centered * inverse_dev, inverse_dev)


def norm_back(grad_normed, normed, inverse_dev):
    return inverse_dev * (
        grad_normed
        - jnp.mean(grad_normed, axis=-1, keepdims=True)
        - normed * jnp.mean(grad_normed * normed, axis=-1, keepdims=True)
    )


def pinv_kernel(queries, key_rows, score_scale):
    scores = jnp.einsum("pie,pje->pij", queries, key_rows, precision=HIGH) * score_scale
    row_max = jnp.max(scores, axis=-1, keepdims=True)
    weights = jnp.exp(scores - row_max)
    kernel = weights / jnp.sum(weights, axis=-1, keepdims=True)
    column_max = jnp.max(jnp.sum(kernel, axis=1), axis=-1)
    inverse = jnp.swapaxes(kernel, -1, -2) / column_max[:, None, None]
    identity = jnp.eye(LAND, dtype=F32)
    for sweep in range(NS_ITERS):
        product = jnp.matmul(kernel, inverse, precision=HIGH)
        bracket = 7.0 * identity - product
        bracket = 15.0 * identity - jnp.matmul(product, bracket, precision=HIGH)
        bracket = 13.0 * identity - jnp.matmul(product, bracket, precision=HIGH)
        inverse = 0.25 * jnp.matmul(inverse, bracket, precision=HIGH)
    return inverse


def small_part(mark_q, mark_k, numer, total, score_scale):
    inverse = pinv_kernel(mark_q, mark_k, score_scale)
    return jnp.einsum("pij,pje->pie", inverse, numer / total, precision=HIGH)


def join_stats(parts):
    parts = [part.astype(F32) for part in parts]
    top = parts[0][..., 65:66]
    for part in parts[1:]:
        top = jnp.maximum(top, part[..., 65:66])
    total = 0.0
    for part in parts:
        total = total + part[..., :65] * jnp.exp(part[..., 65:66] - top)
    rest = jnp.zeros(total.shape[:-1] + (62,), F32)
    return jnp.concatenate([total, top, rest], axis=-1)


def per_device(
    inputs, doc_lengths, w_qkv, bias_q, bias_v, conv_taps, w_out, bias_out, norm1_gain,
    norm1_bias, w_up, bias_up, w_down, bias_down, norm2_gain, norm2_bias, cotangent,
):
    tokens = inputs[0]
    tok_count, width = tokens.shape
    heads, tap_count = conv_taps.shape
    size = width // heads
    radius = (tap_count - 1) // 2
    lengths = doc_lengths[0]
    docs = lengths.shape[0]
    mark_count = docs * LAND
    scale = 1.0 / math.sqrt(size)
    seq_count = lax.axis_size("seq")
    me = lax.axis_index("seq")
    row_first = me * tok_count
    places = row_first + jnp.arange(tok_count, dtype=jnp.int32)
    tok_doc, tok_mark, tok_inside = locate(places, lengths)
    mark_ids = jnp.arange(mark_count, dtype=jnp.int32)
    mark_doc = mark_ids // LAND
    within = mark_ids % LAND
    mark_len = jnp.repeat(lengths, LAND)
    counts = (
        ((within + 1) * mark_len + LAND - 1) // LAND - (within * mark_len + LAND - 1) // LAND
    ).astype(F32)
    rows_in = (((0,), (0,)), ((), ()))
    cols_in = (((1,), (1,)), ((), ()))
    pair_count = docs * heads
    own_pairs = -(-pair_count // seq_count)
    padded = own_pairs * seq_count

    def to_pairs(array):
        array = array.reshape(docs, LAND, heads, -1).transpose(0, 2, 1, 3)
        array = array.reshape(pair_count, LAND, -1)
        return jnp.pad(array, ((0, padded - pair_count), (0, 0), (0, 0)))

    def from_pairs(array):
        array = array[:pair_count].reshape(docs, heads, LAND, -1)
        return array.transpose(0, 2, 1, 3).reshape(mark_count, -1)

    def own(array):
        return lax.dynamic_slice_in_dim(array, me * own_pairs, own_pairs, 0)

    onehot = (tok_mark[:, None] == mark_ids[None, :]).astype(BF)
    sums = lax.dot_general(onehot, tokens, rows_in, preferred_element_type=F32)
    means = (sums / counts[:, None]).reshape(seq_count, mark_count // seq_count, width)
    own_mean = scatter_blocks(means, add_parts, T_X).astype(T_X)
    mean_in = gather_blocks(own_mean).reshape(mark_count, width)
    mean_pre = HIGH if T_X == F32 else None
    mark_q = jnp.dot(
        mean_in, w_qkv[:, :width].astype(T_X), preferred_element_type=F32, precision=mean_pre
    )
    mark_q = (mark_q + bias_q).astype(BF)
    mark_k = jnp.dot(
        mean_in, w_qkv[:, width : 2 * width].astype(T_X), preferred_element_type=F32,
        precision=mean_pre,
    ).astype(BF)

    projected = jnp.dot(tokens, w_qkv, preferred_element_type=F32)
    queries = (projected[:, :width] + bias_q).astype(BF)
    key_rows = projected[:, width : 2 * width].astype(BF)
    values = (projected[:, 2 * width :] + bias_v).astype(BF)
    heads_q = queries.reshape(tok_count, heads, size)
    heads_k = key_rows.reshape(tok_count, heads, size)
    heads_v = values.reshape(tok_count, heads, size)
    heads_mq = mark_q.reshape(mark_count, heads, size)
    heads_mk = mark_k.reshape(mark_count, heads, size)

    allowed = (mark_doc[:, None] == tok_doc[None, :])[None]
    scores_three = (
        jnp.einsum("jhe,the->hjt", heads_mq, heads_k, preferred_element_type=F32) * scale
    )
    scores_three = jnp.where(allowed, scores_three, NEGATIVE)
    local_max = jnp.max(scores_three, axis=-1)
    weights = jnp.where(allowed, jnp.exp(scores_three - local_max[..., None]), 0.0)
    numer = jnp.einsum("hjt,the->hje", weights.astype(BF), heads_v, preferred_element_type=F32)
    total = jnp.sum(weights, axis=-1)
    stats = jnp.concatenate(
        [numer, total[..., None], local_max[..., None], jnp.zeros((heads, mark_count, 62), F32)],
        axis=-1,
    )
    if T_NUM == BF:
        stats = stats.at[..., :64].set(stats[..., :64].astype(BF).astype(F32))
    stats = stats.reshape(heads, docs, LAND, 128).transpose(1, 0, 2, 3)
    stats = stats.reshape(pair_count, LAND, 128)
    stats = jnp.pad(stats, ((0, padded - pair_count), (0, 0), (0, 0)))
    stats = scatter_blocks(stats.reshape(seq_count, own_pairs, LAND, 128), join_stats, F32)
    own_numer, own_total, own_max = stats[..., :64], stats[..., 64:65], stats[..., 65:66]
    own_total = jnp.maximum(own_total, 1e-30)
    own_q = own(to_pairs(mark_q)).astype(F32)
    own_k = own(to_pairs(mark_k)).astype(F32)
    own_mixed, small_pullback = jax.vjp(
        lambda a, b, c, d: small_part(a, b, c, d, scale), own_q, own_k, own_numer, own_total
    )
    own_mixed = own_mixed.astype(T_MIX).astype(F32)
    packed = jnp.concatenate([own_mixed, own_max, jnp.zeros((own_pairs, LAND, 63), F32)], -1)
    packed = gather_blocks(packed).reshape(padded, LAND, 128)[:pair_count]
    heads_mix = packed[..., :64].reshape(docs, heads, LAND, size).transpose(0, 2, 1, 3)
    heads_mix = heads_mix.reshape(mark_count, heads, size)
    row_max = packed[..., 64].reshape(docs, heads, LAND).transpose(1, 0, 2)
    row_max = row_max.reshape(heads, mark_count)

    scores_one = jnp.einsum("the,jhe->htj", heads_q, heads_mk, preferred_element_type=F32) * scale
    allowed_one = (tok_doc[:, None] == mark_doc[None, :])[None]
    scores_one = jnp.where(allowed_one, scores_one, NEGATIVE)
    weights_one = jnp.where(
        allowed_one, jnp.exp(scores_one - jnp.max(scores_one, axis=-1, keepdims=True)), 0.0
    )
    probs_one = weights_one / jnp.sum(weights_one, axis=-1, keepdims=True)
    nystrom = jnp.einsum(
        "htj,jhe->the", probs_one, heads_mix, precision=P_MIX, preferred_element_type=F32
    )

    value_ext = extended(values, radius)
    ext_places = row_first - radius + jnp.arange(tok_count + 2 * radius, dtype=jnp.int32)
    ext_doc, ext_mark, ext_inside = locate(ext_places, lengths)
    ext_doc = jnp.where(ext_inside, ext_doc, -1)
    block = 128
    reach = block + 2 * radius
    blocks = tok_count // block
    rows_at = jnp.arange(block)[:, None]
    cols_at = jnp.arange(reach)[None, :]
    offset_at = cols_at - rows_at
    in_band = (offset_at >= 0) & (offset_at < tap_count)
    taps_hi = conv_taps.astype(BF)
    taps_lo = (conv_taps - taps_hi.astype(F32)).astype(BF)

    def band(taps):
        return jnp.where(in_band[None], taps[:, jnp.clip(offset_at, 0, tap_count - 1)], 0)

    starts = jnp.arange(blocks) * block
    same = jnp.stack(
        [
            (tok_doc[b * block : (b + 1) * block, None] == ext_doc[None, b * block : b * block + reach])
            for b in range(blocks)
        ]
    )

    def windows(cells):
        return jnp.stack([cells[b * block : b * block + reach] for b in range(blocks)]).reshape(
            blocks, reach, heads, size
        )

    def convolve(bands, cells):
        return jnp.einsum("hbts,bshe->bthe", bands, cells, preferred_element_type=F32)

    value_win = windows(value_ext)
    masks = same[None]
    bands_hi = jnp.where(masks, band(taps_hi)[:, None], 0)
    bands_lo = jnp.where(masks, band(taps_lo)[:, None], 0)
    convolved = convolve(bands_hi, value_win) + convolve(bands_lo, value_win)
    mixed = (nystrom.reshape(tok_count, width) + convolved.reshape(tok_count, width)).astype(BF)

    attended = jnp.dot(mixed, w_out, preferred_element_type=F32) + bias_out
    norm_one, inverse_one = normalize(tokens.astype(F32) + attended)
    hidden_one = norm_one * norm1_gain + norm1_bias
    hidden_low = hidden_one.astype(BF)
    upper = jnp.dot(hidden_low, w_up, preferred_element_type=F32) + bias_up
    active, slope = gelu_both(upper)
    active = active.astype(BF)
    lowered = jnp.dot(active, w_down, preferred_element_type=F32) + bias_down
    norm_two, inverse_two = normalize(hidden_one + lowered)
    result = norm_two * norm2_gain + norm2_bias
    upstream = cotangent[0].astype(F32)
    grad_gain_two = jnp.sum(upstream * norm_two, axis=0)
    grad_shift_two = jnp.sum(upstream, axis=0)
    grad_two = norm_back(upstream * norm2_gain, norm_two, inverse_two)
    grad_low_two = grad_two.astype(BF)
    grad_bias_down = jnp.sum(grad_low_two.astype(F32), axis=0)
    grad_w_down = lax.dot_general(active, grad_low_two, rows_in, preferred_element_type=F32)
    grad_active = lax.dot_general(grad_low_two, w_down, cols_in, preferred_element_type=F32)
    grad_upper = (grad_active * slope).astype(BF)
    grad_bias_up = jnp.sum(grad_upper.astype(F32), axis=0)
    grad_w_up = lax.dot_general(hidden_low, grad_upper, rows_in, preferred_element_type=F32)
    grad_hidden = grad_two + lax.dot_general(
        grad_upper, w_up, cols_in, preferred_element_type=F32
    )
    grad_gain_one = jnp.sum(grad_hidden * norm_one, axis=0)
    grad_shift_one = jnp.sum(grad_hidden, axis=0)
    grad_one = norm_back(grad_hidden * norm1_gain, norm_one, inverse_one)
    grad_low_one = grad_one.astype(BF)
    grad_bias_out = jnp.sum(grad_low_one.astype(F32), axis=0)
    grad_w_out = lax.dot_general(mixed, grad_low_one, rows_in, preferred_element_type=F32)
    grad_mixed = lax.dot_general(
        grad_low_one, w_out, cols_in, preferred_element_type=F32
    ).astype(BF)

    heads_grad = grad_mixed.reshape(tok_count, heads, size)
    grad_mix_part = jnp.einsum(
        "htj,the->jhe", probs_one, heads_grad.astype(F32), precision=P_MIX,
        preferred_element_type=F32,
    ).reshape(mark_count, width)
    own_grad_mix = scatter_blocks(
        to_pairs(grad_mix_part).reshape(seq_count, own_pairs, LAND, size), add_parts, T_GMIX
    )
    grad_mq_small, grad_mk_small, grad_numer, grad_total = small_pullback(own_grad_mix)
    grad_numer = grad_numer.astype(T_GNUM).astype(F32)
    grads = jnp.concatenate([grad_numer, grad_total, jnp.zeros((own_pairs, LAND, 63), F32)], -1)
    grads = gather_blocks(grads).reshape(padded, LAND, 128)[:pair_count]
    grads = grads.reshape(docs, heads, LAND, 128).transpose(1, 0, 2, 3)
    grads = grads.reshape(heads, mark_count, 128)
    grad_numer_low, grad_total_all = grads[..., :64].astype(BF), grads[..., 64:65]

    grad_probs = jnp.einsum(
        "the,jhe->htj", heads_grad.astype(F32), heads_mix, precision=P_MIX,
        preferred_element_type=F32,
    )
    shared = jnp.sum(heads_grad.astype(F32) * nystrom, axis=-1).transpose(1, 0)[..., None]
    grad_scores_one = (probs_one * (grad_probs - shared)).astype(BF)
    grad_query_one = (
        jnp.einsum("htj,jhe->the", grad_scores_one, heads_mk, preferred_element_type=F32) * scale
    ).reshape(tok_count, width)
    grad_mk_part = (
        jnp.einsum("htj,the->jhe", grad_scores_one, heads_q, preferred_element_type=F32) * scale
    ).reshape(mark_count, width)

    grad_ext = extended(grad_mixed, radius)
    grad_win = windows(grad_ext)
    back_hi = jnp.where(masks, band(taps_hi[:, ::-1])[:, None], 0)
    back_lo = jnp.where(masks, band(taps_lo[:, ::-1])[:, None], 0)
    grad_values_conv = (convolve(back_hi, grad_win) + convolve(back_lo, grad_win)).reshape(
        tok_count, width
    )
    products = jnp.einsum(
        "bthe,bshe->hbts",
        grad_mixed.reshape(blocks, block, heads, size),
        value_win,
        preferred_element_type=F32,
    )
    products = jnp.sum(jnp.where(masks, products, 0.0), axis=1)
    grad_conv_taps = jnp.stack(
        [jnp.sum(jnp.where(offset_at == o, products, 0.0), axis=(1, 2)) for o in range(tap_count)],
        axis=1,
    )

    weights_three = jnp.where(allowed, jnp.exp(scores_three - row_max[..., None]), 0.0)
    grad_weights = jnp.einsum("hje,the->hjt", grad_numer_low, heads_v, preferred_element_type=F32)
    grad_values_three = jnp.einsum(
        "hjt,hje->the", weights_three.astype(BF), grad_numer_low, preferred_element_type=F32
    ).reshape(tok_count, width)
    grad_scores_three = (weights_three * (grad_weights + grad_total_all)).astype(BF)
    grad_keys_three = (
        jnp.einsum("hjt,jhe->the", grad_scores_three, heads_mq, preferred_element_type=F32) * scale
    ).reshape(tok_count, width)
    grad_mq_part = (
        jnp.einsum("hjt,the->jhe", grad_scores_three, heads_k, preferred_element_type=F32) * scale
    ).reshape(mark_count, width)

    def placed(array):
        empty = jnp.zeros((padded, LAND, size), F32)
        return from_pairs(lax.dynamic_update_slice_in_dim(empty, array, me * own_pairs, 0))

    grad_mq = grad_mq_part + placed(grad_mq_small)
    grad_mk = grad_mk_part + placed(grad_mk_small)
    grad_marks = jnp.concatenate([grad_mq, grad_mk], axis=1).astype(BF)
    mark_back = lax.dot_general(
        grad_marks, w_qkv[:, : 2 * width], cols_in, preferred_element_type=F32
    ) / counts[:, None]
    own_back = scatter_blocks(
        mark_back.reshape(seq_count, mark_count // seq_count, width), add_parts, T_Y
    ).astype(T_Y)
    mark_back = gather_blocks(own_back).reshape(mark_count, width)

    grad_queries = grad_query_one.astype(BF)
    grad_keys = grad_keys_three.astype(BF)
    grad_values = (grad_values_three + grad_values_conv).astype(BF)
    grad_bias_q = jnp.sum(grad_queries.astype(F32), axis=0) + jnp.sum(grad_mq, axis=0)
    grad_bias_v = jnp.sum(grad_values.astype(F32), axis=0)
    grad_projected = jnp.concatenate([grad_queries, grad_keys, grad_values], axis=1)
    grad_w_qkv = lax.dot_general(tokens, grad_projected, rows_in, preferred_element_type=F32)
    grad_w_marks = lax.dot_general(
        mean_in.astype(BF), grad_marks, rows_in, preferred_element_type=F32
    )
    grad_w_qkv = grad_w_qkv + jnp.pad(grad_w_marks, ((0, 0), (0, width)))
    grad_input = (
        grad_one
        + lax.dot_general(grad_projected, w_qkv, cols_in, preferred_element_type=F32)
        + jnp.dot(onehot, mark_back.astype(BF), preferred_element_type=F32)
    )

    small = [
        grad_bias_q, grad_bias_v, grad_conv_taps.reshape(-1), grad_bias_out, grad_gain_one,
        grad_shift_one, grad_bias_up, grad_bias_down, grad_gain_two, grad_shift_two,
    ]
    sizes = [part.shape[0] for part in small]
    flat = jnp.concatenate(small)
    lanes = -(-flat.shape[0] // 1024) * 8
    flat = jnp.pad(flat, (0, lanes * 128 - flat.shape[0])).reshape(lanes, 128)
    flat = small_sum(flat).reshape(-1)
    pieces = []
    at = 0
    for length in sizes:
        pieces.append(flat[at : at + length])
        at += length
    sum_w_down = all_sum(grad_w_down, "row")
    sum_w_up = all_sum(grad_w_up, "seq")
    sum_w_out = all_sum(grad_w_out, "seq")
    sum_w_qkv = all_sum(grad_w_qkv, "row")
    return (
        result[None], grad_input[None], sum_w_qkv, pieces[0], pieces[1],
        pieces[2].reshape(heads, tap_count), sum_w_out, pieces[3], pieces[4], pieces[5],
        sum_w_up, pieces[6], sum_w_down, pieces[7], pieces[8], pieces[9],
    )


def solution(mesh):
    whole, tokens = P(), P("row", "seq", None)
    return jax.shard_map(
        per_device,
        mesh=mesh,
        in_specs=(tokens, P("row", None)) + (whole,) * 14 + (tokens,),
        out_specs=(tokens, tokens) + (whole,) * 14,
        check_vma=False,
    )
```

```python
import math

import jax
import jax.numpy as jnp
from jax import lax
from jax.experimental import pallas as pl
from jax.experimental.pallas import tpu as pltpu
from jax.sharding import PartitionSpec as P

LAND = 64
NS_ITERS = 6
HIGH = lax.Precision.HIGHEST
NEGATIVE = -1e30
BF = jnp.bfloat16
F32 = jnp.float32

T_W = BF
T_INV = BF
P_INV = lax.Precision.DEFAULT
BLOCK = 256
GROUP = 256
SUB = 128
TAPS = 33


def swap(array, axis, bit):
    count = lax.axis_size(axis)
    return lax.ppermute(array, axis, [(i, i ^ bit) for i in range(count)])


def add_parts(parts):
    total = parts[0].astype(F32)
    for part in parts[1:]:
        total = total + part.astype(F32)
    return total


def halves(array, bit):
    rows = array.shape[0] // 2
    side = (lax.axis_index("seq") // bit) % 2
    mine = lax.dynamic_slice_in_dim(array, side * rows, rows, 0)
    other = lax.dynamic_slice_in_dim(array, (1 - side) * rows, rows, 0)
    return mine, other


def seq_total(array, join):
    bits = [1 << i for i in range(lax.axis_size("seq").bit_length() - 1)]
    for bit in bits[:2]:
        mine, other = halves(array, bit)
        array = join(mine, swap(other, "seq", bit))
    for bit in bits[2:]:
        array = join(array, swap(array, "seq", bit))
    for bit in reversed(bits[:2]):
        other = swap(array, "seq", bit)
        side = (lax.axis_index("seq") // bit) % 2
        array = jnp.where(
            side == 0,
            jnp.concatenate([array, other], 0),
            jnp.concatenate([other, array], 0),
        )
    return array


def add_join(first, second):
    return (first.astype(F32) + second.astype(F32)).astype(BF)


def stages(first):
    seq_bits = [("seq", 1 << i) for i in range(1, lax.axis_size("seq").bit_length() - 1)]
    row_bits = [("row", 1 << i) for i in range(lax.axis_size("row").bit_length() - 1)]
    rest = row_bits + seq_bits if first == "row" else seq_bits[:1] + row_bits + seq_bits[1:]
    return [("seq", 1)] + rest


def all_sum(array, first):
    plan = stages(first)
    held = array
    for axis, bit in plan:
        half = held.shape[0] // 2
        side = (lax.axis_index(axis) // bit) % 2
        mine = lax.dynamic_slice_in_dim(held, side * half, half, 0)
        other = lax.dynamic_slice_in_dim(held, (1 - side) * half, half, 0)
        held = mine.astype(F32) + swap(other.astype(T_W), axis, bit).astype(F32)
        held = held.astype(T_W)
    for axis, bit in reversed(plan):
        half = held.shape[0]
        side = (lax.axis_index(axis) // bit) % 2
        other = swap(held, axis, bit)
        held = jnp.where(
            side == 0,
            jnp.concatenate([held, other], 0),
            jnp.concatenate([other, held], 0),
        )
    return held.astype(F32)


def small_sum(array):
    for axis, bit in stages("row"):
        array = array + swap(array, axis, bit)
    return array


def extended(cells, width, rows):
    count = lax.axis_size("seq")
    head = cells[:width]
    tail = cells[-width:]
    return jnp.concatenate(
        [
            lax.ppermute(tail, "seq", [(i, i + 1) for i in range(count - 1)]),
            cells,
            lax.ppermute(head, "seq", [(i + 1, i) for i in range(count - 1)]),
            jnp.zeros((rows - cells.shape[0] - 2 * width, cells.shape[1]), cells.dtype),
        ],
        axis=0,
    )


def dot_nn(a, b):
    return jnp.dot(a, b, preferred_element_type=F32)


def dot_nt(a, b):
    return lax.dot_general(a, b, (((1,), (1,)), ((), ())), preferred_element_type=F32)


def dot_tn(a, b):
    return lax.dot_general(a, b, (((0,), (0,)), ((), ())), preferred_element_type=F32)


def iota(shape, dim):
    return lax.broadcasted_iota(jnp.int32, shape, dim)


def spread(block):
    rows = block.shape[0]
    tall = jnp.concatenate([block] * 4, axis=0).astype(F32)
    shape = (4 * rows, GROUP)
    keep = iota(shape, 0) // rows == iota(shape, 1) // LAND
    return jnp.where(keep, tall, 0.0).astype(BF)


def gathered(square):
    rows = square.shape[0] // 4
    lane = iota((rows, GROUP), 1) // LAND
    out = square[:rows]
    for head in range(1, 4):
        out = jnp.where(lane == head, square[head * rows : (head + 1) * rows], out)
    return out


def by_head(columns, first, shape):
    lane = iota(shape, 1)
    out = jnp.zeros(shape, F32)
    for head, column in enumerate(columns):
        out = jnp.where((lane % 16 == first + head) & (lane < 48), column, out)
    return out


def split_three(cells):
    lane = iota(cells.shape, 1)
    high = cells.astype(BF).astype(F32)
    mid = (cells - high).astype(BF).astype(F32)
    low = cells - high - mid
    return jnp.where(lane < 16, high, jnp.where(lane < 32, mid, low)).astype(BF)


def merge_three(cells):
    cells = cells.astype(F32)
    return cells + pltpu.roll(cells, 112, 1) + pltpu.roll(cells, 96, 1)


def head_lanes(heads, width):
    return (iota((128, width), 0) == iota((128, width), 1) // LAND).astype(F32)


def doc_of(places, bounds, docs):
    out = (places >= bounds[2 * docs - 1]).astype(jnp.int32)
    for doc in range(docs):
        out = out + (places >= bounds[doc]).astype(jnp.int32)
    return out


def landmark_kernel(docs, scale, bounds, mq_ref, k_ref, v_ref, out_ref, max_s, sum_s, acc_s):
    tokens, width = k_ref.shape
    groups = width // GROUP
    heads = width // LAND
    out_ref[:, :width] = jnp.zeros((docs * LAND, width), BF)
    empty = jnp.full((docs * LAND, 128), NEGATIVE, F32)
    out_ref[:, width:] = jnp.where(iota(empty.shape, 1) < 48, split_three(empty).astype(F32), 0.0).astype(BF)
    for doc in range(docs):
        low = jnp.clip(bounds[doc], 0, tokens)
        high = jnp.clip(bounds[docs + doc], 0, tokens)
        rows = slice(doc * LAND, (doc + 1) * LAND)

        @pl.when(high > low)
        def _():
            max_s[...] = jnp.full(max_s.shape, NEGATIVE, F32)
            sum_s[...] = jnp.zeros(sum_s.shape, F32)
            acc_s[...] = jnp.zeros(acc_s.shape, F32)
            wide = [
                spread(mq_ref[rows, g * GROUP : (g + 1) * GROUP]) for g in range(groups)
            ]

            def step(block, carry):
                first = pl.multiple_of(block * BLOCK, BLOCK)
                at = pl.ds(first, BLOCK)
                place = iota((1, BLOCK), 1) + first
                valid = (place >= low) & (place < high)
                for g in range(groups):
                    cols = slice(g * GROUP, (g + 1) * GROUP)
                    scores = dot_nt(wide[g], k_ref[at, cols]) * scale
                    scores = jnp.where(valid, scores, NEGATIVE)
                    old = max_s[cols, :1]
                    top = jnp.maximum(old, jnp.max(scores, axis=1, keepdims=True))
                    weights = jnp.exp(scores - top)
                    shrink = jnp.exp(old - top)
                    sums = sum_s[cols, :1] * shrink + jnp.sum(weights, axis=1, keepdims=True)
                    acc_s[cols, :] = acc_s[cols, :] * shrink + dot_nn(
                        weights.astype(BF), v_ref[at, cols]
                    )
                    max_s[cols, :] = jnp.broadcast_to(top, (GROUP, 128))
                    sum_s[cols, :] = jnp.broadcast_to(sums, (GROUP, 128))
                return carry

            lax.fori_loop(low // BLOCK, (high + BLOCK - 1) // BLOCK, step, 0)
            columns = []
            for g in range(groups):
                cols = slice(g * GROUP, (g + 1) * GROUP)
                sums = sum_s[cols, :1]
                out_ref[rows, cols] = gathered(acc_s[cols, :] / sums).astype(BF)
                level = max_s[cols, :1] + jnp.log(sums)
                columns += [level[h * LAND : (h + 1) * LAND] for h in range(4)]
            out_ref[rows, width:] = split_three(by_head(columns, 0, (LAND, 128)))


def join_kernel(a_ref, b_ref, out_ref):
    width = a_ref.shape[1] - 128
    heads = width // LAND
    first, second = merge_three(a_ref[:, width:]), merge_three(b_ref[:, width:])
    lane = iota(first.shape, 1)
    first = jnp.where(lane < heads, first, 0.0)
    second = jnp.where(lane < heads, second, 0.0)
    top = jnp.maximum(first, second)
    exp_a, exp_b = jnp.exp(first - top), jnp.exp(second - top)
    both = exp_a + exp_b
    level = top + jnp.log(both)
    pick = head_lanes(heads, width)
    share_a = jnp.dot(exp_a / both, pick, precision=HIGH, preferred_element_type=F32)
    share_b = jnp.dot(exp_b / both, pick, precision=HIGH, preferred_element_type=F32)
    joined = a_ref[:, :width].astype(F32) * share_a + b_ref[:, :width].astype(F32) * share_b
    out_ref[:, :width] = joined.astype(BF)
    level = jnp.where(lane < heads, level, 0.0)
    level = level + pltpu.roll(level, 16, 1) + pltpu.roll(level, 32, 1)
    out_ref[:, width:] = split_three(level)


def join(first, second):
    return pl.pallas_call(
        join_kernel, out_shape=jax.ShapeDtypeStruct(first.shape, BF), name="join"
    )(first, second)


def mix_kernel(docs, inv_ref, stat_ref, mix_ref, level_ref):
    width = inv_ref.shape[1]
    for doc in range(docs):
        rows = slice(doc * LAND, (doc + 1) * LAND)
        for g in range(width // GROUP):
            cols = slice(g * GROUP, (g + 1) * GROUP)
            mix_ref[rows, cols] = dot_nn(
                inv_ref[rows, cols].astype(BF), spread(stat_ref[rows, cols])
            ).astype(BF)
    level_ref[...] = merge_three(stat_ref[:, width:])


def mix_back_kernel(docs, inv_ref, stat_ref, grad_ref, out_ref, dots_ref):
    width = inv_ref.shape[1]
    pick = (iota((width, 128), 1) == iota((width, 128), 0) // LAND).astype(BF)
    for doc in range(docs):
        rows = slice(doc * LAND, (doc + 1) * LAND)
        dots = jnp.zeros((LAND, 128), F32)
        for g in range(width // GROUP):
            cols = slice(g * GROUP, (g + 1) * GROUP)
            grad = gathered(dot_tn(inv_ref[rows, cols].astype(BF), grad_ref[rows, cols]))
            out_ref[rows, cols] = grad.astype(BF)
            product = grad * stat_ref[rows, cols].astype(F32)
            high = product.astype(BF)
            low = (product - high.astype(F32)).astype(BF)
            dots = dots + dot_nn(high, pick[cols]) + dot_nn(low, pick[cols])
        dots_ref[rows, :] = dots


def make_band(taps_ref, band_s):
    for head in range(taps_ref.shape[0]):
        row = jnp.broadcast_to(taps_ref[head : head + 1, :], (SUB, GROUP))
        band_s[head * SUB : (head + 1) * SUB, :] = pltpu.roll(row, 0, 1, stride=1, stride_axis=0).astype(BF)


def same_doc(first, bounds, docs, radius):
    rows = iota((SUB, GROUP), 0) + first
    cols = iota((SUB, GROUP), 1) + (first - radius)
    return doc_of(rows, bounds, docs) == doc_of(cols, bounds, docs)


def token_kernel(
    docs, scale, bounds, q_ref, v_ref, mk_ref, mix_ref, taps_ref, mixed_ref, probs_ref, band_s, sum_s
):
    width = q_ref.shape[1]
    groups = width // GROUP
    radius = (TAPS - 1) // 2
    first = pl.program_id(0) * BLOCK

    @pl.when(pl.program_id(0) == 0)
    def _():
        make_band(taps_ref, band_s)

    for sub in range(BLOCK // SUB):
        start = pl.multiple_of(first + sub * SUB, SUB)
        same = same_doc(start, bounds, docs, radius)
        same = jnp.where(jnp.concatenate([same] * 4, axis=0), 1.0, 0.0).astype(BF)
        for g in range(groups):
            cols = slice(g * GROUP, (g + 1) * GROUP)
            band = band_s[g * 4 * SUB : (g + 1) * 4 * SUB, :] * same
            res = dot_nn(band, v_ref[pl.ds(start, GROUP), cols])
            sum_s[sub * SUB : (sub + 1) * SUB, cols] = gathered(res)
    probs_ref[...] = jnp.zeros(probs_ref.shape, BF)
    for doc in range(docs):
        low, high = bounds[doc], bounds[docs + doc]
        rows = slice(doc * LAND, (doc + 1) * LAND)

        @pl.when((high > first) & (low < first + BLOCK))
        def _():
            place = iota((1, BLOCK), 1) + first
            valid = (place >= low) & (place < high)
            for g in range(groups):
                cols = slice(g * GROUP, (g + 1) * GROUP)
                scores = dot_nt(spread(mk_ref[rows, cols]), q_ref[:, cols]) * scale
                scores = scores.reshape(4, LAND, BLOCK)
                weights = jnp.exp(scores - jnp.max(scores, axis=1, keepdims=True))
                probs = weights / jnp.sum(weights, axis=1, keepdims=True)
                probs = jnp.where(valid, probs.reshape(GROUP, BLOCK), 0.0).astype(BF)
                probs_ref[cols, :] = probs_ref[cols, :] + probs
                sum_s[:, cols] = sum_s[:, cols] + dot_tn(probs, spread(mix_ref[rows, cols]))

    mixed_ref[...] = sum_s[...].astype(BF)


def token_back_kernel(
    docs, scale, bounds, q_ref, gm_ref, probs_ref, mk_ref, mix_ref, gq_ref, gmix_ref, gmk_ref, gq_s
):
    width = q_ref.shape[1]
    groups = width // GROUP
    first = pl.program_id(0) * BLOCK

    @pl.when(pl.program_id(0) == 0)
    def _():
        gmix_ref[...] = jnp.zeros(gmix_ref.shape, F32)
        gmk_ref[...] = jnp.zeros(gmk_ref.shape, F32)

    gq_s[...] = jnp.zeros(gq_s.shape, F32)
    for doc in range(docs):
        low, high = bounds[doc], bounds[docs + doc]
        rows = slice(doc * LAND, (doc + 1) * LAND)

        @pl.when((high > first) & (low < first + BLOCK))
        def _():
            place = iota((1, BLOCK), 1) + first
            valid = (place >= low) & (place < high)
            for g in range(groups):
                cols = slice(g * GROUP, (g + 1) * GROUP)
                probs = jnp.where(valid, probs_ref[cols, :].astype(F32), 0.0)
                gmix_ref[rows, cols] += gathered(dot_nn(probs.astype(BF), gm_ref[:, cols]))
                grad = dot_nt(spread(mix_ref[rows, cols]), gm_ref[:, cols])
                heavy = (probs * grad).reshape(4, LAND, BLOCK)
                shared = probs.reshape(4, LAND, BLOCK) * jnp.sum(heavy, axis=1, keepdims=True)
                grad = ((heavy - shared).reshape(GROUP, BLOCK) * scale).astype(BF)
                gmk_ref[rows, cols] += gathered(dot_nn(grad, q_ref[:, cols]))
                gq_s[:, cols] += dot_tn(grad, spread(mk_ref[rows, cols]))

    gq_ref[...] = gq_s[...].astype(BF)


def conv_back_kernel(docs, bounds, gm_ref, v_ref, taps_ref, out_ref, prod_ref, band_s):
    width = gm_ref.shape[1]
    groups = width // GROUP
    radius = (TAPS - 1) // 2
    first = pl.program_id(0) * BLOCK

    @pl.when(pl.program_id(0) == 0)
    def _():
        make_band(taps_ref, band_s)
        prod_ref[...] = jnp.zeros(prod_ref.shape, F32)

    for sub in range(BLOCK // SUB):
        start = pl.multiple_of(first + sub * SUB, SUB)
        same = same_doc(start, bounds, docs, radius)
        same = jnp.where(jnp.concatenate([same] * 4, axis=0), 1.0, 0.0)
        for g in range(groups):
            cols = slice(g * GROUP, (g + 1) * GROUP)
            tall = slice(g * 4 * SUB, (g + 1) * 4 * SUB)
            band = band_s[tall, :] * same.astype(BF)
            res = dot_nn(band, gm_ref[pl.ds(start, GROUP), cols])
            out_ref[sub * SUB : (sub + 1) * SUB, cols] = gathered(res)
            own = gm_ref[pl.ds(pl.multiple_of(start + radius, 16), SUB), cols]
            product = dot_nt(spread(own), v_ref[pl.ds(start, GROUP), cols])
            prod_ref[tall, :] += product * same


def landmark_back_kernel(
    docs, scale, bounds, k_ref, v_ref, conv_ref, mq_ref, grad_ref, level_ref, dots_ref,
    gk_ref, gv_ref, gmq_ref, gk_s, gv_s,
):
    width = k_ref.shape[1]
    groups = width // GROUP
    first = pl.program_id(0) * BLOCK

    @pl.when(pl.program_id(0) == 0)
    def _():
        gmq_ref[...] = jnp.zeros(gmq_ref.shape, F32)

    gk_s[...] = jnp.zeros(gk_s.shape, F32)
    gv_s[...] = conv_ref[...]
    for doc in range(docs):
        low, high = bounds[doc], bounds[docs + doc]
        rows = slice(doc * LAND, (doc + 1) * LAND)

        @pl.when((high > first) & (low < first + BLOCK))
        def _():
            place = iota((1, BLOCK), 1) + first
            valid = (place >= low) & (place < high)

            def column(ref, g):
                return jnp.concatenate(
                    [ref[rows, 4 * g + h : 4 * g + h + 1] for h in range(4)], axis=0
                )

            for g in range(groups):
                cols = slice(g * GROUP, (g + 1) * GROUP)
                wide_q, wide_g = spread(mq_ref[rows, cols]), spread(grad_ref[rows, cols])
                scores = dot_nt(wide_q, k_ref[:, cols]) * scale - column(level_ref, g)
                probs = jnp.exp(jnp.where(valid, scores, NEGATIVE))
                grad = dot_nt(wide_g, v_ref[:, cols]) - column(dots_ref, g)
                grad = (probs * grad * scale).astype(BF)
                gv_s[:, cols] += dot_tn(probs.astype(BF), wide_g)
                gk_s[:, cols] += dot_tn(grad, wide_q)
                gmq_ref[rows, cols] += gathered(dot_nn(grad, k_ref[:, cols]))

    gk_ref[...] = gk_s[...].astype(BF)
    gv_ref[...] = gv_s[...].astype(BF)


def gelu_both(upper):
    tangent = jnp.tanh(0.7978845608028654 * (upper + 0.044715 * upper * upper * upper))
    inner_slope = 0.7978845608028654 * (1.0 + 3.0 * 0.044715 * upper * upper)
    active = 0.5 * upper * (1.0 + tangent)
    slope = 0.5 * (1.0 + tangent) + 0.5 * upper * (1.0 - tangent * tangent) * inner_slope
    return active, slope


def normalize(residual):
    row_mean = jnp.mean(residual, axis=-1, keepdims=True)
    centered = residual - row_mean
    row_var = jnp.mean(centered * centered, axis=-1, keepdims=True)
    inverse_dev = lax.rsqrt(row_var + 1e-05)
    return (centered * inverse_dev, inverse_dev)


def norm_back(grad_normed, normed, inverse_dev):
    return inverse_dev * (
        grad_normed
        - jnp.mean(grad_normed, axis=-1, keepdims=True)
        - normed * jnp.mean(grad_normed * normed, axis=-1, keepdims=True)
    )


def pinv_kernel(queries, key_rows, score_scale):
    scores = jnp.einsum("pie,pje->pij", queries, key_rows, precision=HIGH) * score_scale
    row_max = jnp.max(scores, axis=-1, keepdims=True)
    weights = jnp.exp(scores - row_max)
    kernel = weights / jnp.sum(weights, axis=-1, keepdims=True)
    column_max = jnp.max(jnp.sum(kernel, axis=1), axis=-1)
    inverse = jnp.swapaxes(kernel, -1, -2) / column_max[:, None, None]
    identity = jnp.eye(LAND, dtype=F32)
    for sweep in range(NS_ITERS):
        product = jnp.matmul(kernel, inverse, precision=HIGH)
        bracket = 7.0 * identity - product
        bracket = 15.0 * identity - jnp.matmul(product, bracket, precision=HIGH)
        bracket = 13.0 * identity - jnp.matmul(product, bracket, precision=HIGH)
        inverse = 0.25 * jnp.matmul(inverse, bracket, precision=HIGH)
    return inverse


def per_device(
    inputs, doc_lengths, w_qkv, bias_q, bias_v, conv_taps, w_out, bias_out, norm1_gain,
    norm1_bias, w_up, bias_up, w_down, bias_down, norm2_gain, norm2_bias, cotangent,
):
    tokens = inputs[0]
    tok_count, width = tokens.shape
    heads, tap_count = conv_taps.shape
    size = width // heads
    radius = (tap_count - 1) // 2
    lengths = doc_lengths[0]
    docs = lengths.shape[0]
    mark_count = docs * LAND
    scale = 1.0 / math.sqrt(size)
    seq_count = lax.axis_size("seq")
    me = lax.axis_index("seq")
    row_first = me * tok_count
    ends = jnp.cumsum(lengths)
    starts = ends - lengths
    bounds = (jnp.concatenate([starts, ends]) - row_first).astype(jnp.int32)
    within = jnp.arange(LAND + 1, dtype=jnp.int32)
    edges = starts[:, None] + (within[None, :] * lengths[:, None] + LAND - 1) // LAND
    mark_low = edges[:, :-1].reshape(mark_count, 1)
    mark_high = edges[:, 1:].reshape(mark_count, 1)
    counts = (mark_high - mark_low).astype(F32)
    places = row_first + jnp.arange(tok_count, dtype=jnp.int32)[None, :]
    onehot = ((places >= mark_low) & (places < mark_high)).astype(BF)
    rows_in = (((0,), (0,)), ((), ()))
    cols_in = (((1,), (1,)), ((), ()))
    pair_count = docs * heads
    own_pairs = -(-pair_count // seq_count)
    padded = own_pairs * seq_count
    blocks = tok_count // BLOCK
    window_rows = tok_count + GROUP - SUB
    smem = pl.BlockSpec(memory_space=pltpu.SMEM)
    params = pltpu.CompilerParams(vmem_limit_bytes=40 * 1024 * 1024)
    tok_spec = pl.BlockSpec((BLOCK, width), lambda i: (i, 0))

    def part(col):
        return pl.BlockSpec((BLOCK, width), lambda i: (i, col))

    def fixed(*shape):
        return pl.BlockSpec(shape, lambda i: (0,) * len(shape))

    def shaped(shape, dtype):
        return jax.ShapeDtypeStruct(shape, dtype)

    means = jnp.dot(onehot, tokens, preferred_element_type=F32) / counts
    mean_in = seq_total(means.astype(BF), add_join)
    marks = jnp.dot(mean_in, w_qkv[:, : 2 * width], preferred_element_type=F32)
    mark_q = (marks[:, :width] + bias_q).astype(BF)
    mark_k = marks[:, width:].astype(BF)

    bias = jnp.concatenate([bias_q, jnp.zeros_like(bias_q), bias_v])
    qkv = (jnp.dot(tokens, w_qkv, preferred_element_type=F32) + bias).astype(BF)
    value_ext = extended(qkv[:, 2 * width :], radius, window_rows)

    def one_col(col):
        return pl.BlockSpec((tok_count, width), lambda i: (0, col))

    stats = pl.pallas_call(
        lambda *refs: landmark_kernel(docs, scale, *refs),
        grid=(1,),
        in_specs=[smem, fixed(mark_count, width), one_col(1), one_col(2)],
        out_specs=fixed(mark_count, width + 128),
        out_shape=shaped((mark_count, width + 128), BF),
        scratch_shapes=[
            pltpu.VMEM((width, 128), F32), pltpu.VMEM((width, 128), F32),
            pltpu.VMEM((width, GROUP), F32),
        ],
        compiler_params=params,
        name="landmark",
    )(bounds, mark_q, qkv, qkv)
    stats = seq_total(stats, join)

    def own(array):
        array = array.reshape(docs, LAND, heads, size).transpose(0, 2, 1, 3)
        array = array.reshape(pair_count, LAND, size)
        array = jnp.pad(array, ((0, padded - pair_count), (0, 0), (0, 0)))
        return lax.dynamic_slice_in_dim(array, me * own_pairs, own_pairs, 0)

    own_inverse, inverse_pullback = jax.vjp(
        lambda a, b: pinv_kernel(a, b, scale), own(mark_q).astype(F32), own(mark_k).astype(F32)
    )
    inverse = lax.all_gather(own_inverse.astype(T_INV), "seq", axis=0, tiled=True)[:pair_count]
    inverse = inverse.reshape(docs, heads, LAND, LAND).transpose(0, 2, 1, 3)
    inverse = inverse.reshape(mark_count, width)
    mix, level = pl.pallas_call(
        lambda *refs: mix_kernel(docs, *refs),
        out_shape=(shaped((mark_count, width), BF), shaped((mark_count, 128), F32)),
        name="mix",
    )(inverse, stats)

    taps = jnp.pad(conv_taps, ((0, 0), (0, GROUP - tap_count)))
    mark_spec = fixed(mark_count, width)
    mixed, probs = pl.pallas_call(
        lambda *refs: token_kernel(docs, scale, *refs),
        grid=(blocks,),
        in_specs=[
            smem, part(0), fixed(window_rows, width), mark_spec, mark_spec, fixed(heads, GROUP)
        ],
        out_specs=(tok_spec, pl.BlockSpec((width, BLOCK), lambda i: (0, i))),
        out_shape=(shaped((tok_count, width), BF), shaped((width, tok_count), BF)),
        scratch_shapes=[pltpu.VMEM((heads * SUB, GROUP), BF), pltpu.VMEM((BLOCK, width), F32)],
        compiler_params=params,
        name="token",
    )(bounds, qkv, value_ext, mark_k, mix, taps)

    attended = jnp.dot(mixed, w_out, preferred_element_type=F32) + bias_out
    norm_one, inverse_one = normalize(tokens.astype(F32) + attended)
    hidden_one = norm_one * norm1_gain + norm1_bias
    hidden_low = hidden_one.astype(BF)
    upper = jnp.dot(hidden_low, w_up, preferred_element_type=F32) + bias_up
    active, slope = gelu_both(upper)
    active = active.astype(BF)
    lowered = jnp.dot(active, w_down, preferred_element_type=F32) + bias_down
    norm_two, inverse_two = normalize(hidden_one + lowered)
    result = norm_two * norm2_gain + norm2_bias
    upstream = cotangent[0].astype(F32)
    grad_gain_two = jnp.sum(upstream * norm_two, axis=0)
    grad_shift_two = jnp.sum(upstream, axis=0)
    grad_two = norm_back(upstream * norm2_gain, norm_two, inverse_two)
    grad_low_two = grad_two.astype(BF)
    grad_bias_down = jnp.sum(grad_low_two.astype(F32), axis=0)
    grad_w_down = lax.dot_general(active, grad_low_two, rows_in, preferred_element_type=F32)
    grad_active = lax.dot_general(grad_low_two, w_down, cols_in, preferred_element_type=F32)
    grad_upper = (grad_active * slope).astype(BF)
    grad_bias_up = jnp.sum(grad_upper.astype(F32), axis=0)
    grad_w_up = lax.dot_general(hidden_low, grad_upper, rows_in, preferred_element_type=F32)
    grad_hidden = grad_two + lax.dot_general(
        grad_upper, w_up, cols_in, preferred_element_type=F32
    )
    grad_gain_one = jnp.sum(grad_hidden * norm_one, axis=0)
    grad_shift_one = jnp.sum(grad_hidden, axis=0)
    grad_one = norm_back(grad_hidden * norm1_gain, norm_one, inverse_one)
    grad_low_one = grad_one.astype(BF)
    grad_bias_out = jnp.sum(grad_low_one.astype(F32), axis=0)
    grad_w_out = lax.dot_general(mixed, grad_low_one, rows_in, preferred_element_type=F32)
    grad_mixed = lax.dot_general(
        grad_low_one, w_out, cols_in, preferred_element_type=F32
    ).astype(BF)

    grad_queries, grad_mix, grad_mk = pl.pallas_call(
        lambda *refs: token_back_kernel(docs, scale, *refs),
        grid=(blocks,),
        in_specs=[
            smem, part(0), tok_spec, pl.BlockSpec((width, BLOCK), lambda i: (0, i)), mark_spec,
            mark_spec,
        ],
        out_specs=(tok_spec, mark_spec, mark_spec),
        out_shape=(
            shaped((tok_count, width), BF), shaped((mark_count, width), F32),
            shaped((mark_count, width), F32),
        ),
        scratch_shapes=[pltpu.VMEM((BLOCK, width), F32)],
        compiler_params=params,
        name="token_back",
    )(bounds, qkv, grad_mixed, probs, mark_k, mix)
    grad_mix = seq_total(grad_mix.astype(BF), add_join)

    grad_ext = extended(grad_mixed, radius, window_rows)
    grad_conv, products = pl.pallas_call(
        lambda *refs: conv_back_kernel(docs, *refs),
        grid=(blocks,),
        in_specs=[
            smem, fixed(window_rows, width), fixed(window_rows, width), fixed(heads, GROUP)
        ],
        out_specs=(tok_spec, fixed(heads * SUB, GROUP)),
        out_shape=(shaped((tok_count, width), F32), shaped((heads * SUB, GROUP), F32)),
        scratch_shapes=[pltpu.VMEM((heads * SUB, GROUP), BF)],
        compiler_params=params,
        name="conv_back",
    )(bounds, grad_ext, value_ext, jnp.pad(conv_taps[:, ::-1], ((0, 0), (0, GROUP - tap_count))))
    reach = SUB + tap_count - 1
    products = products.reshape(heads, SUB, GROUP)[:, :, :reach].reshape(heads, SUB * reach)
    products = jnp.pad(products, ((0, 0), (0, SUB))).reshape(heads, SUB, reach + 1)
    grad_conv_taps = jnp.sum(products, axis=1)[:, :tap_count]

    grad_avg, dots = pl.pallas_call(
        lambda *refs: mix_back_kernel(docs, *refs),
        out_shape=(shaped((mark_count, width), BF), shaped((mark_count, 128), F32)),
        name="mix_back",
    )(inverse, stats, grad_mix)
    grad_inverse = jnp.einsum(
        "pie,pje->pij", own(grad_mix), own(stats[:, :width]), preferred_element_type=F32
    )
    grad_mq_small, grad_mk_small = inverse_pullback(grad_inverse)
    lane_spec = fixed(mark_count, 128)
    grad_keys, grad_values, grad_mq = pl.pallas_call(
        lambda *refs: landmark_back_kernel(docs, scale, *refs),
        grid=(blocks,),
        in_specs=[
            smem, part(1), part(2), tok_spec, mark_spec, mark_spec, lane_spec, lane_spec
        ],
        out_specs=(tok_spec, tok_spec, mark_spec),
        out_shape=(
            shaped((tok_count, width), BF), shaped((tok_count, width), BF),
            shaped((mark_count, width), F32),
        ),
        scratch_shapes=[pltpu.VMEM((BLOCK, width), F32), pltpu.VMEM((BLOCK, width), F32)],
        compiler_params=params,
        name="landmark_back",
    )(bounds, qkv, qkv, grad_conv, mark_q, grad_avg, level, dots)

    def placed(array):
        empty = jnp.zeros((padded, LAND, size), F32)
        array = lax.dynamic_update_slice_in_dim(empty, array, me * own_pairs, 0)[:pair_count]
        array = array.reshape(docs, heads, LAND, size).transpose(0, 2, 1, 3)
        return array.reshape(mark_count, width)

    grad_mq = grad_mq + placed(grad_mq_small)
    grad_mk = grad_mk + placed(grad_mk_small)
    grad_marks = jnp.concatenate([grad_mq, grad_mk], axis=1).astype(BF)
    mark_back = lax.dot_general(
        grad_marks, w_qkv[:, : 2 * width], cols_in, preferred_element_type=F32
    ) / counts
    mark_back = seq_total(mark_back.astype(BF), add_join)

    grad_bias_q = jnp.sum(grad_queries.astype(F32), axis=0) + jnp.sum(grad_mq, axis=0)
    grad_bias_v = jnp.sum(grad_values.astype(F32), axis=0)
    grad_projected = jnp.concatenate([grad_queries, grad_keys, grad_values], axis=1)
    grad_w_qkv = lax.dot_general(tokens, grad_projected, rows_in, preferred_element_type=F32)
    grad_w_marks = lax.dot_general(mean_in, grad_marks, rows_in, preferred_element_type=F32)
    grad_w_qkv = grad_w_qkv + jnp.pad(grad_w_marks, ((0, 0), (0, width)))
    grad_input = (
        grad_one
        + lax.dot_general(grad_projected, w_qkv, cols_in, preferred_element_type=F32)
        + lax.dot_general(onehot, mark_back, rows_in, preferred_element_type=F32)
    )

    small = [
        grad_bias_q, grad_bias_v, grad_conv_taps.reshape(-1), grad_bias_out, grad_gain_one,
        grad_shift_one, grad_bias_up, grad_bias_down, grad_gain_two, grad_shift_two,
    ]
    sizes = [piece.shape[0] for piece in small]
    flat = jnp.concatenate(small)
    lanes = -(-flat.shape[0] // 1024) * 8
    flat = jnp.pad(flat, (0, lanes * 128 - flat.shape[0])).reshape(lanes, 128)
    flat = small_sum(flat).reshape(-1)
    pieces = []
    at = 0
    for length in sizes:
        pieces.append(flat[at : at + length])
        at += length
    sum_w_down = all_sum(grad_w_down, "row")
    sum_w_up = all_sum(grad_w_up, "seq")
    sum_w_out = all_sum(grad_w_out, "seq")
    sum_w_qkv = all_sum(grad_w_qkv, "row")
    return (
        result[None], grad_input[None], sum_w_qkv, pieces[0], pieces[1],
        pieces[2].reshape(heads, tap_count), sum_w_out, pieces[3], pieces[4], pieces[5],
        sum_w_up, pieces[6], sum_w_down, pieces[7], pieces[8], pieces[9],
    )


def solution(mesh):
    whole, tokens = P(), P("row", "seq", None)
    return jax.shard_map(
        per_device,
        mesh=mesh,
        in_specs=(tokens, P("row", None)) + (whole,) * 14 + (tokens,),
        out_specs=(tokens, tokens) + (whole,) * 14,
        check_vma=False,
    )
```

```python
import math

import jax
import jax.numpy as jnp
from jax import lax
from jax.experimental import pallas as pl
from jax.experimental.pallas import tpu as pltpu
from jax.sharding import PartitionSpec as P

LAND = 64
NS_ITERS = 6
HIGH = lax.Precision.HIGHEST
NEGATIVE = -1e30
BF = jnp.bfloat16
F32 = jnp.float32

BLOCK = 256
GROUP = 256
SUB = 128
TAPS = 33


def swap(array, axis, bit):
    count = lax.axis_size(axis)
    return lax.ppermute(array, axis, [(i, i ^ bit) for i in range(count)])


def add_parts(parts):
    total = parts[0].astype(F32)
    for part in parts[1:]:
        total = total + part.astype(F32)
    return total


def halves(array, bit):
    rows = array.shape[0] // 2
    side = (lax.axis_index("seq") // bit) % 2
    mine = lax.dynamic_slice_in_dim(array, side * rows, rows, 0)
    other = lax.dynamic_slice_in_dim(array, (1 - side) * rows, rows, 0)
    return mine, other


def seq_quarter(array, join):
    bits = [1 << i for i in range(lax.axis_size("seq").bit_length() - 1)]
    for bit in bits[:2]:
        mine, other = halves(array, bit)
        array = join(mine, swap(other, "seq", bit))
    for bit in bits[2:]:
        array = join(array, swap(array, "seq", bit))
    return array


def paired(array, axis, bit, dim):
    other = swap(array, axis, bit)
    side = (lax.axis_index(axis) // bit) % 2
    return jnp.where(
        side == 0,
        jnp.concatenate([array, other], dim),
        jnp.concatenate([other, array], dim),
    )


def seq_whole(array):
    return paired(paired(array, "seq", 2, 0), "seq", 1, 0)


def add_join(first, second):
    return (first.astype(F32) + second.astype(F32)).astype(BF)


def stages(order):
    row = [("row", 1 << i) for i in range(lax.axis_size("row").bit_length() - 1)]
    seq = [[("seq", 1 << i)] for i in range(lax.axis_size("seq").bit_length() - 1)]
    named = {"core": seq[0], "row": row, "near": seq[1], "far": seq[2], "rest": sum(seq[3:], [])}
    return sum([named[name] for name in ("core",) + order + ("rest",)], [])


ORDERS = (("row", "far", "near"), ("near", "row", "far"), ("far", "near", "row"))


def advance(state, steps):
    held, plan, done = state
    for step in range(done, min(done + steps, 2 * len(plan))):
        if step < len(plan):
            axis, bit = plan[step]
            half = held.shape[0] // 2
            side = (lax.axis_index(axis) // bit) % 2
            mine = lax.dynamic_slice_in_dim(held, side * half, half, 0)
            other = lax.dynamic_slice_in_dim(held, (1 - side) * half, half, 0)
            held = mine.astype(F32) + swap(other.astype(BF), axis, bit).astype(F32)
            held = held.astype(BF)
        else:
            axis, bit = plan[2 * len(plan) - 1 - step]
            held = paired(held, axis, bit, 0)
    return held, plan, min(done + steps, 2 * len(plan))


def tied(values, states):
    values, helds = lax.optimization_barrier((values, [state[0] for state in states]))
    return values, [(held,) + state[1:] for held, state in zip(helds, states)]


def small_steps():
    return stages(("row", "near", "far"))


def extended(cells, width, rows):
    count = lax.axis_size("seq")
    head = cells[:width]
    tail = cells[-width:]
    return jnp.concatenate(
        [
            lax.ppermute(tail, "seq", [(i, i + 1) for i in range(count - 1)]),
            cells,
            lax.ppermute(head, "seq", [(i + 1, i) for i in range(count - 1)]),
            jnp.zeros((rows - cells.shape[0] - 2 * width, cells.shape[1]), cells.dtype),
        ],
        axis=0,
    )


def dot_nn(a, b):
    return jnp.dot(a, b, preferred_element_type=F32)


def dot_nt(a, b):
    return lax.dot_general(a, b, (((1,), (1,)), ((), ())), preferred_element_type=F32)


def dot_tn(a, b):
    return lax.dot_general(a, b, (((0,), (0,)), ((), ())), preferred_element_type=F32)


def iota(shape, dim):
    return lax.broadcasted_iota(jnp.int32, shape, dim)


def spread(block):
    rows = block.shape[0]
    tall = jnp.concatenate([block] * 4, axis=0).astype(F32)
    shape = (4 * rows, GROUP)
    keep = iota(shape, 0) // rows == iota(shape, 1) // LAND
    return jnp.where(keep, tall, 0.0).astype(BF)


def gathered(square):
    rows = square.shape[0] // 4
    lane = iota((rows, GROUP), 1) // LAND
    out = square[:rows]
    for head in range(1, 4):
        out = jnp.where(lane == head, square[head * rows : (head + 1) * rows], out)
    return out


def by_head(columns, first, shape):
    lane = iota(shape, 1)
    out = jnp.zeros(shape, F32)
    for head, column in enumerate(columns):
        out = jnp.where((lane % 16 == first + head) & (lane < 48), column, out)
    return out


def split_three(cells):
    lane = iota(cells.shape, 1)
    high = cells.astype(BF).astype(F32)
    mid = (cells - high).astype(BF).astype(F32)
    low = cells - high - mid
    return jnp.where(lane < 16, high, jnp.where(lane < 32, mid, low)).astype(BF)


def merge_three(cells):
    cells = cells.astype(F32)
    return cells + pltpu.roll(cells, 112, 1) + pltpu.roll(cells, 96, 1)


def head_lanes(heads, width):
    return (iota((128, width), 0) == iota((128, width), 1) // LAND).astype(F32)


def doc_of(places, bounds, docs):
    out = (places >= bounds[2 * docs - 1]).astype(jnp.int32)
    for doc in range(docs):
        out = out + (places >= bounds[doc]).astype(jnp.int32)
    return out


def landmark_kernel(docs, scale, bounds, mq_ref, k_ref, v_ref, out_ref, max_s, sum_s, acc_s):
    tokens, width = k_ref.shape
    groups = width // GROUP
    heads = width // LAND
    out_ref[:, :width] = jnp.zeros((docs * LAND, width), BF)
    empty = jnp.full((docs * LAND, 128), NEGATIVE, F32)
    out_ref[:, width:] = jnp.where(iota(empty.shape, 1) < 48, split_three(empty).astype(F32), 0.0).astype(BF)
    for doc in range(docs):
        low = jnp.clip(bounds[doc], 0, tokens)
        high = jnp.clip(bounds[docs + doc], 0, tokens)
        rows = slice(doc * LAND, (doc + 1) * LAND)

        @pl.when(high > low)
        def _():
            max_s[...] = jnp.full(max_s.shape, NEGATIVE, F32)
            sum_s[...] = jnp.zeros(sum_s.shape, F32)
            acc_s[...] = jnp.zeros(acc_s.shape, F32)
            wide = [
                spread(mq_ref[rows, g * GROUP : (g + 1) * GROUP]) for g in range(groups)
            ]

            def step(block, carry):
                first = pl.multiple_of(block * BLOCK, BLOCK)
                at = pl.ds(first, BLOCK)
                place = iota((1, BLOCK), 1) + first
                valid = (place >= low) & (place < high)
                for g in range(groups):
                    cols = slice(g * GROUP, (g + 1) * GROUP)
                    scores = dot_nt(wide[g], k_ref[at, cols]) * scale
                    scores = jnp.where(valid, scores, NEGATIVE)
                    old = max_s[cols, :1]
                    top = jnp.maximum(old, jnp.max(scores, axis=1, keepdims=True))
                    weights = jnp.exp(scores - top)
                    shrink = jnp.exp(old - top)
                    sums = sum_s[cols, :1] * shrink + jnp.sum(weights, axis=1, keepdims=True)
                    acc_s[cols, :] = acc_s[cols, :] * shrink + dot_nn(
                        weights.astype(BF), v_ref[at, cols]
                    )
                    max_s[cols, :] = jnp.broadcast_to(top, (GROUP, 128))
                    sum_s[cols, :] = jnp.broadcast_to(sums, (GROUP, 128))
                return carry

            lax.fori_loop(low // BLOCK, (high + BLOCK - 1) // BLOCK, step, 0)
            columns = []
            for g in range(groups):
                cols = slice(g * GROUP, (g + 1) * GROUP)
                sums = sum_s[cols, :1]
                out_ref[rows, cols] = gathered(acc_s[cols, :] / sums).astype(BF)
                level = max_s[cols, :1] + jnp.log(sums)
                columns += [level[h * LAND : (h + 1) * LAND] for h in range(4)]
            out_ref[rows, width:] = split_three(by_head(columns, 0, (LAND, 128)))


def join_kernel(a_ref, b_ref, out_ref):
    width = a_ref.shape[1] - 128
    heads = width // LAND
    first, second = merge_three(a_ref[:, width:]), merge_three(b_ref[:, width:])
    lane = iota(first.shape, 1)
    first = jnp.where(lane < heads, first, 0.0)
    second = jnp.where(lane < heads, second, 0.0)
    top = jnp.maximum(first, second)
    exp_a, exp_b = jnp.exp(first - top), jnp.exp(second - top)
    both = exp_a + exp_b
    level = top + jnp.log(both)
    pick = head_lanes(heads, width)
    share_a = jnp.dot(exp_a / both, pick, precision=HIGH, preferred_element_type=F32)
    share_b = jnp.dot(exp_b / both, pick, precision=HIGH, preferred_element_type=F32)
    joined = a_ref[:, :width].astype(F32) * share_a + b_ref[:, :width].astype(F32) * share_b
    out_ref[:, :width] = joined.astype(BF)
    level = jnp.where(lane < heads, level, 0.0)
    level = level + pltpu.roll(level, 16, 1) + pltpu.roll(level, 32, 1)
    out_ref[:, width:] = split_three(level)


def join(first, second):
    return pl.pallas_call(
        join_kernel, out_shape=jax.ShapeDtypeStruct(first.shape, BF), name="join"
    )(first, second)


def mix_kernel(inv_ref, stat_ref, mix_ref):
    width = stat_ref.shape[1] - 128
    for g in range(width // GROUP):
        cols = slice(g * GROUP, (g + 1) * GROUP)
        mix_ref[:, cols] = dot_nn(inv_ref[:, cols], spread(stat_ref[:, cols])).astype(BF)
    mix_ref[:, width:] = stat_ref[:, width:]


def mix_back_kernel(inv_ref, stat_ref, grad_ref, out_ref):
    width = stat_ref.shape[1] - 128
    columns = []
    for g in range(width // GROUP):
        cols = slice(g * GROUP, (g + 1) * GROUP)
        grad = gathered(dot_tn(inv_ref[:, cols], grad_ref[:, cols]))
        out_ref[:, cols] = grad.astype(BF)
        product = grad * stat_ref[:, cols].astype(F32)
        lane = iota(product.shape, 1) // LAND
        for h in range(4):
            columns.append(jnp.sum(jnp.where(lane == h, product, 0.0), axis=1, keepdims=True))
    out_ref[:, width:] = split_three(by_head(columns, 0, (LAND, 128)))


def make_band(taps_ref, band_s):
    for head in range(taps_ref.shape[0]):
        row = jnp.broadcast_to(taps_ref[head : head + 1, :], (SUB, GROUP))
        band_s[head * SUB : (head + 1) * SUB, :] = pltpu.roll(row, 0, 1, stride=1, stride_axis=0).astype(BF)


def same_doc(first, bounds, docs, radius):
    rows = iota((SUB, GROUP), 0) + first
    cols = iota((SUB, GROUP), 1) + (first - radius)
    return doc_of(rows, bounds, docs) == doc_of(cols, bounds, docs)


def token_kernel(
    docs, scale, bounds, q_ref, v_ref, mk_ref, mix_ref, taps_ref, mixed_ref, probs_ref, band_s, sum_s
):
    width = q_ref.shape[1]
    groups = width // GROUP
    radius = (TAPS - 1) // 2
    first = pl.program_id(0) * BLOCK

    @pl.when(pl.program_id(0) == 0)
    def _():
        make_band(taps_ref, band_s)

    for sub in range(BLOCK // SUB):
        start = pl.multiple_of(first + sub * SUB, SUB)
        same = same_doc(start, bounds, docs, radius)
        same = jnp.where(jnp.concatenate([same] * 4, axis=0), 1.0, 0.0).astype(BF)
        for g in range(groups):
            cols = slice(g * GROUP, (g + 1) * GROUP)
            band = band_s[g * 4 * SUB : (g + 1) * 4 * SUB, :] * same
            res = dot_nn(band, v_ref[pl.ds(start, GROUP), cols])
            sum_s[sub * SUB : (sub + 1) * SUB, cols] = gathered(res)
    probs_ref[...] = jnp.zeros(probs_ref.shape, BF)
    for doc in range(docs):
        low, high = bounds[doc], bounds[docs + doc]
        rows = slice(doc * LAND, (doc + 1) * LAND)

        @pl.when((high > first) & (low < first + BLOCK))
        def _():
            place = iota((1, BLOCK), 1) + first
            valid = (place >= low) & (place < high)
            for g in range(groups):
                cols = slice(g * GROUP, (g + 1) * GROUP)
                scores = dot_nt(spread(mk_ref[rows, cols]), q_ref[:, cols]) * scale
                scores = scores.reshape(4, LAND, BLOCK)
                weights = jnp.exp(scores - jnp.max(scores, axis=1, keepdims=True))
                probs = weights / jnp.sum(weights, axis=1, keepdims=True)
                probs = jnp.where(valid, probs.reshape(GROUP, BLOCK), 0.0).astype(BF)
                probs_ref[cols, :] = probs_ref[cols, :] + probs
                sum_s[:, cols] = sum_s[:, cols] + dot_tn(probs, spread(mix_ref[rows, cols]))

    mixed_ref[...] = sum_s[...].astype(BF)


def token_back_kernel(
    docs, scale, bounds, q_ref, gm_ref, probs_ref, mk_ref, mix_ref, gq_ref, gmix_ref, gmk_ref, gq_s
):
    width = q_ref.shape[1]
    groups = width // GROUP
    first = pl.program_id(0) * BLOCK

    @pl.when(pl.program_id(0) == 0)
    def _():
        gmix_ref[...] = jnp.zeros(gmix_ref.shape, F32)
        gmk_ref[...] = jnp.zeros(gmk_ref.shape, F32)

    gq_s[...] = jnp.zeros(gq_s.shape, F32)
    for doc in range(docs):
        low, high = bounds[doc], bounds[docs + doc]
        rows = slice(doc * LAND, (doc + 1) * LAND)

        @pl.when((high > first) & (low < first + BLOCK))
        def _():
            place = iota((1, BLOCK), 1) + first
            valid = (place >= low) & (place < high)
            for g in range(groups):
                cols = slice(g * GROUP, (g + 1) * GROUP)
                probs = jnp.where(valid, probs_ref[cols, :].astype(F32), 0.0)
                gmix_ref[rows, cols] += gathered(dot_nn(probs.astype(BF), gm_ref[:, cols]))
                grad = dot_nt(spread(mix_ref[rows, cols]), gm_ref[:, cols])
                heavy = (probs * grad).reshape(4, LAND, BLOCK)
                shared = probs.reshape(4, LAND, BLOCK) * jnp.sum(heavy, axis=1, keepdims=True)
                grad = ((heavy - shared).reshape(GROUP, BLOCK) * scale).astype(BF)
                gmk_ref[rows, cols] += gathered(dot_nn(grad, q_ref[:, cols]))
                gq_s[:, cols] += dot_tn(grad, spread(mk_ref[rows, cols]))

    gq_ref[...] = gq_s[...].astype(BF)


def conv_back_kernel(docs, bounds, gm_ref, v_ref, taps_ref, out_ref, prod_ref, band_s):
    width = gm_ref.shape[1]
    groups = width // GROUP
    radius = (TAPS - 1) // 2
    first = pl.program_id(0) * BLOCK

    @pl.when(pl.program_id(0) == 0)
    def _():
        make_band(taps_ref, band_s)
        prod_ref[...] = jnp.zeros(prod_ref.shape, F32)

    for sub in range(BLOCK // SUB):
        start = pl.multiple_of(first + sub * SUB, SUB)
        same = same_doc(start, bounds, docs, radius)
        same = jnp.where(jnp.concatenate([same] * 4, axis=0), 1.0, 0.0)
        for g in range(groups):
            cols = slice(g * GROUP, (g + 1) * GROUP)
            tall = slice(g * 4 * SUB, (g + 1) * 4 * SUB)
            band = band_s[tall, :] * same.astype(BF)
            res = dot_nn(band, gm_ref[pl.ds(start, GROUP), cols])
            out_ref[sub * SUB : (sub + 1) * SUB, cols] = gathered(res)
            own = gm_ref[pl.ds(pl.multiple_of(start + radius, 16), SUB), cols]
            product = dot_nt(spread(own), v_ref[pl.ds(start, GROUP), cols])
            prod_ref[tall, :] += product * same


def landmark_back_kernel(
    docs, scale, bounds, k_ref, v_ref, conv_ref, mq_ref, grad_ref, level_ref, dots_ref,
    gk_ref, gv_ref, gmq_ref, gk_s, gv_s,
):
    width = k_ref.shape[1]
    groups = width // GROUP
    first = pl.program_id(0) * BLOCK

    @pl.when(pl.program_id(0) == 0)
    def _():
        gmq_ref[...] = jnp.zeros(gmq_ref.shape, F32)

    gk_s[...] = jnp.zeros(gk_s.shape, F32)
    gv_s[...] = conv_ref[...]
    for doc in range(docs):
        low, high = bounds[doc], bounds[docs + doc]
        rows = slice(doc * LAND, (doc + 1) * LAND)

        @pl.when((high > first) & (low < first + BLOCK))
        def _():
            place = iota((1, BLOCK), 1) + first
            valid = (place >= low) & (place < high)

            level, dots = merge_three(level_ref[rows, :]), merge_three(dots_ref[rows, :])

            def column(lanes, g):
                return jnp.concatenate(
                    [lanes[:, 4 * g + h : 4 * g + h + 1] for h in range(4)], axis=0
                )

            for g in range(groups):
                cols = slice(g * GROUP, (g + 1) * GROUP)
                wide_q, wide_g = spread(mq_ref[rows, cols]), spread(grad_ref[rows, cols])
                scores = dot_nt(wide_q, k_ref[:, cols]) * scale - column(level, g)
                probs = jnp.exp(jnp.where(valid, scores, NEGATIVE))
                grad = dot_nt(wide_g, v_ref[:, cols]) - column(dots, g)
                grad = (probs * grad * scale).astype(BF)
                gv_s[:, cols] += dot_tn(probs.astype(BF), wide_g)
                gk_s[:, cols] += dot_tn(grad, wide_q)
                gmq_ref[rows, cols] += gathered(dot_nn(grad, k_ref[:, cols]))

    gk_ref[...] = gk_s[...].astype(BF)
    gv_ref[...] = gv_s[...].astype(BF)


def gelu_both(upper):
    tangent = jnp.tanh(0.7978845608028654 * (upper + 0.044715 * upper * upper * upper))
    inner_slope = 0.7978845608028654 * (1.0 + 3.0 * 0.044715 * upper * upper)
    active = 0.5 * upper * (1.0 + tangent)
    slope = 0.5 * (1.0 + tangent) + 0.5 * upper * (1.0 - tangent * tangent) * inner_slope
    return active, slope


def normalize(residual):
    row_mean = jnp.mean(residual, axis=-1, keepdims=True)
    centered = residual - row_mean
    row_var = jnp.mean(centered * centered, axis=-1, keepdims=True)
    inverse_dev = lax.rsqrt(row_var + 1e-05)
    return (centered * inverse_dev, inverse_dev)


def norm_back(grad_normed, normed, inverse_dev):
    return inverse_dev * (
        grad_normed
        - jnp.mean(grad_normed, axis=-1, keepdims=True)
        - normed * jnp.mean(grad_normed * normed, axis=-1, keepdims=True)
    )


def pinv_kernel(queries, key_rows, score_scale):
    scores = jnp.einsum("pie,pje->pij", queries, key_rows, precision=HIGH) * score_scale
    row_max = jnp.max(scores, axis=-1, keepdims=True)
    weights = jnp.exp(scores - row_max)
    kernel = weights / jnp.sum(weights, axis=-1, keepdims=True)
    column_max = jnp.max(jnp.sum(kernel, axis=1), axis=-1)
    inverse = jnp.swapaxes(kernel, -1, -2) / column_max[:, None, None]
    identity = jnp.eye(LAND, dtype=F32)
    for sweep in range(NS_ITERS):
        product = jnp.matmul(kernel, inverse, precision=HIGH)
        bracket = 7.0 * identity - product
        bracket = 15.0 * identity - jnp.matmul(product, bracket, precision=HIGH)
        bracket = 13.0 * identity - jnp.matmul(product, bracket, precision=HIGH)
        inverse = 0.25 * jnp.matmul(inverse, bracket, precision=HIGH)
    return inverse


def per_device(
    inputs, doc_lengths, w_qkv, bias_q, bias_v, conv_taps, w_out, bias_out, norm1_gain,
    norm1_bias, w_up, bias_up, w_down, bias_down, norm2_gain, norm2_bias, cotangent,
):
    tokens = inputs[0]
    tok_count, width = tokens.shape
    heads, tap_count = conv_taps.shape
    size = width // heads
    radius = (tap_count - 1) // 2
    lengths = doc_lengths[0]
    docs = lengths.shape[0]
    mark_count = docs * LAND
    scale = 1.0 / math.sqrt(size)
    seq_count = lax.axis_size("seq")
    me = lax.axis_index("seq")
    row_first = me * tok_count
    ends = jnp.cumsum(lengths)
    starts = ends - lengths
    bounds = (jnp.concatenate([starts, ends]) - row_first).astype(jnp.int32)
    within = jnp.arange(LAND + 1, dtype=jnp.int32)
    edges = starts[:, None] + (within[None, :] * lengths[:, None] + LAND - 1) // LAND
    mark_low = edges[:, :-1].reshape(mark_count, 1)
    mark_high = edges[:, 1:].reshape(mark_count, 1)
    counts = (mark_high - mark_low).astype(F32)
    places = row_first + jnp.arange(tok_count, dtype=jnp.int32)[None, :]
    onehot = ((places >= mark_low) & (places < mark_high)).astype(BF)
    rows_in = (((0,), (0,)), ((), ()))
    cols_in = (((1,), (1,)), ((), ()))
    blocks = tok_count // BLOCK
    window_rows = tok_count + GROUP - SUB
    smem = pl.BlockSpec(memory_space=pltpu.SMEM)
    params = pltpu.CompilerParams(vmem_limit_bytes=40 * 1024 * 1024)
    tok_spec = pl.BlockSpec((BLOCK, width), lambda i: (i, 0))

    def part(col):
        return pl.BlockSpec((BLOCK, width), lambda i: (i, col))

    def fixed(*shape):
        return pl.BlockSpec(shape, lambda i: (0,) * len(shape))

    def shaped(shape, dtype):
        return jax.ShapeDtypeStruct(shape, dtype)

    means = jnp.dot(onehot, tokens, preferred_element_type=F32) / counts
    mean_in = seq_whole(seq_quarter(means.astype(BF), add_join))
    marks = jnp.dot(mean_in, w_qkv[:, : 2 * width], preferred_element_type=F32)
    mark_q = (marks[:, :width] + bias_q).astype(BF)
    mark_k = marks[:, width:].astype(BF)

    bias = jnp.concatenate([bias_q, jnp.zeros_like(bias_q), bias_v])
    qkv = (jnp.dot(tokens, w_qkv, preferred_element_type=F32) + bias).astype(BF)
    value_ext = extended(qkv[:, 2 * width :], radius, window_rows)
    value_ext, mark_q, mark_k = lax.optimization_barrier((value_ext, mark_q, mark_k))

    def one_col(col):
        return pl.BlockSpec((tok_count, width), lambda i: (0, col))

    stats = pl.pallas_call(
        lambda *refs: landmark_kernel(docs, scale, *refs),
        grid=(1,),
        in_specs=[smem, fixed(mark_count, width), one_col(1), one_col(2)],
        out_specs=fixed(mark_count, width + 128),
        out_shape=shaped((mark_count, width + 128), BF),
        scratch_shapes=[
            pltpu.VMEM((width, 128), F32), pltpu.VMEM((width, 128), F32),
            pltpu.VMEM((width, GROUP), F32),
        ],
        compiler_params=params,
        name="landmark",
    )(bounds, mark_q, qkv, qkv)
    far_count = seq_count // 4
    own_count = -(-heads // far_count)
    own_doc = (me % 2) * 2 + (me // 2) % 2
    own_at = (me // 4) * own_count * size
    spare = far_count * own_count * size - width

    def own_heads(array):
        array = jnp.pad(array, ((0, 0), (0, spare)))
        array = lax.dynamic_slice_in_dim(array, own_at, own_count * size, 1)
        return array.reshape(LAND, own_count, size).transpose(1, 0, 2)

    def of_doc(array):
        return lax.dynamic_slice_in_dim(array, own_doc * LAND, LAND, 0)

    own_inverse, inverse_pullback = jax.vjp(
        lambda a, b: pinv_kernel(a, b, scale),
        own_heads(of_doc(mark_q)).astype(F32),
        own_heads(of_doc(mark_k)).astype(F32),
    )
    inverse = own_inverse.transpose(1, 0, 2).reshape(LAND, own_count * size).astype(BF)
    for bit in (1, 2):
        mine, other = halves(stats, bit)
        stats = join(mine, swap(other, "seq", bit))
    for i in range(2, seq_count.bit_length() - 1):
        other = swap(jnp.concatenate([stats, inverse], 1), "seq", 1 << i)
        stats = join(stats, other[:, : width + 128])
        other = other[:, width + 128 :]
        inverse = jnp.where(
            (me >> i) % 2 == 0,
            jnp.concatenate([inverse, other], 1),
            jnp.concatenate([other, inverse], 1),
        )
    inverse = inverse[:, :width]
    mix = pl.pallas_call(
        mix_kernel, out_shape=shaped((LAND, width + 128), BF), name="mix"
    )(inverse, stats)
    mix = seq_whole(mix)

    taps = jnp.pad(conv_taps, ((0, 0), (0, GROUP - tap_count)))
    mark_spec = fixed(mark_count, width)
    mixed, probs = pl.pallas_call(
        lambda *refs: token_kernel(docs, scale, *refs),
        grid=(blocks,),
        in_specs=[
            smem, part(0), fixed(window_rows, width), mark_spec, mark_spec, fixed(heads, GROUP)
        ],
        out_specs=(tok_spec, pl.BlockSpec((width, BLOCK), lambda i: (0, i))),
        out_shape=(shaped((tok_count, width), BF), shaped((width, tok_count), BF)),
        scratch_shapes=[pltpu.VMEM((heads * SUB, GROUP), BF), pltpu.VMEM((BLOCK, width), F32)],
        compiler_params=params,
        name="token",
    )(bounds, qkv, value_ext, mark_k, mix, taps)

    attended = jnp.dot(mixed, w_out, preferred_element_type=F32) + bias_out
    norm_one, inverse_one = normalize(tokens.astype(F32) + attended)
    hidden_one = norm_one * norm1_gain + norm1_bias
    hidden_low = hidden_one.astype(BF)
    upper = jnp.dot(hidden_low, w_up, preferred_element_type=F32) + bias_up
    active, slope = gelu_both(upper)
    active = active.astype(BF)
    lowered = jnp.dot(active, w_down, preferred_element_type=F32) + bias_down
    norm_two, inverse_two = normalize(hidden_one + lowered)
    result = norm_two * norm2_gain + norm2_bias
    upstream = cotangent[0].astype(F32)
    grad_gain_two = jnp.sum(upstream * norm_two, axis=0)
    grad_shift_two = jnp.sum(upstream, axis=0)
    grad_two = norm_back(upstream * norm2_gain, norm_two, inverse_two)
    grad_low_two = grad_two.astype(BF)
    grad_bias_down = jnp.sum(grad_low_two.astype(F32), axis=0)
    grad_w_down = lax.dot_general(active, grad_low_two, rows_in, preferred_element_type=F32)
    down = (grad_w_down.astype(BF), stages(ORDERS[0]), 0)
    grad_low_two, (down,) = tied(grad_low_two, [down])
    down = advance(down, 1)
    grad_active = lax.dot_general(grad_low_two, w_down, cols_in, preferred_element_type=F32)
    grad_upper = (grad_active * slope).astype(BF)
    grad_upper, (down,) = tied(grad_upper, [down])
    down = advance(down, 1)
    grad_bias_up = jnp.sum(grad_upper.astype(F32), axis=0)
    grad_w_up = lax.dot_general(hidden_low, grad_upper, rows_in, preferred_element_type=F32)
    up = (grad_w_up.astype(BF), stages(ORDERS[1]), 0)
    grad_upper, (up,) = tied(grad_upper, [up])
    up = advance(up, 1)
    grad_hidden = grad_two + lax.dot_general(
        grad_upper, w_up, cols_in, preferred_element_type=F32
    )
    grad_gain_one = jnp.sum(grad_hidden * norm_one, axis=0)
    grad_shift_one = jnp.sum(grad_hidden, axis=0)
    grad_one = norm_back(grad_hidden * norm1_gain, norm_one, inverse_one)
    grad_low_one = grad_one.astype(BF)
    grad_low_one, (up,) = tied(grad_low_one, [up])
    up = advance(up, 1)
    grad_bias_out = jnp.sum(grad_low_one.astype(F32), axis=0)
    grad_w_out = lax.dot_general(mixed, grad_low_one, rows_in, preferred_element_type=F32)
    out = (grad_w_out.astype(BF), stages(ORDERS[2]), 0)
    grad_mixed = lax.dot_general(
        grad_low_one, w_out, cols_in, preferred_element_type=F32
    ).astype(BF)
    grad_mixed, (down,) = tied(grad_mixed, [down])
    down = advance(down, 1)

    grad_queries, grad_mix, grad_mk = pl.pallas_call(
        lambda *refs: token_back_kernel(docs, scale, *refs),
        grid=(blocks,),
        in_specs=[
            smem, part(0), tok_spec, pl.BlockSpec((width, BLOCK), lambda i: (0, i)), mark_spec,
            mark_spec,
        ],
        out_specs=(tok_spec, mark_spec, mark_spec),
        out_shape=(
            shaped((tok_count, width), BF), shaped((mark_count, width), F32),
            shaped((mark_count, width), F32),
        ),
        scratch_shapes=[pltpu.VMEM((BLOCK, width), F32)],
        compiler_params=params,
        name="token_back",
    )(bounds, qkv, grad_mixed, probs, mark_k, mix)
    grad_mix = seq_quarter(grad_mix.astype(BF), add_join)
    out = advance(out, 1)
    grad_mix, (down, up, out) = tied(grad_mix, [down, up, out])
    down, up, out = advance(down, 1), advance(up, 1), advance(out, 1)

    grad_ext = extended(grad_mixed, radius, window_rows)
    grad_conv, products = pl.pallas_call(
        lambda *refs: conv_back_kernel(docs, *refs),
        grid=(blocks,),
        in_specs=[
            smem, fixed(window_rows, width), fixed(window_rows, width), fixed(heads, GROUP)
        ],
        out_specs=(tok_spec, fixed(heads * SUB, GROUP)),
        out_shape=(shaped((tok_count, width), F32), shaped((heads * SUB, GROUP), F32)),
        scratch_shapes=[pltpu.VMEM((heads * SUB, GROUP), BF)],
        compiler_params=params,
        name="conv_back",
    )(bounds, grad_ext, value_ext, jnp.pad(conv_taps[:, ::-1], ((0, 0), (0, GROUP - tap_count))))
    reach = SUB + tap_count - 1
    products = products.reshape(heads, SUB, GROUP)[:, :, :reach].reshape(heads, SUB * reach)
    products = jnp.pad(products, ((0, 0), (0, SUB))).reshape(heads, SUB, reach + 1)
    grad_conv_taps = jnp.sum(products, axis=1)[:, :tap_count]

    grad_avg = pl.pallas_call(
        mix_back_kernel, out_shape=shaped((LAND, width + 128), BF), name="mix_back"
    )(inverse, stats, grad_mix)
    grad_avg = seq_whole(grad_avg)
    grad_avg, (down, up, out) = tied(grad_avg, [down, up, out])
    down, up, out = advance(down, 1), advance(up, 1), advance(out, 1)
    grad_inverse = jnp.einsum(
        "pie,pje->pij", own_heads(grad_mix), own_heads(stats[:, :width]),
        preferred_element_type=F32,
    )
    grad_mq_small, grad_mk_small = inverse_pullback(grad_inverse)
    lane_spec = pl.BlockSpec((mark_count, 128), lambda i: (0, width // 128))
    grad_keys, grad_values, grad_mq = pl.pallas_call(
        lambda *refs: landmark_back_kernel(docs, scale, *refs),
        grid=(blocks,),
        in_specs=[
            smem, part(1), part(2), tok_spec, mark_spec, mark_spec, lane_spec, lane_spec
        ],
        out_specs=(tok_spec, tok_spec, mark_spec),
        out_shape=(
            shaped((tok_count, width), BF), shaped((tok_count, width), BF),
            shaped((mark_count, width), F32),
        ),
        scratch_shapes=[pltpu.VMEM((BLOCK, width), F32), pltpu.VMEM((BLOCK, width), F32)],
        compiler_params=params,
        name="landmark_back",
    )(bounds, qkv, qkv, grad_conv, mark_q, grad_avg, mix, grad_avg)
    grad_keys, (down, up, out) = tied(grad_keys, [down, up, out])
    down, up, out = advance(down, 1), advance(up, 1), advance(out, 1)

    def placed(array):
        array = array.transpose(1, 0, 2).reshape(LAND, own_count * size)
        array = lax.dynamic_update_slice_in_dim(
            jnp.zeros((LAND, width + spare), F32), array, own_at, 1
        )[:, :width]
        return lax.dynamic_update_slice_in_dim(
            jnp.zeros((mark_count, width), F32), array, own_doc * LAND, 0
        )

    grad_mq = grad_mq + placed(grad_mq_small)
    grad_mk = grad_mk + placed(grad_mk_small)
    grad_marks = jnp.concatenate([grad_mq, grad_mk], axis=1).astype(BF)
    mark_back = lax.dot_general(
        grad_marks, w_qkv[:, : 2 * width], cols_in, preferred_element_type=F32
    ) / counts
    mark_back = mark_back.astype(BF)

    grad_bias_q = jnp.sum(grad_queries.astype(F32), axis=0) + jnp.sum(grad_mq, axis=0)
    grad_bias_v = jnp.sum(grad_values.astype(F32), axis=0)
    grad_projected = jnp.concatenate([grad_queries, grad_keys, grad_values], axis=1)
    grad_w_qkv = lax.dot_general(tokens, grad_projected, rows_in, preferred_element_type=F32)
    grad_w_marks = lax.dot_general(mean_in, grad_marks, rows_in, preferred_element_type=F32)
    grad_w_qkv = grad_w_qkv + jnp.pad(grad_w_marks, ((0, 0), (0, width)))
    small = [
        grad_bias_q, grad_bias_v, grad_conv_taps.reshape(-1), grad_bias_out, grad_gain_one,
        grad_shift_one, grad_bias_up, grad_bias_down, grad_gain_two, grad_shift_two,
    ]
    sizes = [piece.shape[0] for piece in small]
    flat = jnp.concatenate(small)
    lanes = -(-flat.shape[0] // 1024) * 8
    flat = jnp.pad(flat, (0, lanes * 128 - flat.shape[0])).reshape(lanes, 128)
    late = [
        (grad_w_qkv[:, i * width : (i + 1) * width].astype(BF), stages(ORDERS[i]), 0)
        for i in range(3)
    ]
    late = [advance(state, 1) for state in late]
    mark_back = seq_quarter(mark_back, add_join)
    for axis, bit in small_steps():
        flat = flat + swap(flat, axis, bit)
    (mark_back, flat), late = tied((mark_back, flat), late)
    late = [advance(state, 1) for state in late]
    mark_back = seq_whole(mark_back)
    mark_back, late = tied(mark_back, late)
    sum_qkv = [advance(state, 64)[0].astype(F32) for state in late]
    sum_w_down, sum_w_up, sum_w_out = [
        advance(state, 64)[0].astype(F32) for state in (down, up, out)
    ]
    sum_w_qkv = jnp.concatenate(sum_qkv, axis=1)
    flat = flat.reshape(-1)
    pieces = []
    at = 0
    for length in sizes:
        pieces.append(flat[at : at + length])
        at += length
    grad_input = (
        grad_one
        + lax.dot_general(grad_projected, w_qkv, cols_in, preferred_element_type=F32)
        + lax.dot_general(onehot, mark_back, rows_in, preferred_element_type=F32)
    )
    return (
        result[None], grad_input[None], sum_w_qkv, pieces[0], pieces[1],
        pieces[2].reshape(heads, tap_count), sum_w_out, pieces[3], pieces[4], pieces[5],
        sum_w_up, pieces[6], sum_w_down, pieces[7], pieces[8], pieces[9],
    )


def solution(mesh):
    whole, tokens = P(), P("row", "seq", None)
    return jax.shard_map(
        per_device,
        mesh=mesh,
        in_specs=(tokens, P("row", None)) + (whole,) * 14 + (tokens,),
        out_specs=(tokens, tokens) + (whole,) * 14,
        check_vma=False,
    )
```

```python
import math

import jax
import jax.numpy as jnp
from jax import lax
from jax.experimental import pallas as pl
from jax.experimental.pallas import tpu as pltpu
from jax.sharding import PartitionSpec as P

LAND = 64
NS_ITERS = 6
HIGH = lax.Precision.HIGHEST
NEGATIVE = -1e30
BF = jnp.bfloat16
F32 = jnp.float32

BLOCK = 256
GROUP = 256
SUB = 128
TAPS = 33


def swap(array, axis, bit):
    count = lax.axis_size(axis)
    return lax.ppermute(array, axis, [(i, i ^ bit) for i in range(count)])


def add_parts(parts):
    total = parts[0].astype(F32)
    for part in parts[1:]:
        total = total + part.astype(F32)
    return total


def halves(array, bit):
    rows = array.shape[0] // 2
    side = (lax.axis_index("seq") // bit) % 2
    mine = lax.dynamic_slice_in_dim(array, side * rows, rows, 0)
    other = lax.dynamic_slice_in_dim(array, (1 - side) * rows, rows, 0)
    return mine, other


def seq_quarter(array, join):
    bits = [1 << i for i in range(lax.axis_size("seq").bit_length() - 1)]
    for bit in bits[:2]:
        mine, other = halves(array, bit)
        array = join(mine, swap(other, "seq", bit))
    for bit in bits[2:]:
        array = join(array, swap(array, "seq", bit))
    return array


def paired(array, axis, bit, dim):
    other = swap(array, axis, bit)
    side = (lax.axis_index(axis) // bit) % 2
    return jnp.where(
        side == 0,
        jnp.concatenate([array, other], dim),
        jnp.concatenate([other, array], dim),
    )


def seq_whole(array):
    return paired(paired(array, "seq", 2, 0), "seq", 1, 0)


def add_join(first, second):
    return (first.astype(F32) + second.astype(F32)).astype(BF)


def stages(order):
    row = [("row", 1 << i) for i in range(lax.axis_size("row").bit_length() - 1)]
    seq = [[("seq", 1 << i)] for i in range(lax.axis_size("seq").bit_length() - 1)]
    named = {"core": seq[0], "row": row, "near": seq[1], "far": seq[2], "rest": sum(seq[3:], [])}
    return sum([named[name] for name in ("core",) + order + ("rest",)], [])


ORDERS = (("row", "far", "near"), ("near", "row", "far"), ("far", "near", "row"))


def advance(state, steps):
    held, plan, done = state
    for step in range(done, min(done + steps, 2 * len(plan))):
        if step < len(plan):
            axis, bit = plan[step]
            half = held.shape[0] // 2
            side = (lax.axis_index(axis) // bit) % 2
            mine = lax.dynamic_slice_in_dim(held, side * half, half, 0)
            other = lax.dynamic_slice_in_dim(held, (1 - side) * half, half, 0)
            held = mine.astype(F32) + swap(other.astype(BF), axis, bit).astype(F32)
            held = held.astype(BF)
        else:
            axis, bit = plan[2 * len(plan) - 1 - step]
            held = paired(held, axis, bit, 0)
    return held, plan, min(done + steps, 2 * len(plan))


def tied(values, states):
    values, helds = lax.optimization_barrier((values, [state[0] for state in states]))
    return values, [(held,) + state[1:] for held, state in zip(helds, states)]


def extended(cells, width, rows):
    count = lax.axis_size("seq")
    head = cells[:width]
    tail = cells[-width:]
    return jnp.concatenate(
        [
            lax.ppermute(tail, "seq", [(i, i + 1) for i in range(count - 1)]),
            cells,
            lax.ppermute(head, "seq", [(i + 1, i) for i in range(count - 1)]),
            jnp.zeros((rows - cells.shape[0] - 2 * width, cells.shape[1]), cells.dtype),
        ],
        axis=0,
    )


def dot_nn(a, b):
    return jnp.dot(a, b, preferred_element_type=F32)


def dot_nt(a, b):
    return lax.dot_general(a, b, (((1,), (1,)), ((), ())), preferred_element_type=F32)


def dot_tn(a, b):
    return lax.dot_general(a, b, (((0,), (0,)), ((), ())), preferred_element_type=F32)


def iota(shape, dim):
    return lax.broadcasted_iota(jnp.int32, shape, dim)


def spread(block):
    rows = block.shape[0]
    tall = jnp.concatenate([block] * 4, axis=0).astype(F32)
    shape = (4 * rows, GROUP)
    keep = iota(shape, 0) // rows == iota(shape, 1) // LAND
    return jnp.where(keep, tall, 0.0).astype(BF)


def gathered(square):
    rows = square.shape[0] // 4
    lane = iota((rows, GROUP), 1) // LAND
    out = square[:rows]
    for head in range(1, 4):
        out = jnp.where(lane == head, square[head * rows : (head + 1) * rows], out)
    return out


def by_head(columns, first, shape):
    lane = iota(shape, 1)
    out = jnp.zeros(shape, F32)
    for head, column in enumerate(columns):
        out = jnp.where((lane % 16 == first + head) & (lane < 48), column, out)
    return out


def split_three(cells):
    lane = iota(cells.shape, 1)
    high = cells.astype(BF).astype(F32)
    mid = (cells - high).astype(BF).astype(F32)
    low = cells - high - mid
    return jnp.where(lane < 16, high, jnp.where(lane < 32, mid, low)).astype(BF)


def merge_three(cells):
    cells = cells.astype(F32)
    return cells + pltpu.roll(cells, 112, 1) + pltpu.roll(cells, 96, 1)


def head_lanes(heads, width):
    return (iota((128, width), 0) == iota((128, width), 1) // LAND).astype(F32)


def doc_of(places, bounds, docs):
    out = (places >= bounds[2 * docs - 1]).astype(jnp.int32)
    for doc in range(docs):
        out = out + (places >= bounds[doc]).astype(jnp.int32)
    return out


def landmark_kernel(docs, scale, bounds, mq_ref, k_ref, v_ref, out_ref, max_s, sum_s, acc_s):
    tokens, width = k_ref.shape
    groups = width // GROUP
    heads = width // LAND
    out_ref[:, :width] = jnp.zeros((docs * LAND, width), BF)
    empty = jnp.full((docs * LAND, 128), NEGATIVE, F32)
    out_ref[:, width:] = jnp.where(iota(empty.shape, 1) < 48, split_three(empty).astype(F32), 0.0).astype(BF)
    for doc in range(docs):
        low = jnp.clip(bounds[doc], 0, tokens)
        high = jnp.clip(bounds[docs + doc], 0, tokens)
        rows = slice(doc * LAND, (doc + 1) * LAND)

        @pl.when(high > low)
        def _():
            max_s[...] = jnp.full(max_s.shape, NEGATIVE, F32)
            sum_s[...] = jnp.zeros(sum_s.shape, F32)
            acc_s[...] = jnp.zeros(acc_s.shape, F32)
            wide = [
                spread(mq_ref[rows, g * GROUP : (g + 1) * GROUP]) for g in range(groups)
            ]

            def step(block, carry):
                first = pl.multiple_of(block * BLOCK, BLOCK)
                at = pl.ds(first, BLOCK)
                place = iota((1, BLOCK), 1) + first
                valid = (place >= low) & (place < high)
                for g in range(groups):
                    cols = slice(g * GROUP, (g + 1) * GROUP)
                    scores = dot_nt(wide[g], k_ref[at, cols]) * scale
                    scores = jnp.where(valid, scores, NEGATIVE)
                    old = max_s[cols, :1]
                    top = jnp.maximum(old, jnp.max(scores, axis=1, keepdims=True))
                    weights = jnp.exp(scores - top)
                    shrink = jnp.exp(old - top)
                    sums = sum_s[cols, :1] * shrink + jnp.sum(weights, axis=1, keepdims=True)
                    acc_s[cols, :] = acc_s[cols, :] * shrink + dot_nn(
                        weights.astype(BF), v_ref[at, cols]
                    )
                    max_s[cols, :] = jnp.broadcast_to(top, (GROUP, 128))
                    sum_s[cols, :] = jnp.broadcast_to(sums, (GROUP, 128))
                return carry

            lax.fori_loop(low // BLOCK, (high + BLOCK - 1) // BLOCK, step, 0)
            columns = []
            for g in range(groups):
                cols = slice(g * GROUP, (g + 1) * GROUP)
                sums = sum_s[cols, :1]
                out_ref[rows, cols] = gathered(acc_s[cols, :] / sums).astype(BF)
                level = max_s[cols, :1] + jnp.log(sums)
                columns += [level[h * LAND : (h + 1) * LAND] for h in range(4)]
            out_ref[rows, width:] = split_three(by_head(columns, 0, (LAND, 128)))


def join_kernel(a_ref, b_ref, out_ref):
    width = a_ref.shape[1] - 128
    heads = width // LAND
    first, second = merge_three(a_ref[:, width:]), merge_three(b_ref[:, width:])
    lane = iota(first.shape, 1)
    first = jnp.where(lane < heads, first, 0.0)
    second = jnp.where(lane < heads, second, 0.0)
    top = jnp.maximum(first, second)
    exp_a, exp_b = jnp.exp(first - top), jnp.exp(second - top)
    both = exp_a + exp_b
    level = top + jnp.log(both)
    pick = head_lanes(heads, width)
    share_a = jnp.dot(exp_a / both, pick, precision=HIGH, preferred_element_type=F32)
    share_b = jnp.dot(exp_b / both, pick, precision=HIGH, preferred_element_type=F32)
    joined = a_ref[:, :width].astype(F32) * share_a + b_ref[:, :width].astype(F32) * share_b
    out_ref[:, :width] = joined.astype(BF)
    level = jnp.where(lane < heads, level, 0.0)
    level = level + pltpu.roll(level, 16, 1) + pltpu.roll(level, 32, 1)
    out_ref[:, width:] = split_three(level)


def join(first, second):
    return pl.pallas_call(
        join_kernel, out_shape=jax.ShapeDtypeStruct(first.shape, BF), name="join"
    )(first, second)


def mix_kernel(inv_ref, stat_ref, mix_ref):
    width = stat_ref.shape[1] - 128
    for g in range(width // GROUP):
        cols = slice(g * GROUP, (g + 1) * GROUP)
        mix_ref[:, cols] = dot_nn(inv_ref[:, cols], spread(stat_ref[:, cols])).astype(BF)
    mix_ref[:, width:] = stat_ref[:, width:]


def mix_back_kernel(inv_ref, stat_ref, grad_ref, out_ref):
    width = stat_ref.shape[1] - 128
    columns = []
    for g in range(width // GROUP):
        cols = slice(g * GROUP, (g + 1) * GROUP)
        grad = gathered(dot_tn(inv_ref[:, cols], grad_ref[:, cols]))
        out_ref[:, cols] = grad.astype(BF)
        product = grad * stat_ref[:, cols].astype(F32)
        lane = iota(product.shape, 1) // LAND
        for h in range(4):
            columns.append(jnp.sum(jnp.where(lane == h, product, 0.0), axis=1, keepdims=True))
    out_ref[:, width:] = split_three(by_head(columns, 0, (LAND, 128)))


def make_band(taps_ref, band_s):
    for head in range(taps_ref.shape[0]):
        row = jnp.broadcast_to(taps_ref[head : head + 1, :], (SUB, GROUP))
        band_s[head * SUB : (head + 1) * SUB, :] = pltpu.roll(row, 0, 1, stride=1, stride_axis=0).astype(BF)


def same_doc(first, bounds, docs, radius):
    rows = iota((SUB, GROUP), 0) + first
    cols = iota((SUB, GROUP), 1) + (first - radius)
    return doc_of(rows, bounds, docs) == doc_of(cols, bounds, docs)


def token_kernel(
    docs, scale, bounds, q_ref, v_ref, mk_ref, mix_ref, taps_ref, mixed_ref, probs_ref, band_s, sum_s
):
    width = q_ref.shape[1]
    groups = width // GROUP
    radius = (TAPS - 1) // 2
    first = pl.program_id(0) * BLOCK

    @pl.when(pl.program_id(0) == 0)
    def _():
        make_band(taps_ref, band_s)

    for sub in range(BLOCK // SUB):
        start = pl.multiple_of(first + sub * SUB, SUB)
        same = same_doc(start, bounds, docs, radius)
        same = jnp.where(jnp.concatenate([same] * 4, axis=0), 1.0, 0.0).astype(BF)
        for g in range(groups):
            cols = slice(g * GROUP, (g + 1) * GROUP)
            band = band_s[g * 4 * SUB : (g + 1) * 4 * SUB, :] * same
            res = dot_nn(band, v_ref[pl.ds(start, GROUP), cols])
            sum_s[sub * SUB : (sub + 1) * SUB, cols] = gathered(res)
    probs_ref[...] = jnp.zeros(probs_ref.shape, BF)
    for doc in range(docs):
        low, high = bounds[doc], bounds[docs + doc]
        rows = slice(doc * LAND, (doc + 1) * LAND)

        @pl.when((high > first) & (low < first + BLOCK))
        def _():
            place = iota((1, BLOCK), 1) + first
            valid = (place >= low) & (place < high)
            for g in range(groups):
                cols = slice(g * GROUP, (g + 1) * GROUP)
                scores = dot_nt(spread(mk_ref[rows, cols]), q_ref[:, cols]) * scale
                scores = scores.reshape(4, LAND, BLOCK)
                weights = jnp.exp(scores - jnp.max(scores, axis=1, keepdims=True))
                probs = weights / jnp.sum(weights, axis=1, keepdims=True)
                probs = jnp.where(valid, probs.reshape(GROUP, BLOCK), 0.0).astype(BF)
                probs_ref[cols, :] = probs_ref[cols, :] + probs
                sum_s[:, cols] = sum_s[:, cols] + dot_tn(probs, spread(mix_ref[rows, cols]))

    mixed_ref[...] = sum_s[...].astype(BF)


def token_back_kernel(
    docs, scale, bounds, q_ref, gm_ref, probs_ref, mk_ref, mix_ref, gq_ref, gmix_ref, gmk_ref, gq_s
):
    width = q_ref.shape[1]
    groups = width // GROUP
    first = pl.program_id(0) * BLOCK

    @pl.when(pl.program_id(0) == 0)
    def _():
        gmix_ref[...] = jnp.zeros(gmix_ref.shape, F32)
        gmk_ref[...] = jnp.zeros(gmk_ref.shape, F32)

    gq_s[...] = jnp.zeros(gq_s.shape, F32)
    for doc in range(docs):
        low, high = bounds[doc], bounds[docs + doc]
        rows = slice(doc * LAND, (doc + 1) * LAND)

        @pl.when((high > first) & (low < first + BLOCK))
        def _():
            place = iota((1, BLOCK), 1) + first
            valid = (place >= low) & (place < high)
            for g in range(groups):
                cols = slice(g * GROUP, (g + 1) * GROUP)
                probs = jnp.where(valid, probs_ref[cols, :].astype(F32), 0.0)
                gmix_ref[rows, cols] += gathered(dot_nn(probs.astype(BF), gm_ref[:, cols]))
                grad = dot_nt(spread(mix_ref[rows, cols]), gm_ref[:, cols])
                heavy = (probs * grad).reshape(4, LAND, BLOCK)
                shared = probs.reshape(4, LAND, BLOCK) * jnp.sum(heavy, axis=1, keepdims=True)
                grad = ((heavy - shared).reshape(GROUP, BLOCK) * scale).astype(BF)
                gmk_ref[rows, cols] += gathered(dot_nn(grad, q_ref[:, cols]))
                gq_s[:, cols] += dot_tn(grad, spread(mk_ref[rows, cols]))

    gq_ref[...] = gq_s[...].astype(BF)


def conv_back_kernel(docs, bounds, gm_ref, v_ref, taps_ref, out_ref, prod_ref, band_s):
    width = gm_ref.shape[1]
    groups = width // GROUP
    radius = (TAPS - 1) // 2
    first = pl.program_id(0) * BLOCK

    @pl.when(pl.program_id(0) == 0)
    def _():
        make_band(taps_ref, band_s)
        prod_ref[...] = jnp.zeros(prod_ref.shape, F32)

    for sub in range(BLOCK // SUB):
        start = pl.multiple_of(first + sub * SUB, SUB)
        same = same_doc(start, bounds, docs, radius)
        same = jnp.where(jnp.concatenate([same] * 4, axis=0), 1.0, 0.0)
        for g in range(groups):
            cols = slice(g * GROUP, (g + 1) * GROUP)
            tall = slice(g * 4 * SUB, (g + 1) * 4 * SUB)
            band = band_s[tall, :] * same.astype(BF)
            res = dot_nn(band, gm_ref[pl.ds(start, GROUP), cols])
            out_ref[sub * SUB : (sub + 1) * SUB, cols] = gathered(res)
            own = gm_ref[pl.ds(pl.multiple_of(start + radius, 16), SUB), cols]
            product = dot_nt(spread(own), v_ref[pl.ds(start, GROUP), cols])
            prod_ref[tall, :] += product * same


def landmark_back_kernel(
    docs, scale, bounds, k_ref, v_ref, conv_ref, mq_ref, grad_ref, level_ref, dots_ref,
    gk_ref, gv_ref, gmq_ref, gk_s, gv_s,
):
    width = k_ref.shape[1]
    groups = width // GROUP
    first = pl.program_id(0) * BLOCK

    @pl.when(pl.program_id(0) == 0)
    def _():
        gmq_ref[...] = jnp.zeros(gmq_ref.shape, F32)

    gk_s[...] = jnp.zeros(gk_s.shape, F32)
    gv_s[...] = conv_ref[...]
    for doc in range(docs):
        low, high = bounds[doc], bounds[docs + doc]
        rows = slice(doc * LAND, (doc + 1) * LAND)

        @pl.when((high > first) & (low < first + BLOCK))
        def _():
            place = iota((1, BLOCK), 1) + first
            valid = (place >= low) & (place < high)

            level, dots = merge_three(level_ref[rows, :]), merge_three(dots_ref[rows, :])

            def column(lanes, g):
                return jnp.concatenate(
                    [lanes[:, 4 * g + h : 4 * g + h + 1] for h in range(4)], axis=0
                )

            for g in range(groups):
                cols = slice(g * GROUP, (g + 1) * GROUP)
                wide_q, wide_g = spread(mq_ref[rows, cols]), spread(grad_ref[rows, cols])
                scores = dot_nt(wide_q, k_ref[:, cols]) * scale - column(level, g)
                probs = jnp.exp(jnp.where(valid, scores, NEGATIVE))
                grad = dot_nt(wide_g, v_ref[:, cols]) - column(dots, g)
                grad = (probs * grad * scale).astype(BF)
                gv_s[:, cols] += dot_tn(probs.astype(BF), wide_g)
                gk_s[:, cols] += dot_tn(grad, wide_q)
                gmq_ref[rows, cols] += gathered(dot_nn(grad, k_ref[:, cols]))

    gk_ref[...] = gk_s[...].astype(BF)
    gv_ref[...] = gv_s[...].astype(BF)


def gelu_both(upper):
    tangent = jnp.tanh(0.7978845608028654 * (upper + 0.044715 * upper * upper * upper))
    inner_slope = 0.7978845608028654 * (1.0 + 3.0 * 0.044715 * upper * upper)
    active = 0.5 * upper * (1.0 + tangent)
    slope = 0.5 * (1.0 + tangent) + 0.5 * upper * (1.0 - tangent * tangent) * inner_slope
    return active, slope


def normalize(residual):
    row_mean = jnp.mean(residual, axis=-1, keepdims=True)
    centered = residual - row_mean
    row_var = jnp.mean(centered * centered, axis=-1, keepdims=True)
    inverse_dev = lax.rsqrt(row_var + 1e-05)
    return (centered * inverse_dev, inverse_dev)


def norm_back(grad_normed, normed, inverse_dev):
    return inverse_dev * (
        grad_normed
        - jnp.mean(grad_normed, axis=-1, keepdims=True)
        - normed * jnp.mean(grad_normed * normed, axis=-1, keepdims=True)
    )


def pinv_kernel(queries, key_rows, score_scale):
    scores = jnp.einsum("pie,pje->pij", queries, key_rows, precision=HIGH) * score_scale
    row_max = jnp.max(scores, axis=-1, keepdims=True)
    weights = jnp.exp(scores - row_max)
    kernel = weights / jnp.sum(weights, axis=-1, keepdims=True)
    column_max = jnp.max(jnp.sum(kernel, axis=1), axis=-1)
    inverse = jnp.swapaxes(kernel, -1, -2) / column_max[:, None, None]
    identity = jnp.eye(LAND, dtype=F32)
    for sweep in range(NS_ITERS):
        product = jnp.matmul(kernel, inverse, precision=HIGH)
        bracket = 7.0 * identity - product
        bracket = 15.0 * identity - jnp.matmul(product, bracket, precision=HIGH)
        bracket = 13.0 * identity - jnp.matmul(product, bracket, precision=HIGH)
        inverse = 0.25 * jnp.matmul(inverse, bracket, precision=HIGH)
    return inverse


def per_device(
    inputs, doc_lengths, w_qkv, bias_q, bias_v, conv_taps, w_out, bias_out, norm1_gain,
    norm1_bias, w_up, bias_up, w_down, bias_down, norm2_gain, norm2_bias, cotangent,
):
    tokens = inputs[0]
    tok_count, width = tokens.shape
    heads, tap_count = conv_taps.shape
    size = width // heads
    radius = (tap_count - 1) // 2
    lengths = doc_lengths[0]
    docs = lengths.shape[0]
    mark_count = docs * LAND
    scale = 1.0 / math.sqrt(size)
    seq_count = lax.axis_size("seq")
    me = lax.axis_index("seq")
    row_first = me * tok_count
    ends = jnp.cumsum(lengths)
    starts = ends - lengths
    bounds = (jnp.concatenate([starts, ends]) - row_first).astype(jnp.int32)
    within = jnp.arange(LAND + 1, dtype=jnp.int32)
    edges = starts[:, None] + (within[None, :] * lengths[:, None] + LAND - 1) // LAND
    mark_low = edges[:, :-1].reshape(mark_count, 1)
    mark_high = edges[:, 1:].reshape(mark_count, 1)
    counts = (mark_high - mark_low).astype(F32)
    places = row_first + jnp.arange(tok_count, dtype=jnp.int32)[None, :]
    onehot = ((places >= mark_low) & (places < mark_high)).astype(BF)
    rows_in = (((0,), (0,)), ((), ()))
    cols_in = (((1,), (1,)), ((), ()))
    blocks = tok_count // BLOCK
    window_rows = tok_count + GROUP - SUB
    smem = pl.BlockSpec(memory_space=pltpu.SMEM)
    params = pltpu.CompilerParams(vmem_limit_bytes=40 * 1024 * 1024)
    tok_spec = pl.BlockSpec((BLOCK, width), lambda i: (i, 0))

    def part(col):
        return pl.BlockSpec((BLOCK, width), lambda i: (i, col))

    def fixed(*shape):
        return pl.BlockSpec(shape, lambda i: (0,) * len(shape))

    def shaped(shape, dtype):
        return jax.ShapeDtypeStruct(shape, dtype)

    means = jnp.dot(onehot, tokens, preferred_element_type=F32) / counts
    mean_in = seq_whole(seq_quarter(means.astype(BF), add_join))
    marks = jnp.dot(mean_in, w_qkv[:, : 2 * width], preferred_element_type=F32)
    mark_q = (marks[:, :width] + bias_q).astype(BF)
    mark_k = marks[:, width:].astype(BF)

    bias = jnp.concatenate([bias_q, jnp.zeros_like(bias_q), bias_v])
    qkv = (jnp.dot(tokens, w_qkv, preferred_element_type=F32) + bias).astype(BF)
    value_ext = extended(qkv[:, 2 * width :], radius, window_rows)
    value_ext, mark_q, mark_k = lax.optimization_barrier((value_ext, mark_q, mark_k))

    def one_col(col):
        return pl.BlockSpec((tok_count, width), lambda i: (0, col))

    stats = pl.pallas_call(
        lambda *refs: landmark_kernel(docs, scale, *refs),
        grid=(1,),
        in_specs=[smem, fixed(mark_count, width), one_col(1), one_col(2)],
        out_specs=fixed(mark_count, width + 128),
        out_shape=shaped((mark_count, width + 128), BF),
        scratch_shapes=[
            pltpu.VMEM((width, 128), F32), pltpu.VMEM((width, 128), F32),
            pltpu.VMEM((width, GROUP), F32),
        ],
        compiler_params=params,
        name="landmark",
    )(bounds, mark_q, qkv, qkv)
    far_count = seq_count // 4
    own_count = -(-heads // far_count)
    own_doc = (me % 2) * 2 + (me // 2) % 2
    own_at = (me // 4) * own_count * size
    spare = far_count * own_count * size - width

    def own_heads(array):
        array = jnp.pad(array, ((0, 0), (0, spare)))
        array = lax.dynamic_slice_in_dim(array, own_at, own_count * size, 1)
        return array.reshape(LAND, own_count, size).transpose(1, 0, 2)

    def of_doc(array):
        return lax.dynamic_slice_in_dim(array, own_doc * LAND, LAND, 0)

    own_inverse, inverse_pullback = jax.vjp(
        lambda a, b: pinv_kernel(a, b, scale),
        own_heads(of_doc(mark_q)).astype(F32),
        own_heads(of_doc(mark_k)).astype(F32),
    )
    inverse = own_inverse.transpose(1, 0, 2).reshape(LAND, own_count * size).astype(BF)
    for bit in (1, 2):
        mine, other = halves(stats, bit)
        stats = join(mine, swap(other, "seq", bit))
    for i in range(2, seq_count.bit_length() - 1):
        other = swap(jnp.concatenate([stats, inverse], 1), "seq", 1 << i)
        stats = join(stats, other[:, : width + 128])
        other = other[:, width + 128 :]
        inverse = jnp.where(
            (me >> i) % 2 == 0,
            jnp.concatenate([inverse, other], 1),
            jnp.concatenate([other, inverse], 1),
        )
    inverse = inverse[:, :width]
    mix = pl.pallas_call(
        mix_kernel, out_shape=shaped((LAND, width + 128), BF), name="mix"
    )(inverse, stats)
    mix = seq_whole(mix)

    taps = jnp.pad(conv_taps, ((0, 0), (0, GROUP - tap_count)))
    mark_spec = fixed(mark_count, width)
    mixed, probs = pl.pallas_call(
        lambda *refs: token_kernel(docs, scale, *refs),
        grid=(blocks,),
        in_specs=[
            smem, part(0), fixed(window_rows, width), mark_spec, mark_spec, fixed(heads, GROUP)
        ],
        out_specs=(tok_spec, pl.BlockSpec((width, BLOCK), lambda i: (0, i))),
        out_shape=(shaped((tok_count, width), BF), shaped((width, tok_count), BF)),
        scratch_shapes=[pltpu.VMEM((heads * SUB, GROUP), BF), pltpu.VMEM((BLOCK, width), F32)],
        compiler_params=params,
        name="token",
    )(bounds, qkv, value_ext, mark_k, mix, taps)

    attended = jnp.dot(mixed, w_out, preferred_element_type=F32) + bias_out
    norm_one, inverse_one = normalize(tokens.astype(F32) + attended)
    hidden_one = norm_one * norm1_gain + norm1_bias
    hidden_low = hidden_one.astype(BF)
    upper = jnp.dot(hidden_low, w_up, preferred_element_type=F32) + bias_up
    active, slope = gelu_both(upper)
    active = active.astype(BF)
    lowered = jnp.dot(active, w_down, preferred_element_type=F32) + bias_down
    norm_two, inverse_two = normalize(hidden_one + lowered)
    result = norm_two * norm2_gain + norm2_bias
    upstream = cotangent[0].astype(F32)
    grad_gain_two = jnp.sum(upstream * norm_two, axis=0)
    grad_shift_two = jnp.sum(upstream, axis=0)
    grad_two = norm_back(upstream * norm2_gain, norm_two, inverse_two)
    grad_low_two = grad_two.astype(BF)
    grad_bias_down = jnp.sum(grad_low_two.astype(F32), axis=0)
    grad_w_down = lax.dot_general(active, grad_low_two, rows_in, preferred_element_type=F32)
    grad_active = lax.dot_general(grad_low_two, w_down, cols_in, preferred_element_type=F32)
    grad_upper = (grad_active * slope).astype(BF)
    grad_bias_up = jnp.sum(grad_upper.astype(F32), axis=0)
    grad_w_up = lax.dot_general(hidden_low, grad_upper, rows_in, preferred_element_type=F32)
    sum_w_down, sum_w_up = lax.psum(
        (grad_w_down.astype(BF), grad_w_up.astype(BF)), ("row", "seq")
    )
    grad_hidden = grad_two + lax.dot_general(
        grad_upper, w_up, cols_in, preferred_element_type=F32
    )
    grad_gain_one = jnp.sum(grad_hidden * norm_one, axis=0)
    grad_shift_one = jnp.sum(grad_hidden, axis=0)
    grad_one = norm_back(grad_hidden * norm1_gain, norm_one, inverse_one)
    grad_low_one = grad_one.astype(BF)
    grad_bias_out = jnp.sum(grad_low_one.astype(F32), axis=0)
    grad_w_out = lax.dot_general(mixed, grad_low_one, rows_in, preferred_element_type=F32)
    grad_mixed = lax.dot_general(
        grad_low_one, w_out, cols_in, preferred_element_type=F32
    ).astype(BF)

    grad_queries, grad_mix, grad_mk = pl.pallas_call(
        lambda *refs: token_back_kernel(docs, scale, *refs),
        grid=(blocks,),
        in_specs=[
            smem, part(0), tok_spec, pl.BlockSpec((width, BLOCK), lambda i: (0, i)), mark_spec,
            mark_spec,
        ],
        out_specs=(tok_spec, mark_spec, mark_spec),
        out_shape=(
            shaped((tok_count, width), BF), shaped((mark_count, width), F32),
            shaped((mark_count, width), F32),
        ),
        scratch_shapes=[pltpu.VMEM((BLOCK, width), F32)],
        compiler_params=params,
        name="token_back",
    )(bounds, qkv, grad_mixed, probs, mark_k, mix)
    grad_mix = seq_quarter(grad_mix.astype(BF), add_join)

    grad_ext = extended(grad_mixed, radius, window_rows)
    grad_conv, products = pl.pallas_call(
        lambda *refs: conv_back_kernel(docs, *refs),
        grid=(blocks,),
        in_specs=[
            smem, fixed(window_rows, width), fixed(window_rows, width), fixed(heads, GROUP)
        ],
        out_specs=(tok_spec, fixed(heads * SUB, GROUP)),
        out_shape=(shaped((tok_count, width), F32), shaped((heads * SUB, GROUP), F32)),
        scratch_shapes=[pltpu.VMEM((heads * SUB, GROUP), BF)],
        compiler_params=params,
        name="conv_back",
    )(bounds, grad_ext, value_ext, jnp.pad(conv_taps[:, ::-1], ((0, 0), (0, GROUP - tap_count))))
    reach = SUB + tap_count - 1
    products = products.reshape(heads, SUB, GROUP)[:, :, :reach].reshape(heads, SUB * reach)
    products = jnp.pad(products, ((0, 0), (0, SUB))).reshape(heads, SUB, reach + 1)
    grad_conv_taps = jnp.sum(products, axis=1)[:, :tap_count]

    grad_avg = pl.pallas_call(
        mix_back_kernel, out_shape=shaped((LAND, width + 128), BF), name="mix_back"
    )(inverse, stats, grad_mix)
    grad_avg = seq_whole(grad_avg)
    grad_inverse = jnp.einsum(
        "pie,pje->pij", own_heads(grad_mix), own_heads(stats[:, :width]),
        preferred_element_type=F32,
    )
    grad_mq_small, grad_mk_small = inverse_pullback(grad_inverse)
    lane_spec = pl.BlockSpec((mark_count, 128), lambda i: (0, width // 128))
    grad_keys, grad_values, grad_mq = pl.pallas_call(
        lambda *refs: landmark_back_kernel(docs, scale, *refs),
        grid=(blocks,),
        in_specs=[
            smem, part(1), part(2), tok_spec, mark_spec, mark_spec, lane_spec, lane_spec
        ],
        out_specs=(tok_spec, tok_spec, mark_spec),
        out_shape=(
            shaped((tok_count, width), BF), shaped((tok_count, width), BF),
            shaped((mark_count, width), F32),
        ),
        scratch_shapes=[pltpu.VMEM((BLOCK, width), F32), pltpu.VMEM((BLOCK, width), F32)],
        compiler_params=params,
        name="landmark_back",
    )(bounds, qkv, qkv, grad_conv, mark_q, grad_avg, mix, grad_avg)

    def placed(array):
        array = array.transpose(1, 0, 2).reshape(LAND, own_count * size)
        array = lax.dynamic_update_slice_in_dim(
            jnp.zeros((LAND, width + spare), F32), array, own_at, 1
        )[:, :width]
        return lax.dynamic_update_slice_in_dim(
            jnp.zeros((mark_count, width), F32), array, own_doc * LAND, 0
        )

    grad_mq = grad_mq + placed(grad_mq_small)
    grad_mk = grad_mk + placed(grad_mk_small)
    grad_marks = jnp.concatenate([grad_mq, grad_mk], axis=1).astype(BF)
    mark_back = lax.dot_general(
        grad_marks, w_qkv[:, : 2 * width], cols_in, preferred_element_type=F32
    ) / counts
    mark_back = mark_back.astype(BF)

    grad_bias_q = jnp.sum(grad_queries.astype(F32), axis=0) + jnp.sum(grad_mq, axis=0)
    grad_bias_v = jnp.sum(grad_values.astype(F32), axis=0)
    grad_projected = jnp.concatenate([grad_queries, grad_keys, grad_values], axis=1)
    grad_w_qkv = lax.dot_general(tokens, grad_projected, rows_in, preferred_element_type=F32)
    grad_w_marks = lax.dot_general(mean_in, grad_marks, rows_in, preferred_element_type=F32)
    grad_w_qkv = (grad_w_qkv + jnp.pad(grad_w_marks, ((0, 0), (0, width)))).astype(BF)
    small = [
        grad_bias_q, grad_bias_v, grad_conv_taps.reshape(-1), grad_bias_out, grad_gain_one,
        grad_shift_one, grad_bias_up, grad_bias_down, grad_gain_two, grad_shift_two,
    ]
    sizes = [piece.shape[0] for piece in small]
    flat = jnp.concatenate(small)
    third = width // 3
    flat = jnp.pad(flat, (0, third * width - flat.shape[0])).reshape(third, width).astype(BF)
    w_q, w_k, w_v = [grad_w_qkv[:, i * width : (i + 1) * width] for i in range(3)]
    late = [
        jnp.concatenate([grad_w_out.astype(BF), w_q[: 2 * third]], 0),
        jnp.concatenate([w_q[2 * third :], w_k], 0),
        jnp.concatenate([w_v, flat], 0),
    ]
    late = [advance((array, stages(order), 0), 1) for array, order in zip(late, ORDERS)]
    mark_back = seq_quarter(mark_back, add_join)
    mark_back, late = tied(mark_back, late)
    late = [advance(state, 1) for state in late]
    mark_back = seq_whole(mark_back)
    mark_back, late = tied(mark_back, late)
    first, second, last = [advance(state, 64)[0].astype(F32) for state in late]
    sum_w_out = first[:width]
    sum_w_qkv = jnp.concatenate(
        [
            jnp.concatenate([first[width:], second[:third]], 0),
            second[third:],
            last[:width],
        ],
        axis=1,
    )
    sum_w_down, sum_w_up = sum_w_down.astype(F32), sum_w_up.astype(F32)
    flat = last[width:].reshape(-1)
    pieces = []
    at = 0
    for length in sizes:
        pieces.append(flat[at : at + length])
        at += length
    grad_input = (
        grad_one
        + lax.dot_general(grad_projected, w_qkv, cols_in, preferred_element_type=F32)
        + lax.dot_general(onehot, mark_back, rows_in, preferred_element_type=F32)
    )
    return (
        result[None], grad_input[None], sum_w_qkv, pieces[0], pieces[1],
        pieces[2].reshape(heads, tap_count), sum_w_out, pieces[3], pieces[4], pieces[5],
        sum_w_up, pieces[6], sum_w_down, pieces[7], pieces[8], pieces[9],
    )


def solution(mesh):
    whole, tokens = P(), P("row", "seq", None)
    return jax.shard_map(
        per_device,
        mesh=mesh,
        in_specs=(tokens, P("row", None)) + (whole,) * 14 + (tokens,),
        out_specs=(tokens, tokens) + (whole,) * 14,
        check_vma=False,
    )
```

```python
import math

import jax
import jax.numpy as jnp
from jax import lax
from jax.experimental import pallas as pl
from jax.experimental.pallas import tpu as pltpu
from jax.sharding import PartitionSpec as P

LAND = 64
NS_ITERS = 6
HIGH = lax.Precision.HIGHEST
NEGATIVE = -1e30
BF = jnp.bfloat16
F32 = jnp.float32

BLOCK = 256
GROUP = 256
SUB = 128
TAPS = 33
FFN_BLOCK = 256


def swap(array, axis, bit):
    count = lax.axis_size(axis)
    return lax.ppermute(array, axis, [(i, i ^ bit) for i in range(count)])


def add_parts(parts):
    total = parts[0].astype(F32)
    for part in parts[1:]:
        total = total + part.astype(F32)
    return total


def halves(array, bit):
    rows = array.shape[0] // 2
    side = (lax.axis_index("seq") // bit) % 2
    mine = lax.dynamic_slice_in_dim(array, side * rows, rows, 0)
    other = lax.dynamic_slice_in_dim(array, (1 - side) * rows, rows, 0)
    return mine, other


def seq_quarter(array, join):
    bits = [1 << i for i in range(lax.axis_size("seq").bit_length() - 1)]
    for bit in bits[:2]:
        mine, other = halves(array, bit)
        array = join(mine, swap(other, "seq", bit))
    for bit in bits[2:]:
        array = join(array, swap(array, "seq", bit))
    return array


def paired(array, axis, bit, dim):
    other = swap(array, axis, bit)
    side = (lax.axis_index(axis) // bit) % 2
    return jnp.where(
        side == 0,
        jnp.concatenate([array, other], dim),
        jnp.concatenate([other, array], dim),
    )


def seq_whole(array):
    return paired(paired(array, "seq", 2, 0), "seq", 1, 0)


def add_join(first, second):
    return (first.astype(F32) + second.astype(F32)).astype(BF)


def stages(order):
    row = [("row", 1 << i) for i in range(lax.axis_size("row").bit_length() - 1)]
    seq = [[("seq", 1 << i)] for i in range(lax.axis_size("seq").bit_length() - 1)]
    named = {"core": seq[0], "row": row, "near": seq[1], "far": seq[2], "rest": sum(seq[3:], [])}
    return sum([named[name] for name in ("core",) + order + ("rest",)], [])


ORDERS = (("row", "far", "near"), ("near", "row", "far"), ("far", "near", "row"))


def advance(state, steps):
    held, plan, done = state
    for step in range(done, min(done + steps, 2 * len(plan))):
        if step < len(plan):
            axis, bit = plan[step]
            half = held.shape[0] // 2
            side = (lax.axis_index(axis) // bit) % 2
            mine = lax.dynamic_slice_in_dim(held, side * half, half, 0)
            other = lax.dynamic_slice_in_dim(held, (1 - side) * half, half, 0)
            held = mine.astype(F32) + swap(other.astype(BF), axis, bit).astype(F32)
            held = held.astype(BF)
        else:
            axis, bit = plan[2 * len(plan) - 1 - step]
            held = paired(held, axis, bit, 0)
    return held, plan, min(done + steps, 2 * len(plan))


def tied(values, states):
    values, helds = lax.optimization_barrier((values, [state[0] for state in states]))
    return values, [(held,) + state[1:] for held, state in zip(helds, states)]


def extended(cells, width, rows):
    count = lax.axis_size("seq")
    head = cells[:width]
    tail = cells[-width:]
    return jnp.concatenate(
        [
            lax.ppermute(tail, "seq", [(i, i + 1) for i in range(count - 1)]),
            cells,
            lax.ppermute(head, "seq", [(i + 1, i) for i in range(count - 1)]),
            jnp.zeros((rows - cells.shape[0] - 2 * width, cells.shape[1]), cells.dtype),
        ],
        axis=0,
    )


def dot_nn(a, b):
    return jnp.dot(a, b, preferred_element_type=F32)


def dot_nt(a, b):
    return lax.dot_general(a, b, (((1,), (1,)), ((), ())), preferred_element_type=F32)


def dot_tn(a, b):
    return lax.dot_general(a, b, (((0,), (0,)), ((), ())), preferred_element_type=F32)


def iota(shape, dim):
    return lax.broadcasted_iota(jnp.int32, shape, dim)


def spread(block):
    rows = block.shape[0]
    tall = jnp.concatenate([block] * 4, axis=0).astype(F32)
    shape = (4 * rows, GROUP)
    keep = iota(shape, 0) // rows == iota(shape, 1) // LAND
    return jnp.where(keep, tall, 0.0).astype(BF)


def gathered(square):
    rows = square.shape[0] // 4
    lane = iota((rows, GROUP), 1) // LAND
    out = square[:rows]
    for head in range(1, 4):
        out = jnp.where(lane == head, square[head * rows : (head + 1) * rows], out)
    return out


def by_head(columns, first, shape):
    lane = iota(shape, 1)
    out = jnp.zeros(shape, F32)
    for head, column in enumerate(columns):
        out = jnp.where((lane % 16 == first + head) & (lane < 48), column, out)
    return out


def split_three(cells):
    lane = iota(cells.shape, 1)
    high = cells.astype(BF).astype(F32)
    mid = (cells - high).astype(BF).astype(F32)
    low = cells - high - mid
    return jnp.where(lane < 16, high, jnp.where(lane < 32, mid, low)).astype(BF)


def merge_three(cells):
    cells = cells.astype(F32)
    return cells + pltpu.roll(cells, 112, 1) + pltpu.roll(cells, 96, 1)


def head_lanes(heads, width):
    return (iota((128, width), 0) == iota((128, width), 1) // LAND).astype(F32)


def doc_of(places, bounds, docs):
    out = (places >= bounds[2 * docs - 1]).astype(jnp.int32)
    for doc in range(docs):
        out = out + (places >= bounds[doc]).astype(jnp.int32)
    return out


def landmark_kernel(docs, scale, bounds, mq_ref, k_ref, v_ref, out_ref, max_s, sum_s, acc_s):
    tokens, width = k_ref.shape
    groups = width // GROUP
    heads = width // LAND
    out_ref[:, :width] = jnp.zeros((docs * LAND, width), BF)
    empty = jnp.full((docs * LAND, 128), NEGATIVE, F32)
    out_ref[:, width:] = jnp.where(iota(empty.shape, 1) < 48, split_three(empty).astype(F32), 0.0).astype(BF)
    for doc in range(docs):
        low = jnp.clip(bounds[doc], 0, tokens)
        high = jnp.clip(bounds[docs + doc], 0, tokens)
        rows = slice(doc * LAND, (doc + 1) * LAND)

        @pl.when(high > low)
        def _():
            max_s[...] = jnp.full(max_s.shape, NEGATIVE, F32)
            sum_s[...] = jnp.zeros(sum_s.shape, F32)
            acc_s[...] = jnp.zeros(acc_s.shape, F32)
            wide = [
                spread(mq_ref[rows, g * GROUP : (g + 1) * GROUP]) for g in range(groups)
            ]

            def step(block, carry):
                first = pl.multiple_of(block * BLOCK, BLOCK)
                at = pl.ds(first, BLOCK)
                place = iota((1, BLOCK), 1) + first
                valid = (place >= low) & (place < high)
                for g in range(groups):
                    cols = slice(g * GROUP, (g + 1) * GROUP)
                    scores = dot_nt(wide[g], k_ref[at, cols]) * scale
                    scores = jnp.where(valid, scores, NEGATIVE)
                    old = max_s[cols, :1]
                    top = jnp.maximum(old, jnp.max(scores, axis=1, keepdims=True))
                    weights = jnp.exp(scores - top)
                    shrink = jnp.exp(old - top)
                    sums = sum_s[cols, :1] * shrink + jnp.sum(weights, axis=1, keepdims=True)
                    acc_s[cols, :] = acc_s[cols, :] * shrink + dot_nn(
                        weights.astype(BF), v_ref[at, cols]
                    )
                    max_s[cols, :] = jnp.broadcast_to(top, (GROUP, 128))
                    sum_s[cols, :] = jnp.broadcast_to(sums, (GROUP, 128))
                return carry

            lax.fori_loop(low // BLOCK, (high + BLOCK - 1) // BLOCK, step, 0)
            columns = []
            for g in range(groups):
                cols = slice(g * GROUP, (g + 1) * GROUP)
                sums = sum_s[cols, :1]
                out_ref[rows, cols] = gathered(acc_s[cols, :] / sums).astype(BF)
                level = max_s[cols, :1] + jnp.log(sums)
                columns += [level[h * LAND : (h + 1) * LAND] for h in range(4)]
            out_ref[rows, width:] = split_three(by_head(columns, 0, (LAND, 128)))


def join_kernel(a_ref, b_ref, out_ref):
    width = a_ref.shape[1] - 128
    heads = width // LAND
    first, second = merge_three(a_ref[:, width:]), merge_three(b_ref[:, width:])
    lane = iota(first.shape, 1)
    first = jnp.where(lane < heads, first, 0.0)
    second = jnp.where(lane < heads, second, 0.0)
    top = jnp.maximum(first, second)
    exp_a, exp_b = jnp.exp(first - top), jnp.exp(second - top)
    both = exp_a + exp_b
    level = top + jnp.log(both)
    pick = head_lanes(heads, width)
    share_a = jnp.dot(exp_a / both, pick, precision=HIGH, preferred_element_type=F32)
    share_b = jnp.dot(exp_b / both, pick, precision=HIGH, preferred_element_type=F32)
    joined = a_ref[:, :width].astype(F32) * share_a + b_ref[:, :width].astype(F32) * share_b
    out_ref[:, :width] = joined.astype(BF)
    level = jnp.where(lane < heads, level, 0.0)
    level = level + pltpu.roll(level, 16, 1) + pltpu.roll(level, 32, 1)
    out_ref[:, width:] = split_three(level)


def join(first, second):
    return pl.pallas_call(
        join_kernel, out_shape=jax.ShapeDtypeStruct(first.shape, BF), name="join"
    )(first, second)


def mix_kernel(inv_ref, stat_ref, mix_ref):
    width = stat_ref.shape[1] - 128
    for g in range(width // GROUP):
        cols = slice(g * GROUP, (g + 1) * GROUP)
        mix_ref[:, cols] = dot_nn(inv_ref[:, cols], spread(stat_ref[:, cols])).astype(BF)
    mix_ref[:, width:] = stat_ref[:, width:]


def mix_back_kernel(inv_ref, stat_ref, grad_ref, out_ref):
    width = stat_ref.shape[1] - 128
    columns = []
    for g in range(width // GROUP):
        cols = slice(g * GROUP, (g + 1) * GROUP)
        grad = gathered(dot_tn(inv_ref[:, cols], grad_ref[:, cols]))
        out_ref[:, cols] = grad.astype(BF)
        product = grad * stat_ref[:, cols].astype(F32)
        lane = iota(product.shape, 1) // LAND
        for h in range(4):
            columns.append(jnp.sum(jnp.where(lane == h, product, 0.0), axis=1, keepdims=True))
    out_ref[:, width:] = split_three(by_head(columns, 0, (LAND, 128)))


def make_band(taps_ref, band_s):
    for head in range(taps_ref.shape[0]):
        row = jnp.broadcast_to(taps_ref[head : head + 1, :], (SUB, GROUP))
        band_s[head * SUB : (head + 1) * SUB, :] = pltpu.roll(row, 0, 1, stride=1, stride_axis=0).astype(BF)


def same_doc(first, bounds, docs, radius):
    rows = iota((SUB, GROUP), 0) + first
    cols = iota((SUB, GROUP), 1) + (first - radius)
    return doc_of(rows, bounds, docs) == doc_of(cols, bounds, docs)


def token_kernel(
    docs, scale, bounds, q_ref, v_ref, mk_ref, mix_ref, taps_ref, mixed_ref, probs_ref, band_s, sum_s
):
    width = q_ref.shape[1]
    groups = width // GROUP
    radius = (TAPS - 1) // 2
    first = pl.program_id(0) * BLOCK

    @pl.when(pl.program_id(0) == 0)
    def _():
        make_band(taps_ref, band_s)

    for sub in range(BLOCK // SUB):
        start = pl.multiple_of(first + sub * SUB, SUB)
        same = same_doc(start, bounds, docs, radius)
        same = jnp.where(jnp.concatenate([same] * 4, axis=0), 1.0, 0.0).astype(BF)
        for g in range(groups):
            cols = slice(g * GROUP, (g + 1) * GROUP)
            band = band_s[g * 4 * SUB : (g + 1) * 4 * SUB, :] * same
            res = dot_nn(band, v_ref[pl.ds(start, GROUP), cols])
            sum_s[sub * SUB : (sub + 1) * SUB, cols] = gathered(res)
    probs_ref[...] = jnp.zeros(probs_ref.shape, BF)
    for doc in range(docs):
        low, high = bounds[doc], bounds[docs + doc]
        rows = slice(doc * LAND, (doc + 1) * LAND)

        @pl.when((high > first) & (low < first + BLOCK))
        def _():
            place = iota((1, BLOCK), 1) + first
            valid = (place >= low) & (place < high)
            for g in range(groups):
                cols = slice(g * GROUP, (g + 1) * GROUP)
                scores = dot_nt(spread(mk_ref[rows, cols]), q_ref[:, cols]) * scale
                scores = scores.reshape(4, LAND, BLOCK)
                weights = jnp.exp(scores - jnp.max(scores, axis=1, keepdims=True))
                probs = weights / jnp.sum(weights, axis=1, keepdims=True)
                probs = jnp.where(valid, probs.reshape(GROUP, BLOCK), 0.0).astype(BF)
                probs_ref[cols, :] = probs_ref[cols, :] + probs
                sum_s[:, cols] = sum_s[:, cols] + dot_tn(probs, spread(mix_ref[rows, cols]))

    mixed_ref[...] = sum_s[...].astype(BF)


def token_back_kernel(
    docs, scale, bounds, q_ref, gm_ref, probs_ref, mk_ref, mix_ref, gq_ref, gmix_ref, gmk_ref, gq_s
):
    width = q_ref.shape[1]
    groups = width // GROUP
    first = pl.program_id(0) * BLOCK

    @pl.when(pl.program_id(0) == 0)
    def _():
        gmix_ref[...] = jnp.zeros(gmix_ref.shape, F32)
        gmk_ref[...] = jnp.zeros(gmk_ref.shape, F32)

    gq_s[...] = jnp.zeros(gq_s.shape, F32)
    for doc in range(docs):
        low, high = bounds[doc], bounds[docs + doc]
        rows = slice(doc * LAND, (doc + 1) * LAND)

        @pl.when((high > first) & (low < first + BLOCK))
        def _():
            place = iota((1, BLOCK), 1) + first
            valid = (place >= low) & (place < high)
            for g in range(groups):
                cols = slice(g * GROUP, (g + 1) * GROUP)
                probs = jnp.where(valid, probs_ref[cols, :].astype(F32), 0.0)
                gmix_ref[rows, cols] += gathered(dot_nn(probs.astype(BF), gm_ref[:, cols]))
                grad = dot_nt(spread(mix_ref[rows, cols]), gm_ref[:, cols])
                heavy = (probs * grad).reshape(4, LAND, BLOCK)
                shared = probs.reshape(4, LAND, BLOCK) * jnp.sum(heavy, axis=1, keepdims=True)
                grad = ((heavy - shared).reshape(GROUP, BLOCK) * scale).astype(BF)
                gmk_ref[rows, cols] += gathered(dot_nn(grad, q_ref[:, cols]))
                gq_s[:, cols] += dot_tn(grad, spread(mk_ref[rows, cols]))

    gq_ref[...] = gq_s[...].astype(BF)


def conv_back_kernel(docs, bounds, gm_ref, v_ref, taps_ref, out_ref, prod_ref, band_s):
    width = gm_ref.shape[1]
    groups = width // GROUP
    radius = (TAPS - 1) // 2
    first = pl.program_id(0) * BLOCK

    @pl.when(pl.program_id(0) == 0)
    def _():
        make_band(taps_ref, band_s)
        prod_ref[...] = jnp.zeros(prod_ref.shape, F32)

    for sub in range(BLOCK // SUB):
        start = pl.multiple_of(first + sub * SUB, SUB)
        same = same_doc(start, bounds, docs, radius)
        same = jnp.where(jnp.concatenate([same] * 4, axis=0), 1.0, 0.0)
        for g in range(groups):
            cols = slice(g * GROUP, (g + 1) * GROUP)
            tall = slice(g * 4 * SUB, (g + 1) * 4 * SUB)
            band = band_s[tall, :] * same.astype(BF)
            res = dot_nn(band, gm_ref[pl.ds(start, GROUP), cols])
            out_ref[sub * SUB : (sub + 1) * SUB, cols] = gathered(res)
            own = gm_ref[pl.ds(pl.multiple_of(start + radius, 16), SUB), cols]
            product = dot_nt(spread(own), v_ref[pl.ds(start, GROUP), cols])
            prod_ref[tall, :] += product * same


def ffn_kernel(
    x_ref, mixed_ref, cot_ref, w_out_ref, w_up_ref, w_down_ref, rows_ref, bias_up_ref,
    result_ref, grad_one_ref, active_ref, grad_up_ref, low_ref, low_two_ref, low_one_ref,
    grad_mixed_ref, sums_ref, sum_up_ref, slope_s,
):
    width = x_ref.shape[1]
    hidden = w_up_ref.shape[1]
    chunks = [slice(at, at + width) for at in range(0, hidden, width)]

    def row(i):
        return rows_ref[i : i + 1, :]

    @pl.when(pl.program_id(0) == 0)
    def _():
        sums_ref[...] = jnp.zeros(sums_ref.shape, F32)
        sum_up_ref[...] = jnp.zeros(sum_up_ref.shape, F32)

    def add_sum(i, cells):
        sums_ref[i : i + 1, :] += jnp.sum(cells, axis=0, keepdims=True)

    attended = dot_nn(mixed_ref[...], w_out_ref[...]) + row(0)
    norm_one, inverse_one = normalize(x_ref[...].astype(F32) + attended)
    hidden_one = norm_one * row(1) + row(2)
    hidden_low = hidden_one.astype(BF)
    low_ref[...] = hidden_low
    lowered = hidden_one + row(3)
    for cols in chunks:
        upper = dot_nn(hidden_low, w_up_ref[:, cols]) + bias_up_ref[:1, cols]
        active, slope = gelu_both(upper)
        active = active.astype(BF)
        active_ref[:, cols] = active
        slope_s[:, cols] = slope.astype(BF)
        lowered = lowered + dot_nn(active, w_down_ref[cols, :])
    norm_two, inverse_two = normalize(lowered)
    result_ref[...] = norm_two * row(4) + row(5)
    upstream = cot_ref[...].astype(F32)
    add_sum(0, upstream * norm_two)
    add_sum(1, upstream)
    grad_two = norm_back(upstream * row(4), norm_two, inverse_two)
    low_two = grad_two.astype(BF)
    low_two_ref[...] = low_two
    add_sum(2, low_two.astype(F32))
    grad_hidden = grad_two
    for cols in chunks:
        grad_up = dot_nt(low_two, w_down_ref[cols, :]) * slope_s[:, cols].astype(F32)
        grad_up = grad_up.astype(BF)
        grad_up_ref[:, cols] = grad_up
        sum_up_ref[:1, cols] += jnp.sum(grad_up.astype(F32), axis=0, keepdims=True)
        grad_hidden = grad_hidden + dot_nt(grad_up, w_up_ref[:, cols])
    add_sum(3, grad_hidden * norm_one)
    add_sum(4, grad_hidden)
    grad_one = norm_back(grad_hidden * row(1), norm_one, inverse_one)
    grad_one_ref[...] = grad_one
    low_one = grad_one.astype(BF)
    low_one_ref[...] = low_one
    add_sum(5, low_one.astype(F32))
    grad_mixed_ref[...] = dot_nt(low_one, w_out_ref[...]).astype(BF)


def landmark_back_kernel(
    docs, scale, bounds, k_ref, v_ref, conv_ref, mq_ref, grad_ref, level_ref, dots_ref,
    gk_ref, gv_ref, gmq_ref, gk_s, gv_s,
):
    width = k_ref.shape[1]
    groups = width // GROUP
    first = pl.program_id(0) * BLOCK

    @pl.when(pl.program_id(0) == 0)
    def _():
        gmq_ref[...] = jnp.zeros(gmq_ref.shape, F32)

    gk_s[...] = jnp.zeros(gk_s.shape, F32)
    gv_s[...] = conv_ref[...]
    for doc in range(docs):
        low, high = bounds[doc], bounds[docs + doc]
        rows = slice(doc * LAND, (doc + 1) * LAND)

        @pl.when((high > first) & (low < first + BLOCK))
        def _():
            place = iota((1, BLOCK), 1) + first
            valid = (place >= low) & (place < high)

            level, dots = merge_three(level_ref[rows, :]), merge_three(dots_ref[rows, :])

            def column(lanes, g):
                return jnp.concatenate(
                    [lanes[:, 4 * g + h : 4 * g + h + 1] for h in range(4)], axis=0
                )

            for g in range(groups):
                cols = slice(g * GROUP, (g + 1) * GROUP)
                wide_q, wide_g = spread(mq_ref[rows, cols]), spread(grad_ref[rows, cols])
                scores = dot_nt(wide_q, k_ref[:, cols]) * scale - column(level, g)
                probs = jnp.exp(jnp.where(valid, scores, NEGATIVE))
                grad = dot_nt(wide_g, v_ref[:, cols]) - column(dots, g)
                grad = (probs * grad * scale).astype(BF)
                gv_s[:, cols] += dot_tn(probs.astype(BF), wide_g)
                gk_s[:, cols] += dot_tn(grad, wide_q)
                gmq_ref[rows, cols] += gathered(dot_nn(grad, k_ref[:, cols]))

    gk_ref[...] = gk_s[...].astype(BF)
    gv_ref[...] = gv_s[...].astype(BF)


def gelu_both(upper):
    tangent = jnp.tanh(0.7978845608028654 * (upper + 0.044715 * upper * upper * upper))
    inner_slope = 0.7978845608028654 * (1.0 + 3.0 * 0.044715 * upper * upper)
    active = 0.5 * upper * (1.0 + tangent)
    slope = 0.5 * (1.0 + tangent) + 0.5 * upper * (1.0 - tangent * tangent) * inner_slope
    return active, slope


def normalize(residual):
    row_mean = jnp.mean(residual, axis=-1, keepdims=True)
    centered = residual - row_mean
    row_var = jnp.mean(centered * centered, axis=-1, keepdims=True)
    inverse_dev = lax.rsqrt(row_var + 1e-05)
    return (centered * inverse_dev, inverse_dev)


def norm_back(grad_normed, normed, inverse_dev):
    return inverse_dev * (
        grad_normed
        - jnp.mean(grad_normed, axis=-1, keepdims=True)
        - normed * jnp.mean(grad_normed * normed, axis=-1, keepdims=True)
    )


def pinv_kernel(queries, key_rows, score_scale):
    scores = jnp.einsum("pie,pje->pij", queries, key_rows, precision=HIGH) * score_scale
    row_max = jnp.max(scores, axis=-1, keepdims=True)
    weights = jnp.exp(scores - row_max)
    kernel = weights / jnp.sum(weights, axis=-1, keepdims=True)
    column_max = jnp.max(jnp.sum(kernel, axis=1), axis=-1)
    inverse = jnp.swapaxes(kernel, -1, -2) / column_max[:, None, None]
    identity = jnp.eye(LAND, dtype=F32)
    for sweep in range(NS_ITERS):
        product = jnp.matmul(kernel, inverse, precision=HIGH)
        bracket = 7.0 * identity - product
        bracket = 15.0 * identity - jnp.matmul(product, bracket, precision=HIGH)
        bracket = 13.0 * identity - jnp.matmul(product, bracket, precision=HIGH)
        inverse = 0.25 * jnp.matmul(inverse, bracket, precision=HIGH)
    return inverse


def per_device(
    inputs, doc_lengths, w_qkv, bias_q, bias_v, conv_taps, w_out, bias_out, norm1_gain,
    norm1_bias, w_up, bias_up, w_down, bias_down, norm2_gain, norm2_bias, cotangent,
):
    tokens = inputs[0]
    tok_count, width = tokens.shape
    heads, tap_count = conv_taps.shape
    size = width // heads
    radius = (tap_count - 1) // 2
    lengths = doc_lengths[0]
    docs = lengths.shape[0]
    mark_count = docs * LAND
    scale = 1.0 / math.sqrt(size)
    seq_count = lax.axis_size("seq")
    me = lax.axis_index("seq")
    row_first = me * tok_count
    ends = jnp.cumsum(lengths)
    starts = ends - lengths
    bounds = (jnp.concatenate([starts, ends]) - row_first).astype(jnp.int32)
    within = jnp.arange(LAND + 1, dtype=jnp.int32)
    edges = starts[:, None] + (within[None, :] * lengths[:, None] + LAND - 1) // LAND
    mark_low = edges[:, :-1].reshape(mark_count, 1)
    mark_high = edges[:, 1:].reshape(mark_count, 1)
    counts = (mark_high - mark_low).astype(F32)
    places = row_first + jnp.arange(tok_count, dtype=jnp.int32)[None, :]
    onehot = ((places >= mark_low) & (places < mark_high)).astype(BF)
    rows_in = (((0,), (0,)), ((), ()))
    cols_in = (((1,), (1,)), ((), ()))
    blocks = tok_count // BLOCK
    window_rows = tok_count + GROUP - SUB
    smem = pl.BlockSpec(memory_space=pltpu.SMEM)
    params = pltpu.CompilerParams(vmem_limit_bytes=40 * 1024 * 1024)
    tok_spec = pl.BlockSpec((BLOCK, width), lambda i: (i, 0))

    def part(col):
        return pl.BlockSpec((BLOCK, width), lambda i: (i, col))

    def fixed(*shape):
        return pl.BlockSpec(shape, lambda i: (0,) * len(shape))

    def shaped(shape, dtype):
        return jax.ShapeDtypeStruct(shape, dtype)

    means = jnp.dot(onehot, tokens, preferred_element_type=F32) / counts
    mean_in = seq_whole(seq_quarter(means.astype(BF), add_join))
    marks = jnp.dot(mean_in, w_qkv[:, : 2 * width], preferred_element_type=F32)
    mark_q = (marks[:, :width] + bias_q).astype(BF)
    mark_k = marks[:, width:].astype(BF)

    bias = jnp.concatenate([bias_q, jnp.zeros_like(bias_q), bias_v])
    qkv = (jnp.dot(tokens, w_qkv, preferred_element_type=F32) + bias).astype(BF)
    value_ext = extended(qkv[:, 2 * width :], radius, window_rows)
    value_ext, mark_q, mark_k = lax.optimization_barrier((value_ext, mark_q, mark_k))

    def one_col(col):
        return pl.BlockSpec((tok_count, width), lambda i: (0, col))

    stats = pl.pallas_call(
        lambda *refs: landmark_kernel(docs, scale, *refs),
        grid=(1,),
        in_specs=[smem, fixed(mark_count, width), one_col(1), one_col(2)],
        out_specs=fixed(mark_count, width + 128),
        out_shape=shaped((mark_count, width + 128), BF),
        scratch_shapes=[
            pltpu.VMEM((width, 128), F32), pltpu.VMEM((width, 128), F32),
            pltpu.VMEM((width, GROUP), F32),
        ],
        compiler_params=params,
        name="landmark",
    )(bounds, mark_q, qkv, qkv)
    far_count = seq_count // 4
    own_count = -(-heads // far_count)
    own_doc = (me % 2) * 2 + (me // 2) % 2
    own_at = (me // 4) * own_count * size
    spare = far_count * own_count * size - width

    def own_heads(array):
        array = jnp.pad(array, ((0, 0), (0, spare)))
        array = lax.dynamic_slice_in_dim(array, own_at, own_count * size, 1)
        return array.reshape(LAND, own_count, size).transpose(1, 0, 2)

    def of_doc(array):
        return lax.dynamic_slice_in_dim(array, own_doc * LAND, LAND, 0)

    own_inverse, inverse_pullback = jax.vjp(
        lambda a, b: pinv_kernel(a, b, scale),
        own_heads(of_doc(mark_q)).astype(F32),
        own_heads(of_doc(mark_k)).astype(F32),
    )
    inverse = own_inverse.transpose(1, 0, 2).reshape(LAND, own_count * size).astype(BF)
    for bit in (1, 2):
        mine, other = halves(stats, bit)
        stats = join(mine, swap(other, "seq", bit))
    for i in range(2, seq_count.bit_length() - 1):
        other = swap(jnp.concatenate([stats, inverse], 1), "seq", 1 << i)
        stats = join(stats, other[:, : width + 128])
        other = other[:, width + 128 :]
        inverse = jnp.where(
            (me >> i) % 2 == 0,
            jnp.concatenate([inverse, other], 1),
            jnp.concatenate([other, inverse], 1),
        )
    inverse = inverse[:, :width]
    mix = pl.pallas_call(
        mix_kernel, out_shape=shaped((LAND, width + 128), BF), name="mix"
    )(inverse, stats)
    mix = seq_whole(mix)

    taps = jnp.pad(conv_taps, ((0, 0), (0, GROUP - tap_count)))
    mark_spec = fixed(mark_count, width)
    mixed, probs = pl.pallas_call(
        lambda *refs: token_kernel(docs, scale, *refs),
        grid=(blocks,),
        in_specs=[
            smem, part(0), fixed(window_rows, width), mark_spec, mark_spec, fixed(heads, GROUP)
        ],
        out_specs=(tok_spec, pl.BlockSpec((width, BLOCK), lambda i: (0, i))),
        out_shape=(shaped((tok_count, width), BF), shaped((width, tok_count), BF)),
        scratch_shapes=[pltpu.VMEM((heads * SUB, GROUP), BF), pltpu.VMEM((BLOCK, width), F32)],
        compiler_params=params,
        name="token",
    )(bounds, qkv, value_ext, mark_k, mix, taps)

    hidden = w_up.shape[1]
    vectors = jnp.stack([bias_out, norm1_gain, norm1_bias, bias_down, norm2_gain, norm2_bias])
    vectors = jnp.pad(vectors, ((0, 2), (0, 0)))
    wide_spec = pl.BlockSpec((FFN_BLOCK, hidden), lambda i: (i, 0))
    ffn_spec = pl.BlockSpec((FFN_BLOCK, width), lambda i: (i, 0))
    narrow = shaped((tok_count, width), BF)
    (
        result, grad_one, active, grad_upper, hidden_low, grad_low_two, grad_low_one,
        grad_mixed, sums, sum_up,
    ) = pl.pallas_call(
        ffn_kernel,
        grid=(tok_count // FFN_BLOCK,),
        in_specs=[
            ffn_spec, ffn_spec, ffn_spec, fixed(width, width), fixed(width, hidden),
            fixed(hidden, width), fixed(8, width), fixed(8, hidden),
        ],
        out_specs=(
            ffn_spec, ffn_spec, wide_spec, wide_spec, ffn_spec, ffn_spec, ffn_spec, ffn_spec,
            fixed(8, width), fixed(8, hidden),
        ),
        out_shape=(
            shaped((tok_count, width), F32), shaped((tok_count, width), F32),
            shaped((tok_count, hidden), BF), shaped((tok_count, hidden), BF),
            narrow, narrow, narrow, narrow, shaped((8, width), F32), shaped((8, hidden), F32),
        ),
        scratch_shapes=[pltpu.VMEM((FFN_BLOCK, hidden), BF)],
        compiler_params=pltpu.CompilerParams(vmem_limit_bytes=58 * 1024 * 1024),
        name="ffn",
    )(
        tokens, mixed, cotangent[0], w_out, w_up, w_down, vectors,
        jnp.broadcast_to(bias_up[None, :], (8, hidden)),
    )
    grad_gain_two, grad_shift_two, grad_bias_down = sums[0], sums[1], sums[2]
    grad_gain_one, grad_shift_one, grad_bias_out = sums[3], sums[4], sums[5]
    grad_bias_up = sum_up[0]

    grad_queries, grad_mix, grad_mk = pl.pallas_call(
        lambda *refs: token_back_kernel(docs, scale, *refs),
        grid=(blocks,),
        in_specs=[
            smem, part(0), tok_spec, pl.BlockSpec((width, BLOCK), lambda i: (0, i)), mark_spec,
            mark_spec,
        ],
        out_specs=(tok_spec, mark_spec, mark_spec),
        out_shape=(
            shaped((tok_count, width), BF), shaped((mark_count, width), F32),
            shaped((mark_count, width), F32),
        ),
        scratch_shapes=[pltpu.VMEM((BLOCK, width), F32)],
        compiler_params=params,
        name="token_back",
    )(bounds, qkv, grad_mixed, probs, mark_k, mix)
    grad_w_down = lax.dot_general(active, grad_low_two, rows_in, preferred_element_type=F32)
    grad_w_up = lax.dot_general(hidden_low, grad_upper, rows_in, preferred_element_type=F32)
    grad_w_down, grad_w_up = grad_w_down.astype(BF), grad_w_up.astype(BF)
    grad_mix = seq_quarter(grad_mix.astype(BF), add_join)
    grad_mix, grad_w_down, grad_w_up = lax.optimization_barrier(
        (grad_mix, grad_w_down, grad_w_up)
    )
    sum_w_down, sum_w_up = lax.psum((grad_w_down, grad_w_up), ("row", "seq"))
    grad_w_out = lax.dot_general(mixed, grad_low_one, rows_in, preferred_element_type=F32)

    grad_ext = extended(grad_mixed, radius, window_rows)
    grad_conv, products = pl.pallas_call(
        lambda *refs: conv_back_kernel(docs, *refs),
        grid=(blocks,),
        in_specs=[
            smem, fixed(window_rows, width), fixed(window_rows, width), fixed(heads, GROUP)
        ],
        out_specs=(tok_spec, fixed(heads * SUB, GROUP)),
        out_shape=(shaped((tok_count, width), F32), shaped((heads * SUB, GROUP), F32)),
        scratch_shapes=[pltpu.VMEM((heads * SUB, GROUP), BF)],
        compiler_params=params,
        name="conv_back",
    )(bounds, grad_ext, value_ext, jnp.pad(conv_taps[:, ::-1], ((0, 0), (0, GROUP - tap_count))))
    reach = SUB + tap_count - 1
    products = products.reshape(heads, SUB, GROUP)[:, :, :reach].reshape(heads, SUB * reach)
    products = jnp.pad(products, ((0, 0), (0, SUB))).reshape(heads, SUB, reach + 1)
    grad_conv_taps = jnp.sum(products, axis=1)[:, :tap_count]

    grad_avg = pl.pallas_call(
        mix_back_kernel, out_shape=shaped((LAND, width + 128), BF), name="mix_back"
    )(inverse, stats, grad_mix)
    grad_avg = seq_whole(grad_avg)
    grad_inverse = jnp.einsum(
        "pie,pje->pij", own_heads(grad_mix), own_heads(stats[:, :width]),
        preferred_element_type=F32,
    )
    grad_mq_small, grad_mk_small = inverse_pullback(grad_inverse)
    lane_spec = pl.BlockSpec((mark_count, 128), lambda i: (0, width // 128))
    grad_keys, grad_values, grad_mq = pl.pallas_call(
        lambda *refs: landmark_back_kernel(docs, scale, *refs),
        grid=(blocks,),
        in_specs=[
            smem, part(1), part(2), tok_spec, mark_spec, mark_spec, lane_spec, lane_spec
        ],
        out_specs=(tok_spec, tok_spec, mark_spec),
        out_shape=(
            shaped((tok_count, width), BF), shaped((tok_count, width), BF),
            shaped((mark_count, width), F32),
        ),
        scratch_shapes=[pltpu.VMEM((BLOCK, width), F32), pltpu.VMEM((BLOCK, width), F32)],
        compiler_params=params,
        name="landmark_back",
    )(bounds, qkv, qkv, grad_conv, mark_q, grad_avg, mix, grad_avg)

    def placed(array):
        array = array.transpose(1, 0, 2).reshape(LAND, own_count * size)
        array = lax.dynamic_update_slice_in_dim(
            jnp.zeros((LAND, width + spare), F32), array, own_at, 1
        )[:, :width]
        return lax.dynamic_update_slice_in_dim(
            jnp.zeros((mark_count, width), F32), array, own_doc * LAND, 0
        )

    grad_mq = grad_mq + placed(grad_mq_small)
    grad_mk = grad_mk + placed(grad_mk_small)
    grad_marks = jnp.concatenate([grad_mq, grad_mk], axis=1).astype(BF)
    mark_back = lax.dot_general(
        grad_marks, w_qkv[:, : 2 * width], cols_in, preferred_element_type=F32
    ) / counts
    mark_back = mark_back.astype(BF)

    grad_bias_q = jnp.sum(grad_queries.astype(F32), axis=0) + jnp.sum(grad_mq, axis=0)
    grad_bias_v = jnp.sum(grad_values.astype(F32), axis=0)
    grad_projected = jnp.concatenate([grad_queries, grad_keys, grad_values], axis=1)
    grad_w_qkv = lax.dot_general(tokens, grad_projected, rows_in, preferred_element_type=F32)
    grad_w_marks = lax.dot_general(mean_in, grad_marks, rows_in, preferred_element_type=F32)
    grad_w_qkv = (grad_w_qkv + jnp.pad(grad_w_marks, ((0, 0), (0, width)))).astype(BF)
    small = [
        grad_bias_q, grad_bias_v, grad_conv_taps.reshape(-1), grad_bias_out, grad_gain_one,
        grad_shift_one, grad_bias_up, grad_bias_down, grad_gain_two, grad_shift_two,
    ]
    sizes = [piece.shape[0] for piece in small]
    flat = jnp.concatenate(small)
    third = width // 3
    flat = jnp.pad(flat, (0, third * width - flat.shape[0])).reshape(third, width).astype(BF)
    w_q, w_k, w_v = [grad_w_qkv[:, i * width : (i + 1) * width] for i in range(3)]
    late = [
        jnp.concatenate([grad_w_out.astype(BF), w_q[: 2 * third]], 0),
        jnp.concatenate([w_q[2 * third :], w_k], 0),
        jnp.concatenate([w_v, flat], 0),
    ]
    late = [advance((array, stages(order), 0), 1) for array, order in zip(late, ORDERS)]
    mark_back = seq_quarter(mark_back, add_join)
    mark_back, late = tied(mark_back, late)
    late = [advance(state, 1) for state in late]
    mark_back = seq_whole(mark_back)
    mark_back, late = tied(mark_back, late)
    first, second, last = [advance(state, 64)[0].astype(F32) for state in late]
    sum_w_out = first[:width]
    sum_w_qkv = jnp.concatenate(
        [
            jnp.concatenate([first[width:], second[:third]], 0),
            second[third:],
            last[:width],
        ],
        axis=1,
    )
    sum_w_down, sum_w_up = sum_w_down.astype(F32), sum_w_up.astype(F32)
    flat = last[width:].reshape(-1)
    pieces = []
    at = 0
    for length in sizes:
        pieces.append(flat[at : at + length])
        at += length
    grad_input = (
        grad_one
        + lax.dot_general(grad_projected, w_qkv, cols_in, preferred_element_type=F32)
        + lax.dot_general(onehot, mark_back, rows_in, preferred_element_type=F32)
    )
    return (
        result[None], grad_input[None], sum_w_qkv, pieces[0], pieces[1],
        pieces[2].reshape(heads, tap_count), sum_w_out, pieces[3], pieces[4], pieces[5],
        sum_w_up, pieces[6], sum_w_down, pieces[7], pieces[8], pieces[9],
    )


def solution(mesh):
    whole, tokens = P(), P("row", "seq", None)
    return jax.shard_map(
        per_device,
        mesh=mesh,
        in_specs=(tokens, P("row", None)) + (whole,) * 14 + (tokens,),
        out_specs=(tokens, tokens) + (whole,) * 14,
        check_vma=False,
    )
```

```python
import math

import jax
import jax.numpy as jnp
from jax import lax
from jax.experimental import pallas as pl
from jax.experimental.pallas import tpu as pltpu
from jax.sharding import PartitionSpec as P

LAND = 64
NS_ITERS = 6
HIGH = lax.Precision.HIGHEST
NEGATIVE = -1e30
BF = jnp.bfloat16
F32 = jnp.float32

BLOCK = 256
GROUP = 256
SUB = 128
TAPS = 33
FFN_BLOCK = 256


def swap(array, axis, bit):
    count = lax.axis_size(axis)
    return lax.ppermute(array, axis, [(i, i ^ bit) for i in range(count)])


def add_parts(parts):
    total = parts[0].astype(F32)
    for part in parts[1:]:
        total = total + part.astype(F32)
    return total


def halves(array, bit):
    rows = array.shape[0] // 2
    side = (lax.axis_index("seq") // bit) % 2
    mine = lax.dynamic_slice_in_dim(array, side * rows, rows, 0)
    other = lax.dynamic_slice_in_dim(array, (1 - side) * rows, rows, 0)
    return mine, other


def seq_quarter(array, join):
    bits = [1 << i for i in range(lax.axis_size("seq").bit_length() - 1)]
    for bit in bits[:2]:
        mine, other = halves(array, bit)
        array = join(mine, swap(other, "seq", bit))
    for bit in bits[2:]:
        array = join(array, swap(array, "seq", bit))
    return array


def paired(array, axis, bit, dim):
    other = swap(array, axis, bit)
    side = (lax.axis_index(axis) // bit) % 2
    return jnp.where(
        side == 0,
        jnp.concatenate([array, other], dim),
        jnp.concatenate([other, array], dim),
    )


def seq_whole(array):
    return paired(paired(array, "seq", 2, 0), "seq", 1, 0)


def add_join(first, second):
    return (first.astype(F32) + second.astype(F32)).astype(BF)


def stages(order):
    row = [("row", 1 << i) for i in range(lax.axis_size("row").bit_length() - 1)]
    seq = [[("seq", 1 << i)] for i in range(lax.axis_size("seq").bit_length() - 1)]
    named = {"core": seq[0], "row": row, "near": seq[1], "far": seq[2], "rest": sum(seq[3:], [])}
    return sum([named[name] for name in ("core",) + order + ("rest",)], [])


def begin(array, down, back):
    return array, stages(down), stages(back), 0


def advance(state, steps):
    held, down, back, done = state
    for step in range(done, min(done + steps, 2 * len(down))):
        if step < len(down):
            axis, bit = down[step]
            half = held.shape[0] // 2
            side = (lax.axis_index(axis) // bit) % 2
            mine = lax.dynamic_slice_in_dim(held, side * half, half, 0)
            other = lax.dynamic_slice_in_dim(held, (1 - side) * half, half, 0)
            held = mine.astype(F32) + swap(other, axis, bit).astype(F32)
            held = held.astype(BF)
        else:
            axis, bit = back[2 * len(down) - 1 - step]
            held = paired(held, axis, bit, 0)
    return held, down, back, min(done + steps, 2 * len(down))


def last_swap(state):
    down, back = state[1], state[2]
    held = advance(state, 2 * len(down) - 1 - state[3])[0]
    return held, swap(held, *down[0]), down, back


def tied(values, states):
    values, helds = lax.optimization_barrier((values, [state[0] for state in states]))
    return values, [(held,) + state[1:] for held, state in zip(helds, states)]


def extended(cells, width, rows):
    count = lax.axis_size("seq")
    head = cells[:width]
    tail = cells[-width:]
    return jnp.concatenate(
        [
            lax.ppermute(tail, "seq", [(i, i + 1) for i in range(count - 1)]),
            cells,
            lax.ppermute(head, "seq", [(i + 1, i) for i in range(count - 1)]),
            jnp.zeros((rows - cells.shape[0] - 2 * width, cells.shape[1]), cells.dtype),
        ],
        axis=0,
    )


def dot_nn(a, b):
    return jnp.dot(a, b, preferred_element_type=F32)


def dot_nt(a, b):
    return lax.dot_general(a, b, (((1,), (1,)), ((), ())), preferred_element_type=F32)


def dot_tn(a, b):
    return lax.dot_general(a, b, (((0,), (0,)), ((), ())), preferred_element_type=F32)


def iota(shape, dim):
    return lax.broadcasted_iota(jnp.int32, shape, dim)


def spread(block):
    rows = block.shape[0]
    tall = jnp.concatenate([block] * 4, axis=0).astype(F32)
    shape = (4 * rows, GROUP)
    keep = iota(shape, 0) // rows == iota(shape, 1) // LAND
    return jnp.where(keep, tall, 0.0).astype(BF)


def gathered(square):
    rows = square.shape[0] // 4
    lane = iota((rows, GROUP), 1) // LAND
    out = square[:rows]
    for head in range(1, 4):
        out = jnp.where(lane == head, square[head * rows : (head + 1) * rows], out)
    return out


def by_head(columns, first, shape):
    lane = iota(shape, 1)
    out = jnp.zeros(shape, F32)
    for head, column in enumerate(columns):
        out = jnp.where((lane % 16 == first + head) & (lane < 48), column, out)
    return out


def split_three(cells):
    lane = iota(cells.shape, 1)
    high = cells.astype(BF).astype(F32)
    mid = (cells - high).astype(BF).astype(F32)
    low = cells - high - mid
    return jnp.where(lane < 16, high, jnp.where(lane < 32, mid, low)).astype(BF)


def merge_three(cells):
    cells = cells.astype(F32)
    return cells + pltpu.roll(cells, 112, 1) + pltpu.roll(cells, 96, 1)


def head_lanes(heads, width):
    return (iota((128, width), 0) == iota((128, width), 1) // LAND).astype(F32)


def doc_of(places, bounds, docs):
    out = (places >= bounds[2 * docs - 1]).astype(jnp.int32)
    for doc in range(docs):
        out = out + (places >= bounds[doc]).astype(jnp.int32)
    return out


def landmark_kernel(docs, scale, bounds, mq_ref, k_ref, v_ref, out_ref, max_s, sum_s, acc_s):
    tokens, width = k_ref.shape
    groups = width // GROUP
    heads = width // LAND
    out_ref[:, :width] = jnp.zeros((docs * LAND, width), BF)
    empty = jnp.full((docs * LAND, 128), NEGATIVE, F32)
    out_ref[:, width:] = jnp.where(iota(empty.shape, 1) < 48, split_three(empty).astype(F32), 0.0).astype(BF)
    for doc in range(docs):
        low = jnp.clip(bounds[doc], 0, tokens)
        high = jnp.clip(bounds[docs + doc], 0, tokens)
        rows = slice(doc * LAND, (doc + 1) * LAND)

        @pl.when(high > low)
        def _():
            max_s[...] = jnp.full(max_s.shape, NEGATIVE, F32)
            sum_s[...] = jnp.zeros(sum_s.shape, F32)
            acc_s[...] = jnp.zeros(acc_s.shape, F32)
            wide = [
                spread(mq_ref[rows, g * GROUP : (g + 1) * GROUP]) for g in range(groups)
            ]

            ones = jnp.ones((BLOCK, 128), BF)

            def step(block, carry):
                first = pl.multiple_of(block * BLOCK, BLOCK)
                at = pl.ds(first, BLOCK)
                place = iota((1, BLOCK), 1) + first
                valid = (place >= low) & (place < high)
                for g in range(groups):
                    cols = slice(g * GROUP, (g + 1) * GROUP)
                    scores = dot_nt(wide[g], k_ref[at, cols]) * scale
                    scores = jnp.where(valid, scores, NEGATIVE)
                    old = max_s[cols, :]
                    top = jnp.maximum(old, jnp.max(scores, axis=1, keepdims=True))
                    weights = jnp.exp(scores - twice(top)).astype(BF)
                    shrink = jnp.exp(old - top)
                    max_s[cols, :] = top
                    sum_s[cols, :] = sum_s[cols, :] * shrink + dot_nn(weights, ones)
                    acc_s[cols, :] = acc_s[cols, :] * twice(shrink) + dot_nn(weights, v_ref[at, cols])
                return carry

            lax.fori_loop(low // BLOCK, (high + BLOCK - 1) // BLOCK, step, 0)
            columns = []
            for g in range(groups):
                cols = slice(g * GROUP, (g + 1) * GROUP)
                sums = sum_s[cols, :]
                out_ref[rows, cols] = gathered(acc_s[cols, :] / twice(sums)).astype(BF)
                level = max_s[cols, :] + jnp.log(sums)
                columns += [level[h * LAND : (h + 1) * LAND] for h in range(4)]
            out_ref[rows, width:] = split_three(by_head(columns, 0, (LAND, 128)))


def twice(cells):
    return jnp.concatenate([cells, cells], axis=1)


def join_kernel(a_ref, b_ref, out_ref):
    width = a_ref.shape[1] - 128
    heads = width // LAND
    first, second = merge_three(a_ref[:, width:]), merge_three(b_ref[:, width:])
    lane = iota(first.shape, 1)
    first = jnp.where(lane < heads, first, 0.0)
    second = jnp.where(lane < heads, second, 0.0)
    top = jnp.maximum(first, second)
    exp_a, exp_b = jnp.exp(first - top), jnp.exp(second - top)
    both = exp_a + exp_b
    level = top + jnp.log(both)
    pick = head_lanes(heads, width)
    share_a = jnp.dot(exp_a / both, pick, precision=HIGH, preferred_element_type=F32)
    share_b = jnp.dot(exp_b / both, pick, precision=HIGH, preferred_element_type=F32)
    joined = a_ref[:, :width].astype(F32) * share_a + b_ref[:, :width].astype(F32) * share_b
    out_ref[:, :width] = joined.astype(BF)
    level = jnp.where(lane < heads, level, 0.0)
    level = level + pltpu.roll(level, 16, 1) + pltpu.roll(level, 32, 1)
    out_ref[:, width:] = split_three(level)


def join(first, second):
    return pl.pallas_call(
        join_kernel, out_shape=jax.ShapeDtypeStruct(first.shape, BF), name="join"
    )(first, second)


def mix_kernel(inv_ref, stat_ref, mix_ref):
    width = stat_ref.shape[1] - 128
    for g in range(width // GROUP):
        cols = slice(g * GROUP, (g + 1) * GROUP)
        mix_ref[:, cols] = dot_nn(inv_ref[:, cols], spread(stat_ref[:, cols])).astype(BF)
    mix_ref[:, width:] = stat_ref[:, width:]


def mix_back_kernel(inv_ref, stat_ref, grad_ref, out_ref):
    width = stat_ref.shape[1] - 128
    columns = []
    for g in range(width // GROUP):
        cols = slice(g * GROUP, (g + 1) * GROUP)
        grad = gathered(dot_tn(inv_ref[:, cols], grad_ref[:, cols]))
        out_ref[:, cols] = grad.astype(BF)
        product = grad * stat_ref[:, cols].astype(F32)
        lane = iota(product.shape, 1) // LAND
        for h in range(4):
            columns.append(jnp.sum(jnp.where(lane == h, product, 0.0), axis=1, keepdims=True))
    out_ref[:, width:] = split_three(by_head(columns, 0, (LAND, 128)))


def make_band(taps_ref, band_s):
    for head in range(taps_ref.shape[0]):
        row = jnp.broadcast_to(taps_ref[head : head + 1, :], (SUB, GROUP))
        band_s[head * SUB : (head + 1) * SUB, :] = pltpu.roll(row, 0, 1, stride=1, stride_axis=0).astype(BF)


def same_doc(first, bounds, docs, radius):
    rows = iota((SUB, GROUP), 0) + first
    cols = iota((SUB, GROUP), 1) + (first - radius)
    return doc_of(rows, bounds, docs) == doc_of(cols, bounds, docs)


def token_kernel(
    docs, scale, bounds, q_ref, v_ref, mk_ref, mix_ref, taps_ref, mixed_ref, probs_ref, band_s, sum_s
):
    width = q_ref.shape[1]
    groups = width // GROUP
    radius = (TAPS - 1) // 2
    first = pl.program_id(0) * BLOCK

    @pl.when(pl.program_id(0) == 0)
    def _():
        make_band(taps_ref, band_s)

    for sub in range(BLOCK // SUB):
        start = pl.multiple_of(first + sub * SUB, SUB)
        same = same_doc(start, bounds, docs, radius)
        same = jnp.where(jnp.concatenate([same] * 4, axis=0), 1.0, 0.0).astype(BF)
        for g in range(groups):
            cols = slice(g * GROUP, (g + 1) * GROUP)
            band = band_s[g * 4 * SUB : (g + 1) * 4 * SUB, :] * same
            res = dot_nn(band, v_ref[pl.ds(start, GROUP), cols])
            sum_s[sub * SUB : (sub + 1) * SUB, cols] = gathered(res)
    probs_ref[...] = jnp.zeros(probs_ref.shape, BF)
    for doc in range(docs):
        low, high = bounds[doc], bounds[docs + doc]
        rows = slice(doc * LAND, (doc + 1) * LAND)

        @pl.when((high > first) & (low < first + BLOCK))
        def _():
            place = iota((1, BLOCK), 1) + first
            valid = (place >= low) & (place < high)
            for g in range(groups):
                cols = slice(g * GROUP, (g + 1) * GROUP)
                scores = dot_nt(spread(mk_ref[rows, cols]), q_ref[:, cols]) * scale
                scores = scores.reshape(4, LAND, BLOCK)
                weights = jnp.exp(scores - jnp.max(scores, axis=1, keepdims=True))
                probs = weights / jnp.sum(weights, axis=1, keepdims=True)
                probs = jnp.where(valid, probs.reshape(GROUP, BLOCK), 0.0).astype(BF)
                probs_ref[cols, :] = probs_ref[cols, :] + probs
                sum_s[:, cols] = sum_s[:, cols] + dot_tn(probs, spread(mix_ref[rows, cols]))

    mixed_ref[...] = sum_s[...].astype(BF)


def token_back_kernel(
    docs, scale, bounds, q_ref, gm_ref, probs_ref, mk_ref, mix_ref, gq_ref, gmix_ref, gmk_ref, gq_s
):
    width = q_ref.shape[1]
    groups = width // GROUP
    first = pl.program_id(0) * BLOCK

    @pl.when(pl.program_id(0) == 0)
    def _():
        gmix_ref[...] = jnp.zeros(gmix_ref.shape, F32)
        gmk_ref[...] = jnp.zeros(gmk_ref.shape, F32)

    gq_s[...] = jnp.zeros(gq_s.shape, F32)
    for doc in range(docs):
        low, high = bounds[doc], bounds[docs + doc]
        rows = slice(doc * LAND, (doc + 1) * LAND)

        @pl.when((high > first) & (low < first + BLOCK))
        def _():
            place = iota((1, BLOCK), 1) + first
            valid = (place >= low) & (place < high)
            for g in range(groups):
                cols = slice(g * GROUP, (g + 1) * GROUP)
                probs = jnp.where(valid, probs_ref[cols, :].astype(F32), 0.0)
                gmix_ref[rows, cols] += gathered(dot_nn(probs.astype(BF), gm_ref[:, cols]))
                grad = dot_nt(spread(mix_ref[rows, cols]), gm_ref[:, cols])
                heavy = (probs * grad).reshape(4, LAND, BLOCK)
                shared = probs.reshape(4, LAND, BLOCK) * jnp.sum(heavy, axis=1, keepdims=True)
                grad = ((heavy - shared).reshape(GROUP, BLOCK) * scale).astype(BF)
                gmk_ref[rows, cols] += gathered(dot_nn(grad, q_ref[:, cols]))
                gq_s[:, cols] += dot_tn(grad, spread(mk_ref[rows, cols]))

    gq_ref[...] = gq_s[...].astype(BF)


def conv_back_kernel(docs, bounds, gm_ref, v_ref, taps_ref, out_ref, prod_ref, band_s):
    width = gm_ref.shape[1]
    groups = width // GROUP
    radius = (TAPS - 1) // 2
    first = pl.program_id(0) * BLOCK

    @pl.when(pl.program_id(0) == 0)
    def _():
        make_band(taps_ref, band_s)
        prod_ref[...] = jnp.zeros(prod_ref.shape, F32)

    for sub in range(BLOCK // SUB):
        start = pl.multiple_of(first + sub * SUB, SUB)
        same = same_doc(start, bounds, docs, radius)
        same = jnp.where(jnp.concatenate([same] * 4, axis=0), 1.0, 0.0)
        for g in range(groups):
            cols = slice(g * GROUP, (g + 1) * GROUP)
            tall = slice(g * 4 * SUB, (g + 1) * 4 * SUB)
            band = band_s[tall, :] * same.astype(BF)
            res = dot_nn(band, gm_ref[pl.ds(start, GROUP), cols])
            out_ref[sub * SUB : (sub + 1) * SUB, cols] = gathered(res)
            own = gm_ref[pl.ds(pl.multiple_of(start + radius, 16), SUB), cols]
            product = dot_nt(spread(own), v_ref[pl.ds(start, GROUP), cols])
            prod_ref[tall, :] += product * same


def ffn_kernel(
    x_ref, mixed_ref, cot_ref, w_out_ref, w_up_ref, w_down_ref, rows_ref, bias_up_ref,
    result_ref, grad_one_ref, active_ref, grad_up_ref, low_ref, low_two_ref, low_one_ref,
    grad_mixed_ref, sums_ref, sum_up_ref, slope_s,
):
    width = x_ref.shape[1]
    hidden = w_up_ref.shape[1]
    chunks = [slice(at, at + width) for at in range(0, hidden, width)]

    def row(i):
        return rows_ref[i : i + 1, :]

    @pl.when(pl.program_id(0) == 0)
    def _():
        sums_ref[...] = jnp.zeros(sums_ref.shape, F32)
        sum_up_ref[...] = jnp.zeros(sum_up_ref.shape, F32)

    def add_sum(i, cells):
        sums_ref[i : i + 1, :] += jnp.sum(cells, axis=0, keepdims=True)

    attended = dot_nn(mixed_ref[...], w_out_ref[...]) + row(0)
    norm_one, inverse_one = normalize(x_ref[...].astype(F32) + attended)
    hidden_one = norm_one * row(1) + row(2)
    hidden_low = hidden_one.astype(BF)
    low_ref[...] = hidden_low
    lowered = hidden_one + row(3)
    for cols in chunks:
        upper = dot_nn(hidden_low, w_up_ref[:, cols]) + bias_up_ref[:1, cols]
        active, slope = gelu_both(upper)
        active = active.astype(BF)
        active_ref[:, cols] = active
        slope_s[:, cols] = slope.astype(BF)
        lowered = lowered + dot_nn(active, w_down_ref[cols, :])
    norm_two, inverse_two = normalize(lowered)
    result_ref[...] = norm_two * row(4) + row(5)
    upstream = cot_ref[...].astype(F32)
    add_sum(0, upstream * norm_two)
    add_sum(1, upstream)
    grad_two = norm_back(upstream * row(4), norm_two, inverse_two)
    low_two = grad_two.astype(BF)
    low_two_ref[...] = low_two
    add_sum(2, low_two.astype(F32))
    grad_hidden = grad_two
    for cols in chunks:
        grad_up = dot_nt(low_two, w_down_ref[cols, :]) * slope_s[:, cols].astype(F32)
        grad_up = grad_up.astype(BF)
        grad_up_ref[:, cols] = grad_up
        sum_up_ref[:1, cols] += jnp.sum(grad_up.astype(F32), axis=0, keepdims=True)
        grad_hidden = grad_hidden + dot_nt(grad_up, w_up_ref[:, cols])
    add_sum(3, grad_hidden * norm_one)
    add_sum(4, grad_hidden)
    grad_one = norm_back(grad_hidden * row(1), norm_one, inverse_one)
    grad_one_ref[...] = grad_one
    low_one = grad_one.astype(BF)
    low_one_ref[...] = low_one
    add_sum(5, low_one.astype(F32))
    grad_mixed_ref[...] = dot_nt(low_one, w_out_ref[...]).astype(BF)


def landmark_back_kernel(
    docs, scale, bounds, k_ref, v_ref, conv_ref, mq_ref, grad_ref, level_ref, dots_ref,
    gk_ref, gv_ref, gmq_ref, gk_s, gv_s,
):
    width = k_ref.shape[1]
    groups = width // GROUP
    first = pl.program_id(0) * BLOCK

    @pl.when(pl.program_id(0) == 0)
    def _():
        gmq_ref[...] = jnp.zeros(gmq_ref.shape, F32)

    gk_s[...] = jnp.zeros(gk_s.shape, F32)
    gv_s[...] = conv_ref[...]
    for doc in range(docs):
        low, high = bounds[doc], bounds[docs + doc]
        rows = slice(doc * LAND, (doc + 1) * LAND)

        @pl.when((high > first) & (low < first + BLOCK))
        def _():
            place = iota((1, BLOCK), 1) + first
            valid = (place >= low) & (place < high)

            level, dots = merge_three(level_ref[rows, :]), merge_three(dots_ref[rows, :])

            def column(lanes, g):
                return jnp.concatenate(
                    [lanes[:, 4 * g + h : 4 * g + h + 1] for h in range(4)], axis=0
                )

            for g in range(groups):
                cols = slice(g * GROUP, (g + 1) * GROUP)
                wide_q, wide_g = spread(mq_ref[rows, cols]), spread(grad_ref[rows, cols])
                scores = dot_nt(wide_q, k_ref[:, cols]) * scale - column(level, g)
                probs = jnp.exp(jnp.where(valid, scores, NEGATIVE))
                grad = dot_nt(wide_g, v_ref[:, cols]) - column(dots, g)
                grad = (probs * grad * scale).astype(BF)
                gv_s[:, cols] += dot_tn(probs.astype(BF), wide_g)
                gk_s[:, cols] += dot_tn(grad, wide_q)
                gmq_ref[rows, cols] += gathered(dot_nn(grad, k_ref[:, cols]))

    gk_ref[...] = gk_s[...].astype(BF)
    gv_ref[...] = gv_s[...].astype(BF)


def gelu_both(upper):
    tangent = jnp.tanh(0.7978845608028654 * (upper + 0.044715 * upper * upper * upper))
    inner_slope = 0.7978845608028654 * (1.0 + 3.0 * 0.044715 * upper * upper)
    active = 0.5 * upper * (1.0 + tangent)
    slope = 0.5 * (1.0 + tangent) + 0.5 * upper * (1.0 - tangent * tangent) * inner_slope
    return active, slope


def normalize(residual):
    row_mean = jnp.mean(residual, axis=-1, keepdims=True)
    centered = residual - row_mean
    row_var = jnp.mean(centered * centered, axis=-1, keepdims=True)
    inverse_dev = lax.rsqrt(row_var + 1e-05)
    return (centered * inverse_dev, inverse_dev)


def norm_back(grad_normed, normed, inverse_dev):
    return inverse_dev * (
        grad_normed
        - jnp.mean(grad_normed, axis=-1, keepdims=True)
        - normed * jnp.mean(grad_normed * normed, axis=-1, keepdims=True)
    )


def dot_high(a, b, dims):
    return lax.dot_general(
        a, b, (dims, ((), ())), precision=HIGH, preferred_element_type=F32
    )


NN, NT, TN = ((1,), (0,)), ((1,), (1,)), ((0,), (0,))


def pinv_kernel(scale, q_ref, k_ref, inverse_ref, kernel_ref, saved_ref):
    count = q_ref.shape[0]
    eye = (iota((LAND, LAND), 0) == iota((LAND, LAND), 1)).astype(F32)
    kernels, inverses = [], []
    for p in range(count):
        scores = dot_high(q_ref[p], k_ref[p], NT) * scale
        weights = jnp.exp(scores - jnp.max(scores, axis=1, keepdims=True))
        kernel = weights / jnp.sum(weights, axis=1, keepdims=True)
        kernel_ref[p] = kernel
        kernels.append(kernel)
        largest = jnp.max(jnp.sum(kernel, axis=0, keepdims=True), axis=1, keepdims=True)
        inverses.append(kernel.T / largest)
    for sweep in range(NS_ITERS):
        products = [dot_high(kernels[p], inverses[p], NN) for p in range(count)]
        second = [
            15.0 * eye - dot_high(products[p], 7.0 * eye - products[p], NN) for p in range(count)
        ]
        third = [13.0 * eye - dot_high(products[p], second[p], NN) for p in range(count)]
        for p in range(count):
            at = (sweep * count + p) * 4
            saved_ref[at], saved_ref[at + 1] = inverses[p], products[p]
            saved_ref[at + 2], saved_ref[at + 3] = second[p], third[p]
        inverses = [0.25 * dot_high(inverses[p], third[p], NN) for p in range(count)]
    for p in range(count):
        inverse_ref[p] = inverses[p]


def pinv_back_kernel(scale, q_ref, k_ref, kernel_ref, saved_ref, grad_ref, avg_ref, gq_ref, gk_ref):
    count = q_ref.shape[0]
    each = range(count)
    eye = (iota((LAND, LAND), 0) == iota((LAND, LAND), 1)).astype(F32)
    grads = [dot_nt(grad_ref[p], avg_ref[p]) for p in each]
    kernels = [kernel_ref[p] for p in each]
    totals = [jnp.zeros((LAND, LAND), F32) for p in each]
    for sweep in reversed(range(NS_ITERS)):
        first = [(sweep * count + p) * 4 for p in each]
        inverses, products = [saved_ref[a] for a in first], [saved_ref[a + 1] for a in first]
        grad_third = [0.25 * dot_high(inverses[p], grads[p], TN) for p in each]
        nexts = [0.25 * dot_high(grads[p], saved_ref[first[p] + 3], NT) for p in each]
        grad_second = [-dot_high(products[p], grad_third[p], TN) for p in each]
        grad_product = [-dot_high(grad_third[p], saved_ref[first[p] + 2], NT) for p in each]
        grad_first = [-dot_high(products[p], grad_second[p], TN) for p in each]
        grad_product = [
            grad_product[p]
            - dot_high(grad_second[p], 7.0 * eye - products[p], NT)
            - grad_first[p]
            for p in each
        ]
        totals = [totals[p] + dot_high(grad_product[p], inverses[p], NT) for p in each]
        grads = [nexts[p] + dot_high(kernels[p], grad_product[p], TN) for p in each]
    for p in each:
        kernel = kernels[p]
        sums = jnp.sum(kernel, axis=0, keepdims=True)
        largest = jnp.max(sums, axis=1, keepdims=True)
        flipped = grads[p].T
        loss = jnp.sum(jnp.sum(flipped * kernel, axis=1, keepdims=True), axis=0, keepdims=True)
        at_top = (sums == largest).astype(F32)
        at_top = at_top / jnp.sum(at_top, axis=1, keepdims=True)
        grad = totals[p] + flipped / largest - at_top * (loss / (largest * largest))
        grad = kernel * (grad - jnp.sum(grad * kernel, axis=1, keepdims=True)) * scale
        gq_ref[p] = dot_high(grad, k_ref[p], NN)
        gk_ref[p] = dot_high(grad, q_ref[p], TN)


def settle_kernel(side_ref, mine_ref, other_ref, out_ref):
    own = pl.program_id(0) == side_ref[0]

    @pl.when(own)
    def _():
        out_ref[...] = mine_ref[...].astype(F32)

    @pl.when(jnp.logical_not(own))
    def _():
        out_ref[...] = other_ref[...].astype(F32)


def settle(state):
    mine, other, down, back = last_swap(state)
    moved = len(stages(("row", "near", "far"))) - len(stages(()))
    down, back = down[1 : 1 + moved], back[1 : 1 + moved]
    blocks = 1 << moved
    rows, columns = mine.shape[0] // blocks, mine.shape[1]

    def source(j):
        bits = {stage: (j >> (moved - 1 - i)) % 2 for i, stage in enumerate(down)}
        at = 0
        for stage in back:
            at = at * 2 + bits[stage]
        return at

    side = (lax.axis_index("seq") % 2).astype(jnp.int32).reshape(1)
    return pl.pallas_call(
        settle_kernel,
        grid_spec=pltpu.PrefetchScalarGridSpec(
            num_scalar_prefetch=1,
            grid=(2, blocks),
            in_specs=[
                pl.BlockSpec((rows, columns), lambda h, j, s: (jnp.where(h == s[0], source(j), 0), 0)),
                pl.BlockSpec((rows, columns), lambda h, j, s: (jnp.where(h == s[0], 0, source(j)), 0)),
            ],
            out_specs=pl.BlockSpec((rows, columns), lambda h, j, s: (h * blocks + j, 0)),
        ),
        out_shape=jax.ShapeDtypeStruct((2 * blocks * rows, columns), F32),
        name="settle",
    )(side, mine, other)


def settle_qkv_kernel(side_ref, late_ref, late_other_ref, early_ref, early_other_ref, out_ref):
    part = pl.program_id(0)
    own = jnp.where(part == 0, 0, 1) == side_ref[0]
    choices = [
        (late_ref, own & (part < 2)),
        (late_other_ref, jnp.logical_not(own) & (part < 2)),
        (early_ref, own & (part == 2)),
        (early_other_ref, jnp.logical_not(own) & (part == 2)),
    ]
    for ref, chosen in choices:

        @pl.when(chosen)
        def _():
            out_ref[...] = ref[...].astype(F32)


def settle_qkv(late, late_other, early, early_other, width):
    side = (lax.axis_index("seq") % 2).astype(jnp.int32).reshape(1)
    rows = width // 3

    def spec(used):
        return pl.BlockSpec((rows, width), lambda j, i, s: (jnp.where(used(j), i, 0), 0))

    return pl.pallas_call(
        settle_qkv_kernel,
        grid_spec=pltpu.PrefetchScalarGridSpec(
            num_scalar_prefetch=1,
            grid=(3, 3),
            in_specs=[spec(lambda j: j < 2), spec(lambda j: j < 2)] + [spec(lambda j: j == 2)] * 2,
            out_specs=pl.BlockSpec((rows, width), lambda j, i, s: (i, j)),
        ),
        out_shape=jax.ShapeDtypeStruct((width, 3 * width), F32),
        name="settle_qkv",
    )(side, late, late_other, early, early_other)


def per_device(
    inputs, doc_lengths, w_qkv, bias_q, bias_v, conv_taps, w_out, bias_out, norm1_gain,
    norm1_bias, w_up, bias_up, w_down, bias_down, norm2_gain, norm2_bias, cotangent,
):
    tokens = inputs[0]
    tok_count, width = tokens.shape
    heads, tap_count = conv_taps.shape
    size = width // heads
    radius = (tap_count - 1) // 2
    lengths = doc_lengths[0]
    docs = lengths.shape[0]
    mark_count = docs * LAND
    scale = 1.0 / math.sqrt(size)
    seq_count = lax.axis_size("seq")
    me = lax.axis_index("seq")
    row_first = me * tok_count
    ends = jnp.cumsum(lengths)
    starts = ends - lengths
    bounds = (jnp.concatenate([starts, ends]) - row_first).astype(jnp.int32)
    within = jnp.arange(LAND + 1, dtype=jnp.int32)
    edges = starts[:, None] + (within[None, :] * lengths[:, None] + LAND - 1) // LAND
    mark_low = edges[:, :-1].reshape(mark_count, 1)
    mark_high = edges[:, 1:].reshape(mark_count, 1)
    counts = (mark_high - mark_low).astype(F32)
    places = row_first + jnp.arange(tok_count, dtype=jnp.int32)[None, :]
    onehot = ((places >= mark_low) & (places < mark_high)).astype(BF)
    rows_in = (((0,), (0,)), ((), ()))
    cols_in = (((1,), (1,)), ((), ()))
    blocks = tok_count // BLOCK
    window_rows = tok_count + GROUP - SUB
    smem = pl.BlockSpec(memory_space=pltpu.SMEM)
    params = pltpu.CompilerParams(vmem_limit_bytes=40 * 1024 * 1024)
    tok_spec = pl.BlockSpec((BLOCK, width), lambda i: (i, 0))

    def part(col):
        return pl.BlockSpec((BLOCK, width), lambda i: (i, col))

    def fixed(*shape):
        return pl.BlockSpec(shape, lambda i: (0,) * len(shape))

    def shaped(shape, dtype):
        return jax.ShapeDtypeStruct(shape, dtype)

    means = jnp.dot(onehot, tokens, preferred_element_type=F32) / counts
    mean_in = seq_whole(seq_quarter(means.astype(BF), add_join))
    marks = jnp.dot(mean_in, w_qkv[:, : 2 * width], preferred_element_type=F32)
    mark_q = (marks[:, :width] + bias_q).astype(BF)
    mark_k = marks[:, width:].astype(BF)

    bias = jnp.concatenate([bias_q, jnp.zeros_like(bias_q), bias_v])
    qkv = (jnp.dot(tokens, w_qkv, preferred_element_type=F32) + bias).astype(BF)
    value_ext = extended(qkv[:, 2 * width :], radius, window_rows)
    value_ext, mark_q, mark_k = lax.optimization_barrier((value_ext, mark_q, mark_k))

    def one_col(col):
        return pl.BlockSpec((tok_count, width), lambda i: (0, col))

    stats = pl.pallas_call(
        lambda *refs: landmark_kernel(docs, scale, *refs),
        grid=(1,),
        in_specs=[smem, fixed(mark_count, width), one_col(1), one_col(2)],
        out_specs=fixed(mark_count, width + 128),
        out_shape=shaped((mark_count, width + 128), BF),
        scratch_shapes=[
            pltpu.VMEM((width, 128), F32), pltpu.VMEM((width, 128), F32),
            pltpu.VMEM((width, GROUP), F32),
        ],
        compiler_params=params,
        name="landmark",
    )(bounds, mark_q, qkv, qkv)
    far_count = seq_count // 4
    own_count = -(-heads // far_count)
    own_doc = (me % 2) * 2 + (me // 2) % 2
    own_at = (me // 4) * own_count * size
    spare = far_count * own_count * size - width

    def own_heads(array):
        array = jnp.pad(array, ((0, 0), (0, spare)))
        array = lax.dynamic_slice_in_dim(array, own_at, own_count * size, 1)
        return array.reshape(LAND, own_count, size).transpose(1, 0, 2)

    def of_doc(array):
        return lax.dynamic_slice_in_dim(array, own_doc * LAND, LAND, 0)

    mine, other = halves(stats, 1)
    stats = join(mine, swap(other, "seq", 1))
    stats, later_q, later_k = lax.optimization_barrier((stats, mark_q, mark_k))
    own_q = own_heads(of_doc(later_q)).astype(F32)
    own_k = own_heads(of_doc(later_k)).astype(F32)
    square = (own_count, LAND, LAND)
    own_inverse, kernel, saved = pl.pallas_call(
        lambda *refs: pinv_kernel(scale, *refs),
        out_shape=(
            shaped(square, F32), shaped(square, F32),
            shaped((4 * NS_ITERS * own_count, LAND, LAND), F32),
        ),
        name="pinv",
    )(own_q, own_k)
    inverse = own_inverse.transpose(1, 0, 2).reshape(LAND, own_count * size).astype(BF)
    mine, other = halves(stats, 2)
    stats = join(mine, swap(other, "seq", 2))
    for i in range(2, seq_count.bit_length() - 1):
        other = swap(jnp.concatenate([stats, inverse], 1), "seq", 1 << i)
        stats = join(stats, other[:, : width + 128])
        other = other[:, width + 128 :]
        inverse = jnp.where(
            (me >> i) % 2 == 0,
            jnp.concatenate([inverse, other], 1),
            jnp.concatenate([other, inverse], 1),
        )
    inverse = inverse[:, :width]
    mix = pl.pallas_call(
        mix_kernel, out_shape=shaped((LAND, width + 128), BF), name="mix"
    )(inverse, stats)
    mix = seq_whole(mix)

    taps = jnp.pad(conv_taps, ((0, 0), (0, GROUP - tap_count)))
    mark_spec = fixed(mark_count, width)
    mixed, probs = pl.pallas_call(
        lambda *refs: token_kernel(docs, scale, *refs),
        grid=(blocks,),
        in_specs=[
            smem, part(0), fixed(window_rows, width), mark_spec, mark_spec, fixed(heads, GROUP)
        ],
        out_specs=(tok_spec, pl.BlockSpec((width, BLOCK), lambda i: (0, i))),
        out_shape=(shaped((tok_count, width), BF), shaped((width, tok_count), BF)),
        scratch_shapes=[pltpu.VMEM((heads * SUB, GROUP), BF), pltpu.VMEM((BLOCK, width), F32)],
        compiler_params=params,
        name="token",
    )(bounds, qkv, value_ext, mark_k, mix, taps)

    hidden = w_up.shape[1]
    vectors = jnp.stack([bias_out, norm1_gain, norm1_bias, bias_down, norm2_gain, norm2_bias])
    vectors = jnp.pad(vectors, ((0, 2), (0, 0)))
    wide_spec = pl.BlockSpec((FFN_BLOCK, hidden), lambda i: (i, 0))
    ffn_spec = pl.BlockSpec((FFN_BLOCK, width), lambda i: (i, 0))
    narrow = shaped((tok_count, width), BF)
    (
        result, grad_one, active, grad_upper, hidden_low, grad_low_two, grad_low_one,
        grad_mixed, sums, sum_up,
    ) = pl.pallas_call(
        ffn_kernel,
        grid=(tok_count // FFN_BLOCK,),
        in_specs=[
            ffn_spec, ffn_spec, ffn_spec, fixed(width, width), fixed(width, hidden),
            fixed(hidden, width), fixed(8, width), fixed(8, hidden),
        ],
        out_specs=(
            ffn_spec, ffn_spec, wide_spec, wide_spec, ffn_spec, ffn_spec, ffn_spec, ffn_spec,
            fixed(8, width), fixed(8, hidden),
        ),
        out_shape=(
            shaped((tok_count, width), F32), shaped((tok_count, width), F32),
            shaped((tok_count, hidden), BF), shaped((tok_count, hidden), BF),
            narrow, narrow, narrow, narrow, shaped((8, width), F32), shaped((8, hidden), F32),
        ),
        scratch_shapes=[pltpu.VMEM((FFN_BLOCK, hidden), BF)],
        compiler_params=pltpu.CompilerParams(vmem_limit_bytes=58 * 1024 * 1024),
        name="ffn",
    )(
        tokens, mixed, cotangent[0], w_out, w_up, w_down, vectors,
        jnp.broadcast_to(bias_up[None, :], (8, hidden)),
    )

    grad_queries, grad_mix, grad_mk = pl.pallas_call(
        lambda *refs: token_back_kernel(docs, scale, *refs),
        grid=(blocks,),
        in_specs=[
            smem, part(0), tok_spec, pl.BlockSpec((width, BLOCK), lambda i: (0, i)), mark_spec,
            mark_spec,
        ],
        out_specs=(tok_spec, mark_spec, mark_spec),
        out_shape=(
            shaped((tok_count, width), BF), shaped((mark_count, width), F32),
            shaped((mark_count, width), F32),
        ),
        scratch_shapes=[pltpu.VMEM((BLOCK, width), F32)],
        compiler_params=params,
        name="token_back",
    )(bounds, qkv, grad_mixed, probs, mark_k, mix)
    grad_w_down = lax.dot_general(active, grad_low_two, rows_in, preferred_element_type=F32)
    grad_w_up = lax.dot_general(hidden_low, grad_upper, rows_in, preferred_element_type=F32)
    down = begin(grad_w_down.astype(BF), ("row", "far", "near"), ("far", "near", "row"))
    up = begin(grad_w_up.astype(BF), ("row", "near", "far"), ("near", "far", "row"))
    grad_mix = seq_quarter(grad_mix.astype(BF), add_join)
    down, up = advance(down, 1), advance(up, 1)
    grad_mix, (down, up) = tied(grad_mix, [down, up])
    down, up = advance(down, 1), advance(up, 1)
    grad_w_out = lax.dot_general(mixed, grad_low_one, rows_in, preferred_element_type=F32)

    grad_ext = extended(grad_mixed, radius, window_rows)
    grad_conv, products = pl.pallas_call(
        lambda *refs: conv_back_kernel(docs, *refs),
        grid=(blocks,),
        in_specs=[
            smem, fixed(window_rows, width), fixed(window_rows, width), fixed(heads, GROUP)
        ],
        out_specs=(tok_spec, fixed(heads * SUB, GROUP)),
        out_shape=(shaped((tok_count, width), F32), shaped((heads * SUB, GROUP), F32)),
        scratch_shapes=[pltpu.VMEM((heads * SUB, GROUP), BF)],
        compiler_params=params,
        name="conv_back",
    )(bounds, grad_ext, value_ext, jnp.pad(conv_taps[:, ::-1], ((0, 0), (0, GROUP - tap_count))))
    grad_avg = pl.pallas_call(
        mix_back_kernel, out_shape=shaped((LAND, width + 128), BF), name="mix_back"
    )(inverse, stats, grad_mix)
    grad_avg = seq_whole(grad_avg)
    lane_spec = pl.BlockSpec((mark_count, 128), lambda i: (0, width // 128))
    grad_keys, grad_values, grad_mq = pl.pallas_call(
        lambda *refs: landmark_back_kernel(docs, scale, *refs),
        grid=(blocks,),
        in_specs=[
            smem, part(1), part(2), tok_spec, mark_spec, mark_spec, lane_spec, lane_spec
        ],
        out_specs=(tok_spec, tok_spec, mark_spec),
        out_shape=(
            shaped((tok_count, width), BF), shaped((tok_count, width), BF),
            shaped((mark_count, width), F32),
        ),
        scratch_shapes=[pltpu.VMEM((BLOCK, width), F32), pltpu.VMEM((BLOCK, width), F32)],
        compiler_params=params,
        name="landmark_back",
    )(bounds, qkv, qkv, grad_conv, mark_q, grad_avg, mix, grad_avg)

    grad_keys, (down, up) = tied(grad_keys, [down, up])
    down, up = advance(down, 1), advance(up, 1)
    grad_mix, grad_values = lax.optimization_barrier((grad_mix, grad_values))
    grad_mq_small, grad_mk_small = pl.pallas_call(
        lambda *refs: pinv_back_kernel(scale, *refs),
        out_shape=(shaped(square, F32), shaped(square, F32)),
        name="pinv_back",
    )(own_q, own_k, kernel, saved, own_heads(grad_mix), own_heads(stats[:, :width]))

    def placed(array):
        array = array.transpose(1, 0, 2).reshape(LAND, own_count * size)
        array = lax.dynamic_update_slice_in_dim(
            jnp.zeros((LAND, width + spare), F32), array, own_at, 1
        )[:, :width]
        return lax.dynamic_update_slice_in_dim(
            jnp.zeros((mark_count, width), F32), array, own_doc * LAND, 0
        )

    grad_mq = grad_mq + placed(grad_mq_small)
    grad_mk = grad_mk + placed(grad_mk_small)
    grad_marks = jnp.concatenate([grad_mq, grad_mk], axis=1).astype(BF)
    mark_back = lax.dot_general(
        grad_marks, w_qkv[:, : 2 * width], cols_in, preferred_element_type=F32
    ) / counts
    mark_back = mark_back.astype(BF)

    grad_bias_q = jnp.sum(grad_queries.astype(F32), axis=0) + jnp.sum(grad_mq, axis=0)
    grad_bias_v = jnp.sum(grad_values.astype(F32), axis=0)
    grad_projected = jnp.concatenate([grad_queries, grad_keys, grad_values], axis=1)

    def weight_grad(grads):
        return lax.dot_general(tokens, grads, rows_in, preferred_element_type=F32)

    early = jnp.concatenate([grad_w_out.astype(BF), weight_grad(grad_values).astype(BF)], 0)
    early = begin(early, ("row", "near", "far"), ("row", "near", "far"))
    early = advance(early, 1)
    grad_marks, (early,) = tied(grad_marks, [early])
    early = advance(early, 1)
    mark_grad_q = lax.dot_general(
        mean_in, grad_marks[:, :width], rows_in, preferred_element_type=F32
    )
    mark_grad_k = lax.dot_general(
        mean_in, grad_marks[:, width:], rows_in, preferred_element_type=F32
    )
    products, (early,) = tied(products, [early])
    reach = SUB + tap_count - 1
    products = products.reshape(heads, SUB, GROUP)[:, :, :reach].reshape(heads, SUB * reach)
    products = jnp.pad(products, ((0, 0), (0, SUB))).reshape(heads, SUB, reach + 1)
    grad_conv_taps = jnp.sum(products, axis=1)[:, :tap_count]
    others = jnp.concatenate(
        [
            sum_up[0].reshape(hidden // width, width),
            grad_bias_q[None],
            grad_bias_v[None],
            jnp.pad(grad_conv_taps.reshape(1, -1), ((0, 0), (0, width - heads * tap_count))),
            jnp.zeros((4 - hidden // width + 1, width), F32),
        ],
        0,
    )
    spare_rows = width // 6
    small = jnp.concatenate([sums, others], 0).astype(BF)
    small = jnp.pad(small, ((0, spare_rows - small.shape[0]), (0, 0)))
    small = lax.optimization_barrier(small)
    late = jnp.concatenate(
        [
            (weight_grad(grad_queries) + mark_grad_q).astype(BF),
            small,
            (weight_grad(grad_keys) + mark_grad_k).astype(BF),
            jnp.zeros((spare_rows, width), BF),
        ],
        0,
    )
    late = begin(late, ("row", "far", "near"), ("row", "far", "near"))
    late = advance(late, 1)
    mark_back = seq_quarter(mark_back, add_join)
    mark_back, (early, late, down, up) = tied(mark_back, [early, late, down, up])
    early, late = advance(early, 1), advance(late, 1)
    down, up = advance(down, 1), advance(up, 1)
    mark_back = seq_whole(mark_back)
    mark_back, (early, late, down, up) = tied(mark_back, [early, late, down, up])
    early, early_other = last_swap(early)[:2]
    late, late_other = last_swap(late)[:2]
    sum_w_down, sum_w_up = settle(down), settle(up)
    sum_w_qkv = settle_qkv(late, late_other, early, early_other, width)
    first_core = me % 2 == 0
    sum_w_out = jnp.where(first_core, early, early_other).astype(F32)
    flat = jnp.where(first_core, late[width:], late_other[width:])[:16].astype(F32)
    at = sums.shape[0] + hidden // width
    pieces = [
        flat[at], flat[at + 1], flat[at + 2, : heads * tap_count], flat[5], flat[3], flat[4],
        flat[sums.shape[0] : at].reshape(hidden), flat[2], flat[0], flat[1],
    ]
    grad_input = (
        grad_one
        + lax.dot_general(grad_projected, w_qkv, cols_in, preferred_element_type=F32)
        + lax.dot_general(onehot, mark_back, rows_in, preferred_element_type=F32)
    )
    return (
        result[None], grad_input[None], sum_w_qkv, pieces[0], pieces[1],
        pieces[2].reshape(heads, tap_count), sum_w_out, pieces[3], pieces[4], pieces[5],
        sum_w_up, pieces[6], sum_w_down, pieces[7], pieces[8], pieces[9],
    )


def solution(mesh):
    whole, tokens = P(), P("row", "seq", None)
    return jax.shard_map(
        per_device,
        mesh=mesh,
        in_specs=(tokens, P("row", None)) + (whole,) * 14 + (tokens,),
        out_specs=(tokens, tokens) + (whole,) * 14,
        check_vma=False,
    )
```

```python
import math

import jax
import jax.numpy as jnp
from jax import lax
from jax.experimental import pallas as pl
from jax.experimental.pallas import tpu as pltpu
from jax.sharding import PartitionSpec as P

LAND = 64
NS_ITERS = 6
HIGH = lax.Precision.HIGHEST
NEGATIVE = -1e30
BF = jnp.bfloat16
F32 = jnp.float32

BLOCK = 256
GROUP = 256
SUB = 128
TAPS = 33
FFN_BLOCK = 256


def swap(array, axis, bit):
    count = lax.axis_size(axis)
    return lax.ppermute(array, axis, [(i, i ^ bit) for i in range(count)])


def add_parts(parts):
    total = parts[0].astype(F32)
    for part in parts[1:]:
        total = total + part.astype(F32)
    return total


def halves(array, bit):
    rows = array.shape[0] // 2
    side = (lax.axis_index("seq") // bit) % 2
    mine = lax.dynamic_slice_in_dim(array, side * rows, rows, 0)
    other = lax.dynamic_slice_in_dim(array, (1 - side) * rows, rows, 0)
    return mine, other


def seq_quarter(array, join):
    bits = [1 << i for i in range(lax.axis_size("seq").bit_length() - 1)]
    for bit in bits[:2]:
        mine, other = halves(array, bit)
        array = join(mine, swap(other, "seq", bit))
    for bit in bits[2:]:
        array = join(array, swap(array, "seq", bit))
    return array


def paired(array, axis, bit, dim):
    other = swap(array, axis, bit)
    side = (lax.axis_index(axis) // bit) % 2
    return jnp.where(
        side == 0,
        jnp.concatenate([array, other], dim),
        jnp.concatenate([other, array], dim),
    )


def seq_whole(array):
    return paired(paired(array, "seq", 2, 0), "seq", 1, 0)


def add_join(first, second):
    return (first.astype(F32) + second.astype(F32)).astype(BF)


def stages(order):
    row = [("row", 1 << i) for i in range(lax.axis_size("row").bit_length() - 1)]
    seq = [[("seq", 1 << i)] for i in range(lax.axis_size("seq").bit_length() - 1)]
    named = {"core": seq[0], "row": row, "near": seq[1], "far": seq[2], "rest": sum(seq[3:], [])}
    return sum([named[name] for name in ("core",) + order + ("rest",)], [])


def begin(array, down, back):
    return array, stages(down), stages(back), 0


def advance(state, steps):
    held, down, back, done = state
    for step in range(done, min(done + steps, 2 * len(down))):
        if step < len(down):
            axis, bit = down[step]
            half = held.shape[0] // 2
            side = (lax.axis_index(axis) // bit) % 2
            mine = lax.dynamic_slice_in_dim(held, side * half, half, 0)
            other = lax.dynamic_slice_in_dim(held, (1 - side) * half, half, 0)
            held = mine.astype(F32) + swap(other, axis, bit).astype(F32)
            held = held.astype(BF)
        else:
            axis, bit = back[2 * len(down) - 1 - step]
            held = paired(held, axis, bit, 0)
    return held, down, back, min(done + steps, 2 * len(down))


def last_swap(state):
    down, back = state[1], state[2]
    held = advance(state, 2 * len(down) - 1 - state[3])[0]
    return held, swap(held, *down[0]), down, back


def tied(values, states):
    values, helds = lax.optimization_barrier((values, [state[0] for state in states]))
    return values, [(held,) + state[1:] for held, state in zip(helds, states)]


def extended(cells, width, rows):
    count = lax.axis_size("seq")
    head = cells[:width]
    tail = cells[-width:]
    return jnp.concatenate(
        [
            lax.ppermute(tail, "seq", [(i, i + 1) for i in range(count - 1)]),
            cells,
            lax.ppermute(head, "seq", [(i + 1, i) for i in range(count - 1)]),
            jnp.zeros((rows - cells.shape[0] - 2 * width, cells.shape[1]), cells.dtype),
        ],
        axis=0,
    )


def dot_nn(a, b):
    return jnp.dot(a, b, preferred_element_type=F32)


def dot_nt(a, b):
    return lax.dot_general(a, b, (((1,), (1,)), ((), ())), preferred_element_type=F32)


def dot_tn(a, b):
    return lax.dot_general(a, b, (((0,), (0,)), ((), ())), preferred_element_type=F32)


def iota(shape, dim):
    return lax.broadcasted_iota(jnp.int32, shape, dim)


def spread(block):
    rows = block.shape[0]
    tall = jnp.concatenate([block] * 4, axis=0).astype(F32)
    shape = (4 * rows, GROUP)
    keep = iota(shape, 0) // rows == iota(shape, 1) // LAND
    return jnp.where(keep, tall, 0.0).astype(BF)


def gathered(square):
    rows = square.shape[0] // 4
    lane = iota((rows, GROUP), 1) // LAND
    out = square[:rows]
    for head in range(1, 4):
        out = jnp.where(lane == head, square[head * rows : (head + 1) * rows], out)
    return out


def by_head(columns, first, shape):
    lane = iota(shape, 1)
    out = jnp.zeros(shape, F32)
    for head, column in enumerate(columns):
        out = jnp.where((lane % 16 == first + head) & (lane < 48), column, out)
    return out


def split_three(cells):
    lane = iota(cells.shape, 1)
    high = cells.astype(BF).astype(F32)
    mid = (cells - high).astype(BF).astype(F32)
    low = cells - high - mid
    return jnp.where(lane < 16, high, jnp.where(lane < 32, mid, low)).astype(BF)


def merge_three(cells):
    cells = cells.astype(F32)
    return cells + pltpu.roll(cells, 112, 1) + pltpu.roll(cells, 96, 1)


def head_lanes(heads, width):
    return (iota((128, width), 0) == iota((128, width), 1) // LAND).astype(F32)


def doc_of(places, bounds, docs):
    out = (places >= bounds[2 * docs - 1]).astype(jnp.int32)
    for doc in range(docs):
        out = out + (places >= bounds[doc]).astype(jnp.int32)
    return out


def landmark_kernel(docs, scale, bounds, mq_ref, k_ref, v_ref, out_ref, max_s, sum_s, acc_s):
    tokens, width = k_ref.shape
    groups = width // GROUP
    heads = width // LAND
    out_ref[:, :width] = jnp.zeros((docs * LAND, width), BF)
    empty = jnp.full((docs * LAND, 128), NEGATIVE, F32)
    out_ref[:, width:] = jnp.where(iota(empty.shape, 1) < 48, split_three(empty).astype(F32), 0.0).astype(BF)
    for doc in range(docs):
        low = jnp.clip(bounds[doc], 0, tokens)
        high = jnp.clip(bounds[docs + doc], 0, tokens)
        rows = slice(doc * LAND, (doc + 1) * LAND)

        @pl.when(high > low)
        def _():
            max_s[...] = jnp.full(max_s.shape, NEGATIVE, F32)
            sum_s[...] = jnp.zeros(sum_s.shape, F32)
            acc_s[...] = jnp.zeros(acc_s.shape, F32)
            wide = [
                spread(mq_ref[rows, g * GROUP : (g + 1) * GROUP]) for g in range(groups)
            ]

            ones = jnp.ones((BLOCK, 128), BF)

            def step(block, carry):
                first = pl.multiple_of(block * BLOCK, BLOCK)
                at = pl.ds(first, BLOCK)
                place = iota((1, BLOCK), 1) + first
                valid = (place >= low) & (place < high)
                for g in range(groups):
                    cols = slice(g * GROUP, (g + 1) * GROUP)
                    scores = dot_nt(wide[g], k_ref[at, cols]) * scale
                    scores = jnp.where(valid, scores, NEGATIVE)
                    old = max_s[cols, :]
                    top = jnp.maximum(old, jnp.max(scores, axis=1, keepdims=True))
                    weights = jnp.exp(scores - twice(top)).astype(BF)
                    shrink = jnp.exp(old - top)
                    max_s[cols, :] = top
                    sum_s[cols, :] = sum_s[cols, :] * shrink + dot_nn(weights, ones)
                    acc_s[cols, :] = acc_s[cols, :] * twice(shrink) + dot_nn(weights, v_ref[at, cols])
                return carry

            lax.fori_loop(low // BLOCK, (high + BLOCK - 1) // BLOCK, step, 0)
            columns = []
            for g in range(groups):
                cols = slice(g * GROUP, (g + 1) * GROUP)
                sums = sum_s[cols, :]
                out_ref[rows, cols] = gathered(acc_s[cols, :] / twice(sums)).astype(BF)
                level = max_s[cols, :] + jnp.log(sums)
                columns += [level[h * LAND : (h + 1) * LAND] for h in range(4)]
            out_ref[rows, width:] = split_three(by_head(columns, 0, (LAND, 128)))


def twice(cells):
    return jnp.concatenate([cells, cells], axis=1)


def join_kernel(a_ref, b_ref, out_ref):
    width = a_ref.shape[1] - 128
    heads = width // LAND
    first, second = merge_three(a_ref[:, width:]), merge_three(b_ref[:, width:])
    lane = iota(first.shape, 1)
    first = jnp.where(lane < heads, first, 0.0)
    second = jnp.where(lane < heads, second, 0.0)
    top = jnp.maximum(first, second)
    exp_a, exp_b = jnp.exp(first - top), jnp.exp(second - top)
    both = exp_a + exp_b
    level = top + jnp.log(both)
    pick = head_lanes(heads, width)
    share_a = jnp.dot(exp_a / both, pick, precision=HIGH, preferred_element_type=F32)
    share_b = jnp.dot(exp_b / both, pick, precision=HIGH, preferred_element_type=F32)
    joined = a_ref[:, :width].astype(F32) * share_a + b_ref[:, :width].astype(F32) * share_b
    out_ref[:, :width] = joined.astype(BF)
    level = jnp.where(lane < heads, level, 0.0)
    level = level + pltpu.roll(level, 16, 1) + pltpu.roll(level, 32, 1)
    out_ref[:, width:] = split_three(level)


def join(first, second):
    return pl.pallas_call(
        join_kernel, out_shape=jax.ShapeDtypeStruct(first.shape, BF), name="join"
    )(first, second)


def mix_kernel(inv_ref, stat_ref, mix_ref):
    width = stat_ref.shape[1] - 128
    for g in range(width // GROUP):
        cols = slice(g * GROUP, (g + 1) * GROUP)
        mix_ref[:, cols] = dot_nn(inv_ref[:, cols], spread(stat_ref[:, cols])).astype(BF)
    mix_ref[:, width:] = stat_ref[:, width:]


def mix_back_kernel(inv_ref, stat_ref, grad_ref, out_ref):
    width = stat_ref.shape[1] - 128
    columns = []
    for g in range(width // GROUP):
        cols = slice(g * GROUP, (g + 1) * GROUP)
        grad = gathered(dot_tn(inv_ref[:, cols], grad_ref[:, cols]))
        out_ref[:, cols] = grad.astype(BF)
        product = grad * stat_ref[:, cols].astype(F32)
        lane = iota(product.shape, 1) // LAND
        for h in range(4):
            columns.append(jnp.sum(jnp.where(lane == h, product, 0.0), axis=1, keepdims=True))
    out_ref[:, width:] = split_three(by_head(columns, 0, (LAND, 128)))


def make_band(taps_ref, band_s):
    for head in range(taps_ref.shape[0]):
        row = jnp.broadcast_to(taps_ref[head : head + 1, :], (SUB, GROUP))
        band_s[head * SUB : (head + 1) * SUB, :] = pltpu.roll(row, 0, 1, stride=1, stride_axis=0).astype(BF)


def same_doc(first, bounds, docs, radius):
    rows = iota((SUB, GROUP), 0) + first
    cols = iota((SUB, GROUP), 1) + (first - radius)
    return doc_of(rows, bounds, docs) == doc_of(cols, bounds, docs)


def token_kernel(
    docs, scale, bounds, q_ref, v_ref, mk_ref, mix_ref, taps_ref, mixed_ref, probs_ref, band_s, sum_s
):
    width = q_ref.shape[1]
    groups = width // GROUP
    radius = (TAPS - 1) // 2
    first = pl.program_id(0) * BLOCK

    @pl.when(pl.program_id(0) == 0)
    def _():
        make_band(taps_ref, band_s)

    for sub in range(BLOCK // SUB):
        start = pl.multiple_of(first + sub * SUB, SUB)
        same = same_doc(start, bounds, docs, radius)
        same = jnp.where(jnp.concatenate([same] * 4, axis=0), 1.0, 0.0).astype(BF)
        for g in range(groups):
            cols = slice(g * GROUP, (g + 1) * GROUP)
            band = band_s[g * 4 * SUB : (g + 1) * 4 * SUB, :] * same
            res = dot_nn(band, v_ref[pl.ds(start, GROUP), cols])
            sum_s[sub * SUB : (sub + 1) * SUB, cols] = gathered(res)
    probs_ref[...] = jnp.zeros(probs_ref.shape, BF)
    for doc in range(docs):
        low, high = bounds[doc], bounds[docs + doc]
        rows = slice(doc * LAND, (doc + 1) * LAND)

        @pl.when((high > first) & (low < first + BLOCK))
        def _():
            place = iota((1, BLOCK), 1) + first
            valid = (place >= low) & (place < high)
            for g in range(groups):
                cols = slice(g * GROUP, (g + 1) * GROUP)
                scores = dot_nt(spread(mk_ref[rows, cols]), q_ref[:, cols]) * scale
                scores = scores.reshape(4, LAND, BLOCK)
                weights = jnp.exp(scores - jnp.max(scores, axis=1, keepdims=True))
                probs = weights / jnp.sum(weights, axis=1, keepdims=True)
                probs = jnp.where(valid, probs.reshape(GROUP, BLOCK), 0.0).astype(BF)
                probs_ref[cols, :] = probs_ref[cols, :] + probs
                sum_s[:, cols] = sum_s[:, cols] + dot_tn(probs, spread(mix_ref[rows, cols]))

    mixed_ref[...] = sum_s[...].astype(BF)


def token_back_kernel(
    docs, scale, bounds, q_ref, gm_ref, probs_ref, mk_ref, mix_ref, gq_ref, gmix_ref, gmk_ref, gq_s
):
    width = q_ref.shape[1]
    groups = width // GROUP
    first = pl.program_id(0) * BLOCK

    @pl.when(pl.program_id(0) == 0)
    def _():
        gmix_ref[...] = jnp.zeros(gmix_ref.shape, F32)
        gmk_ref[...] = jnp.zeros(gmk_ref.shape, F32)

    gq_s[...] = jnp.zeros(gq_s.shape, F32)
    for doc in range(docs):
        low, high = bounds[doc], bounds[docs + doc]
        rows = slice(doc * LAND, (doc + 1) * LAND)

        @pl.when((high > first) & (low < first + BLOCK))
        def _():
            place = iota((1, BLOCK), 1) + first
            valid = (place >= low) & (place < high)
            for g in range(groups):
                cols = slice(g * GROUP, (g + 1) * GROUP)
                probs = jnp.where(valid, probs_ref[cols, :].astype(F32), 0.0)
                gmix_ref[rows, cols] += gathered(dot_nn(probs.astype(BF), gm_ref[:, cols]))
                grad = dot_nt(spread(mix_ref[rows, cols]), gm_ref[:, cols])
                heavy = (probs * grad).reshape(4, LAND, BLOCK)
                shared = probs.reshape(4, LAND, BLOCK) * jnp.sum(heavy, axis=1, keepdims=True)
                grad = ((heavy - shared).reshape(GROUP, BLOCK) * scale).astype(BF)
                gmk_ref[rows, cols] += gathered(dot_nn(grad, q_ref[:, cols]))
                gq_s[:, cols] += dot_tn(grad, spread(mk_ref[rows, cols]))

    gq_ref[...] = gq_s[...].astype(BF)


def conv_back_kernel(docs, bounds, gm_ref, v_ref, taps_ref, out_ref, prod_ref, band_s):
    width = gm_ref.shape[1]
    groups = width // GROUP
    radius = (TAPS - 1) // 2
    first = pl.program_id(0) * BLOCK

    @pl.when(pl.program_id(0) == 0)
    def _():
        make_band(taps_ref, band_s)
        prod_ref[...] = jnp.zeros(prod_ref.shape, F32)

    for sub in range(BLOCK // SUB):
        start = pl.multiple_of(first + sub * SUB, SUB)
        same = same_doc(start, bounds, docs, radius)
        same = jnp.where(jnp.concatenate([same] * 4, axis=0), 1.0, 0.0)
        for g in range(groups):
            cols = slice(g * GROUP, (g + 1) * GROUP)
            tall = slice(g * 4 * SUB, (g + 1) * 4 * SUB)
            band = band_s[tall, :] * same.astype(BF)
            res = dot_nn(band, gm_ref[pl.ds(start, GROUP), cols])
            out_ref[sub * SUB : (sub + 1) * SUB, cols] = gathered(res)
            own = gm_ref[pl.ds(pl.multiple_of(start + radius, 16), SUB), cols]
            product = dot_nt(spread(own), v_ref[pl.ds(start, GROUP), cols])
            prod_ref[tall, :] += product * same


def ffn_kernel(
    x_ref, mixed_ref, cot_ref, w_out_ref, w_up_ref, w_down_ref, rows_ref, bias_up_ref,
    result_ref, grad_one_ref, active_ref, grad_up_ref, low_ref, low_two_ref, low_one_ref,
    grad_mixed_ref, sums_ref, sum_up_ref, slope_s,
):
    width = x_ref.shape[1]
    hidden = w_up_ref.shape[1]
    chunks = [slice(at, at + width) for at in range(0, hidden, width)]

    def row(i):
        return rows_ref[i : i + 1, :]

    @pl.when(pl.program_id(0) == 0)
    def _():
        sums_ref[...] = jnp.zeros(sums_ref.shape, F32)
        sum_up_ref[...] = jnp.zeros(sum_up_ref.shape, F32)

    def add_sum(i, cells):
        sums_ref[i : i + 1, :] += jnp.sum(cells, axis=0, keepdims=True)

    attended = dot_nn(mixed_ref[...], w_out_ref[...]) + row(0)
    norm_one, inverse_one = normalize(x_ref[...].astype(F32) + attended)
    hidden_one = norm_one * row(1) + row(2)
    hidden_low = hidden_one.astype(BF)
    low_ref[...] = hidden_low
    lowered = hidden_one + row(3)
    for cols in chunks:
        upper = dot_nn(hidden_low, w_up_ref[:, cols]) + bias_up_ref[:1, cols]
        active, slope = gelu_both(upper)
        active = active.astype(BF)
        active_ref[:, cols] = active
        slope_s[:, cols] = slope.astype(BF)
        lowered = lowered + dot_nn(active, w_down_ref[cols, :])
    norm_two, inverse_two = normalize(lowered)
    result_ref[...] = norm_two * row(4) + row(5)
    upstream = cot_ref[...].astype(F32)
    add_sum(0, upstream * norm_two)
    add_sum(1, upstream)
    grad_two = norm_back(upstream * row(4), norm_two, inverse_two)
    low_two = grad_two.astype(BF)
    low_two_ref[...] = low_two
    add_sum(2, low_two.astype(F32))
    grad_hidden = grad_two
    for cols in chunks:
        grad_up = dot_nt(low_two, w_down_ref[cols, :]) * slope_s[:, cols].astype(F32)
        grad_up = grad_up.astype(BF)
        grad_up_ref[:, cols] = grad_up
        sum_up_ref[:1, cols] += jnp.sum(grad_up.astype(F32), axis=0, keepdims=True)
        grad_hidden = grad_hidden + dot_nt(grad_up, w_up_ref[:, cols])
    add_sum(3, grad_hidden * norm_one)
    add_sum(4, grad_hidden)
    grad_one = norm_back(grad_hidden * row(1), norm_one, inverse_one)
    grad_one_ref[...] = grad_one
    low_one = grad_one.astype(BF)
    low_one_ref[...] = low_one
    add_sum(5, low_one.astype(F32))
    grad_mixed_ref[...] = dot_nt(low_one, w_out_ref[...]).astype(BF)


def landmark_back_kernel(
    docs, scale, bounds, k_ref, v_ref, conv_ref, mq_ref, grad_ref, level_ref, dots_ref,
    gk_ref, gv_ref, gmq_ref, gk_s, gv_s,
):
    width = k_ref.shape[1]
    groups = width // GROUP
    first = pl.program_id(0) * BLOCK

    @pl.when(pl.program_id(0) == 0)
    def _():
        gmq_ref[...] = jnp.zeros(gmq_ref.shape, F32)

    gk_s[...] = jnp.zeros(gk_s.shape, F32)
    gv_s[...] = conv_ref[...]
    for doc in range(docs):
        low, high = bounds[doc], bounds[docs + doc]
        rows = slice(doc * LAND, (doc + 1) * LAND)

        @pl.when((high > first) & (low < first + BLOCK))
        def _():
            place = iota((1, BLOCK), 1) + first
            valid = (place >= low) & (place < high)

            level, dots = merge_three(level_ref[rows, :]), merge_three(dots_ref[rows, :])

            def column(lanes, g):
                return jnp.concatenate(
                    [lanes[:, 4 * g + h : 4 * g + h + 1] for h in range(4)], axis=0
                )

            for g in range(groups):
                cols = slice(g * GROUP, (g + 1) * GROUP)
                wide_q, wide_g = spread(mq_ref[rows, cols]), spread(grad_ref[rows, cols])
                scores = dot_nt(wide_q, k_ref[:, cols]) * scale - column(level, g)
                probs = jnp.exp(jnp.where(valid, scores, NEGATIVE))
                grad = dot_nt(wide_g, v_ref[:, cols]) - column(dots, g)
                grad = (probs * grad * scale).astype(BF)
                gv_s[:, cols] += dot_tn(probs.astype(BF), wide_g)
                gk_s[:, cols] += dot_tn(grad, wide_q)
                gmq_ref[rows, cols] += gathered(dot_nn(grad, k_ref[:, cols]))

    gk_ref[...] = gk_s[...].astype(BF)
    gv_ref[...] = gv_s[...].astype(BF)


def gelu_both(upper):
    tangent = jnp.tanh(0.7978845608028654 * (upper + 0.044715 * upper * upper * upper))
    inner_slope = 0.7978845608028654 * (1.0 + 3.0 * 0.044715 * upper * upper)
    active = 0.5 * upper * (1.0 + tangent)
    slope = 0.5 * (1.0 + tangent) + 0.5 * upper * (1.0 - tangent * tangent) * inner_slope
    return active, slope


def normalize(residual):
    row_mean = jnp.mean(residual, axis=-1, keepdims=True)
    centered = residual - row_mean
    row_var = jnp.mean(centered * centered, axis=-1, keepdims=True)
    inverse_dev = lax.rsqrt(row_var + 1e-05)
    return (centered * inverse_dev, inverse_dev)


def norm_back(grad_normed, normed, inverse_dev):
    return inverse_dev * (
        grad_normed
        - jnp.mean(grad_normed, axis=-1, keepdims=True)
        - normed * jnp.mean(grad_normed * normed, axis=-1, keepdims=True)
    )


def dot_high(a, b, dims):
    return lax.dot_general(
        a, b, (dims, ((), ())), precision=HIGH, preferred_element_type=F32
    )


NN, NT, TN = ((1,), (0,)), ((1,), (1,)), ((0,), (0,))


def pinv_kernel(scale, q_ref, k_ref, inverse_ref, kernel_ref, saved_ref):
    count = q_ref.shape[0]
    eye = (iota((LAND, LAND), 0) == iota((LAND, LAND), 1)).astype(F32)
    kernels, inverses = [], []
    for p in range(count):
        scores = dot_high(q_ref[p], k_ref[p], NT) * scale
        weights = jnp.exp(scores - jnp.max(scores, axis=1, keepdims=True))
        kernel = weights / jnp.sum(weights, axis=1, keepdims=True)
        kernel_ref[p] = kernel
        kernels.append(kernel)
        largest = jnp.max(jnp.sum(kernel, axis=0, keepdims=True), axis=1, keepdims=True)
        inverses.append(kernel.T / largest)
    for sweep in range(NS_ITERS):
        products = [dot_high(kernels[p], inverses[p], NN) for p in range(count)]
        second = [
            15.0 * eye - dot_high(products[p], 7.0 * eye - products[p], NN) for p in range(count)
        ]
        third = [13.0 * eye - dot_high(products[p], second[p], NN) for p in range(count)]
        for p in range(count):
            at = (sweep * count + p) * 4
            saved_ref[at], saved_ref[at + 1] = inverses[p], products[p]
            saved_ref[at + 2], saved_ref[at + 3] = second[p], third[p]
        inverses = [0.25 * dot_high(inverses[p], third[p], NN) for p in range(count)]
    for p in range(count):
        inverse_ref[p] = inverses[p]


def pinv_back_kernel(scale, q_ref, k_ref, kernel_ref, saved_ref, grad_ref, avg_ref, gq_ref, gk_ref):
    count = q_ref.shape[0]
    each = range(count)
    eye = (iota((LAND, LAND), 0) == iota((LAND, LAND), 1)).astype(F32)
    grads = [dot_nt(grad_ref[p], avg_ref[p]) for p in each]
    kernels = [kernel_ref[p] for p in each]
    totals = [jnp.zeros((LAND, LAND), F32) for p in each]
    for sweep in reversed(range(NS_ITERS)):
        first = [(sweep * count + p) * 4 for p in each]
        inverses, products = [saved_ref[a] for a in first], [saved_ref[a + 1] for a in first]
        grad_third = [0.25 * dot_high(inverses[p], grads[p], TN) for p in each]
        nexts = [0.25 * dot_high(grads[p], saved_ref[first[p] + 3], NT) for p in each]
        grad_second = [-dot_high(products[p], grad_third[p], TN) for p in each]
        grad_product = [-dot_high(grad_third[p], saved_ref[first[p] + 2], NT) for p in each]
        grad_first = [-dot_high(products[p], grad_second[p], TN) for p in each]
        grad_product = [
            grad_product[p]
            - dot_high(grad_second[p], 7.0 * eye - products[p], NT)
            - grad_first[p]
            for p in each
        ]
        totals = [totals[p] + dot_high(grad_product[p], inverses[p], NT) for p in each]
        grads = [nexts[p] + dot_high(kernels[p], grad_product[p], TN) for p in each]
    for p in each:
        kernel = kernels[p]
        sums = jnp.sum(kernel, axis=0, keepdims=True)
        largest = jnp.max(sums, axis=1, keepdims=True)
        flipped = grads[p].T
        loss = jnp.sum(jnp.sum(flipped * kernel, axis=1, keepdims=True), axis=0, keepdims=True)
        at_top = (sums == largest).astype(F32)
        at_top = at_top / jnp.sum(at_top, axis=1, keepdims=True)
        grad = totals[p] + flipped / largest - at_top * (loss / (largest * largest))
        grad = kernel * (grad - jnp.sum(grad * kernel, axis=1, keepdims=True)) * scale
        gq_ref[p] = dot_high(grad, k_ref[p], NN)
        gk_ref[p] = dot_high(grad, q_ref[p], TN)


def settle_kernel(side_ref, mine_ref, other_ref, out_ref):
    own = pl.program_id(0) == side_ref[0]

    @pl.when(own)
    def _():
        out_ref[...] = mine_ref[...].astype(F32)

    @pl.when(jnp.logical_not(own))
    def _():
        out_ref[...] = other_ref[...].astype(F32)


def settle(state):
    mine, other, down, back = last_swap(state)
    moved = len(stages(("row", "near", "far"))) - len(stages(()))
    down, back = down[1 : 1 + moved], back[1 : 1 + moved]
    blocks = 1 << moved
    rows, columns = mine.shape[0] // blocks, mine.shape[1]

    def source(j):
        bits = {stage: (j >> (moved - 1 - i)) % 2 for i, stage in enumerate(down)}
        at = 0
        for stage in back:
            at = at * 2 + bits[stage]
        return at

    side = (lax.axis_index("seq") % 2).astype(jnp.int32).reshape(1)
    return pl.pallas_call(
        settle_kernel,
        grid_spec=pltpu.PrefetchScalarGridSpec(
            num_scalar_prefetch=1,
            grid=(2, blocks),
            in_specs=[
                pl.BlockSpec((rows, columns), lambda h, j, s: (jnp.where(h == s[0], source(j), 0), 0)),
                pl.BlockSpec((rows, columns), lambda h, j, s: (jnp.where(h == s[0], 0, source(j)), 0)),
            ],
            out_specs=pl.BlockSpec((rows, columns), lambda h, j, s: (h * blocks + j, 0)),
        ),
        out_shape=jax.ShapeDtypeStruct((2 * blocks * rows, columns), F32),
        name="settle",
    )(side, mine, other)


def settle_qkv_kernel(side_ref, late_ref, late_other_ref, early_ref, early_other_ref, out_ref):
    part = pl.program_id(0)
    own = jnp.where(part == 0, 0, 1) == side_ref[0]
    choices = [
        (late_ref, own & (part < 2)),
        (late_other_ref, jnp.logical_not(own) & (part < 2)),
        (early_ref, own & (part == 2)),
        (early_other_ref, jnp.logical_not(own) & (part == 2)),
    ]
    for ref, chosen in choices:

        @pl.when(chosen)
        def _():
            out_ref[...] = ref[...].astype(F32)


def settle_qkv(late, late_other, early, early_other, width):
    side = (lax.axis_index("seq") % 2).astype(jnp.int32).reshape(1)
    rows = width // 3

    def spec(used):
        return pl.BlockSpec((rows, width), lambda j, i, s: (jnp.where(used(j), i, 0), 0))

    return pl.pallas_call(
        settle_qkv_kernel,
        grid_spec=pltpu.PrefetchScalarGridSpec(
            num_scalar_prefetch=1,
            grid=(3, 3),
            in_specs=[spec(lambda j: j < 2), spec(lambda j: j < 2)] + [spec(lambda j: j == 2)] * 2,
            out_specs=pl.BlockSpec((rows, width), lambda j, i, s: (i, j)),
        ),
        out_shape=jax.ShapeDtypeStruct((width, 3 * width), F32),
        name="settle_qkv",
    )(side, late, late_other, early, early_other)


def per_device(
    inputs, doc_lengths, w_qkv, bias_q, bias_v, conv_taps, w_out, bias_out, norm1_gain,
    norm1_bias, w_up, bias_up, w_down, bias_down, norm2_gain, norm2_bias, cotangent,
):
    tokens = inputs[0]
    tok_count, width = tokens.shape
    heads, tap_count = conv_taps.shape
    size = width // heads
    radius = (tap_count - 1) // 2
    lengths = doc_lengths[0]
    docs = lengths.shape[0]
    mark_count = docs * LAND
    scale = 1.0 / math.sqrt(size)
    seq_count = lax.axis_size("seq")
    me = lax.axis_index("seq")
    row_first = me * tok_count
    ends = jnp.cumsum(lengths)
    starts = ends - lengths
    bounds = (jnp.concatenate([starts, ends]) - row_first).astype(jnp.int32)
    within = jnp.arange(LAND + 1, dtype=jnp.int32)
    edges = starts[:, None] + (within[None, :] * lengths[:, None] + LAND - 1) // LAND
    mark_low = edges[:, :-1].reshape(mark_count, 1)
    mark_high = edges[:, 1:].reshape(mark_count, 1)
    counts = (mark_high - mark_low).astype(F32)
    places = row_first + jnp.arange(tok_count, dtype=jnp.int32)[None, :]
    onehot = ((places >= mark_low) & (places < mark_high)).astype(BF)
    rows_in = (((0,), (0,)), ((), ()))
    cols_in = (((1,), (1,)), ((), ()))
    blocks = tok_count // BLOCK
    window_rows = tok_count + GROUP - SUB
    smem = pl.BlockSpec(memory_space=pltpu.SMEM)
    params = pltpu.CompilerParams(vmem_limit_bytes=40 * 1024 * 1024)
    tok_spec = pl.BlockSpec((BLOCK, width), lambda i: (i, 0))

    def part(col):
        return pl.BlockSpec((BLOCK, width), lambda i: (i, col))

    def fixed(*shape):
        return pl.BlockSpec(shape, lambda i: (0,) * len(shape))

    def shaped(shape, dtype):
        return jax.ShapeDtypeStruct(shape, dtype)

    means = jnp.dot(onehot, tokens, preferred_element_type=F32) / counts
    mean_in = seq_whole(seq_quarter(means.astype(BF), add_join))
    marks = jnp.dot(mean_in, w_qkv[:, : 2 * width], preferred_element_type=F32)
    mark_q = (marks[:, :width] + bias_q).astype(BF)
    mark_k = marks[:, width:].astype(BF)

    bias = jnp.concatenate([bias_q, jnp.zeros_like(bias_q), bias_v])
    qkv = (jnp.dot(tokens, w_qkv, preferred_element_type=F32) + bias).astype(BF)
    value_ext = extended(qkv[:, 2 * width :], radius, window_rows)
    value_ext, mark_q, mark_k = lax.optimization_barrier((value_ext, mark_q, mark_k))

    def one_col(col):
        return pl.BlockSpec((tok_count, width), lambda i: (0, col))

    stats = pl.pallas_call(
        lambda *refs: landmark_kernel(docs, scale, *refs),
        grid=(1,),
        in_specs=[smem, fixed(mark_count, width), one_col(1), one_col(2)],
        out_specs=fixed(mark_count, width + 128),
        out_shape=shaped((mark_count, width + 128), BF),
        scratch_shapes=[
            pltpu.VMEM((width, 128), F32), pltpu.VMEM((width, 128), F32),
            pltpu.VMEM((width, GROUP), F32),
        ],
        compiler_params=params,
        name="landmark",
    )(bounds, mark_q, qkv, qkv)
    far_count = seq_count // 4
    own_count = -(-heads // far_count)
    own_doc = (me % 2) * 2 + (me // 2) % 2
    own_at = (me // 4) * own_count * size
    spare = far_count * own_count * size - width

    def own_heads(array):
        array = jnp.pad(array, ((0, 0), (0, spare)))
        array = lax.dynamic_slice_in_dim(array, own_at, own_count * size, 1)
        return array.reshape(LAND, own_count, size).transpose(1, 0, 2)

    def of_doc(array):
        return lax.dynamic_slice_in_dim(array, own_doc * LAND, LAND, 0)

    mine, other = halves(stats, 1)
    stats = join(mine, swap(other, "seq", 1))
    stats, later_q, later_k = lax.optimization_barrier((stats, mark_q, mark_k))
    own_q = own_heads(of_doc(later_q)).astype(F32)
    own_k = own_heads(of_doc(later_k)).astype(F32)
    square = (own_count, LAND, LAND)
    own_inverse, kernel, saved = pl.pallas_call(
        lambda *refs: pinv_kernel(scale, *refs),
        out_shape=(
            shaped(square, F32), shaped(square, F32),
            shaped((4 * NS_ITERS * own_count, LAND, LAND), F32),
        ),
        name="pinv",
    )(own_q, own_k)
    inverse = own_inverse.transpose(1, 0, 2).reshape(LAND, own_count * size).astype(BF)
    mine, other = halves(stats, 2)
    stats = join(mine, swap(other, "seq", 2))
    for i in range(2, seq_count.bit_length() - 1):
        other = swap(jnp.concatenate([stats, inverse], 1), "seq", 1 << i)
        stats = join(stats, other[:, : width + 128])
        other = other[:, width + 128 :]
        inverse = jnp.where(
            (me >> i) % 2 == 0,
            jnp.concatenate([inverse, other], 1),
            jnp.concatenate([other, inverse], 1),
        )
    inverse = inverse[:, :width]
    mix = pl.pallas_call(
        mix_kernel, out_shape=shaped((LAND, width + 128), BF), name="mix"
    )(inverse, stats)
    mix = seq_whole(mix)

    taps = jnp.pad(conv_taps, ((0, 0), (0, GROUP - tap_count)))
    mark_spec = fixed(mark_count, width)
    mixed, probs = pl.pallas_call(
        lambda *refs: token_kernel(docs, scale, *refs),
        grid=(blocks,),
        in_specs=[
            smem, part(0), fixed(window_rows, width), mark_spec, mark_spec, fixed(heads, GROUP)
        ],
        out_specs=(tok_spec, pl.BlockSpec((width, BLOCK), lambda i: (0, i))),
        out_shape=(shaped((tok_count, width), BF), shaped((width, tok_count), BF)),
        scratch_shapes=[pltpu.VMEM((heads * SUB, GROUP), BF), pltpu.VMEM((BLOCK, width), F32)],
        compiler_params=params,
        name="token",
    )(bounds, qkv, value_ext, mark_k, mix, taps)

    hidden = w_up.shape[1]
    vectors = jnp.stack([bias_out, norm1_gain, norm1_bias, bias_down, norm2_gain, norm2_bias])
    vectors = jnp.pad(vectors, ((0, 2), (0, 0)))
    wide_spec = pl.BlockSpec((FFN_BLOCK, hidden), lambda i: (i, 0))
    ffn_spec = pl.BlockSpec((FFN_BLOCK, width), lambda i: (i, 0))
    narrow = shaped((tok_count, width), BF)
    (
        result, grad_one, active, grad_upper, hidden_low, grad_low_two, grad_low_one,
        grad_mixed, sums, sum_up,
    ) = pl.pallas_call(
        ffn_kernel,
        grid=(tok_count // FFN_BLOCK,),
        in_specs=[
            ffn_spec, ffn_spec, ffn_spec, fixed(width, width), fixed(width, hidden),
            fixed(hidden, width), fixed(8, width), fixed(8, hidden),
        ],
        out_specs=(
            ffn_spec, ffn_spec, wide_spec, wide_spec, ffn_spec, ffn_spec, ffn_spec, ffn_spec,
            fixed(8, width), fixed(8, hidden),
        ),
        out_shape=(
            shaped((tok_count, width), F32), shaped((tok_count, width), F32),
            shaped((tok_count, hidden), BF), shaped((tok_count, hidden), BF),
            narrow, narrow, narrow, narrow, shaped((8, width), F32), shaped((8, hidden), F32),
        ),
        scratch_shapes=[pltpu.VMEM((FFN_BLOCK, hidden), BF)],
        compiler_params=pltpu.CompilerParams(vmem_limit_bytes=58 * 1024 * 1024),
        name="ffn",
    )(
        tokens, mixed, cotangent[0], w_out, w_up, w_down, vectors,
        jnp.broadcast_to(bias_up[None, :], (8, hidden)),
    )

    grad_queries, grad_mix, grad_mk = pl.pallas_call(
        lambda *refs: token_back_kernel(docs, scale, *refs),
        grid=(blocks,),
        in_specs=[
            smem, part(0), tok_spec, pl.BlockSpec((width, BLOCK), lambda i: (0, i)), mark_spec,
            mark_spec,
        ],
        out_specs=(tok_spec, mark_spec, mark_spec),
        out_shape=(
            shaped((tok_count, width), BF), shaped((mark_count, width), F32),
            shaped((mark_count, width), F32),
        ),
        scratch_shapes=[pltpu.VMEM((BLOCK, width), F32)],
        compiler_params=params,
        name="token_back",
    )(bounds, qkv, grad_mixed, probs, mark_k, mix)
    grad_w_down = lax.dot_general(active, grad_low_two, rows_in, preferred_element_type=F32)
    grad_w_up = lax.dot_general(hidden_low, grad_upper, rows_in, preferred_element_type=F32)
    grad_mix, grad_w_down, grad_w_up = lax.optimization_barrier(
        (grad_mix.astype(BF), grad_w_down.astype(BF), grad_w_up.astype(BF))
    )
    sum_w_down, sum_w_up = lax.psum((grad_w_down, grad_w_up), ("row", "seq"))

    def remaining(grad_mix, grad_mk, stats, mix):
        grad_mix = seq_quarter(grad_mix.astype(BF), add_join)
        grad_w_out = lax.dot_general(mixed, grad_low_one, rows_in, preferred_element_type=F32)

        grad_ext = extended(grad_mixed, radius, window_rows)
        grad_conv, products = pl.pallas_call(
            lambda *refs: conv_back_kernel(docs, *refs),
            grid=(blocks,),
            in_specs=[
                smem, fixed(window_rows, width), fixed(window_rows, width), fixed(heads, GROUP)
            ],
            out_specs=(tok_spec, fixed(heads * SUB, GROUP)),
            out_shape=(shaped((tok_count, width), F32), shaped((heads * SUB, GROUP), F32)),
            scratch_shapes=[pltpu.VMEM((heads * SUB, GROUP), BF)],
            compiler_params=params,
            name="conv_back",
        )(bounds, grad_ext, value_ext, jnp.pad(conv_taps[:, ::-1], ((0, 0), (0, GROUP - tap_count))))
        grad_avg = pl.pallas_call(
            mix_back_kernel, out_shape=shaped((LAND, width + 128), BF), name="mix_back"
        )(inverse, stats, grad_mix)
        grad_avg = seq_whole(grad_avg)
        lane_spec = pl.BlockSpec((mark_count, 128), lambda i: (0, width // 128))
        grad_keys, grad_values, grad_mq = pl.pallas_call(
            lambda *refs: landmark_back_kernel(docs, scale, *refs),
            grid=(blocks,),
            in_specs=[
                smem, part(1), part(2), tok_spec, mark_spec, mark_spec, lane_spec, lane_spec
            ],
            out_specs=(tok_spec, tok_spec, mark_spec),
            out_shape=(
                shaped((tok_count, width), BF), shaped((tok_count, width), BF),
                shaped((mark_count, width), F32),
            ),
            scratch_shapes=[pltpu.VMEM((BLOCK, width), F32), pltpu.VMEM((BLOCK, width), F32)],
            compiler_params=params,
            name="landmark_back",
        )(bounds, qkv, qkv, grad_conv, mark_q, grad_avg, mix, grad_avg)

        grad_mix, grad_values = lax.optimization_barrier((grad_mix, grad_values))
        grad_mq_small, grad_mk_small = pl.pallas_call(
            lambda *refs: pinv_back_kernel(scale, *refs),
            out_shape=(shaped(square, F32), shaped(square, F32)),
            name="pinv_back",
        )(own_q, own_k, kernel, saved, own_heads(grad_mix), own_heads(stats[:, :width]))

        def placed(array):
            array = array.transpose(1, 0, 2).reshape(LAND, own_count * size)
            array = lax.dynamic_update_slice_in_dim(
                jnp.zeros((LAND, width + spare), F32), array, own_at, 1
            )[:, :width]
            return lax.dynamic_update_slice_in_dim(
                jnp.zeros((mark_count, width), F32), array, own_doc * LAND, 0
            )

        grad_mq = grad_mq + placed(grad_mq_small)
        grad_mk = grad_mk + placed(grad_mk_small)
        grad_marks = jnp.concatenate([grad_mq, grad_mk], axis=1).astype(BF)
        mark_back = lax.dot_general(
            grad_marks, w_qkv[:, : 2 * width], cols_in, preferred_element_type=F32
        ) / counts
        mark_back = mark_back.astype(BF)

        grad_bias_q = jnp.sum(grad_queries.astype(F32), axis=0) + jnp.sum(grad_mq, axis=0)
        grad_bias_v = jnp.sum(grad_values.astype(F32), axis=0)
        grad_projected = jnp.concatenate([grad_queries, grad_keys, grad_values], axis=1)

        def weight_grad(grads):
            return lax.dot_general(tokens, grads, rows_in, preferred_element_type=F32)

        early = jnp.concatenate([grad_w_out.astype(BF), weight_grad(grad_values).astype(BF)], 0)
        early = begin(early, ("row", "near", "far"), ("row", "near", "far"))
        early = advance(early, 1)
        grad_marks, (early,) = tied(grad_marks, [early])
        early = advance(early, 1)
        mark_grad_q = lax.dot_general(
            mean_in, grad_marks[:, :width], rows_in, preferred_element_type=F32
        )
        mark_grad_k = lax.dot_general(
            mean_in, grad_marks[:, width:], rows_in, preferred_element_type=F32
        )
        products, (early,) = tied(products, [early])
        reach = SUB + tap_count - 1
        products = products.reshape(heads, SUB, GROUP)[:, :, :reach].reshape(heads, SUB * reach)
        products = jnp.pad(products, ((0, 0), (0, SUB))).reshape(heads, SUB, reach + 1)
        grad_conv_taps = jnp.sum(products, axis=1)[:, :tap_count]
        others = jnp.concatenate(
            [
                sum_up[0].reshape(hidden // width, width),
                grad_bias_q[None],
                grad_bias_v[None],
                jnp.pad(grad_conv_taps.reshape(1, -1), ((0, 0), (0, width - heads * tap_count))),
                jnp.zeros((4 - hidden // width + 1, width), F32),
            ],
            0,
        )
        spare_rows = width // 6
        small = jnp.concatenate([sums, others], 0).astype(BF)
        small = jnp.pad(small, ((0, spare_rows - small.shape[0]), (0, 0)))
        small = lax.optimization_barrier(small)
        late = jnp.concatenate(
            [
                (weight_grad(grad_queries) + mark_grad_q).astype(BF),
                small,
                (weight_grad(grad_keys) + mark_grad_k).astype(BF),
                jnp.zeros((spare_rows, width), BF),
            ],
            0,
        )
        late = begin(late, ("row", "far", "near"), ("row", "far", "near"))
        late = advance(late, 1)
        mark_back = seq_quarter(mark_back, add_join)
        mark_back, (early, late) = tied(mark_back, [early, late])
        early, late = advance(early, 1), advance(late, 1)
        mark_back = seq_whole(mark_back)
        mark_back, (early, late) = tied(mark_back, [early, late])
        early, early_other = last_swap(early)[:2]
        late, late_other = last_swap(late)[:2]
        sum_w_qkv = settle_qkv(late, late_other, early, early_other, width)
        first_core = me % 2 == 0
        sum_w_out = jnp.where(first_core, early, early_other).astype(F32)
        flat = jnp.where(first_core, late[width:], late_other[width:])[:16].astype(F32)
        grad_input = (
            grad_one
            + lax.dot_general(grad_projected, w_qkv, cols_in, preferred_element_type=F32)
            + lax.dot_general(onehot, mark_back, rows_in, preferred_element_type=F32)
        )
        return grad_input, sum_w_qkv, sum_w_out, flat

    def nothing(*unused):
        return (
            jnp.zeros((tok_count, width), F32), jnp.zeros((width, 3 * width), F32),
            jnp.zeros((width, width), F32), jnp.zeros((16, width), F32),
        )

    grad_input, sum_w_qkv, sum_w_out, flat = lax.cond(
        lengths[0] > 0, remaining, nothing, grad_mix, grad_mk, stats, mix
    )
    sum_w_down, sum_w_up = sum_w_down.astype(F32), sum_w_up.astype(F32)
    at = sums.shape[0] + hidden // width
    pieces = [
        flat[at], flat[at + 1], flat[at + 2, : heads * tap_count], flat[5], flat[3], flat[4],
        flat[sums.shape[0] : at].reshape(hidden), flat[2], flat[0], flat[1],
    ]
    return (
        result[None], grad_input[None], sum_w_qkv, pieces[0], pieces[1],
        pieces[2].reshape(heads, tap_count), sum_w_out, pieces[3], pieces[4], pieces[5],
        sum_w_up, pieces[6], sum_w_down, pieces[7], pieces[8], pieces[9],
    )


def solution(mesh):
    whole, tokens = P(), P("row", "seq", None)
    return jax.shard_map(
        per_device,
        mesh=mesh,
        in_specs=(tokens, P("row", None)) + (whole,) * 14 + (tokens,),
        out_specs=(tokens, tokens) + (whole,) * 14,
        check_vma=False,
    )
```

```python
import math

import jax
import jax.numpy as jnp
from jax import lax
from jax.experimental import pallas as pl
from jax.experimental.pallas import tpu as pltpu
from jax.sharding import PartitionSpec as P

LAND = 64
NS_ITERS = 6
HIGH = lax.Precision.HIGHEST
NEGATIVE = -1e30
BF = jnp.bfloat16
F32 = jnp.float32

BLOCK = 256
GROUP = 256
SUB = 128
TAPS = 33
FFN_BLOCK = 256
ORDER = ("row", "near", "far")


def swap(array, axis, bit):
    count = lax.axis_size(axis)
    return lax.ppermute(array, axis, [(i, i ^ bit) for i in range(count)])


def add_parts(parts):
    total = parts[0].astype(F32)
    for part in parts[1:]:
        total = total + part.astype(F32)
    return total


def halves(array, bit):
    rows = array.shape[0] // 2
    side = (lax.axis_index("seq") // bit) % 2
    mine = lax.dynamic_slice_in_dim(array, side * rows, rows, 0)
    other = lax.dynamic_slice_in_dim(array, (1 - side) * rows, rows, 0)
    return mine, other


def seq_quarter(array, join):
    bits = [1 << i for i in range(lax.axis_size("seq").bit_length() - 1)]
    for bit in bits[:2]:
        mine, other = halves(array, bit)
        array = join(mine, swap(other, "seq", bit))
    for bit in bits[2:]:
        array = join(array, swap(array, "seq", bit))
    return array


def paired(array, axis, bit, dim):
    other = swap(array, axis, bit)
    side = (lax.axis_index(axis) // bit) % 2
    return jnp.where(
        side == 0,
        jnp.concatenate([array, other], dim),
        jnp.concatenate([other, array], dim),
    )


def seq_whole(array):
    return paired(paired(array, "seq", 2, 0), "seq", 1, 0)


def seq_steps():
    bits = [1 << i for i in range(lax.axis_size("seq").bit_length() - 1)]

    def halve(bit):
        def step(array):
            mine, other = halves(array, bit)
            return add_join(mine, swap(other, "seq", bit))

        return step

    def whole(bit):
        return lambda array: add_join(array, swap(array, "seq", bit))

    def double(bit):
        return lambda array: paired(array, "seq", bit, 0)

    return (
        [halve(bit) for bit in bits[:2]]
        + [whole(bit) for bit in bits[2:]]
        + [double(bit) for bit in reversed(bits[:2])]
    )


def add_join(first, second):
    return (first.astype(F32) + second.astype(F32)).astype(BF)


def stages(order):
    row = [("row", 1 << i) for i in range(lax.axis_size("row").bit_length() - 1)]
    seq = [[("seq", 1 << i)] for i in range(lax.axis_size("seq").bit_length() - 1)]
    named = {"core": seq[0], "row": row, "near": seq[1], "far": seq[2], "rest": sum(seq[3:], [])}
    return sum([named[name] for name in ("core",) + order + ("rest",)], [])


def begin(array, down, back):
    return array, stages(down), stages(back), 0


def advance(state, steps):
    held, down, back, done = state
    for step in range(done, min(done + steps, 2 * len(down))):
        if step < len(down):
            axis, bit = down[step]
            half = held.shape[0] // 2
            side = (lax.axis_index(axis) // bit) % 2
            mine = lax.dynamic_slice_in_dim(held, side * half, half, 0)
            other = lax.dynamic_slice_in_dim(held, (1 - side) * half, half, 0)
            held = mine.astype(F32) + swap(other, axis, bit).astype(F32)
            held = held.astype(BF)
        else:
            axis, bit = back[2 * len(down) - 1 - step]
            held = paired(held, axis, bit, 0)
    return held, down, back, min(done + steps, 2 * len(down))


def last_swap(state):
    down, back = state[1], state[2]
    held = advance(state, 2 * len(down) - 1 - state[3])[0]
    return held, swap(held, *down[0]), down, back


def tied(values, states):
    values, helds = lax.optimization_barrier((values, [state[0] for state in states]))
    return values, [(held,) + state[1:] for held, state in zip(helds, states)]


def extended(cells, width, rows):
    count = lax.axis_size("seq")
    head = cells[:width]
    tail = cells[-width:]
    return jnp.concatenate(
        [
            lax.ppermute(tail, "seq", [(i, i + 1) for i in range(count - 1)]),
            cells,
            lax.ppermute(head, "seq", [(i + 1, i) for i in range(count - 1)]),
            jnp.zeros((rows - cells.shape[0] - 2 * width, cells.shape[1]), cells.dtype),
        ],
        axis=0,
    )


def dot_nn(a, b):
    return jnp.dot(a, b, preferred_element_type=F32)


def dot_nt(a, b):
    return lax.dot_general(a, b, (((1,), (1,)), ((), ())), preferred_element_type=F32)


def dot_tn(a, b):
    return lax.dot_general(a, b, (((0,), (0,)), ((), ())), preferred_element_type=F32)


def iota(shape, dim):
    return lax.broadcasted_iota(jnp.int32, shape, dim)


def spread(block):
    rows = block.shape[0]
    tall = jnp.concatenate([block] * 4, axis=0).astype(F32)
    shape = (4 * rows, GROUP)
    keep = iota(shape, 0) // rows == iota(shape, 1) // LAND
    return jnp.where(keep, tall, 0.0).astype(BF)


def gathered(square):
    rows = square.shape[0] // 4
    lane = iota((rows, GROUP), 1) // LAND
    out = square[:rows]
    for head in range(1, 4):
        out = jnp.where(lane == head, square[head * rows : (head + 1) * rows], out)
    return out


def by_head(columns, first, shape):
    lane = iota(shape, 1)
    out = jnp.zeros(shape, F32)
    for head, column in enumerate(columns):
        out = jnp.where((lane % 16 == first + head) & (lane < 48), column, out)
    return out


def split_three(cells):
    lane = iota(cells.shape, 1)
    high = cells.astype(BF).astype(F32)
    mid = (cells - high).astype(BF).astype(F32)
    low = cells - high - mid
    return jnp.where(lane < 16, high, jnp.where(lane < 32, mid, low)).astype(BF)


def merge_three(cells):
    cells = cells.astype(F32)
    return cells + pltpu.roll(cells, 112, 1) + pltpu.roll(cells, 96, 1)


def head_lanes(heads, width):
    return (iota((128, width), 0) == iota((128, width), 1) // LAND).astype(F32)


def doc_of(places, bounds, docs):
    out = (places >= bounds[2 * docs - 1]).astype(jnp.int32)
    for doc in range(docs):
        out = out + (places >= bounds[doc]).astype(jnp.int32)
    return out


def landmark_kernel(docs, scale, bounds, mq_ref, k_ref, v_ref, out_ref, max_s, sum_s, acc_s):
    tokens, width = k_ref.shape
    groups = width // GROUP
    heads = width // LAND
    out_ref[:, :width] = jnp.zeros((docs * LAND, width), BF)
    empty = jnp.full((docs * LAND, 128), NEGATIVE, F32)
    out_ref[:, width:] = jnp.where(iota(empty.shape, 1) < 48, split_three(empty).astype(F32), 0.0).astype(BF)
    for doc in range(docs):
        low = jnp.clip(bounds[doc], 0, tokens)
        high = jnp.clip(bounds[docs + doc], 0, tokens)
        rows = slice(doc * LAND, (doc + 1) * LAND)

        @pl.when(high > low)
        def _():
            max_s[...] = jnp.full(max_s.shape, NEGATIVE, F32)
            sum_s[...] = jnp.zeros(sum_s.shape, F32)
            acc_s[...] = jnp.zeros(acc_s.shape, F32)
            wide = [
                spread(mq_ref[rows, g * GROUP : (g + 1) * GROUP]) for g in range(groups)
            ]

            ones = jnp.ones((BLOCK, 128), BF)

            def step(block, carry):
                first = pl.multiple_of(block * BLOCK, BLOCK)
                at = pl.ds(first, BLOCK)
                place = iota((1, BLOCK), 1) + first
                valid = (place >= low) & (place < high)
                for g in range(groups):
                    cols = slice(g * GROUP, (g + 1) * GROUP)
                    scores = dot_nt(wide[g], k_ref[at, cols]) * scale
                    scores = jnp.where(valid, scores, NEGATIVE)
                    old = max_s[cols, :]
                    top = jnp.maximum(old, jnp.max(scores, axis=1, keepdims=True))
                    weights = jnp.exp(scores - twice(top)).astype(BF)
                    shrink = jnp.exp(old - top)
                    max_s[cols, :] = top
                    sum_s[cols, :] = sum_s[cols, :] * shrink + dot_nn(weights, ones)
                    acc_s[cols, :] = acc_s[cols, :] * twice(shrink) + dot_nn(weights, v_ref[at, cols])
                return carry

            lax.fori_loop(low // BLOCK, (high + BLOCK - 1) // BLOCK, step, 0)
            columns = []
            for g in range(groups):
                cols = slice(g * GROUP, (g + 1) * GROUP)
                sums = sum_s[cols, :]
                out_ref[rows, cols] = gathered(acc_s[cols, :] / twice(sums)).astype(BF)
                level = max_s[cols, :] + jnp.log(sums)
                columns += [level[h * LAND : (h + 1) * LAND] for h in range(4)]
            out_ref[rows, width:] = split_three(by_head(columns, 0, (LAND, 128)))


def twice(cells):
    return jnp.concatenate([cells, cells], axis=1)


def join_kernel(a_ref, b_ref, out_ref):
    width = a_ref.shape[1] - 128
    heads = width // LAND
    first, second = merge_three(a_ref[:, width:]), merge_three(b_ref[:, width:])
    lane = iota(first.shape, 1)
    first = jnp.where(lane < heads, first, 0.0)
    second = jnp.where(lane < heads, second, 0.0)
    top = jnp.maximum(first, second)
    exp_a, exp_b = jnp.exp(first - top), jnp.exp(second - top)
    both = exp_a + exp_b
    level = top + jnp.log(both)
    pick = head_lanes(heads, width)
    share_a = jnp.dot(exp_a / both, pick, precision=HIGH, preferred_element_type=F32)
    share_b = jnp.dot(exp_b / both, pick, precision=HIGH, preferred_element_type=F32)
    joined = a_ref[:, :width].astype(F32) * share_a + b_ref[:, :width].astype(F32) * share_b
    out_ref[:, :width] = joined.astype(BF)
    level = jnp.where(lane < heads, level, 0.0)
    level = level + pltpu.roll(level, 16, 1) + pltpu.roll(level, 32, 1)
    out_ref[:, width:] = split_three(level)


def join(first, second):
    return pl.pallas_call(
        join_kernel, out_shape=jax.ShapeDtypeStruct(first.shape, BF), name="join"
    )(first, second)


def mix_kernel(inv_ref, stat_ref, mix_ref):
    width = stat_ref.shape[1] - 128
    for g in range(width // GROUP):
        cols = slice(g * GROUP, (g + 1) * GROUP)
        mix_ref[:, cols] = dot_nn(inv_ref[:, cols], spread(stat_ref[:, cols])).astype(BF)
    mix_ref[:, width:] = stat_ref[:, width:]


def mix_back_kernel(inv_ref, stat_ref, grad_ref, out_ref):
    width = stat_ref.shape[1] - 128
    columns = []
    for g in range(width // GROUP):
        cols = slice(g * GROUP, (g + 1) * GROUP)
        grad = gathered(dot_tn(inv_ref[:, cols], grad_ref[:, cols]))
        out_ref[:, cols] = grad.astype(BF)
        product = grad * stat_ref[:, cols].astype(F32)
        lane = iota(product.shape, 1) // LAND
        for h in range(4):
            columns.append(jnp.sum(jnp.where(lane == h, product, 0.0), axis=1, keepdims=True))
    out_ref[:, width:] = split_three(by_head(columns, 0, (LAND, 128)))


def make_band(taps_ref, band_s):
    for head in range(taps_ref.shape[0]):
        row = jnp.broadcast_to(taps_ref[head : head + 1, :], (SUB, GROUP))
        band_s[head * SUB : (head + 1) * SUB, :] = pltpu.roll(row, 0, 1, stride=1, stride_axis=0).astype(BF)


def same_doc(first, bounds, docs, radius):
    rows = iota((SUB, GROUP), 0) + first
    cols = iota((SUB, GROUP), 1) + (first - radius)
    return doc_of(rows, bounds, docs) == doc_of(cols, bounds, docs)


def token_kernel(
    docs, scale, bounds, q_ref, v_ref, mk_ref, mix_ref, taps_ref, mixed_ref, probs_ref, band_s, sum_s
):
    width = q_ref.shape[1]
    groups = width // GROUP
    radius = (TAPS - 1) // 2
    first = pl.program_id(0) * BLOCK

    @pl.when(pl.program_id(0) == 0)
    def _():
        make_band(taps_ref, band_s)

    for sub in range(BLOCK // SUB):
        start = pl.multiple_of(first + sub * SUB, SUB)
        same = same_doc(start, bounds, docs, radius)
        same = jnp.where(jnp.concatenate([same] * 4, axis=0), 1.0, 0.0).astype(BF)
        for g in range(groups):
            cols = slice(g * GROUP, (g + 1) * GROUP)
            band = band_s[g * 4 * SUB : (g + 1) * 4 * SUB, :] * same
            res = dot_nn(band, v_ref[pl.ds(start, GROUP), cols])
            sum_s[sub * SUB : (sub + 1) * SUB, cols] = gathered(res)
    probs_ref[...] = jnp.zeros(probs_ref.shape, BF)
    for doc in range(docs):
        low, high = bounds[doc], bounds[docs + doc]
        rows = slice(doc * LAND, (doc + 1) * LAND)

        @pl.when((high > first) & (low < first + BLOCK))
        def _():
            place = iota((1, BLOCK), 1) + first
            valid = (place >= low) & (place < high)
            for g in range(groups):
                cols = slice(g * GROUP, (g + 1) * GROUP)
                scores = dot_nt(spread(mk_ref[rows, cols]), q_ref[:, cols]) * scale
                scores = scores.reshape(4, LAND, BLOCK)
                weights = jnp.exp(scores - jnp.max(scores, axis=1, keepdims=True))
                probs = weights / jnp.sum(weights, axis=1, keepdims=True)
                probs = jnp.where(valid, probs.reshape(GROUP, BLOCK), 0.0).astype(BF)
                probs_ref[cols, :] = probs_ref[cols, :] + probs
                sum_s[:, cols] = sum_s[:, cols] + dot_tn(probs, spread(mix_ref[rows, cols]))

    mixed_ref[...] = sum_s[...].astype(BF)


def token_back_kernel(
    docs, scale, bounds, q_ref, gm_ref, probs_ref, mk_ref, mix_ref, gq_ref, gmix_ref, gmk_ref, gq_s
):
    width = q_ref.shape[1]
    groups = width // GROUP
    first = pl.program_id(0) * BLOCK

    @pl.when(pl.program_id(0) == 0)
    def _():
        gmix_ref[...] = jnp.zeros(gmix_ref.shape, F32)
        gmk_ref[...] = jnp.zeros(gmk_ref.shape, F32)

    gq_s[...] = jnp.zeros(gq_s.shape, F32)
    for doc in range(docs):
        low, high = bounds[doc], bounds[docs + doc]
        rows = slice(doc * LAND, (doc + 1) * LAND)

        @pl.when((high > first) & (low < first + BLOCK))
        def _():
            place = iota((1, BLOCK), 1) + first
            valid = (place >= low) & (place < high)
            for g in range(groups):
                cols = slice(g * GROUP, (g + 1) * GROUP)
                probs = jnp.where(valid, probs_ref[cols, :].astype(F32), 0.0)
                gmix_ref[rows, cols] += gathered(dot_nn(probs.astype(BF), gm_ref[:, cols]))
                grad = dot_nt(spread(mix_ref[rows, cols]), gm_ref[:, cols])
                heavy = (probs * grad).reshape(4, LAND, BLOCK)
                shared = probs.reshape(4, LAND, BLOCK) * jnp.sum(heavy, axis=1, keepdims=True)
                grad = ((heavy - shared).reshape(GROUP, BLOCK) * scale).astype(BF)
                gmk_ref[rows, cols] += gathered(dot_nn(grad, q_ref[:, cols]))
                gq_s[:, cols] += dot_tn(grad, spread(mk_ref[rows, cols]))

    gq_ref[...] = gq_s[...].astype(BF)


def conv_back_kernel(docs, bounds, gm_ref, v_ref, taps_ref, out_ref, prod_ref, band_s):
    width = gm_ref.shape[1]
    groups = width // GROUP
    radius = (TAPS - 1) // 2
    first = pl.program_id(0) * BLOCK

    @pl.when(pl.program_id(0) == 0)
    def _():
        make_band(taps_ref, band_s)
        prod_ref[...] = jnp.zeros(prod_ref.shape, F32)

    for sub in range(BLOCK // SUB):
        start = pl.multiple_of(first + sub * SUB, SUB)
        same = same_doc(start, bounds, docs, radius)
        same = jnp.where(jnp.concatenate([same] * 4, axis=0), 1.0, 0.0)
        for g in range(groups):
            cols = slice(g * GROUP, (g + 1) * GROUP)
            tall = slice(g * 4 * SUB, (g + 1) * 4 * SUB)
            band = band_s[tall, :] * same.astype(BF)
            res = dot_nn(band, gm_ref[pl.ds(start, GROUP), cols])
            out_ref[sub * SUB : (sub + 1) * SUB, cols] = gathered(res)
            own = gm_ref[pl.ds(pl.multiple_of(start + radius, 16), SUB), cols]
            product = dot_nt(spread(own), v_ref[pl.ds(start, GROUP), cols])
            prod_ref[tall, :] += product * same


def ffn_kernel(
    x_ref, mixed_ref, cot_ref, w_out_ref, w_up_ref, w_down_ref, rows_ref, bias_up_ref,
    result_ref, grad_one_ref, active_ref, grad_up_ref, low_ref, low_two_ref, low_one_ref,
    grad_mixed_ref, sums_ref, sum_up_ref, slope_s,
):
    width = x_ref.shape[1]
    hidden = w_up_ref.shape[1]
    chunks = [slice(at, at + width) for at in range(0, hidden, width)]

    def row(i):
        return rows_ref[i : i + 1, :]

    @pl.when(pl.program_id(0) == 0)
    def _():
        sums_ref[...] = jnp.zeros(sums_ref.shape, F32)
        sum_up_ref[...] = jnp.zeros(sum_up_ref.shape, F32)

    def add_sum(i, cells):
        sums_ref[i : i + 1, :] += jnp.sum(cells, axis=0, keepdims=True)

    attended = dot_nn(mixed_ref[...], w_out_ref[...]) + row(0)
    norm_one, inverse_one = normalize(x_ref[...].astype(F32) + attended)
    hidden_one = norm_one * row(1) + row(2)
    hidden_low = hidden_one.astype(BF)
    low_ref[...] = hidden_low
    lowered = hidden_one + row(3)
    for cols in chunks:
        upper = dot_nn(hidden_low, w_up_ref[:, cols]) + bias_up_ref[:1, cols]
        active, slope = gelu_both(upper)
        active = active.astype(BF)
        active_ref[:, cols] = active
        slope_s[:, cols] = slope.astype(BF)
        lowered = lowered + dot_nn(active, w_down_ref[cols, :])
    norm_two, inverse_two = normalize(lowered)
    result_ref[...] = norm_two * row(4) + row(5)
    upstream = cot_ref[...].astype(F32)
    add_sum(0, upstream * norm_two)
    add_sum(1, upstream)
    grad_two = norm_back(upstream * row(4), norm_two, inverse_two)
    low_two = grad_two.astype(BF)
    low_two_ref[...] = low_two
    add_sum(2, low_two.astype(F32))
    grad_hidden = grad_two
    for cols in chunks:
        grad_up = dot_nt(low_two, w_down_ref[cols, :]) * slope_s[:, cols].astype(F32)
        grad_up = grad_up.astype(BF)
        grad_up_ref[:, cols] = grad_up
        sum_up_ref[:1, cols] += jnp.sum(grad_up.astype(F32), axis=0, keepdims=True)
        grad_hidden = grad_hidden + dot_nt(grad_up, w_up_ref[:, cols])
    add_sum(3, grad_hidden * norm_one)
    add_sum(4, grad_hidden)
    grad_one = norm_back(grad_hidden * row(1), norm_one, inverse_one)
    grad_one_ref[...] = grad_one
    low_one = grad_one.astype(BF)
    low_one_ref[...] = low_one
    add_sum(5, low_one.astype(F32))
    grad_mixed_ref[...] = dot_nt(low_one, w_out_ref[...]).astype(BF)


def landmark_back_kernel(
    docs, scale, bounds, k_ref, v_ref, conv_ref, mq_ref, grad_ref, level_ref, dots_ref,
    gk_ref, gv_ref, gmq_ref, gk_s, gv_s,
):
    width = k_ref.shape[1]
    groups = width // GROUP
    first = pl.program_id(0) * BLOCK

    @pl.when(pl.program_id(0) == 0)
    def _():
        gmq_ref[...] = jnp.zeros(gmq_ref.shape, F32)

    gk_s[...] = jnp.zeros(gk_s.shape, F32)
    gv_s[...] = conv_ref[...]
    for doc in range(docs):
        low, high = bounds[doc], bounds[docs + doc]
        rows = slice(doc * LAND, (doc + 1) * LAND)

        @pl.when((high > first) & (low < first + BLOCK))
        def _():
            place = iota((1, BLOCK), 1) + first
            valid = (place >= low) & (place < high)

            level, dots = merge_three(level_ref[rows, :]), merge_three(dots_ref[rows, :])

            def column(lanes, g):
                return jnp.concatenate(
                    [lanes[:, 4 * g + h : 4 * g + h + 1] for h in range(4)], axis=0
                )

            for g in range(groups):
                cols = slice(g * GROUP, (g + 1) * GROUP)
                wide_q, wide_g = spread(mq_ref[rows, cols]), spread(grad_ref[rows, cols])
                scores = dot_nt(wide_q, k_ref[:, cols]) * scale - column(level, g)
                probs = jnp.exp(jnp.where(valid, scores, NEGATIVE))
                grad = dot_nt(wide_g, v_ref[:, cols]) - column(dots, g)
                grad = (probs * grad * scale).astype(BF)
                gv_s[:, cols] += dot_tn(probs.astype(BF), wide_g)
                gk_s[:, cols] += dot_tn(grad, wide_q)
                gmq_ref[rows, cols] += gathered(dot_nn(grad, k_ref[:, cols]))

    gk_ref[...] = gk_s[...].astype(BF)
    gv_ref[...] = gv_s[...].astype(BF)


def gelu_both(upper):
    tangent = jnp.tanh(0.7978845608028654 * (upper + 0.044715 * upper * upper * upper))
    inner_slope = 0.7978845608028654 * (1.0 + 3.0 * 0.044715 * upper * upper)
    active = 0.5 * upper * (1.0 + tangent)
    slope = 0.5 * (1.0 + tangent) + 0.5 * upper * (1.0 - tangent * tangent) * inner_slope
    return active, slope


def normalize(residual):
    row_mean = jnp.mean(residual, axis=-1, keepdims=True)
    centered = residual - row_mean
    row_var = jnp.mean(centered * centered, axis=-1, keepdims=True)
    inverse_dev = lax.rsqrt(row_var + 1e-05)
    return (centered * inverse_dev, inverse_dev)


def norm_back(grad_normed, normed, inverse_dev):
    return inverse_dev * (
        grad_normed
        - jnp.mean(grad_normed, axis=-1, keepdims=True)
        - normed * jnp.mean(grad_normed * normed, axis=-1, keepdims=True)
    )


def dot_high(a, b, dims):
    return lax.dot_general(
        a, b, (dims, ((), ())), precision=HIGH, preferred_element_type=F32
    )


NN, NT, TN = ((1,), (0,)), ((1,), (1,)), ((0,), (0,))


def pinv_kernel(scale, q_ref, k_ref, inverse_ref, kernel_ref, saved_ref):
    count = q_ref.shape[0]
    eye = (iota((LAND, LAND), 0) == iota((LAND, LAND), 1)).astype(F32)
    kernels, inverses = [], []
    for p in range(count):
        scores = dot_high(q_ref[p], k_ref[p], NT) * scale
        weights = jnp.exp(scores - jnp.max(scores, axis=1, keepdims=True))
        kernel = weights / jnp.sum(weights, axis=1, keepdims=True)
        kernel_ref[p] = kernel
        kernels.append(kernel)
        largest = jnp.max(jnp.sum(kernel, axis=0, keepdims=True), axis=1, keepdims=True)
        inverses.append(kernel.T / largest)
    for sweep in range(NS_ITERS):
        products = [dot_high(kernels[p], inverses[p], NN) for p in range(count)]
        second = [
            15.0 * eye - dot_high(products[p], 7.0 * eye - products[p], NN) for p in range(count)
        ]
        third = [13.0 * eye - dot_high(products[p], second[p], NN) for p in range(count)]
        for p in range(count):
            at = (sweep * count + p) * 4
            saved_ref[at], saved_ref[at + 1] = inverses[p], products[p]
            saved_ref[at + 2], saved_ref[at + 3] = second[p], third[p]
        inverses = [0.25 * dot_high(inverses[p], third[p], NN) for p in range(count)]
    for p in range(count):
        inverse_ref[p] = inverses[p]


def pinv_back_kernel(scale, q_ref, k_ref, kernel_ref, saved_ref, grad_ref, avg_ref, gq_ref, gk_ref):
    count = q_ref.shape[0]
    each = range(count)
    eye = (iota((LAND, LAND), 0) == iota((LAND, LAND), 1)).astype(F32)
    grads = [dot_nt(grad_ref[p], avg_ref[p]) for p in each]
    kernels = [kernel_ref[p] for p in each]
    totals = [jnp.zeros((LAND, LAND), F32) for p in each]
    for sweep in reversed(range(NS_ITERS)):
        first = [(sweep * count + p) * 4 for p in each]
        inverses, products = [saved_ref[a] for a in first], [saved_ref[a + 1] for a in first]
        grad_third = [0.25 * dot_high(inverses[p], grads[p], TN) for p in each]
        nexts = [0.25 * dot_high(grads[p], saved_ref[first[p] + 3], NT) for p in each]
        grad_second = [-dot_high(products[p], grad_third[p], TN) for p in each]
        grad_product = [-dot_high(grad_third[p], saved_ref[first[p] + 2], NT) for p in each]
        grad_first = [-dot_high(products[p], grad_second[p], TN) for p in each]
        grad_product = [
            grad_product[p]
            - dot_high(grad_second[p], 7.0 * eye - products[p], NT)
            - grad_first[p]
            for p in each
        ]
        totals = [totals[p] + dot_high(grad_product[p], inverses[p], NT) for p in each]
        grads = [nexts[p] + dot_high(kernels[p], grad_product[p], TN) for p in each]
    for p in each:
        kernel = kernels[p]
        sums = jnp.sum(kernel, axis=0, keepdims=True)
        largest = jnp.max(sums, axis=1, keepdims=True)
        flipped = grads[p].T
        loss = jnp.sum(jnp.sum(flipped * kernel, axis=1, keepdims=True), axis=0, keepdims=True)
        at_top = (sums == largest).astype(F32)
        at_top = at_top / jnp.sum(at_top, axis=1, keepdims=True)
        grad = totals[p] + flipped / largest - at_top * (loss / (largest * largest))
        grad = kernel * (grad - jnp.sum(grad * kernel, axis=1, keepdims=True)) * scale
        gq_ref[p] = dot_high(grad, k_ref[p], NN)
        gk_ref[p] = dot_high(grad, q_ref[p], TN)


def settle_qkv_kernel(side_ref, late_ref, late_other_ref, early_ref, early_other_ref, out_ref):
    part = pl.program_id(0)
    own = jnp.where(part == 0, 0, 1) == side_ref[0]
    choices = [
        (late_ref, own & (part < 2)),
        (late_other_ref, jnp.logical_not(own) & (part < 2)),
        (early_ref, own & (part == 2)),
        (early_other_ref, jnp.logical_not(own) & (part == 2)),
    ]
    for ref, chosen in choices:

        @pl.when(chosen)
        def _():
            out_ref[...] = ref[...].astype(F32)


def settle_qkv(late, late_other, early, early_other, width):
    side = (lax.axis_index("seq") % 2).astype(jnp.int32).reshape(1)
    rows = width // 2

    def spec(used):
        return pl.BlockSpec((rows, width), lambda j, i, s: (jnp.where(used(j), i, 0), 0))

    return pl.pallas_call(
        settle_qkv_kernel,
        grid_spec=pltpu.PrefetchScalarGridSpec(
            num_scalar_prefetch=1,
            grid=(3, 2),
            in_specs=[spec(lambda j: j < 2), spec(lambda j: j < 2)] + [spec(lambda j: j == 2)] * 2,
            out_specs=pl.BlockSpec((rows, width), lambda j, i, s: (i, j)),
        ),
        out_shape=jax.ShapeDtypeStruct((width, 3 * width), F32),
        name="settle_qkv",
    )(side, late, late_other, early, early_other)


def per_device(
    inputs, doc_lengths, w_qkv, bias_q, bias_v, conv_taps, w_out, bias_out, norm1_gain,
    norm1_bias, w_up, bias_up, w_down, bias_down, norm2_gain, norm2_bias, cotangent,
):
    tokens = inputs[0]
    tok_count, width = tokens.shape
    heads, tap_count = conv_taps.shape
    size = width // heads
    radius = (tap_count - 1) // 2
    lengths = doc_lengths[0]
    docs = lengths.shape[0]
    mark_count = docs * LAND
    scale = 1.0 / math.sqrt(size)
    seq_count = lax.axis_size("seq")
    me = lax.axis_index("seq")
    row_first = me * tok_count
    ends = jnp.cumsum(lengths)
    starts = ends - lengths
    bounds = (jnp.concatenate([starts, ends]) - row_first).astype(jnp.int32)
    within = jnp.arange(LAND + 1, dtype=jnp.int32)
    edges = starts[:, None] + (within[None, :] * lengths[:, None] + LAND - 1) // LAND
    mark_low = edges[:, :-1].reshape(mark_count, 1)
    mark_high = edges[:, 1:].reshape(mark_count, 1)
    counts = (mark_high - mark_low).astype(F32)
    places = row_first + jnp.arange(tok_count, dtype=jnp.int32)[None, :]
    onehot = ((places >= mark_low) & (places < mark_high)).astype(BF)
    rows_in = (((0,), (0,)), ((), ()))
    cols_in = (((1,), (1,)), ((), ()))
    blocks = tok_count // BLOCK
    window_rows = tok_count + GROUP - SUB
    smem = pl.BlockSpec(memory_space=pltpu.SMEM)
    params = pltpu.CompilerParams(vmem_limit_bytes=40 * 1024 * 1024)
    tok_spec = pl.BlockSpec((BLOCK, width), lambda i: (i, 0))

    def part(col):
        return pl.BlockSpec((BLOCK, width), lambda i: (i, col))

    def fixed(*shape):
        return pl.BlockSpec(shape, lambda i: (0,) * len(shape))

    def shaped(shape, dtype):
        return jax.ShapeDtypeStruct(shape, dtype)

    means = jnp.dot(onehot, tokens, preferred_element_type=F32) / counts
    mean_in = seq_whole(seq_quarter(means.astype(BF), add_join))
    marks = jnp.dot(mean_in, w_qkv[:, : 2 * width], preferred_element_type=F32)
    mark_q = (marks[:, :width] + bias_q).astype(BF)
    mark_k = marks[:, width:].astype(BF)

    bias = jnp.concatenate([bias_q, jnp.zeros_like(bias_q), bias_v])
    qkv = (jnp.dot(tokens, w_qkv, preferred_element_type=F32) + bias).astype(BF)
    value_ext = extended(qkv[:, 2 * width :], radius, window_rows)
    value_ext, mark_q, mark_k = lax.optimization_barrier((value_ext, mark_q, mark_k))

    def one_col(col):
        return pl.BlockSpec((tok_count, width), lambda i: (0, col))

    stats = pl.pallas_call(
        lambda *refs: landmark_kernel(docs, scale, *refs),
        grid=(1,),
        in_specs=[smem, fixed(mark_count, width), one_col(1), one_col(2)],
        out_specs=fixed(mark_count, width + 128),
        out_shape=shaped((mark_count, width + 128), BF),
        scratch_shapes=[
            pltpu.VMEM((width, 128), F32), pltpu.VMEM((width, 128), F32),
            pltpu.VMEM((width, GROUP), F32),
        ],
        compiler_params=params,
        name="landmark",
    )(bounds, mark_q, qkv, qkv)
    far_count = seq_count // 4
    own_count = -(-heads // far_count)
    own_doc = (me % 2) * 2 + (me // 2) % 2
    own_at = (me // 4) * own_count * size
    spare = far_count * own_count * size - width

    def own_heads(array):
        array = jnp.pad(array, ((0, 0), (0, spare)))
        array = lax.dynamic_slice_in_dim(array, own_at, own_count * size, 1)
        return array.reshape(LAND, own_count, size).transpose(1, 0, 2)

    def of_doc(array):
        return lax.dynamic_slice_in_dim(array, own_doc * LAND, LAND, 0)

    mine, other = halves(stats, 1)
    stats = join(mine, swap(other, "seq", 1))
    stats, later_q, later_k = lax.optimization_barrier((stats, mark_q, mark_k))
    own_q = own_heads(of_doc(later_q)).astype(F32)
    own_k = own_heads(of_doc(later_k)).astype(F32)
    square = (own_count, LAND, LAND)
    own_inverse, kernel, saved = pl.pallas_call(
        lambda *refs: pinv_kernel(scale, *refs),
        out_shape=(
            shaped(square, F32), shaped(square, F32),
            shaped((4 * NS_ITERS * own_count, LAND, LAND), F32),
        ),
        name="pinv",
    )(own_q, own_k)
    inverse = own_inverse.transpose(1, 0, 2).reshape(LAND, own_count * size).astype(BF)
    mine, other = halves(stats, 2)
    stats = join(mine, swap(other, "seq", 2))
    for i in range(2, seq_count.bit_length() - 1):
        other = swap(jnp.concatenate([stats, inverse], 1), "seq", 1 << i)
        stats = join(stats, other[:, : width + 128])
        other = other[:, width + 128 :]
        inverse = jnp.where(
            (me >> i) % 2 == 0,
            jnp.concatenate([inverse, other], 1),
            jnp.concatenate([other, inverse], 1),
        )
    inverse = inverse[:, :width]
    mix = pl.pallas_call(
        mix_kernel, out_shape=shaped((LAND, width + 128), BF), name="mix"
    )(inverse, stats)
    mix = seq_whole(mix)

    taps = jnp.pad(conv_taps, ((0, 0), (0, GROUP - tap_count)))
    mark_spec = fixed(mark_count, width)
    mixed, probs = pl.pallas_call(
        lambda *refs: token_kernel(docs, scale, *refs),
        grid=(blocks,),
        in_specs=[
            smem, part(0), fixed(window_rows, width), mark_spec, mark_spec, fixed(heads, GROUP)
        ],
        out_specs=(tok_spec, pl.BlockSpec((width, BLOCK), lambda i: (0, i))),
        out_shape=(shaped((tok_count, width), BF), shaped((width, tok_count), BF)),
        scratch_shapes=[pltpu.VMEM((heads * SUB, GROUP), BF), pltpu.VMEM((BLOCK, width), F32)],
        compiler_params=params,
        name="token",
    )(bounds, qkv, value_ext, mark_k, mix, taps)

    hidden = w_up.shape[1]
    vectors = jnp.stack([bias_out, norm1_gain, norm1_bias, bias_down, norm2_gain, norm2_bias])
    vectors = jnp.pad(vectors, ((0, 2), (0, 0)))
    wide_spec = pl.BlockSpec((FFN_BLOCK, hidden), lambda i: (i, 0))
    ffn_spec = pl.BlockSpec((FFN_BLOCK, width), lambda i: (i, 0))
    narrow = shaped((tok_count, width), BF)
    (
        result, grad_one, active, grad_upper, hidden_low, grad_low_two, grad_low_one,
        grad_mixed, sums, sum_up,
    ) = pl.pallas_call(
        ffn_kernel,
        grid=(tok_count // FFN_BLOCK,),
        in_specs=[
            ffn_spec, ffn_spec, ffn_spec, fixed(width, width), fixed(width, hidden),
            fixed(hidden, width), fixed(8, width), fixed(8, hidden),
        ],
        out_specs=(
            ffn_spec, ffn_spec, wide_spec, wide_spec, ffn_spec, ffn_spec, ffn_spec, ffn_spec,
            fixed(8, width), fixed(8, hidden),
        ),
        out_shape=(
            shaped((tok_count, width), F32), shaped((tok_count, width), F32),
            shaped((tok_count, hidden), BF), shaped((tok_count, hidden), BF),
            narrow, narrow, narrow, narrow, shaped((8, width), F32), shaped((8, hidden), F32),
        ),
        scratch_shapes=[pltpu.VMEM((FFN_BLOCK, hidden), BF)],
        compiler_params=pltpu.CompilerParams(vmem_limit_bytes=58 * 1024 * 1024),
        name="ffn",
    )(
        tokens, mixed, cotangent[0], w_out, w_up, w_down, vectors,
        jnp.broadcast_to(bias_up[None, :], (8, hidden)),
    )

    grad_queries, grad_mix, grad_mk = pl.pallas_call(
        lambda *refs: token_back_kernel(docs, scale, *refs),
        grid=(blocks,),
        in_specs=[
            smem, part(0), tok_spec, pl.BlockSpec((width, BLOCK), lambda i: (0, i)), mark_spec,
            mark_spec,
        ],
        out_specs=(tok_spec, mark_spec, mark_spec),
        out_shape=(
            shaped((tok_count, width), BF), shaped((mark_count, width), F32),
            shaped((mark_count, width), F32),
        ),
        scratch_shapes=[pltpu.VMEM((BLOCK, width), F32)],
        compiler_params=params,
        name="token_back",
    )(bounds, qkv, grad_mixed, probs, mark_k, mix)
    grad_w_down = lax.dot_general(active, grad_low_two, rows_in, preferred_element_type=F32)
    grad_w_up = lax.dot_general(hidden_low, grad_upper, rows_in, preferred_element_type=F32)
    grad_mix, grad_w_down, grad_w_up = lax.optimization_barrier(
        (grad_mix.astype(BF), grad_w_down.astype(BF), grad_w_up.astype(BF))
    )
    sum_w_down, sum_w_up = lax.psum((grad_w_down, grad_w_up), ("row", "seq"))

    def remaining(grad_mix, grad_mk, stats, mix):
        grad_mix = seq_quarter(grad_mix.astype(BF), add_join)
        grad_w_out = lax.dot_general(mixed, grad_low_one, rows_in, preferred_element_type=F32)

        grad_ext = extended(grad_mixed, radius, window_rows)
        grad_conv, products = pl.pallas_call(
            lambda *refs: conv_back_kernel(docs, *refs),
            grid=(blocks,),
            in_specs=[
                smem, fixed(window_rows, width), fixed(window_rows, width), fixed(heads, GROUP)
            ],
            out_specs=(tok_spec, fixed(heads * SUB, GROUP)),
            out_shape=(shaped((tok_count, width), F32), shaped((heads * SUB, GROUP), F32)),
            scratch_shapes=[pltpu.VMEM((heads * SUB, GROUP), BF)],
            compiler_params=params,
            name="conv_back",
        )(bounds, grad_ext, value_ext, jnp.pad(conv_taps[:, ::-1], ((0, 0), (0, GROUP - tap_count))))
        reach = SUB + tap_count - 1
        products = products.reshape(heads, SUB, GROUP)[:, :, :reach].reshape(heads, SUB * reach)
        products = jnp.pad(products, ((0, 0), (0, SUB))).reshape(heads, SUB, reach + 1)
        grad_conv_taps = jnp.sum(products, axis=1)[:, :tap_count]
        grad_mix, grad_conv, grad_conv_taps = lax.optimization_barrier(
            (grad_mix, grad_conv, grad_conv_taps)
        )

        grad_avg = pl.pallas_call(
            mix_back_kernel, out_shape=shaped((LAND, width + 128), BF), name="mix_back"
        )(inverse, stats, grad_mix)
        grad_avg = seq_whole(grad_avg)
        lane_spec = pl.BlockSpec((mark_count, 128), lambda i: (0, width // 128))
        grad_keys, grad_values, grad_mq = pl.pallas_call(
            lambda *refs: landmark_back_kernel(docs, scale, *refs),
            grid=(blocks,),
            in_specs=[
                smem, part(1), part(2), tok_spec, mark_spec, mark_spec, lane_spec, lane_spec
            ],
            out_specs=(tok_spec, tok_spec, mark_spec),
            out_shape=(
                shaped((tok_count, width), BF), shaped((tok_count, width), BF),
                shaped((mark_count, width), F32),
            ),
            scratch_shapes=[pltpu.VMEM((BLOCK, width), F32), pltpu.VMEM((BLOCK, width), F32)],
            compiler_params=params,
            name="landmark_back",
        )(bounds, qkv, qkv, grad_conv, mark_q, grad_avg, mix, grad_avg)


        def weight_grad(grads):
            return lax.dot_general(tokens, grads, rows_in, preferred_element_type=F32)

        early = jnp.concatenate(
            [grad_w_out.astype(BF), weight_grad(grad_values).astype(BF)], 0
        )
        grad_mix, early = lax.optimization_barrier((grad_mix, early))
        early = advance(begin(early, ORDER, ORDER), 1)
        grad_mq_small, grad_mk_small = pl.pallas_call(
            lambda *refs: pinv_back_kernel(scale, *refs),
            out_shape=(shaped(square, F32), shaped(square, F32)),
            name="pinv_back",
        )(own_q, own_k, kernel, saved, own_heads(grad_mix), own_heads(stats[:, :width]))

        def with_small(array, small):
            small = small.transpose(1, 0, 2).reshape(LAND, own_count * size)
            small = lax.dynamic_update_slice_in_dim(
                jnp.zeros((LAND, width + spare), F32), small, own_at, 1
            )[:, :width]
            first = own_doc * LAND
            rows = lax.dynamic_slice_in_dim(array, first, LAND, 0) + small
            return lax.dynamic_update_slice_in_dim(array, rows, first, 0)

        grad_mq = with_small(grad_mq, grad_mq_small)
        grad_mk = with_small(grad_mk, grad_mk_small)
        grad_marks = jnp.concatenate([grad_mq, grad_mk], axis=1).astype(BF)
        mark_back = lax.dot_general(
            grad_marks, w_qkv[:, : 2 * width], cols_in, preferred_element_type=F32
        ) / counts
        mark_back = mark_back.astype(BF)

        grad_bias_q = jnp.sum(grad_queries.astype(F32), axis=0) + jnp.sum(grad_mq, axis=0)
        grad_bias_v = jnp.sum(grad_values.astype(F32), axis=0)
        mark_grad_q = lax.dot_general(
            mean_in, grad_marks[:, :width], rows_in, preferred_element_type=F32
        )
        mark_grad_k = lax.dot_general(
            mean_in, grad_marks[:, width:], rows_in, preferred_element_type=F32
        )
        others = jnp.concatenate(
            [
                sum_up[0].reshape(hidden // width, width),
                grad_bias_q[None],
                grad_bias_v[None],
                jnp.pad(grad_conv_taps.reshape(1, -1), ((0, 0), (0, width - heads * tap_count))),
                jnp.zeros((4 - hidden // width + 1, width), F32),
            ],
            0,
        )
        spare_rows = width // 6
        small = jnp.concatenate([sums, others], 0).astype(BF)
        small = jnp.pad(small, ((0, spare_rows - small.shape[0]), (0, 0)))
        small = lax.optimization_barrier(small)
        late = jnp.concatenate(
            [
                (weight_grad(grad_queries) + mark_grad_q).astype(BF),
                small,
                (weight_grad(grad_keys) + mark_grad_k).astype(BF),
                jnp.zeros((spare_rows, width), BF),
            ],
            0,
        )
        late = begin(late, ORDER, ORDER)
        for step in seq_steps():
            mark_back = step(mark_back)
            early, late = advance(early, 1), advance(late, 1)
            mark_back, (early, late) = tied(mark_back, [early, late])
        return early[0], late[0], mark_back, grad_keys, grad_values

    plan = stages(ORDER)
    sent = len(seq_steps())

    def rows_left(rows, done):
        return rows >> min(done, 2 * len(plan) - done)

    early_rows = rows_left(2 * width, sent + 1)
    late_rows = rows_left(2 * width + width // 3, sent)

    def nothing(*unused):
        return tuple(
            jnp.zeros((rows, width), BF)
            for rows in (early_rows, late_rows, mark_count, tok_count, tok_count)
        )

    early, late, mark_back, grad_keys, grad_values = lax.cond(
        lengths[0] > 0, remaining, nothing, grad_mix, grad_mk, stats, mix
    )
    early, late = (early, plan, plan, sent + 1), (late, plan, plan, sent)
    last = 2 * len(plan) - 1
    early, late = advance(early, last - sent - 1), advance(late, last - sent)
    sum_w_down, sum_w_up = sum_w_down.astype(F32), sum_w_up.astype(F32)
    grad_projected = jnp.concatenate([grad_queries, grad_keys, grad_values], axis=1)
    grad_input = (
        grad_one
        + lax.dot_general(grad_projected, w_qkv, cols_in, preferred_element_type=F32)
        + lax.dot_general(onehot, mark_back, rows_in, preferred_element_type=F32)
    )
    (sum_w_down, sum_w_up, grad_input), (early, late) = tied(
        (sum_w_down, sum_w_up, grad_input), [early, late]
    )
    early, early_other = last_swap(early)[:2]
    late, late_other = last_swap(late)[:2]
    sum_w_qkv = settle_qkv(late, late_other, early, early_other, width)
    first_core = me % 2 == 0
    sum_w_out = jnp.where(first_core, early, early_other).astype(F32)
    flat = jnp.where(first_core, late[width:], late_other[width:])[:16].astype(F32)
    at = sums.shape[0] + hidden // width
    pieces = [
        flat[at], flat[at + 1], flat[at + 2, : heads * tap_count], flat[5], flat[3], flat[4],
        flat[sums.shape[0] : at].reshape(hidden), flat[2], flat[0], flat[1],
    ]
    return (
        result[None], grad_input[None], sum_w_qkv, pieces[0], pieces[1],
        pieces[2].reshape(heads, tap_count), sum_w_out, pieces[3], pieces[4], pieces[5],
        sum_w_up, pieces[6], sum_w_down, pieces[7], pieces[8], pieces[9],
    )


def solution(mesh):
    whole, tokens = P(), P("row", "seq", None)
    return jax.shard_map(
        per_device,
        mesh=mesh,
        in_specs=(tokens, P("row", None)) + (whole,) * 14 + (tokens,),
        out_specs=(tokens, tokens) + (whole,) * 14,
        check_vma=False,
    )
```

```python
import math

import jax
import jax.numpy as jnp
from jax import lax
from jax.experimental import pallas as pl
from jax.experimental.pallas import tpu as pltpu
from jax.sharding import PartitionSpec as P

LAND = 64
NS_ITERS = 6
HIGH = lax.Precision.HIGHEST
NEGATIVE = -1e30
BF = jnp.bfloat16
F32 = jnp.float32

BLOCK = 256
GROUP = 256
SUB = 128
TAPS = 33
FFN_BLOCK = 256
ORDER = ("row", "near", "far")


def swap(array, axis, bit):
    count = lax.axis_size(axis)
    return lax.ppermute(array, axis, [(i, i ^ bit) for i in range(count)])


def add_parts(parts):
    total = parts[0].astype(F32)
    for part in parts[1:]:
        total = total + part.astype(F32)
    return total


def halves(array, bit):
    rows = array.shape[0] // 2
    side = (lax.axis_index("seq") // bit) % 2
    mine = lax.dynamic_slice_in_dim(array, side * rows, rows, 0)
    other = lax.dynamic_slice_in_dim(array, (1 - side) * rows, rows, 0)
    return mine, other


def seq_quarter(array, join):
    bits = [1 << i for i in range(lax.axis_size("seq").bit_length() - 1)]
    for bit in bits[:2]:
        mine, other = halves(array, bit)
        array = join(mine, swap(other, "seq", bit))
    for bit in bits[2:]:
        array = join(array, swap(array, "seq", bit))
    return array


def paired(array, axis, bit, dim):
    other = swap(array, axis, bit)
    side = (lax.axis_index(axis) // bit) % 2
    return jnp.where(
        side == 0,
        jnp.concatenate([array, other], dim),
        jnp.concatenate([other, array], dim),
    )


def seq_whole(array):
    return paired(paired(array, "seq", 2, 0), "seq", 1, 0)


def seq_steps():
    bits = [1 << i for i in range(lax.axis_size("seq").bit_length() - 1)]

    def halve(bit):
        def step(array):
            mine, other = halves(array, bit)
            return add_join(mine, swap(other, "seq", bit))

        return step

    def whole(bit):
        return lambda array: add_join(array, swap(array, "seq", bit))

    def double(bit):
        return lambda array: paired(array, "seq", bit, 0)

    return (
        [halve(bit) for bit in bits[:2]]
        + [whole(bit) for bit in bits[2:]]
        + [double(bit) for bit in reversed(bits[:2])]
    )


def add_join(first, second):
    return (first.astype(F32) + second.astype(F32)).astype(BF)


def stages(order):
    row = [("row", 1 << i) for i in range(lax.axis_size("row").bit_length() - 1)]
    seq = [[("seq", 1 << i)] for i in range(lax.axis_size("seq").bit_length() - 1)]
    named = {"core": seq[0], "row": row, "near": seq[1], "far": seq[2], "rest": sum(seq[3:], [])}
    return sum([named[name] for name in ("core",) + order + ("rest",)], [])


def begin(array, down, back):
    return array, stages(down), stages(back), 0


def advance(state, steps):
    held, down, back, done = state
    for step in range(done, min(done + steps, 2 * len(down))):
        if step < len(down):
            axis, bit = down[step]
            half = held.shape[0] // 2
            side = (lax.axis_index(axis) // bit) % 2
            mine = lax.dynamic_slice_in_dim(held, side * half, half, 0)
            other = lax.dynamic_slice_in_dim(held, (1 - side) * half, half, 0)
            held = mine.astype(F32) + swap(other, axis, bit).astype(F32)
            held = held.astype(BF)
        else:
            axis, bit = back[2 * len(down) - 1 - step]
            held = paired(held, axis, bit, 0)
    return held, down, back, min(done + steps, 2 * len(down))


def last_swap(state):
    down, back = state[1], state[2]
    held = advance(state, 2 * len(down) - 1 - state[3])[0]
    return held, swap(held, *down[0]), down, back


def tied(values, states):
    values, helds = lax.optimization_barrier((values, [state[0] for state in states]))
    return values, [(held,) + state[1:] for held, state in zip(helds, states)]


def extended(cells, width, rows):
    count = lax.axis_size("seq")
    head = cells[:width]
    tail = cells[-width:]
    return jnp.concatenate(
        [
            lax.ppermute(tail, "seq", [(i, i + 1) for i in range(count - 1)]),
            cells,
            lax.ppermute(head, "seq", [(i + 1, i) for i in range(count - 1)]),
            jnp.zeros((rows - cells.shape[0] - 2 * width, cells.shape[1]), cells.dtype),
        ],
        axis=0,
    )


def dot_nn(a, b):
    return jnp.dot(a, b, preferred_element_type=F32)


def dot_nt(a, b):
    return lax.dot_general(a, b, (((1,), (1,)), ((), ())), preferred_element_type=F32)


def dot_tn(a, b):
    return lax.dot_general(a, b, (((0,), (0,)), ((), ())), preferred_element_type=F32)


def iota(shape, dim):
    return lax.broadcasted_iota(jnp.int32, shape, dim)


def spread(block):
    rows = block.shape[0]
    tall = jnp.concatenate([block] * 4, axis=0).astype(F32)
    shape = (4 * rows, GROUP)
    keep = iota(shape, 0) // rows == iota(shape, 1) // LAND
    return jnp.where(keep, tall, 0.0).astype(BF)


def gathered(square):
    rows = square.shape[0] // 4
    lane = iota((rows, GROUP), 1) // LAND
    out = square[:rows]
    for head in range(1, 4):
        out = jnp.where(lane == head, square[head * rows : (head + 1) * rows], out)
    return out


def by_head(columns, first, shape):
    lane = iota(shape, 1)
    out = jnp.zeros(shape, F32)
    for head, column in enumerate(columns):
        out = jnp.where((lane % 16 == first + head) & (lane < 48), column, out)
    return out


def split_three(cells):
    lane = iota(cells.shape, 1)
    high = cells.astype(BF).astype(F32)
    mid = (cells - high).astype(BF).astype(F32)
    low = cells - high - mid
    return jnp.where(lane < 16, high, jnp.where(lane < 32, mid, low)).astype(BF)


def merge_three(cells):
    cells = cells.astype(F32)
    return cells + pltpu.roll(cells, 112, 1) + pltpu.roll(cells, 96, 1)


def head_lanes(heads, width):
    return (iota((128, width), 0) == iota((128, width), 1) // LAND).astype(F32)


def doc_of(places, bounds, docs):
    out = (places >= bounds[2 * docs - 1]).astype(jnp.int32)
    for doc in range(docs):
        out = out + (places >= bounds[doc]).astype(jnp.int32)
    return out


def landmark_kernel(docs, scale, bounds, mq_ref, k_ref, v_ref, out_ref, max_s, sum_s, acc_s):
    tokens, width = k_ref.shape
    groups = width // GROUP
    heads = width // LAND
    out_ref[:, :width] = jnp.zeros((docs * LAND, width), BF)
    empty = jnp.full((docs * LAND, 128), NEGATIVE, F32)
    out_ref[:, width:] = jnp.where(iota(empty.shape, 1) < 48, split_three(empty).astype(F32), 0.0).astype(BF)
    for doc in range(docs):
        low = jnp.clip(bounds[doc], 0, tokens)
        high = jnp.clip(bounds[docs + doc], 0, tokens)
        rows = slice(doc * LAND, (doc + 1) * LAND)

        @pl.when(high > low)
        def _():
            max_s[...] = jnp.full(max_s.shape, NEGATIVE, F32)
            sum_s[...] = jnp.zeros(sum_s.shape, F32)
            acc_s[...] = jnp.zeros(acc_s.shape, F32)
            wide = [
                spread(mq_ref[rows, g * GROUP : (g + 1) * GROUP]) for g in range(groups)
            ]

            ones = jnp.ones((BLOCK, 128), BF)

            def step(block, carry):
                first = pl.multiple_of(block * BLOCK, BLOCK)
                at = pl.ds(first, BLOCK)
                place = iota((1, BLOCK), 1) + first
                valid = (place >= low) & (place < high)
                for g in range(groups):
                    cols = slice(g * GROUP, (g + 1) * GROUP)
                    scores = dot_nt(wide[g], k_ref[at, cols]) * scale
                    scores = jnp.where(valid, scores, NEGATIVE)
                    old = max_s[cols, :]
                    top = jnp.maximum(old, jnp.max(scores, axis=1, keepdims=True))
                    weights = jnp.exp(scores - twice(top)).astype(BF)
                    shrink = jnp.exp(old - top)
                    max_s[cols, :] = top
                    sum_s[cols, :] = sum_s[cols, :] * shrink + dot_nn(weights, ones)
                    acc_s[cols, :] = acc_s[cols, :] * twice(shrink) + dot_nn(weights, v_ref[at, cols])
                return carry

            lax.fori_loop(low // BLOCK, (high + BLOCK - 1) // BLOCK, step, 0)
            columns = []
            for g in range(groups):
                cols = slice(g * GROUP, (g + 1) * GROUP)
                sums = sum_s[cols, :]
                out_ref[rows, cols] = gathered(acc_s[cols, :] / twice(sums)).astype(BF)
                level = max_s[cols, :] + jnp.log(sums)
                columns += [level[h * LAND : (h + 1) * LAND] for h in range(4)]
            out_ref[rows, width:] = split_three(by_head(columns, 0, (LAND, 128)))


def twice(cells):
    return jnp.concatenate([cells, cells], axis=1)


def join_kernel(a_ref, b_ref, out_ref):
    width = a_ref.shape[1] - 128
    heads = width // LAND
    first, second = merge_three(a_ref[:, width:]), merge_three(b_ref[:, width:])
    lane = iota(first.shape, 1)
    first = jnp.where(lane < heads, first, 0.0)
    second = jnp.where(lane < heads, second, 0.0)
    top = jnp.maximum(first, second)
    exp_a, exp_b = jnp.exp(first - top), jnp.exp(second - top)
    both = exp_a + exp_b
    level = top + jnp.log(both)
    pick = head_lanes(heads, width)
    share_a = jnp.dot(exp_a / both, pick, precision=HIGH, preferred_element_type=F32)
    share_b = jnp.dot(exp_b / both, pick, precision=HIGH, preferred_element_type=F32)
    joined = a_ref[:, :width].astype(F32) * share_a + b_ref[:, :width].astype(F32) * share_b
    out_ref[:, :width] = joined.astype(BF)
    level = jnp.where(lane < heads, level, 0.0)
    level = level + pltpu.roll(level, 16, 1) + pltpu.roll(level, 32, 1)
    out_ref[:, width:] = split_three(level)


def join(first, second):
    return pl.pallas_call(
        join_kernel, out_shape=jax.ShapeDtypeStruct(first.shape, BF), name="join"
    )(first, second)


def mix_kernel(inv_ref, stat_ref, mix_ref):
    width = stat_ref.shape[1] - 128
    for g in range(width // GROUP):
        cols = slice(g * GROUP, (g + 1) * GROUP)
        mix_ref[:, cols] = dot_nn(inv_ref[:, cols], spread(stat_ref[:, cols])).astype(BF)
    mix_ref[:, width:] = stat_ref[:, width:]


def mix_back_kernel(inv_ref, stat_ref, grad_ref, out_ref):
    width = stat_ref.shape[1] - 128
    columns = []
    for g in range(width // GROUP):
        cols = slice(g * GROUP, (g + 1) * GROUP)
        grad = gathered(dot_tn(inv_ref[:, cols], grad_ref[:, cols]))
        out_ref[:, cols] = grad.astype(BF)
        product = grad * stat_ref[:, cols].astype(F32)
        lane = iota(product.shape, 1) // LAND
        for h in range(4):
            columns.append(jnp.sum(jnp.where(lane == h, product, 0.0), axis=1, keepdims=True))
    out_ref[:, width:] = split_three(by_head(columns, 0, (LAND, 128)))


def make_band(taps_ref, band_s):
    for head in range(taps_ref.shape[0]):
        row = jnp.broadcast_to(taps_ref[head : head + 1, :], (SUB, GROUP))
        band_s[head * SUB : (head + 1) * SUB, :] = pltpu.roll(row, 0, 1, stride=1, stride_axis=0).astype(BF)


def same_doc(first, bounds, docs, radius):
    rows = iota((SUB, GROUP), 0) + first
    cols = iota((SUB, GROUP), 1) + (first - radius)
    return doc_of(rows, bounds, docs) == doc_of(cols, bounds, docs)


def token_kernel(
    docs, scale, bounds, q_ref, v_ref, mk_ref, mix_ref, taps_ref, mixed_ref, probs_ref, band_s, sum_s
):
    width = q_ref.shape[1]
    groups = width // GROUP
    radius = (TAPS - 1) // 2
    first = pl.program_id(0) * BLOCK

    @pl.when(pl.program_id(0) == 0)
    def _():
        make_band(taps_ref, band_s)

    for sub in range(BLOCK // SUB):
        start = pl.multiple_of(first + sub * SUB, SUB)
        same = same_doc(start, bounds, docs, radius)
        same = jnp.where(jnp.concatenate([same] * 4, axis=0), 1.0, 0.0).astype(BF)
        for g in range(groups):
            cols = slice(g * GROUP, (g + 1) * GROUP)
            band = band_s[g * 4 * SUB : (g + 1) * 4 * SUB, :] * same
            res = dot_nn(band, v_ref[pl.ds(start, GROUP), cols])
            sum_s[sub * SUB : (sub + 1) * SUB, cols] = gathered(res)
    probs_ref[...] = jnp.zeros(probs_ref.shape, BF)
    for doc in range(docs):
        low, high = bounds[doc], bounds[docs + doc]
        rows = slice(doc * LAND, (doc + 1) * LAND)

        @pl.when((high > first) & (low < first + BLOCK))
        def _():
            place = iota((1, BLOCK), 1) + first
            valid = (place >= low) & (place < high)
            for g in range(groups):
                cols = slice(g * GROUP, (g + 1) * GROUP)
                scores = dot_nt(spread(mk_ref[rows, cols]), q_ref[:, cols]) * scale
                scores = scores.reshape(4, LAND, BLOCK)
                weights = jnp.exp(scores - jnp.max(scores, axis=1, keepdims=True))
                probs = weights / jnp.sum(weights, axis=1, keepdims=True)
                probs = jnp.where(valid, probs.reshape(GROUP, BLOCK), 0.0).astype(BF)
                probs_ref[cols, :] = probs_ref[cols, :] + probs
                sum_s[:, cols] = sum_s[:, cols] + dot_tn(probs, spread(mix_ref[rows, cols]))

    mixed_ref[...] = sum_s[...].astype(BF)


def token_back_kernel(
    docs, scale, bounds, q_ref, gm_ref, probs_ref, mk_ref, mix_ref, gq_ref, gmix_ref, gmk_ref, gq_s
):
    width = q_ref.shape[1]
    groups = width // GROUP
    first = pl.program_id(0) * BLOCK

    @pl.when(pl.program_id(0) == 0)
    def _():
        gmix_ref[...] = jnp.zeros(gmix_ref.shape, F32)
        gmk_ref[...] = jnp.zeros(gmk_ref.shape, F32)

    gq_s[...] = jnp.zeros(gq_s.shape, F32)
    for doc in range(docs):
        low, high = bounds[doc], bounds[docs + doc]
        rows = slice(doc * LAND, (doc + 1) * LAND)

        @pl.when((high > first) & (low < first + BLOCK))
        def _():
            place = iota((1, BLOCK), 1) + first
            valid = (place >= low) & (place < high)
            for g in range(groups):
                cols = slice(g * GROUP, (g + 1) * GROUP)
                probs = jnp.where(valid, probs_ref[cols, :].astype(F32), 0.0)
                gmix_ref[rows, cols] += gathered(dot_nn(probs.astype(BF), gm_ref[:, cols]))
                grad = dot_nt(spread(mix_ref[rows, cols]), gm_ref[:, cols])
                heavy = (probs * grad).reshape(4, LAND, BLOCK)
                shared = probs.reshape(4, LAND, BLOCK) * jnp.sum(heavy, axis=1, keepdims=True)
                grad = ((heavy - shared).reshape(GROUP, BLOCK) * scale).astype(BF)
                gmk_ref[rows, cols] += gathered(dot_nn(grad, q_ref[:, cols]))
                gq_s[:, cols] += dot_tn(grad, spread(mk_ref[rows, cols]))

    gq_ref[...] = gq_s[...].astype(BF)


def conv_back_kernel(docs, bounds, gm_ref, v_ref, taps_ref, out_ref, sum_ref, band_s, prod_s):
    width = gm_ref.shape[1]
    groups = width // GROUP
    radius = (TAPS - 1) // 2
    first = pl.program_id(0) * BLOCK

    @pl.when(pl.program_id(0) == 0)
    def _():
        make_band(taps_ref, band_s)
        prod_s[...] = jnp.zeros(prod_s.shape, F32)

    for sub in range(BLOCK // SUB):
        start = pl.multiple_of(first + sub * SUB, SUB)
        same = same_doc(start, bounds, docs, radius)
        same = jnp.where(jnp.concatenate([same] * 4, axis=0), 1.0, 0.0)
        for g in range(groups):
            cols = slice(g * GROUP, (g + 1) * GROUP)
            tall = slice(g * 4 * SUB, (g + 1) * 4 * SUB)
            band = band_s[tall, :] * same.astype(BF)
            res = dot_nn(band, gm_ref[pl.ds(start, GROUP), cols])
            out_ref[sub * SUB : (sub + 1) * SUB, cols] = gathered(res)
            own = gm_ref[pl.ds(pl.multiple_of(start + radius, 16), SUB), cols]
            product = dot_nt(spread(own), v_ref[pl.ds(start, GROUP), cols])
            prod_s[tall, :] += product * same

    @pl.when(pl.program_id(0) == pl.num_programs(0) - 1)
    def _():
        flip = (iota((SUB, SUB), 0) + iota((SUB, SUB), 1) == SUB - 1).astype(F32).astype(BF)
        sum_ref[...] = jnp.zeros(sum_ref.shape, F32)
        for head in range(taps_ref.shape[0]):
            product = prod_s[head * SUB : (head + 1) * SUB, :]
            high = product.astype(BF)
            low = (product - high.astype(F32)).astype(BF)
            turned = pltpu.roll(dot_nn(flip, high) + dot_nn(flip, low), 0, 1, stride=1, stride_axis=0)
            sum_ref[head : head + 1, :] = jnp.sum(turned, axis=0, keepdims=True)


def ffn_kernel(
    x_ref, mixed_ref, cot_ref, w_out_ref, w_up_ref, w_down_ref, rows_ref, bias_up_ref,
    result_ref, grad_one_ref, active_ref, grad_up_ref, low_ref, low_two_ref, low_one_ref,
    grad_mixed_ref, sums_ref, sum_up_ref, slope_s,
):
    width = x_ref.shape[1]
    hidden = w_up_ref.shape[1]
    chunks = [slice(at, at + width) for at in range(0, hidden, width)]

    def row(i):
        return rows_ref[i : i + 1, :]

    @pl.when(pl.program_id(0) == 0)
    def _():
        sums_ref[...] = jnp.zeros(sums_ref.shape, F32)
        sum_up_ref[...] = jnp.zeros(sum_up_ref.shape, F32)

    def add_sum(i, cells):
        sums_ref[i : i + 1, :] += jnp.sum(cells, axis=0, keepdims=True)

    attended = dot_nn(mixed_ref[...], w_out_ref[...]) + row(0)
    norm_one, inverse_one = normalize(x_ref[...].astype(F32) + attended)
    hidden_one = norm_one * row(1) + row(2)
    hidden_low = hidden_one.astype(BF)
    low_ref[...] = hidden_low
    lowered = hidden_one + row(3)
    for cols in chunks:
        upper = dot_nn(hidden_low, w_up_ref[:, cols]) + bias_up_ref[:1, cols]
        active, slope = gelu_both(upper)
        active = active.astype(BF)
        active_ref[:, cols] = active
        slope_s[:, cols] = slope.astype(BF)
        lowered = lowered + dot_nn(active, w_down_ref[cols, :])
    norm_two, inverse_two = normalize(lowered)
    result_ref[...] = norm_two * row(4) + row(5)
    upstream = cot_ref[...].astype(F32)
    add_sum(0, upstream * norm_two)
    add_sum(1, upstream)
    grad_two = norm_back(upstream * row(4), norm_two, inverse_two)
    low_two = grad_two.astype(BF)
    low_two_ref[...] = low_two
    add_sum(2, low_two.astype(F32))
    grad_hidden = grad_two
    for cols in chunks:
        grad_up = dot_nt(low_two, w_down_ref[cols, :]) * slope_s[:, cols].astype(F32)
        grad_up = grad_up.astype(BF)
        grad_up_ref[:, cols] = grad_up
        sum_up_ref[:1, cols] += jnp.sum(grad_up.astype(F32), axis=0, keepdims=True)
        grad_hidden = grad_hidden + dot_nt(grad_up, w_up_ref[:, cols])
    add_sum(3, grad_hidden * norm_one)
    add_sum(4, grad_hidden)
    grad_one = norm_back(grad_hidden * row(1), norm_one, inverse_one)
    grad_one_ref[...] = grad_one
    low_one = grad_one.astype(BF)
    low_one_ref[...] = low_one
    add_sum(5, low_one.astype(F32))
    grad_mixed_ref[...] = dot_nt(low_one, w_out_ref[...]).astype(BF)


def landmark_back_kernel(
    docs, scale, bounds, k_ref, v_ref, conv_ref, mq_ref, grad_ref, level_ref, dots_ref,
    gk_ref, gv_ref, gmq_ref, gk_s, gv_s,
):
    width = k_ref.shape[1]
    groups = width // GROUP
    first = pl.program_id(0) * BLOCK

    @pl.when(pl.program_id(0) == 0)
    def _():
        gmq_ref[...] = jnp.zeros(gmq_ref.shape, F32)

    gk_s[...] = jnp.zeros(gk_s.shape, F32)
    gv_s[...] = conv_ref[...]
    for doc in range(docs):
        low, high = bounds[doc], bounds[docs + doc]
        rows = slice(doc * LAND, (doc + 1) * LAND)

        @pl.when((high > first) & (low < first + BLOCK))
        def _():
            place = iota((1, BLOCK), 1) + first
            valid = (place >= low) & (place < high)

            level, dots = merge_three(level_ref[rows, :]), merge_three(dots_ref[rows, :])

            def column(lanes, g):
                return jnp.concatenate(
                    [lanes[:, 4 * g + h : 4 * g + h + 1] for h in range(4)], axis=0
                )

            for g in range(groups):
                cols = slice(g * GROUP, (g + 1) * GROUP)
                wide_q, wide_g = spread(mq_ref[rows, cols]), spread(grad_ref[rows, cols])
                scores = dot_nt(wide_q, k_ref[:, cols]) * scale - column(level, g)
                probs = jnp.exp(jnp.where(valid, scores, NEGATIVE))
                grad = dot_nt(wide_g, v_ref[:, cols]) - column(dots, g)
                grad = (probs * grad * scale).astype(BF)
                gv_s[:, cols] += dot_tn(probs.astype(BF), wide_g)
                gk_s[:, cols] += dot_tn(grad, wide_q)
                gmq_ref[rows, cols] += gathered(dot_nn(grad, k_ref[:, cols]))

    gk_ref[...] = gk_s[...].astype(BF)
    gv_ref[...] = gv_s[...].astype(BF)


def gelu_both(upper):
    tangent = jnp.tanh(0.7978845608028654 * (upper + 0.044715 * upper * upper * upper))
    inner_slope = 0.7978845608028654 * (1.0 + 3.0 * 0.044715 * upper * upper)
    active = 0.5 * upper * (1.0 + tangent)
    slope = 0.5 * (1.0 + tangent) + 0.5 * upper * (1.0 - tangent * tangent) * inner_slope
    return active, slope


def normalize(residual):
    row_mean = jnp.mean(residual, axis=-1, keepdims=True)
    centered = residual - row_mean
    row_var = jnp.mean(centered * centered, axis=-1, keepdims=True)
    inverse_dev = lax.rsqrt(row_var + 1e-05)
    return (centered * inverse_dev, inverse_dev)


def norm_back(grad_normed, normed, inverse_dev):
    return inverse_dev * (
        grad_normed
        - jnp.mean(grad_normed, axis=-1, keepdims=True)
        - normed * jnp.mean(grad_normed * normed, axis=-1, keepdims=True)
    )


def dot_high(a, b, dims):
    return lax.dot_general(
        a, b, (dims, ((), ())), precision=HIGH, preferred_element_type=F32
    )


NN, NT, TN = ((1,), (0,)), ((1,), (1,)), ((0,), (0,))


def pinv_kernel(scale, q_ref, k_ref, inverse_ref, kernel_ref, saved_ref):
    count = q_ref.shape[0]
    eye = (iota((LAND, LAND), 0) == iota((LAND, LAND), 1)).astype(F32)
    kernels, inverses = [], []
    for p in range(count):
        scores = dot_high(q_ref[p], k_ref[p], NT) * scale
        weights = jnp.exp(scores - jnp.max(scores, axis=1, keepdims=True))
        kernel = weights / jnp.sum(weights, axis=1, keepdims=True)
        kernel_ref[p] = kernel
        kernels.append(kernel)
        largest = jnp.max(jnp.sum(kernel, axis=0, keepdims=True), axis=1, keepdims=True)
        inverses.append(kernel.T / largest)
    for sweep in range(NS_ITERS):
        products = [dot_high(kernels[p], inverses[p], NN) for p in range(count)]
        second = [
            15.0 * eye - dot_high(products[p], 7.0 * eye - products[p], NN) for p in range(count)
        ]
        third = [13.0 * eye - dot_high(products[p], second[p], NN) for p in range(count)]
        for p in range(count):
            at = (sweep * count + p) * 4
            saved_ref[at], saved_ref[at + 1] = inverses[p], products[p]
            saved_ref[at + 2], saved_ref[at + 3] = second[p], third[p]
        inverses = [0.25 * dot_high(inverses[p], third[p], NN) for p in range(count)]
    for p in range(count):
        inverse_ref[p] = inverses[p]


def pinv_back_kernel(scale, q_ref, k_ref, kernel_ref, saved_ref, grad_ref, avg_ref, gq_ref, gk_ref):
    count = q_ref.shape[0]
    each = range(count)
    eye = (iota((LAND, LAND), 0) == iota((LAND, LAND), 1)).astype(F32)
    grads = [dot_nt(grad_ref[p], avg_ref[p]) for p in each]
    kernels = [kernel_ref[p] for p in each]
    totals = [jnp.zeros((LAND, LAND), F32) for p in each]
    for sweep in reversed(range(NS_ITERS)):
        first = [(sweep * count + p) * 4 for p in each]
        inverses, products = [saved_ref[a] for a in first], [saved_ref[a + 1] for a in first]
        grad_third = [0.25 * dot_high(inverses[p], grads[p], TN) for p in each]
        nexts = [0.25 * dot_high(grads[p], saved_ref[first[p] + 3], NT) for p in each]
        grad_second = [-dot_high(products[p], grad_third[p], TN) for p in each]
        grad_product = [-dot_high(grad_third[p], saved_ref[first[p] + 2], NT) for p in each]
        grad_first = [-dot_high(products[p], grad_second[p], TN) for p in each]
        grad_product = [
            grad_product[p]
            - dot_high(grad_second[p], 7.0 * eye - products[p], NT)
            - grad_first[p]
            for p in each
        ]
        totals = [totals[p] + dot_high(grad_product[p], inverses[p], NT) for p in each]
        grads = [nexts[p] + dot_high(kernels[p], grad_product[p], TN) for p in each]
    for p in each:
        kernel = kernels[p]
        sums = jnp.sum(kernel, axis=0, keepdims=True)
        largest = jnp.max(sums, axis=1, keepdims=True)
        flipped = grads[p].T
        loss = jnp.sum(jnp.sum(flipped * kernel, axis=1, keepdims=True), axis=0, keepdims=True)
        at_top = (sums == largest).astype(F32)
        at_top = at_top / jnp.sum(at_top, axis=1, keepdims=True)
        grad = totals[p] + flipped / largest - at_top * (loss / (largest * largest))
        grad = kernel * (grad - jnp.sum(grad * kernel, axis=1, keepdims=True)) * scale
        gq_ref[p] = dot_high(grad, k_ref[p], NN)
        gk_ref[p] = dot_high(grad, q_ref[p], TN)


def settle_qkv_kernel(side_ref, late_ref, late_other_ref, early_ref, early_other_ref, out_ref):
    part = pl.program_id(0)
    own = jnp.where(part == 0, 0, 1) == side_ref[0]
    choices = [
        (late_ref, own & (part < 2)),
        (late_other_ref, jnp.logical_not(own) & (part < 2)),
        (early_ref, own & (part == 2)),
        (early_other_ref, jnp.logical_not(own) & (part == 2)),
    ]
    for ref, chosen in choices:

        @pl.when(chosen)
        def _():
            out_ref[...] = ref[...].astype(F32)


def settle_qkv(late, late_other, early, early_other, width):
    side = (lax.axis_index("seq") % 2).astype(jnp.int32).reshape(1)
    rows = width // 2

    def spec(used):
        return pl.BlockSpec((rows, width), lambda j, i, s: (jnp.where(used(j), i, 0), 0))

    return pl.pallas_call(
        settle_qkv_kernel,
        grid_spec=pltpu.PrefetchScalarGridSpec(
            num_scalar_prefetch=1,
            grid=(3, 2),
            in_specs=[spec(lambda j: j < 2), spec(lambda j: j < 2)] + [spec(lambda j: j == 2)] * 2,
            out_specs=pl.BlockSpec((rows, width), lambda j, i, s: (i, j)),
        ),
        out_shape=jax.ShapeDtypeStruct((width, 3 * width), F32),
        name="settle_qkv",
    )(side, late, late_other, early, early_other)


def per_device(
    inputs, doc_lengths, w_qkv, bias_q, bias_v, conv_taps, w_out, bias_out, norm1_gain,
    norm1_bias, w_up, bias_up, w_down, bias_down, norm2_gain, norm2_bias, cotangent,
):
    tokens = inputs[0]
    tok_count, width = tokens.shape
    heads, tap_count = conv_taps.shape
    size = width // heads
    radius = (tap_count - 1) // 2
    lengths = doc_lengths[0]
    docs = lengths.shape[0]
    mark_count = docs * LAND
    scale = 1.0 / math.sqrt(size)
    seq_count = lax.axis_size("seq")
    me = lax.axis_index("seq")
    row_first = me * tok_count
    ends = jnp.cumsum(lengths)
    starts = ends - lengths
    bounds = (jnp.concatenate([starts, ends]) - row_first).astype(jnp.int32)
    within = jnp.arange(LAND + 1, dtype=jnp.int32)
    edges = starts[:, None] + (within[None, :] * lengths[:, None] + LAND - 1) // LAND
    mark_low = edges[:, :-1].reshape(mark_count, 1)
    mark_high = edges[:, 1:].reshape(mark_count, 1)
    counts = (mark_high - mark_low).astype(F32)
    places = row_first + jnp.arange(tok_count, dtype=jnp.int32)[None, :]
    onehot = ((places >= mark_low) & (places < mark_high)).astype(BF)
    rows_in = (((0,), (0,)), ((), ()))
    cols_in = (((1,), (1,)), ((), ()))
    blocks = tok_count // BLOCK
    window_rows = tok_count + GROUP - SUB
    smem = pl.BlockSpec(memory_space=pltpu.SMEM)
    params = pltpu.CompilerParams(vmem_limit_bytes=40 * 1024 * 1024)
    tok_spec = pl.BlockSpec((BLOCK, width), lambda i: (i, 0))

    def part(col):
        return pl.BlockSpec((BLOCK, width), lambda i: (i, col))

    def fixed(*shape):
        return pl.BlockSpec(shape, lambda i: (0,) * len(shape))

    def shaped(shape, dtype):
        return jax.ShapeDtypeStruct(shape, dtype)

    means = jnp.dot(onehot, tokens, preferred_element_type=F32) / counts
    mean_in = seq_whole(seq_quarter(means.astype(BF), add_join))
    marks = jnp.dot(mean_in, w_qkv[:, : 2 * width], preferred_element_type=F32)
    mark_q = (marks[:, :width] + bias_q).astype(BF)
    mark_k = marks[:, width:].astype(BF)

    bias = jnp.concatenate([bias_q, jnp.zeros_like(bias_q), bias_v])
    qkv = (jnp.dot(tokens, w_qkv, preferred_element_type=F32) + bias).astype(BF)
    value_ext = extended(qkv[:, 2 * width :], radius, window_rows)
    value_ext, mark_q, mark_k = lax.optimization_barrier((value_ext, mark_q, mark_k))

    def one_col(col):
        return pl.BlockSpec((tok_count, width), lambda i: (0, col))

    stats = pl.pallas_call(
        lambda *refs: landmark_kernel(docs, scale, *refs),
        grid=(1,),
        in_specs=[smem, fixed(mark_count, width), one_col(1), one_col(2)],
        out_specs=fixed(mark_count, width + 128),
        out_shape=shaped((mark_count, width + 128), BF),
        scratch_shapes=[
            pltpu.VMEM((width, 128), F32), pltpu.VMEM((width, 128), F32),
            pltpu.VMEM((width, GROUP), F32),
        ],
        compiler_params=params,
        name="landmark",
    )(bounds, mark_q, qkv, qkv)
    far_count = seq_count // 4
    own_count = -(-heads // far_count)
    own_doc = (me % 2) * 2 + (me // 2) % 2
    own_at = (me // 4) * own_count * size
    spare = far_count * own_count * size - width

    def own_heads(array):
        array = jnp.pad(array, ((0, 0), (0, spare)))
        array = lax.dynamic_slice_in_dim(array, own_at, own_count * size, 1)
        return array.reshape(LAND, own_count, size).transpose(1, 0, 2)

    def of_doc(array):
        return lax.dynamic_slice_in_dim(array, own_doc * LAND, LAND, 0)

    mine, other = halves(stats, 1)
    stats = join(mine, swap(other, "seq", 1))
    stats, later_q, later_k = lax.optimization_barrier((stats, mark_q, mark_k))
    own_q = own_heads(of_doc(later_q)).astype(F32)
    own_k = own_heads(of_doc(later_k)).astype(F32)
    square = (own_count, LAND, LAND)
    own_inverse, kernel, saved = pl.pallas_call(
        lambda *refs: pinv_kernel(scale, *refs),
        out_shape=(
            shaped(square, F32), shaped(square, F32),
            shaped((4 * NS_ITERS * own_count, LAND, LAND), F32),
        ),
        name="pinv",
    )(own_q, own_k)
    inverse = own_inverse.transpose(1, 0, 2).reshape(LAND, own_count * size).astype(BF)
    mine, other = halves(stats, 2)
    stats = join(mine, swap(other, "seq", 2))
    for i in range(2, seq_count.bit_length() - 1):
        other = swap(jnp.concatenate([stats, inverse], 1), "seq", 1 << i)
        stats = join(stats, other[:, : width + 128])
        other = other[:, width + 128 :]
        inverse = jnp.where(
            (me >> i) % 2 == 0,
            jnp.concatenate([inverse, other], 1),
            jnp.concatenate([other, inverse], 1),
        )
    inverse = inverse[:, :width]
    mix = pl.pallas_call(
        mix_kernel, out_shape=shaped((LAND, width + 128), BF), name="mix"
    )(inverse, stats)
    mix = seq_whole(mix)

    taps = jnp.pad(conv_taps, ((0, 0), (0, GROUP - tap_count)))
    mark_spec = fixed(mark_count, width)
    mixed, probs = pl.pallas_call(
        lambda *refs: token_kernel(docs, scale, *refs),
        grid=(blocks,),
        in_specs=[
            smem, part(0), fixed(window_rows, width), mark_spec, mark_spec, fixed(heads, GROUP)
        ],
        out_specs=(tok_spec, pl.BlockSpec((width, BLOCK), lambda i: (0, i))),
        out_shape=(shaped((tok_count, width), BF), shaped((width, tok_count), BF)),
        scratch_shapes=[pltpu.VMEM((heads * SUB, GROUP), BF), pltpu.VMEM((BLOCK, width), F32)],
        compiler_params=params,
        name="token",
    )(bounds, qkv, value_ext, mark_k, mix, taps)

    hidden = w_up.shape[1]
    vectors = jnp.stack([bias_out, norm1_gain, norm1_bias, bias_down, norm2_gain, norm2_bias])
    vectors = jnp.pad(vectors, ((0, 2), (0, 0)))
    wide_spec = pl.BlockSpec((FFN_BLOCK, hidden), lambda i: (i, 0))
    ffn_spec = pl.BlockSpec((FFN_BLOCK, width), lambda i: (i, 0))
    narrow = shaped((tok_count, width), BF)
    (
        result, grad_one, active, grad_upper, hidden_low, grad_low_two, grad_low_one,
        grad_mixed, sums, sum_up,
    ) = pl.pallas_call(
        ffn_kernel,
        grid=(tok_count // FFN_BLOCK,),
        in_specs=[
            ffn_spec, ffn_spec, ffn_spec, fixed(width, width), fixed(width, hidden),
            fixed(hidden, width), fixed(8, width), fixed(8, hidden),
        ],
        out_specs=(
            ffn_spec, ffn_spec, wide_spec, wide_spec, ffn_spec, ffn_spec, ffn_spec, ffn_spec,
            fixed(8, width), fixed(8, hidden),
        ),
        out_shape=(
            shaped((tok_count, width), F32), shaped((tok_count, width), F32),
            shaped((tok_count, hidden), BF), shaped((tok_count, hidden), BF),
            narrow, narrow, narrow, narrow, shaped((8, width), F32), shaped((8, hidden), F32),
        ),
        scratch_shapes=[pltpu.VMEM((FFN_BLOCK, hidden), BF)],
        compiler_params=pltpu.CompilerParams(vmem_limit_bytes=58 * 1024 * 1024),
        name="ffn",
    )(
        tokens, mixed, cotangent[0], w_out, w_up, w_down, vectors,
        jnp.broadcast_to(bias_up[None, :], (8, hidden)),
    )

    grad_queries, grad_mix, grad_mk = pl.pallas_call(
        lambda *refs: token_back_kernel(docs, scale, *refs),
        grid=(blocks,),
        in_specs=[
            smem, part(0), tok_spec, pl.BlockSpec((width, BLOCK), lambda i: (0, i)), mark_spec,
            mark_spec,
        ],
        out_specs=(tok_spec, mark_spec, mark_spec),
        out_shape=(
            shaped((tok_count, width), BF), shaped((mark_count, width), F32),
            shaped((mark_count, width), F32),
        ),
        scratch_shapes=[pltpu.VMEM((BLOCK, width), F32)],
        compiler_params=params,
        name="token_back",
    )(bounds, qkv, grad_mixed, probs, mark_k, mix)
    grad_w_down = lax.dot_general(active, grad_low_two, rows_in, preferred_element_type=F32)
    grad_w_up = lax.dot_general(hidden_low, grad_upper, rows_in, preferred_element_type=F32)
    grad_mix, grad_w_down, grad_w_up = lax.optimization_barrier(
        (grad_mix.astype(BF), grad_w_down.astype(BF), grad_w_up.astype(BF))
    )
    sum_w_down, sum_w_up = lax.psum((grad_w_down, grad_w_up), ("row", "seq"))

    def remaining(grad_mix, grad_mk, stats, mix):
        grad_mix = seq_quarter(grad_mix.astype(BF), add_join)
        grad_w_out = lax.dot_general(mixed, grad_low_one, rows_in, preferred_element_type=F32)

        grad_ext = extended(grad_mixed, radius, window_rows)
        grad_conv, products = pl.pallas_call(
            lambda *refs: conv_back_kernel(docs, *refs),
            grid=(blocks,),
            in_specs=[
                smem, fixed(window_rows, width), fixed(window_rows, width), fixed(heads, GROUP)
            ],
            out_specs=(tok_spec, fixed(16, GROUP)),
            out_shape=(shaped((tok_count, width), F32), shaped((16, GROUP), F32)),
            scratch_shapes=[
                pltpu.VMEM((heads * SUB, GROUP), BF), pltpu.VMEM((heads * SUB, GROUP), F32)
            ],
            compiler_params=params,
            name="conv_back",
        )(bounds, grad_ext, value_ext, jnp.pad(conv_taps[:, ::-1], ((0, 0), (0, GROUP - tap_count))))
        grad_conv_taps = products[:heads, SUB - 1 : SUB - 1 + tap_count]
        grad_mix, grad_conv, grad_conv_taps = lax.optimization_barrier(
            (grad_mix, grad_conv, grad_conv_taps)
        )

        grad_avg = pl.pallas_call(
            mix_back_kernel, out_shape=shaped((LAND, width + 128), BF), name="mix_back"
        )(inverse, stats, grad_mix)
        grad_avg = seq_whole(grad_avg)
        lane_spec = pl.BlockSpec((mark_count, 128), lambda i: (0, width // 128))
        grad_keys, grad_values, grad_mq = pl.pallas_call(
            lambda *refs: landmark_back_kernel(docs, scale, *refs),
            grid=(blocks,),
            in_specs=[
                smem, part(1), part(2), tok_spec, mark_spec, mark_spec, lane_spec, lane_spec
            ],
            out_specs=(tok_spec, tok_spec, mark_spec),
            out_shape=(
                shaped((tok_count, width), BF), shaped((tok_count, width), BF),
                shaped((mark_count, width), F32),
            ),
            scratch_shapes=[pltpu.VMEM((BLOCK, width), F32), pltpu.VMEM((BLOCK, width), F32)],
            compiler_params=params,
            name="landmark_back",
        )(bounds, qkv, qkv, grad_conv, mark_q, grad_avg, mix, grad_avg)


        def weight_grad(grads):
            return lax.dot_general(tokens, grads, rows_in, preferred_element_type=F32)

        early = jnp.pad(grad_w_out.astype(BF), ((0, width), (0, 0)))
        early = lax.dynamic_update_slice_in_dim(
            early, weight_grad(grad_values).astype(BF), width, 0
        )
        grad_mix, early = lax.optimization_barrier((grad_mix, early))
        early = advance(begin(early, ORDER, ORDER), 1)
        grad_mq_small, grad_mk_small = pl.pallas_call(
            lambda *refs: pinv_back_kernel(scale, *refs),
            out_shape=(shaped(square, F32), shaped(square, F32)),
            name="pinv_back",
        )(own_q, own_k, kernel, saved, own_heads(grad_mix), own_heads(stats[:, :width]))

        grad_mq_small, (early,) = tied(grad_mq_small, [early])
        early = advance(early, 1)

        def with_small(array, small):
            small = small.transpose(1, 0, 2).reshape(LAND, own_count * size)
            small = lax.dynamic_update_slice_in_dim(
                jnp.zeros((LAND, width + spare), F32), small, own_at, 1
            )[:, :width]
            first = own_doc * LAND
            rows = lax.dynamic_slice_in_dim(array, first, LAND, 0) + small
            return lax.dynamic_update_slice_in_dim(array, rows, first, 0)

        grad_mq = with_small(grad_mq, grad_mq_small)
        grad_mk = with_small(grad_mk, grad_mk_small)
        grad_marks = jnp.concatenate([grad_mq, grad_mk], axis=1).astype(BF)
        mark_back = lax.dot_general(
            grad_marks, w_qkv[:, : 2 * width], cols_in, preferred_element_type=F32
        ) / counts
        mark_back = mark_back.astype(BF)

        grad_bias_q = jnp.sum(grad_queries.astype(F32), axis=0) + jnp.sum(grad_mq, axis=0)
        grad_bias_v = jnp.sum(grad_values.astype(F32), axis=0)
        mark_grad_q = lax.dot_general(
            mean_in, grad_marks[:, :width], rows_in, preferred_element_type=F32
        )
        mark_grad_k = lax.dot_general(
            mean_in, grad_marks[:, width:], rows_in, preferred_element_type=F32
        )
        others = jnp.concatenate(
            [
                sum_up[0].reshape(hidden // width, width),
                grad_bias_q[None],
                grad_bias_v[None],
                jnp.pad(grad_conv_taps.reshape(1, -1), ((0, 0), (0, width - heads * tap_count))),
                jnp.zeros((4 - hidden // width + 1, width), F32),
            ],
            0,
        )
        spare_rows = width // 6
        small = jnp.concatenate([sums, others], 0).astype(BF)
        below = width + 2 * spare_rows - small.shape[0]
        late = jnp.pad(small, ((width, below), (0, 0)))
        late = lax.dynamic_update_slice_in_dim(
            late, (weight_grad(grad_queries) + mark_grad_q).astype(BF), 0, 0
        )
        late = lax.dynamic_update_slice_in_dim(
            late, (weight_grad(grad_keys) + mark_grad_k).astype(BF), width + spare_rows, 0
        )
        late, (early,) = tied(late, [early])
        late = begin(late, ORDER, ORDER)
        for step in seq_steps():
            mark_back = step(mark_back)
            early, late = advance(early, 1), advance(late, 1)
            mark_back, (early, late) = tied(mark_back, [early, late])
        return early[0], late[0], mark_back, grad_keys, grad_values

    plan = stages(ORDER)
    sent = len(seq_steps())

    def rows_left(rows, done):
        return rows >> min(done, 2 * len(plan) - done)

    early_rows = rows_left(2 * width, sent + 2)
    late_rows = rows_left(2 * width + width // 3, sent)

    def nothing(*unused):
        return tuple(
            jnp.zeros((rows, width), BF)
            for rows in (early_rows, late_rows, mark_count, tok_count, tok_count)
        )

    early, late, mark_back, grad_keys, grad_values = lax.cond(
        lengths[0] > 0, remaining, nothing, grad_mix, grad_mk, stats, mix
    )
    early, late = (early, plan, plan, sent + 2), (late, plan, plan, sent)
    last = 2 * len(plan) - 1
    late = advance(late, 2)
    (sum_w_down, sum_w_up), (late,) = tied(
        (sum_w_down.astype(F32), sum_w_up.astype(F32)), [late]
    )
    early, late = advance(early, last - early[3]), advance(late, last - late[3])
    grad_projected = jnp.concatenate([grad_queries, grad_keys, grad_values], axis=1)
    grad_input = (
        grad_one
        + lax.dot_general(grad_projected, w_qkv, cols_in, preferred_element_type=F32)
        + lax.dot_general(onehot, mark_back, rows_in, preferred_element_type=F32)
    )
    grad_input, (early, late) = tied(grad_input, [early, late])
    early, early_other = last_swap(early)[:2]
    late, late_other = last_swap(late)[:2]
    sum_w_qkv = settle_qkv(late, late_other, early, early_other, width)
    first_core = me % 2 == 0
    sum_w_out = jnp.where(first_core, early, early_other).astype(F32)
    flat = jnp.where(first_core, late[width:], late_other[width:])[:16].astype(F32)
    at = sums.shape[0] + hidden // width
    pieces = [
        flat[at], flat[at + 1], flat[at + 2, : heads * tap_count], flat[5], flat[3], flat[4],
        flat[sums.shape[0] : at].reshape(hidden), flat[2], flat[0], flat[1],
    ]
    return (
        result[None], grad_input[None], sum_w_qkv, pieces[0], pieces[1],
        pieces[2].reshape(heads, tap_count), sum_w_out, pieces[3], pieces[4], pieces[5],
        sum_w_up, pieces[6], sum_w_down, pieces[7], pieces[8], pieces[9],
    )


def solution(mesh):
    whole, tokens = P(), P("row", "seq", None)
    return jax.shard_map(
        per_device,
        mesh=mesh,
        in_specs=(tokens, P("row", None)) + (whole,) * 14 + (tokens,),
        out_specs=(tokens, tokens) + (whole,) * 14,
        check_vma=False,
    )
```

```python
import math

import jax
import jax.numpy as jnp
from jax import lax
from jax.experimental import pallas as pl
from jax.experimental.pallas import tpu as pltpu
from jax.sharding import PartitionSpec as P

LAND = 64
NS_ITERS = 6
HIGH = lax.Precision.HIGHEST
NEGATIVE = -1e30
BF = jnp.bfloat16
F32 = jnp.float32

BLOCK = 256
GROUP = 256
SUB = 128
TAPS = 33
FFN_BLOCK = 256
ORDER = ("row", "near", "far")


def swap(array, axis, bit):
    count = lax.axis_size(axis)
    return lax.ppermute(array, axis, [(i, i ^ bit) for i in range(count)])


def add_parts(parts):
    total = parts[0].astype(F32)
    for part in parts[1:]:
        total = total + part.astype(F32)
    return total


def halves(array, bit):
    rows = array.shape[0] // 2
    side = (lax.axis_index("seq") // bit) % 2
    mine = lax.dynamic_slice_in_dim(array, side * rows, rows, 0)
    other = lax.dynamic_slice_in_dim(array, (1 - side) * rows, rows, 0)
    return mine, other


def seq_quarter(array, join):
    bits = [1 << i for i in range(lax.axis_size("seq").bit_length() - 1)]
    for bit in bits[:2]:
        mine, other = halves(array, bit)
        array = join(mine, swap(other, "seq", bit))
    for bit in bits[2:]:
        array = join(array, swap(array, "seq", bit))
    return array


def paired(array, axis, bit, dim):
    other = swap(array, axis, bit)
    side = (lax.axis_index(axis) // bit) % 2
    return jnp.where(
        side == 0,
        jnp.concatenate([array, other], dim),
        jnp.concatenate([other, array], dim),
    )


def seq_whole(array):
    return paired(paired(array, "seq", 2, 0), "seq", 1, 0)


def seq_steps():
    bits = [1 << i for i in range(lax.axis_size("seq").bit_length() - 1)]

    def halve(bit):
        def step(array):
            mine, other = halves(array, bit)
            return add_join(mine, swap(other, "seq", bit))

        return step

    def whole(bit):
        return lambda array: add_join(array, swap(array, "seq", bit))

    def double(bit):
        return lambda array: paired(array, "seq", bit, 0)

    return (
        [halve(bit) for bit in bits[:2]]
        + [whole(bit) for bit in bits[2:]]
        + [double(bit) for bit in reversed(bits[:2])]
    )


def add_join(first, second):
    return (first.astype(F32) + second.astype(F32)).astype(BF)


def stages(order):
    row = [("row", 1 << i) for i in range(lax.axis_size("row").bit_length() - 1)]
    seq = [[("seq", 1 << i)] for i in range(lax.axis_size("seq").bit_length() - 1)]
    named = {"core": seq[0], "row": row, "near": seq[1], "far": seq[2], "rest": sum(seq[3:], [])}
    return sum([named[name] for name in ("core",) + order + ("rest",)], [])


def begin(array, down, back):
    return array, stages(down), stages(back), 0


def advance(state, steps):
    held, down, back, done = state
    for step in range(done, min(done + steps, 2 * len(down))):
        if step < len(down):
            axis, bit = down[step]
            half = held.shape[0] // 2
            side = (lax.axis_index(axis) // bit) % 2
            mine = lax.dynamic_slice_in_dim(held, side * half, half, 0)
            other = lax.dynamic_slice_in_dim(held, (1 - side) * half, half, 0)
            held = mine.astype(F32) + swap(other, axis, bit).astype(F32)
            held = held.astype(BF)
        else:
            axis, bit = back[2 * len(down) - 1 - step]
            held = paired(held, axis, bit, 0)
    return held, down, back, min(done + steps, 2 * len(down))


def last_swap(state):
    down, back = state[1], state[2]
    held = advance(state, 2 * len(down) - 1 - state[3])[0]
    return held, swap(held, *down[0]), down, back


def tied(values, states):
    values, helds = lax.optimization_barrier((values, [state[0] for state in states]))
    return values, [(held,) + state[1:] for held, state in zip(helds, states)]


def extended(cells, width, rows):
    count = lax.axis_size("seq")
    head = cells[:width]
    tail = cells[-width:]
    return jnp.concatenate(
        [
            lax.ppermute(tail, "seq", [(i, i + 1) for i in range(count - 1)]),
            cells,
            lax.ppermute(head, "seq", [(i + 1, i) for i in range(count - 1)]),
            jnp.zeros((rows - cells.shape[0] - 2 * width, cells.shape[1]), cells.dtype),
        ],
        axis=0,
    )


def dot_nn(a, b):
    return jnp.dot(a, b, preferred_element_type=F32)


def dot_nt(a, b):
    return lax.dot_general(a, b, (((1,), (1,)), ((), ())), preferred_element_type=F32)


def dot_tn(a, b):
    return lax.dot_general(a, b, (((0,), (0,)), ((), ())), preferred_element_type=F32)


def iota(shape, dim):
    return lax.broadcasted_iota(jnp.int32, shape, dim)


def spread(block):
    rows = block.shape[0]
    tall = jnp.concatenate([block] * 4, axis=0).astype(F32)
    shape = (4 * rows, GROUP)
    keep = iota(shape, 0) // rows == iota(shape, 1) // LAND
    return jnp.where(keep, tall, 0.0).astype(BF)


def gathered(square):
    rows = square.shape[0] // 4
    lane = iota((rows, GROUP), 1) // LAND
    out = square[:rows]
    for head in range(1, 4):
        out = jnp.where(lane == head, square[head * rows : (head + 1) * rows], out)
    return out


def by_head(columns, first, shape):
    lane = iota(shape, 1)
    out = jnp.zeros(shape, F32)
    for head, column in enumerate(columns):
        out = jnp.where((lane % 16 == first + head) & (lane < 48), column, out)
    return out


def split_three(cells):
    lane = iota(cells.shape, 1)
    high = cells.astype(BF).astype(F32)
    mid = (cells - high).astype(BF).astype(F32)
    low = cells - high - mid
    return jnp.where(lane < 16, high, jnp.where(lane < 32, mid, low)).astype(BF)


def merge_three(cells):
    cells = cells.astype(F32)
    return cells + pltpu.roll(cells, 112, 1) + pltpu.roll(cells, 96, 1)


def head_lanes(heads, width):
    return (iota((128, width), 0) == iota((128, width), 1) // LAND).astype(F32)


def doc_of(places, bounds, docs):
    out = (places >= bounds[2 * docs - 1]).astype(jnp.int32)
    for doc in range(docs):
        out = out + (places >= bounds[doc]).astype(jnp.int32)
    return out


def landmark_kernel(docs, scale, bounds, mq_ref, k_ref, v_ref, out_ref, max_s, sum_s, acc_s):
    tokens, width = k_ref.shape
    groups = width // GROUP
    heads = width // LAND
    out_ref[:, :width] = jnp.zeros((docs * LAND, width), BF)
    empty = jnp.full((docs * LAND, 128), NEGATIVE, F32)
    out_ref[:, width:] = jnp.where(iota(empty.shape, 1) < 48, split_three(empty).astype(F32), 0.0).astype(BF)
    for doc in range(docs):
        low = jnp.clip(bounds[doc], 0, tokens)
        high = jnp.clip(bounds[docs + doc], 0, tokens)
        rows = slice(doc * LAND, (doc + 1) * LAND)

        @pl.when(high > low)
        def _():
            max_s[...] = jnp.full(max_s.shape, NEGATIVE, F32)
            sum_s[...] = jnp.zeros(sum_s.shape, F32)
            acc_s[...] = jnp.zeros(acc_s.shape, F32)
            wide = [
                spread(mq_ref[rows, g * GROUP : (g + 1) * GROUP]) for g in range(groups)
            ]

            ones = jnp.ones((BLOCK, 128), BF)

            def step(block, carry):
                first = pl.multiple_of(block * BLOCK, BLOCK)
                at = pl.ds(first, BLOCK)
                place = iota((1, BLOCK), 1) + first
                valid = (place >= low) & (place < high)
                for g in range(groups):
                    cols = slice(g * GROUP, (g + 1) * GROUP)
                    scores = dot_nt(wide[g], k_ref[at, cols]) * scale
                    scores = jnp.where(valid, scores, NEGATIVE)
                    old = max_s[cols, :]
                    top = jnp.maximum(old, jnp.max(scores, axis=1, keepdims=True))
                    weights = jnp.exp(scores - twice(top)).astype(BF)
                    shrink = jnp.exp(old - top)
                    max_s[cols, :] = top
                    sum_s[cols, :] = sum_s[cols, :] * shrink + dot_nn(weights, ones)
                    acc_s[cols, :] = acc_s[cols, :] * twice(shrink) + dot_nn(weights, v_ref[at, cols])
                return carry

            lax.fori_loop(low // BLOCK, (high + BLOCK - 1) // BLOCK, step, 0)
            columns = []
            for g in range(groups):
                cols = slice(g * GROUP, (g + 1) * GROUP)
                sums = sum_s[cols, :]
                out_ref[rows, cols] = gathered(acc_s[cols, :] / twice(sums)).astype(BF)
                level = max_s[cols, :] + jnp.log(sums)
                columns += [level[h * LAND : (h + 1) * LAND] for h in range(4)]
            out_ref[rows, width:] = split_three(by_head(columns, 0, (LAND, 128)))


def twice(cells):
    return jnp.concatenate([cells, cells], axis=1)


def join_kernel(a_ref, b_ref, out_ref):
    width = a_ref.shape[1] - 128
    heads = width // LAND
    first, second = merge_three(a_ref[:, width:]), merge_three(b_ref[:, width:])
    lane = iota(first.shape, 1)
    first = jnp.where(lane < heads, first, 0.0)
    second = jnp.where(lane < heads, second, 0.0)
    top = jnp.maximum(first, second)
    exp_a, exp_b = jnp.exp(first - top), jnp.exp(second - top)
    both = exp_a + exp_b
    level = top + jnp.log(both)
    pick = head_lanes(heads, width).astype(BF)
    share = exp_b / both
    high = share.astype(BF)
    low = (share - high.astype(F32)).astype(BF)
    share = dot_nn(jnp.concatenate([high, low], 1), jnp.concatenate([pick, pick], 0))
    from_a, from_b = a_ref[:, :width].astype(F32), b_ref[:, :width].astype(F32)
    out_ref[:, :width] = (from_a + share * (from_b - from_a)).astype(BF)
    level = jnp.where(lane < heads, level, 0.0)
    level = level + pltpu.roll(level, 16, 1) + pltpu.roll(level, 32, 1)
    out_ref[:, width:] = split_three(level)


def join(first, second):
    return pl.pallas_call(
        join_kernel, out_shape=jax.ShapeDtypeStruct(first.shape, BF), name="join"
    )(first, second)


def mix_kernel(inv_ref, stat_ref, mix_ref):
    width = stat_ref.shape[1] - 128
    for g in range(width // GROUP):
        cols = slice(g * GROUP, (g + 1) * GROUP)
        mix_ref[:, cols] = dot_nn(inv_ref[:, cols], spread(stat_ref[:, cols])).astype(BF)
    mix_ref[:, width:] = stat_ref[:, width:]


def mix_back_kernel(inv_ref, stat_ref, grad_ref, out_ref):
    width = stat_ref.shape[1] - 128
    columns = []
    for g in range(width // GROUP):
        cols = slice(g * GROUP, (g + 1) * GROUP)
        grad = gathered(dot_tn(inv_ref[:, cols], grad_ref[:, cols]))
        out_ref[:, cols] = grad.astype(BF)
        product = grad * stat_ref[:, cols].astype(F32)
        lane = iota(product.shape, 1) // LAND
        for h in range(4):
            columns.append(jnp.sum(jnp.where(lane == h, product, 0.0), axis=1, keepdims=True))
    out_ref[:, width:] = split_three(by_head(columns, 0, (LAND, 128)))


def make_band(taps_ref, band_s):
    for head in range(taps_ref.shape[0]):
        row = jnp.broadcast_to(taps_ref[head : head + 1, :], (SUB, GROUP))
        band_s[head * SUB : (head + 1) * SUB, :] = pltpu.roll(row, 0, 1, stride=1, stride_axis=0).astype(BF)


def same_doc(first, bounds, docs, radius):
    rows = iota((SUB, GROUP), 0) + first
    cols = iota((SUB, GROUP), 1) + (first - radius)
    return doc_of(rows, bounds, docs) == doc_of(cols, bounds, docs)


def token_kernel(
    docs, scale, bounds, q_ref, v_ref, mk_ref, mix_ref, taps_ref, mixed_ref, probs_ref, band_s, sum_s
):
    width = q_ref.shape[1]
    groups = width // GROUP
    radius = (TAPS - 1) // 2
    first = pl.program_id(0) * BLOCK

    @pl.when(pl.program_id(0) == 0)
    def _():
        make_band(taps_ref, band_s)

    for sub in range(BLOCK // SUB):
        start = pl.multiple_of(first + sub * SUB, SUB)
        same = same_doc(start, bounds, docs, radius)
        same = jnp.where(jnp.concatenate([same] * 4, axis=0), 1.0, 0.0).astype(BF)
        for g in range(groups):
            cols = slice(g * GROUP, (g + 1) * GROUP)
            band = band_s[g * 4 * SUB : (g + 1) * 4 * SUB, :] * same
            res = dot_nn(band, v_ref[pl.ds(start, GROUP), cols])
            sum_s[sub * SUB : (sub + 1) * SUB, cols] = gathered(res)
    probs_ref[...] = jnp.zeros(probs_ref.shape, BF)
    for doc in range(docs):
        low, high = bounds[doc], bounds[docs + doc]
        rows = slice(doc * LAND, (doc + 1) * LAND)

        @pl.when((high > first) & (low < first + BLOCK))
        def _():
            place = iota((1, BLOCK), 1) + first
            valid = (place >= low) & (place < high)
            for g in range(groups):
                cols = slice(g * GROUP, (g + 1) * GROUP)
                scores = dot_nt(spread(mk_ref[rows, cols]), q_ref[:, cols]) * scale
                scores = scores.reshape(4, LAND, BLOCK)
                weights = jnp.exp(scores - jnp.max(scores, axis=1, keepdims=True))
                probs = weights / jnp.sum(weights, axis=1, keepdims=True)
                probs = jnp.where(valid, probs.reshape(GROUP, BLOCK), 0.0).astype(BF)
                probs_ref[cols, :] = probs_ref[cols, :] + probs
                sum_s[:, cols] = sum_s[:, cols] + dot_tn(probs, spread(mix_ref[rows, cols]))

    mixed_ref[...] = sum_s[...].astype(BF)


def token_back_kernel(
    docs, scale, bounds, q_ref, gm_ref, probs_ref, mk_ref, mix_ref, gq_ref, gmix_ref, gmk_ref, gq_s
):
    width = q_ref.shape[1]
    groups = width // GROUP
    first = pl.program_id(0) * BLOCK

    @pl.when(pl.program_id(0) == 0)
    def _():
        gmix_ref[...] = jnp.zeros(gmix_ref.shape, F32)
        gmk_ref[...] = jnp.zeros(gmk_ref.shape, F32)

    gq_s[...] = jnp.zeros(gq_s.shape, F32)
    for doc in range(docs):
        low, high = bounds[doc], bounds[docs + doc]
        rows = slice(doc * LAND, (doc + 1) * LAND)

        @pl.when((high > first) & (low < first + BLOCK))
        def _():
            place = iota((1, BLOCK), 1) + first
            valid = (place >= low) & (place < high)
            for g in range(groups):
                cols = slice(g * GROUP, (g + 1) * GROUP)
                probs = jnp.where(valid, probs_ref[cols, :].astype(F32), 0.0)
                gmix_ref[rows, cols] += gathered(dot_nn(probs.astype(BF), gm_ref[:, cols]))
                grad = dot_nt(spread(mix_ref[rows, cols]), gm_ref[:, cols])
                heavy = (probs * grad).reshape(4, LAND, BLOCK)
                shared = probs.reshape(4, LAND, BLOCK) * jnp.sum(heavy, axis=1, keepdims=True)
                grad = ((heavy - shared).reshape(GROUP, BLOCK) * scale).astype(BF)
                gmk_ref[rows, cols] += gathered(dot_nn(grad, q_ref[:, cols]))
                gq_s[:, cols] += dot_tn(grad, spread(mk_ref[rows, cols]))

    gq_ref[...] = gq_s[...].astype(BF)


def conv_back_kernel(docs, bounds, gm_ref, v_ref, taps_ref, out_ref, sum_ref, band_s, prod_s):
    width = gm_ref.shape[1]
    groups = width // GROUP
    radius = (TAPS - 1) // 2
    first = pl.program_id(0) * BLOCK

    @pl.when(pl.program_id(0) == 0)
    def _():
        make_band(taps_ref, band_s)
        prod_s[...] = jnp.zeros(prod_s.shape, F32)

    for sub in range(BLOCK // SUB):
        start = pl.multiple_of(first + sub * SUB, SUB)
        same = same_doc(start, bounds, docs, radius)
        same = jnp.where(jnp.concatenate([same] * 4, axis=0), 1.0, 0.0)
        for g in range(groups):
            cols = slice(g * GROUP, (g + 1) * GROUP)
            tall = slice(g * 4 * SUB, (g + 1) * 4 * SUB)
            band = band_s[tall, :] * same.astype(BF)
            res = dot_nn(band, gm_ref[pl.ds(start, GROUP), cols])
            out_ref[sub * SUB : (sub + 1) * SUB, cols] = gathered(res)
            own = gm_ref[pl.ds(pl.multiple_of(start + radius, 16), SUB), cols]
            product = dot_nt(spread(own), v_ref[pl.ds(start, GROUP), cols])
            prod_s[tall, :] += product * same

    @pl.when(pl.program_id(0) == pl.num_programs(0) - 1)
    def _():
        flip = (iota((SUB, SUB), 0) + iota((SUB, SUB), 1) == SUB - 1).astype(F32).astype(BF)
        sum_ref[...] = jnp.zeros(sum_ref.shape, F32)
        for head in range(taps_ref.shape[0]):
            product = prod_s[head * SUB : (head + 1) * SUB, :]
            high = product.astype(BF)
            low = (product - high.astype(F32)).astype(BF)
            turned = pltpu.roll(dot_nn(flip, high) + dot_nn(flip, low), 0, 1, stride=1, stride_axis=0)
            sum_ref[head : head + 1, :] = jnp.sum(turned, axis=0, keepdims=True)


def ffn_kernel(
    x_ref, mixed_ref, cot_ref, w_out_ref, w_up_ref, w_down_ref, rows_ref, bias_up_ref,
    result_ref, grad_one_ref, active_ref, grad_up_ref, low_ref, low_two_ref, low_one_ref,
    grad_mixed_ref, sums_ref, sum_up_ref, slope_s,
):
    width = x_ref.shape[1]
    hidden = w_up_ref.shape[1]
    chunks = [slice(at, at + width) for at in range(0, hidden, width)]

    def row(i):
        return rows_ref[i : i + 1, :]

    @pl.when(pl.program_id(0) == 0)
    def _():
        sums_ref[...] = jnp.zeros(sums_ref.shape, F32)
        sum_up_ref[...] = jnp.zeros(sum_up_ref.shape, F32)

    def add_sum(i, cells):
        sums_ref[i : i + 1, :] += jnp.sum(cells, axis=0, keepdims=True)

    attended = dot_nn(mixed_ref[...], w_out_ref[...]) + row(0)
    norm_one, inverse_one = normalize(x_ref[...].astype(F32) + attended)
    hidden_one = norm_one * row(1) + row(2)
    hidden_low = hidden_one.astype(BF)
    low_ref[...] = hidden_low
    lowered = hidden_one + row(3)
    for cols in chunks:
        upper = dot_nn(hidden_low, w_up_ref[:, cols]) + bias_up_ref[:1, cols]
        active, slope = gelu_both(upper)
        active = active.astype(BF)
        active_ref[:, cols] = active
        slope_s[:, cols] = slope.astype(BF)
        lowered = lowered + dot_nn(active, w_down_ref[cols, :])
    norm_two, inverse_two = normalize(lowered)
    result_ref[...] = norm_two * row(4) + row(5)
    upstream = cot_ref[...].astype(F32)
    add_sum(0, upstream * norm_two)
    add_sum(1, upstream)
    grad_two = norm_back(upstream * row(4), norm_two, inverse_two)
    low_two = grad_two.astype(BF)
    low_two_ref[...] = low_two
    add_sum(2, low_two.astype(F32))
    grad_hidden = grad_two
    for cols in chunks:
        grad_up = dot_nt(low_two, w_down_ref[cols, :]) * slope_s[:, cols].astype(F32)
        grad_up = grad_up.astype(BF)
        grad_up_ref[:, cols] = grad_up
        sum_up_ref[:1, cols] += jnp.sum(grad_up.astype(F32), axis=0, keepdims=True)
        grad_hidden = grad_hidden + dot_nt(grad_up, w_up_ref[:, cols])
    add_sum(3, grad_hidden * norm_one)
    add_sum(4, grad_hidden)
    grad_one = norm_back(grad_hidden * row(1), norm_one, inverse_one)
    grad_one_ref[...] = grad_one
    low_one = grad_one.astype(BF)
    low_one_ref[...] = low_one
    add_sum(5, low_one.astype(F32))
    grad_mixed_ref[...] = dot_nt(low_one, w_out_ref[...]).astype(BF)


def landmark_back_kernel(
    docs, scale, bounds, k_ref, v_ref, conv_ref, mq_ref, grad_ref, level_ref, dots_ref,
    gk_ref, gv_ref, gmq_ref, gk_s, gv_s,
):
    width = k_ref.shape[1]
    groups = width // GROUP
    first = pl.program_id(0) * BLOCK

    @pl.when(pl.program_id(0) == 0)
    def _():
        gmq_ref[...] = jnp.zeros(gmq_ref.shape, F32)

    gk_s[...] = jnp.zeros(gk_s.shape, F32)
    gv_s[...] = conv_ref[...]
    for doc in range(docs):
        low, high = bounds[doc], bounds[docs + doc]
        rows = slice(doc * LAND, (doc + 1) * LAND)

        @pl.when((high > first) & (low < first + BLOCK))
        def _():
            place = iota((1, BLOCK), 1) + first
            valid = (place >= low) & (place < high)

            level, dots = merge_three(level_ref[rows, :]), merge_three(dots_ref[rows, :])

            def column(lanes, g):
                return jnp.concatenate(
                    [lanes[:, 4 * g + h : 4 * g + h + 1] for h in range(4)], axis=0
                )

            for g in range(groups):
                cols = slice(g * GROUP, (g + 1) * GROUP)
                wide_q, wide_g = spread(mq_ref[rows, cols]), spread(grad_ref[rows, cols])
                scores = dot_nt(wide_q, k_ref[:, cols]) * scale - column(level, g)
                probs = jnp.exp(jnp.where(valid, scores, NEGATIVE))
                grad = dot_nt(wide_g, v_ref[:, cols]) - column(dots, g)
                grad = (probs * grad * scale).astype(BF)
                gv_s[:, cols] += dot_tn(probs.astype(BF), wide_g)
                gk_s[:, cols] += dot_tn(grad, wide_q)
                gmq_ref[rows, cols] += gathered(dot_nn(grad, k_ref[:, cols]))

    gk_ref[...] = gk_s[...].astype(BF)
    gv_ref[...] = gv_s[...].astype(BF)


def gelu_both(upper):
    tangent = jnp.tanh(0.7978845608028654 * (upper + 0.044715 * upper * upper * upper))
    inner_slope = 0.7978845608028654 * (1.0 + 3.0 * 0.044715 * upper * upper)
    active = 0.5 * upper * (1.0 + tangent)
    slope = 0.5 * (1.0 + tangent) + 0.5 * upper * (1.0 - tangent * tangent) * inner_slope
    return active, slope


def normalize(residual):
    row_mean = jnp.mean(residual, axis=-1, keepdims=True)
    centered = residual - row_mean
    row_var = jnp.mean(centered * centered, axis=-1, keepdims=True)
    inverse_dev = lax.rsqrt(row_var + 1e-05)
    return (centered * inverse_dev, inverse_dev)


def norm_back(grad_normed, normed, inverse_dev):
    return inverse_dev * (
        grad_normed
        - jnp.mean(grad_normed, axis=-1, keepdims=True)
        - normed * jnp.mean(grad_normed * normed, axis=-1, keepdims=True)
    )


def dot_high(a, b, dims):
    return lax.dot_general(
        a, b, (dims, ((), ())), precision=HIGH, preferred_element_type=F32
    )


NN, NT, TN = ((1,), (0,)), ((1,), (1,)), ((0,), (0,))


def pinv_kernel(scale, q_ref, k_ref, inverse_ref, kernel_ref, saved_ref):
    count = q_ref.shape[0]
    eye = (iota((LAND, LAND), 0) == iota((LAND, LAND), 1)).astype(F32)
    kernels, inverses = [], []
    for p in range(count):
        scores = dot_high(q_ref[p], k_ref[p], NT) * scale
        weights = jnp.exp(scores - jnp.max(scores, axis=1, keepdims=True))
        kernel = weights / jnp.sum(weights, axis=1, keepdims=True)
        kernel_ref[p] = kernel
        kernels.append(kernel)
        largest = jnp.max(jnp.sum(kernel, axis=0, keepdims=True), axis=1, keepdims=True)
        inverses.append(kernel.T / largest)
    for sweep in range(NS_ITERS):
        products = [dot_high(kernels[p], inverses[p], NN) for p in range(count)]
        second = [
            15.0 * eye - dot_high(products[p], 7.0 * eye - products[p], NN) for p in range(count)
        ]
        third = [13.0 * eye - dot_high(products[p], second[p], NN) for p in range(count)]
        for p in range(count):
            at = (sweep * count + p) * 4
            saved_ref[at], saved_ref[at + 1] = inverses[p], products[p]
            saved_ref[at + 2], saved_ref[at + 3] = second[p], third[p]
        inverses = [0.25 * dot_high(inverses[p], third[p], NN) for p in range(count)]
    for p in range(count):
        inverse_ref[p] = inverses[p]


def pinv_back_kernel(scale, q_ref, k_ref, kernel_ref, saved_ref, grad_ref, avg_ref, gq_ref, gk_ref):
    count = q_ref.shape[0]
    each = range(count)
    eye = (iota((LAND, LAND), 0) == iota((LAND, LAND), 1)).astype(F32)
    grads = [dot_nt(grad_ref[p], avg_ref[p]) for p in each]
    kernels = [kernel_ref[p] for p in each]
    totals = [jnp.zeros((LAND, LAND), F32) for p in each]
    for sweep in reversed(range(NS_ITERS)):
        first = [(sweep * count + p) * 4 for p in each]
        inverses, products = [saved_ref[a] for a in first], [saved_ref[a + 1] for a in first]
        grad_third = [0.25 * dot_high(inverses[p], grads[p], TN) for p in each]
        nexts = [0.25 * dot_high(grads[p], saved_ref[first[p] + 3], NT) for p in each]
        grad_second = [-dot_high(products[p], grad_third[p], TN) for p in each]
        grad_product = [-dot_high(grad_third[p], saved_ref[first[p] + 2], NT) for p in each]
        grad_first = [-dot_high(products[p], grad_second[p], TN) for p in each]
        grad_product = [
            grad_product[p]
            - dot_high(grad_second[p], 7.0 * eye - products[p], NT)
            - grad_first[p]
            for p in each
        ]
        totals = [totals[p] + dot_high(grad_product[p], inverses[p], NT) for p in each]
        grads = [nexts[p] + dot_high(kernels[p], grad_product[p], TN) for p in each]
    for p in each:
        kernel = kernels[p]
        sums = jnp.sum(kernel, axis=0, keepdims=True)
        largest = jnp.max(sums, axis=1, keepdims=True)
        flipped = grads[p].T
        loss = jnp.sum(jnp.sum(flipped * kernel, axis=1, keepdims=True), axis=0, keepdims=True)
        at_top = (sums == largest).astype(F32)
        at_top = at_top / jnp.sum(at_top, axis=1, keepdims=True)
        grad = totals[p] + flipped / largest - at_top * (loss / (largest * largest))
        grad = kernel * (grad - jnp.sum(grad * kernel, axis=1, keepdims=True)) * scale
        gq_ref[p] = dot_high(grad, k_ref[p], NN)
        gk_ref[p] = dot_high(grad, q_ref[p], TN)


def settle_qkv_kernel(side_ref, late_ref, late_other_ref, early_ref, early_other_ref, out_ref):
    part = pl.program_id(0)
    own = jnp.where(part == 0, 0, 1) == side_ref[0]
    choices = [
        (late_ref, own & (part < 2)),
        (late_other_ref, jnp.logical_not(own) & (part < 2)),
        (early_ref, own & (part == 2)),
        (early_other_ref, jnp.logical_not(own) & (part == 2)),
    ]
    for ref, chosen in choices:

        @pl.when(chosen)
        def _():
            out_ref[...] = ref[...].astype(F32)


def settle_qkv(late, late_other, early, early_other, width):
    side = (lax.axis_index("seq") % 2).astype(jnp.int32).reshape(1)
    rows = width // 2

    def spec(used):
        return pl.BlockSpec((rows, width), lambda j, i, s: (jnp.where(used(j), i, 0), 0))

    return pl.pallas_call(
        settle_qkv_kernel,
        grid_spec=pltpu.PrefetchScalarGridSpec(
            num_scalar_prefetch=1,
            grid=(3, 2),
            in_specs=[spec(lambda j: j < 2), spec(lambda j: j < 2)] + [spec(lambda j: j == 2)] * 2,
            out_specs=pl.BlockSpec((rows, width), lambda j, i, s: (i, j)),
        ),
        out_shape=jax.ShapeDtypeStruct((width, 3 * width), F32),
        name="settle_qkv",
    )(side, late, late_other, early, early_other)


def per_device(
    inputs, doc_lengths, w_qkv, bias_q, bias_v, conv_taps, w_out, bias_out, norm1_gain,
    norm1_bias, w_up, bias_up, w_down, bias_down, norm2_gain, norm2_bias, cotangent,
):
    tokens = inputs[0]
    tok_count, width = tokens.shape
    heads, tap_count = conv_taps.shape
    size = width // heads
    radius = (tap_count - 1) // 2
    lengths = doc_lengths[0]
    docs = lengths.shape[0]
    mark_count = docs * LAND
    scale = 1.0 / math.sqrt(size)
    seq_count = lax.axis_size("seq")
    me = lax.axis_index("seq")
    row_first = me * tok_count
    ends = jnp.cumsum(lengths)
    starts = ends - lengths
    bounds = (jnp.concatenate([starts, ends]) - row_first).astype(jnp.int32)
    within = jnp.arange(LAND + 1, dtype=jnp.int32)
    edges = starts[:, None] + (within[None, :] * lengths[:, None] + LAND - 1) // LAND
    mark_low = edges[:, :-1].reshape(mark_count, 1)
    mark_high = edges[:, 1:].reshape(mark_count, 1)
    counts = (mark_high - mark_low).astype(F32)
    places = row_first + jnp.arange(tok_count, dtype=jnp.int32)[None, :]
    onehot = ((places >= mark_low) & (places < mark_high)).astype(BF)
    rows_in = (((0,), (0,)), ((), ()))
    cols_in = (((1,), (1,)), ((), ()))
    blocks = tok_count // BLOCK
    window_rows = tok_count + GROUP - SUB
    smem = pl.BlockSpec(memory_space=pltpu.SMEM)
    params = pltpu.CompilerParams(vmem_limit_bytes=40 * 1024 * 1024)
    tok_spec = pl.BlockSpec((BLOCK, width), lambda i: (i, 0))

    def part(col):
        return pl.BlockSpec((BLOCK, width), lambda i: (i, col))

    def fixed(*shape):
        return pl.BlockSpec(shape, lambda i: (0,) * len(shape))

    def shaped(shape, dtype):
        return jax.ShapeDtypeStruct(shape, dtype)

    means = jnp.dot(onehot, tokens, preferred_element_type=F32) / counts
    mean_in = seq_whole(seq_quarter(means.astype(BF), add_join))
    marks = jnp.dot(mean_in, w_qkv[:, : 2 * width], preferred_element_type=F32)
    mark_q = (marks[:, :width] + bias_q).astype(BF)
    mark_k = marks[:, width:].astype(BF)

    bias = jnp.concatenate([bias_q, jnp.zeros_like(bias_q), bias_v])
    qkv = (jnp.dot(tokens, w_qkv, preferred_element_type=F32) + bias).astype(BF)
    value_ext = extended(qkv[:, 2 * width :], radius, window_rows)
    value_ext, mark_q, mark_k = lax.optimization_barrier((value_ext, mark_q, mark_k))

    def one_col(col):
        return pl.BlockSpec((tok_count, width), lambda i: (0, col))

    stats = pl.pallas_call(
        lambda *refs: landmark_kernel(docs, scale, *refs),
        grid=(1,),
        in_specs=[smem, fixed(mark_count, width), one_col(1), one_col(2)],
        out_specs=fixed(mark_count, width + 128),
        out_shape=shaped((mark_count, width + 128), BF),
        scratch_shapes=[
            pltpu.VMEM((width, 128), F32), pltpu.VMEM((width, 128), F32),
            pltpu.VMEM((width, GROUP), F32),
        ],
        compiler_params=params,
        name="landmark",
    )(bounds, mark_q, qkv, qkv)
    far_count = seq_count // 4
    own_count = -(-heads // far_count)
    own_doc = (me % 2) * 2 + (me // 2) % 2
    own_at = (me // 4) * own_count * size
    spare = far_count * own_count * size - width

    def own_heads(array):
        array = jnp.pad(array, ((0, 0), (0, spare)))
        array = lax.dynamic_slice_in_dim(array, own_at, own_count * size, 1)
        return array.reshape(LAND, own_count, size).transpose(1, 0, 2)

    def of_doc(array):
        return lax.dynamic_slice_in_dim(array, own_doc * LAND, LAND, 0)

    mine, other = halves(stats, 1)
    stats = join(mine, swap(other, "seq", 1))
    stats, later_q, later_k = lax.optimization_barrier((stats, mark_q, mark_k))
    own_q = own_heads(of_doc(later_q)).astype(F32)
    own_k = own_heads(of_doc(later_k)).astype(F32)
    square = (own_count, LAND, LAND)
    own_inverse, kernel, saved = pl.pallas_call(
        lambda *refs: pinv_kernel(scale, *refs),
        out_shape=(
            shaped(square, F32), shaped(square, F32),
            shaped((4 * NS_ITERS * own_count, LAND, LAND), F32),
        ),
        name="pinv",
    )(own_q, own_k)
    inverse = own_inverse.transpose(1, 0, 2).reshape(LAND, own_count * size).astype(BF)
    mine, other = halves(stats, 2)
    stats = join(mine, swap(other, "seq", 2))
    for i in range(2, seq_count.bit_length() - 1):
        other = swap(jnp.concatenate([stats, inverse], 1), "seq", 1 << i)
        stats = join(stats, other[:, : width + 128])
        other = other[:, width + 128 :]
        inverse = jnp.where(
            (me >> i) % 2 == 0,
            jnp.concatenate([inverse, other], 1),
            jnp.concatenate([other, inverse], 1),
        )
    inverse = inverse[:, :width]
    mix = pl.pallas_call(
        mix_kernel, out_shape=shaped((LAND, width + 128), BF), name="mix"
    )(inverse, stats)
    mix = seq_whole(mix)

    taps = jnp.pad(conv_taps, ((0, 0), (0, GROUP - tap_count)))
    mark_spec = fixed(mark_count, width)
    mixed, probs = pl.pallas_call(
        lambda *refs: token_kernel(docs, scale, *refs),
        grid=(blocks,),
        in_specs=[
            smem, part(0), fixed(window_rows, width), mark_spec, mark_spec, fixed(heads, GROUP)
        ],
        out_specs=(tok_spec, pl.BlockSpec((width, BLOCK), lambda i: (0, i))),
        out_shape=(shaped((tok_count, width), BF), shaped((width, tok_count), BF)),
        scratch_shapes=[pltpu.VMEM((heads * SUB, GROUP), BF), pltpu.VMEM((BLOCK, width), F32)],
        compiler_params=params,
        name="token",
    )(bounds, qkv, value_ext, mark_k, mix, taps)

    hidden = w_up.shape[1]
    vectors = jnp.stack([bias_out, norm1_gain, norm1_bias, bias_down, norm2_gain, norm2_bias])
    vectors = jnp.pad(vectors, ((0, 2), (0, 0)))
    wide_spec = pl.BlockSpec((FFN_BLOCK, hidden), lambda i: (i, 0))
    ffn_spec = pl.BlockSpec((FFN_BLOCK, width), lambda i: (i, 0))
    narrow = shaped((tok_count, width), BF)
    (
        result, grad_one, active, grad_upper, hidden_low, grad_low_two, grad_low_one,
        grad_mixed, sums, sum_up,
    ) = pl.pallas_call(
        ffn_kernel,
        grid=(tok_count // FFN_BLOCK,),
        in_specs=[
            ffn_spec, ffn_spec, ffn_spec, fixed(width, width), fixed(width, hidden),
            fixed(hidden, width), fixed(8, width), fixed(8, hidden),
        ],
        out_specs=(
            ffn_spec, ffn_spec, wide_spec, wide_spec, ffn_spec, ffn_spec, ffn_spec, ffn_spec,
            fixed(8, width), fixed(8, hidden),
        ),
        out_shape=(
            shaped((tok_count, width), F32), shaped((tok_count, width), F32),
            shaped((tok_count, hidden), BF), shaped((tok_count, hidden), BF),
            narrow, narrow, narrow, narrow, shaped((8, width), F32), shaped((8, hidden), F32),
        ),
        scratch_shapes=[pltpu.VMEM((FFN_BLOCK, hidden), BF)],
        compiler_params=pltpu.CompilerParams(vmem_limit_bytes=58 * 1024 * 1024),
        name="ffn",
    )(
        tokens, mixed, cotangent[0], w_out, w_up, w_down, vectors,
        jnp.broadcast_to(bias_up[None, :], (8, hidden)),
    )

    grad_queries, grad_mix, grad_mk = pl.pallas_call(
        lambda *refs: token_back_kernel(docs, scale, *refs),
        grid=(blocks,),
        in_specs=[
            smem, part(0), tok_spec, pl.BlockSpec((width, BLOCK), lambda i: (0, i)), mark_spec,
            mark_spec,
        ],
        out_specs=(tok_spec, mark_spec, mark_spec),
        out_shape=(
            shaped((tok_count, width), BF), shaped((mark_count, width), F32),
            shaped((mark_count, width), F32),
        ),
        scratch_shapes=[pltpu.VMEM((BLOCK, width), F32)],
        compiler_params=params,
        name="token_back",
    )(bounds, qkv, grad_mixed, probs, mark_k, mix)
    grad_w_down = lax.dot_general(active, grad_low_two, rows_in, preferred_element_type=F32)
    grad_w_up = lax.dot_general(hidden_low, grad_upper, rows_in, preferred_element_type=F32)
    grad_ext = extended(grad_mixed, radius, window_rows)
    grad_mix, grad_w_down, grad_w_up, grad_ext = lax.optimization_barrier(
        (grad_mix.astype(BF), grad_w_down.astype(BF), grad_w_up.astype(BF), grad_ext)
    )
    sum_w_down, sum_w_up = lax.psum((grad_w_down, grad_w_up), ("row", "seq"))

    def remaining(grad_mix, grad_mk, stats, mix):
        grad_mix = seq_quarter(grad_mix.astype(BF), add_join)
        grad_w_out = lax.dot_general(mixed, grad_low_one, rows_in, preferred_element_type=F32)

        grad_conv, products = pl.pallas_call(
            lambda *refs: conv_back_kernel(docs, *refs),
            grid=(blocks,),
            in_specs=[
                smem, fixed(window_rows, width), fixed(window_rows, width), fixed(heads, GROUP)
            ],
            out_specs=(tok_spec, fixed(16, GROUP)),
            out_shape=(shaped((tok_count, width), F32), shaped((16, GROUP), F32)),
            scratch_shapes=[
                pltpu.VMEM((heads * SUB, GROUP), BF), pltpu.VMEM((heads * SUB, GROUP), F32)
            ],
            compiler_params=params,
            name="conv_back",
        )(bounds, grad_ext, value_ext, jnp.pad(conv_taps[:, ::-1], ((0, 0), (0, GROUP - tap_count))))
        grad_conv_taps = products[:heads, SUB - 1 : SUB - 1 + tap_count]
        grad_mix, grad_conv, grad_conv_taps = lax.optimization_barrier(
            (grad_mix, grad_conv, grad_conv_taps)
        )

        grad_avg = pl.pallas_call(
            mix_back_kernel, out_shape=shaped((LAND, width + 128), BF), name="mix_back"
        )(inverse, stats, grad_mix)
        grad_avg = seq_whole(grad_avg)
        lane_spec = pl.BlockSpec((mark_count, 128), lambda i: (0, width // 128))
        grad_keys, grad_values, grad_mq = pl.pallas_call(
            lambda *refs: landmark_back_kernel(docs, scale, *refs),
            grid=(blocks,),
            in_specs=[
                smem, part(1), part(2), tok_spec, mark_spec, mark_spec, lane_spec, lane_spec
            ],
            out_specs=(tok_spec, tok_spec, mark_spec),
            out_shape=(
                shaped((tok_count, width), BF), shaped((tok_count, width), BF),
                shaped((mark_count, width), F32),
            ),
            scratch_shapes=[pltpu.VMEM((BLOCK, width), F32), pltpu.VMEM((BLOCK, width), F32)],
            compiler_params=params,
            name="landmark_back",
        )(bounds, qkv, qkv, grad_conv, mark_q, grad_avg, mix, grad_avg)


        def weight_grad(grads):
            return lax.dot_general(tokens, grads, rows_in, preferred_element_type=F32)

        early = jnp.pad(grad_w_out.astype(BF), ((0, width), (0, 0)))
        early = lax.dynamic_update_slice_in_dim(
            early, weight_grad(grad_values).astype(BF), width, 0
        )
        grad_mix, early = lax.optimization_barrier((grad_mix, early))
        early = advance(begin(early, ORDER, ORDER), 1)
        grad_mq_small, grad_mk_small = pl.pallas_call(
            lambda *refs: pinv_back_kernel(scale, *refs),
            out_shape=(shaped(square, F32), shaped(square, F32)),
            name="pinv_back",
        )(own_q, own_k, kernel, saved, own_heads(grad_mix), own_heads(stats[:, :width]))

        grad_mq_small, (early,) = tied(grad_mq_small, [early])
        early = advance(early, 1)

        def with_small(array, small):
            small = small.transpose(1, 0, 2).reshape(LAND, own_count * size)
            small = lax.dynamic_update_slice_in_dim(
                jnp.zeros((LAND, width + spare), F32), small, own_at, 1
            )[:, :width]
            first = own_doc * LAND
            rows = lax.dynamic_slice_in_dim(array, first, LAND, 0) + small
            return lax.dynamic_update_slice_in_dim(array, rows, first, 0)

        grad_mq = with_small(grad_mq, grad_mq_small)
        grad_mk = with_small(grad_mk, grad_mk_small)
        grad_marks = jnp.concatenate([grad_mq, grad_mk], axis=1).astype(BF)
        mark_back = lax.dot_general(
            grad_marks, w_qkv[:, : 2 * width], cols_in, preferred_element_type=F32
        ) / counts
        mark_back = mark_back.astype(BF)

        grad_bias_q = jnp.sum(grad_queries.astype(F32), axis=0) + jnp.sum(grad_mq, axis=0)
        grad_bias_v = jnp.sum(grad_values.astype(F32), axis=0)
        mark_grad_q = lax.dot_general(
            mean_in, grad_marks[:, :width], rows_in, preferred_element_type=F32
        )
        mark_grad_k = lax.dot_general(
            mean_in, grad_marks[:, width:], rows_in, preferred_element_type=F32
        )
        others = jnp.concatenate(
            [
                sum_up[0].reshape(hidden // width, width),
                grad_bias_q[None],
                grad_bias_v[None],
                jnp.pad(grad_conv_taps.reshape(1, -1), ((0, 0), (0, width - heads * tap_count))),
                jnp.zeros((4 - hidden // width + 1, width), F32),
            ],
            0,
        )
        spare_rows = width // 6
        small = jnp.concatenate([sums, others], 0).astype(BF)
        below = width + 2 * spare_rows - small.shape[0]
        late = jnp.pad(small, ((width, below), (0, 0)))
        late = lax.dynamic_update_slice_in_dim(
            late, (weight_grad(grad_queries) + mark_grad_q).astype(BF), 0, 0
        )
        late = lax.dynamic_update_slice_in_dim(
            late, (weight_grad(grad_keys) + mark_grad_k).astype(BF), width + spare_rows, 0
        )
        late = begin(late, ORDER, ORDER)
        grad_projected = jnp.concatenate([grad_queries, grad_keys, grad_values], axis=1)
        grad_input = grad_one + lax.dot_general(
            grad_projected, w_qkv, cols_in, preferred_element_type=F32
        )
        for step in seq_steps():
            mark_back = step(mark_back)
            early, late = advance(early, 1), advance(late, 1)
            (mark_back, grad_input), (early, late) = tied((mark_back, grad_input), [early, late])
        return early[0], late[0], mark_back, grad_input

    plan = stages(ORDER)
    sent = len(seq_steps())

    def rows_left(rows, done):
        return rows >> min(done, 2 * len(plan) - done)

    early_rows = rows_left(2 * width, sent + 2)
    late_rows = rows_left(2 * width + width // 3, sent)

    def nothing(*unused):
        return tuple(
            jnp.zeros((rows, width), BF) for rows in (early_rows, late_rows, mark_count)
        ) + (jnp.zeros((tok_count, width), F32),)

    early, late, mark_back, grad_input = lax.cond(
        lengths[0] > 0, remaining, nothing, grad_mix, grad_mk, stats, mix
    )
    early, late = (early, plan, plan, sent + 2), (late, plan, plan, sent)
    last = 2 * len(plan) - 1
    late = advance(late, 2)
    (sum_w_down, sum_w_up), (late,) = tied(
        (sum_w_down.astype(F32), sum_w_up.astype(F32)), [late]
    )
    early, late = advance(early, last - early[3]), advance(late, last - late[3])
    grad_input = grad_input + lax.dot_general(
        onehot, mark_back, rows_in, preferred_element_type=F32
    )
    grad_input, (early, late) = tied(grad_input, [early, late])
    early, early_other = last_swap(early)[:2]
    late, late_other = last_swap(late)[:2]
    sum_w_qkv = settle_qkv(late, late_other, early, early_other, width)
    first_core = me % 2 == 0
    sum_w_out = jnp.where(first_core, early, early_other).astype(F32)
    flat = jnp.where(first_core, late[width:], late_other[width:])[:16].astype(F32)
    at = sums.shape[0] + hidden // width
    pieces = [
        flat[at], flat[at + 1], flat[at + 2, : heads * tap_count], flat[5], flat[3], flat[4],
        flat[sums.shape[0] : at].reshape(hidden), flat[2], flat[0], flat[1],
    ]
    return (
        result[None], grad_input[None], sum_w_qkv, pieces[0], pieces[1],
        pieces[2].reshape(heads, tap_count), sum_w_out, pieces[3], pieces[4], pieces[5],
        sum_w_up, pieces[6], sum_w_down, pieces[7], pieces[8], pieces[9],
    )


def solution(mesh):
    whole, tokens = P(), P("row", "seq", None)
    return jax.shard_map(
        per_device,
        mesh=mesh,
        in_specs=(tokens, P("row", None)) + (whole,) * 14 + (tokens,),
        out_specs=(tokens, tokens) + (whole,) * 14,
        check_vma=False,
    )
```

```python
import math

import jax
import jax.numpy as jnp
from jax import lax
from jax.experimental import pallas as pl
from jax.experimental.pallas import tpu as pltpu
from jax.sharding import PartitionSpec as P

LAND = 64
NS_ITERS = 6
HIGH = lax.Precision.HIGHEST
NEGATIVE = -1e30
BF = jnp.bfloat16
F32 = jnp.float32

BLOCK = 256
GROUP = 256
SUB = 128
TAPS = 33
FFN_BLOCK = 256
ORDER = ("row", "near", "far")


def swap(array, axis, bit):
    count = lax.axis_size(axis)
    return lax.ppermute(array, axis, [(i, i ^ bit) for i in range(count)])


def add_parts(parts):
    total = parts[0].astype(F32)
    for part in parts[1:]:
        total = total + part.astype(F32)
    return total


def halves(array, bit):
    rows = array.shape[0] // 2
    side = (lax.axis_index("seq") // bit) % 2
    mine = lax.dynamic_slice_in_dim(array, side * rows, rows, 0)
    other = lax.dynamic_slice_in_dim(array, (1 - side) * rows, rows, 0)
    return mine, other


def seq_quarter(array, join):
    bits = [1 << i for i in range(lax.axis_size("seq").bit_length() - 1)]
    for bit in bits[:2]:
        mine, other = halves(array, bit)
        array = join(mine, swap(other, "seq", bit))
    for bit in bits[2:]:
        array = join(array, swap(array, "seq", bit))
    return array


def paired(array, axis, bit, dim):
    other = swap(array, axis, bit)
    side = (lax.axis_index(axis) // bit) % 2
    return jnp.where(
        side == 0,
        jnp.concatenate([array, other], dim),
        jnp.concatenate([other, array], dim),
    )


def seq_whole(array):
    return paired(paired(array, "seq", 2, 0), "seq", 1, 0)


def seq_steps():
    bits = [1 << i for i in range(lax.axis_size("seq").bit_length() - 1)]

    def halve(bit):
        def step(array):
            mine, other = halves(array, bit)
            return add_join(mine, swap(other, "seq", bit))

        return step

    def whole(bit):
        return lambda array: add_join(array, swap(array, "seq", bit))

    def double(bit):
        return lambda array: paired(array, "seq", bit, 0)

    return (
        [halve(bit) for bit in bits[:2]]
        + [whole(bit) for bit in bits[2:]]
        + [double(bit) for bit in reversed(bits[:2])]
    )


def add_join(first, second):
    return (first.astype(F32) + second.astype(F32)).astype(BF)


def stages(order):
    row = [("row", 1 << i) for i in range(lax.axis_size("row").bit_length() - 1)]
    seq = [[("seq", 1 << i)] for i in range(lax.axis_size("seq").bit_length() - 1)]
    named = {"core": seq[0], "row": row, "near": seq[1], "far": seq[2], "rest": sum(seq[3:], [])}
    return sum([named[name] for name in ("core",) + order + ("rest",)], [])


def begin(array, down, back):
    return array, stages(down), stages(back), 0


def advance(state, steps):
    held, down, back, done = state
    for step in range(done, min(done + steps, 2 * len(down))):
        if step < len(down):
            axis, bit = down[step]
            half = held.shape[0] // 2
            side = (lax.axis_index(axis) // bit) % 2
            mine = lax.dynamic_slice_in_dim(held, side * half, half, 0)
            other = lax.dynamic_slice_in_dim(held, (1 - side) * half, half, 0)
            held = mine.astype(F32) + swap(other, axis, bit).astype(F32)
            held = held.astype(BF)
        else:
            axis, bit = back[2 * len(down) - 1 - step]
            held = paired(held, axis, bit, 0)
    return held, down, back, min(done + steps, 2 * len(down))


def last_swap(state):
    down, back = state[1], state[2]
    held = advance(state, 2 * len(down) - 1 - state[3])[0]
    return held, swap(held, *down[0]), down, back


def tied(values, states):
    values, helds = lax.optimization_barrier((values, [state[0] for state in states]))
    return values, [(held,) + state[1:] for held, state in zip(helds, states)]


def extended(cells, width, rows):
    count = lax.axis_size("seq")
    head = cells[:width]
    tail = cells[-width:]
    return jnp.concatenate(
        [
            lax.ppermute(tail, "seq", [(i, i + 1) for i in range(count - 1)]),
            cells,
            lax.ppermute(head, "seq", [(i + 1, i) for i in range(count - 1)]),
            jnp.zeros((rows - cells.shape[0] - 2 * width, cells.shape[1]), cells.dtype),
        ],
        axis=0,
    )


def dot_nn(a, b):
    return jnp.dot(a, b, preferred_element_type=F32)


def dot_nt(a, b):
    return lax.dot_general(a, b, (((1,), (1,)), ((), ())), preferred_element_type=F32)


def dot_tn(a, b):
    return lax.dot_general(a, b, (((0,), (0,)), ((), ())), preferred_element_type=F32)


def iota(shape, dim):
    return lax.broadcasted_iota(jnp.int32, shape, dim)


def spread(block):
    rows = block.shape[0]
    tall = jnp.concatenate([block] * 4, axis=0).astype(F32)
    shape = (4 * rows, GROUP)
    keep = iota(shape, 0) // rows == iota(shape, 1) // LAND
    return jnp.where(keep, tall, 0.0).astype(BF)


def gathered(square):
    rows = square.shape[0] // 4
    lane = iota((rows, GROUP), 1) // LAND
    out = square[:rows]
    for head in range(1, 4):
        out = jnp.where(lane == head, square[head * rows : (head + 1) * rows], out)
    return out


def by_head(columns, first, shape):
    lane = iota(shape, 1)
    out = jnp.zeros(shape, F32)
    for head, column in enumerate(columns):
        out = jnp.where((lane % 16 == first + head) & (lane < 48), column, out)
    return out


def split_three(cells):
    lane = iota(cells.shape, 1)
    high = cells.astype(BF).astype(F32)
    mid = (cells - high).astype(BF).astype(F32)
    low = cells - high - mid
    return jnp.where(lane < 16, high, jnp.where(lane < 32, mid, low)).astype(BF)


def merge_three(cells):
    cells = cells.astype(F32)
    return cells + pltpu.roll(cells, 112, 1) + pltpu.roll(cells, 96, 1)


def head_lanes(heads, width):
    return (iota((128, width), 0) == iota((128, width), 1) // LAND).astype(F32)


def doc_of(places, bounds, docs):
    out = (places >= bounds[2 * docs - 1]).astype(jnp.int32)
    for doc in range(docs):
        out = out + (places >= bounds[doc]).astype(jnp.int32)
    return out


def landmark_kernel(docs, scale, bounds, mq_ref, k_ref, v_ref, out_ref, max_s, sum_s, acc_s):
    tokens, width = k_ref.shape
    groups = width // GROUP
    heads = width // LAND
    out_ref[:, :width] = jnp.zeros((docs * LAND, width), BF)
    empty = jnp.full((docs * LAND, 128), NEGATIVE, F32)
    out_ref[:, width:] = jnp.where(iota(empty.shape, 1) < 48, split_three(empty).astype(F32), 0.0).astype(BF)
    for doc in range(docs):
        low = jnp.clip(bounds[doc], 0, tokens)
        high = jnp.clip(bounds[docs + doc], 0, tokens)
        rows = slice(doc * LAND, (doc + 1) * LAND)

        @pl.when(high > low)
        def _():
            max_s[...] = jnp.full(max_s.shape, NEGATIVE, F32)
            sum_s[...] = jnp.zeros(sum_s.shape, F32)
            acc_s[...] = jnp.zeros(acc_s.shape, F32)
            wide = [
                spread(mq_ref[rows, g * GROUP : (g + 1) * GROUP]) for g in range(groups)
            ]

            ones = jnp.ones((BLOCK, 128), BF)

            def step(block, carry):
                first = pl.multiple_of(block * BLOCK, BLOCK)
                at = pl.ds(first, BLOCK)
                place = iota((1, BLOCK), 1) + first
                valid = (place >= low) & (place < high)
                for g in range(groups):
                    cols = slice(g * GROUP, (g + 1) * GROUP)
                    scores = dot_nt(wide[g], k_ref[at, cols]) * scale
                    scores = jnp.where(valid, scores, NEGATIVE)
                    old = max_s[cols, :]
                    top = jnp.maximum(old, jnp.max(scores, axis=1, keepdims=True))
                    weights = jnp.exp(scores - twice(top)).astype(BF)
                    shrink = jnp.exp(old - top)
                    max_s[cols, :] = top
                    sum_s[cols, :] = sum_s[cols, :] * shrink + dot_nn(weights, ones)
                    acc_s[cols, :] = acc_s[cols, :] * twice(shrink) + dot_nn(weights, v_ref[at, cols])
                return carry

            lax.fori_loop(low // BLOCK, (high + BLOCK - 1) // BLOCK, step, 0)
            columns = []
            for g in range(groups):
                cols = slice(g * GROUP, (g + 1) * GROUP)
                sums = sum_s[cols, :]
                out_ref[rows, cols] = gathered(acc_s[cols, :] / twice(sums)).astype(BF)
                level = max_s[cols, :] + jnp.log(sums)
                columns += [level[h * LAND : (h + 1) * LAND] for h in range(4)]
            out_ref[rows, width:] = split_three(by_head(columns, 0, (LAND, 128)))


def twice(cells):
    return jnp.concatenate([cells, cells], axis=1)


def join_kernel(a_ref, b_ref, out_ref):
    width = a_ref.shape[1] - 128
    heads = width // LAND
    first, second = merge_three(a_ref[:, width:]), merge_three(b_ref[:, width:])
    lane = iota(first.shape, 1)
    first = jnp.where(lane < heads, first, 0.0)
    second = jnp.where(lane < heads, second, 0.0)
    top = jnp.maximum(first, second)
    exp_a, exp_b = jnp.exp(first - top), jnp.exp(second - top)
    both = exp_a + exp_b
    level = top + jnp.log(both)
    pick = head_lanes(heads, width).astype(BF)
    share = exp_b / both
    high = share.astype(BF)
    low = (share - high.astype(F32)).astype(BF)
    share = dot_nn(jnp.concatenate([high, low], 1), jnp.concatenate([pick, pick], 0))
    from_a, from_b = a_ref[:, :width].astype(F32), b_ref[:, :width].astype(F32)
    out_ref[:, :width] = (from_a + share * (from_b - from_a)).astype(BF)
    level = jnp.where(lane < heads, level, 0.0)
    level = level + pltpu.roll(level, 16, 1) + pltpu.roll(level, 32, 1)
    out_ref[:, width:] = split_three(level)


def join(first, second):
    return pl.pallas_call(
        join_kernel, out_shape=jax.ShapeDtypeStruct(first.shape, BF), name="join"
    )(first, second)


def mix_kernel(inv_ref, stat_ref, mix_ref):
    width = stat_ref.shape[1] - 128
    for g in range(width // GROUP):
        cols = slice(g * GROUP, (g + 1) * GROUP)
        mix_ref[:, cols] = dot_nn(inv_ref[:, cols], spread(stat_ref[:, cols])).astype(BF)
    mix_ref[:, width:] = stat_ref[:, width:]


def mix_back_kernel(inv_ref, stat_ref, grad_ref, out_ref):
    width = stat_ref.shape[1] - 128
    columns = []
    for g in range(width // GROUP):
        cols = slice(g * GROUP, (g + 1) * GROUP)
        grad = gathered(dot_tn(inv_ref[:, cols], grad_ref[:, cols]))
        out_ref[:, cols] = grad.astype(BF)
        product = grad * stat_ref[:, cols].astype(F32)
        lane = iota(product.shape, 1) // LAND
        for h in range(4):
            columns.append(jnp.sum(jnp.where(lane == h, product, 0.0), axis=1, keepdims=True))
    out_ref[:, width:] = split_three(by_head(columns, 0, (LAND, 128)))


def make_band(taps_ref, band_s):
    for head in range(taps_ref.shape[0]):
        row = jnp.broadcast_to(taps_ref[head : head + 1, :], (SUB, GROUP))
        band_s[head * SUB : (head + 1) * SUB, :] = pltpu.roll(row, 0, 1, stride=1, stride_axis=0).astype(BF)


def same_doc(first, bounds, docs, radius):
    rows = iota((SUB, GROUP), 0) + first
    cols = iota((SUB, GROUP), 1) + (first - radius)
    return doc_of(rows, bounds, docs) == doc_of(cols, bounds, docs)


def token_kernel(
    docs, scale, bounds, q_ref, v_ref, mk_ref, mix_ref, taps_ref, mixed_ref, probs_ref, band_s, sum_s
):
    width = q_ref.shape[1]
    groups = width // GROUP
    radius = (TAPS - 1) // 2
    first = pl.program_id(0) * BLOCK

    @pl.when(pl.program_id(0) == 0)
    def _():
        make_band(taps_ref, band_s)

    for sub in range(BLOCK // SUB):
        start = pl.multiple_of(first + sub * SUB, SUB)
        same = same_doc(start, bounds, docs, radius)
        same = jnp.where(jnp.concatenate([same] * 4, axis=0), 1.0, 0.0).astype(BF)
        for g in range(groups):
            cols = slice(g * GROUP, (g + 1) * GROUP)
            band = band_s[g * 4 * SUB : (g + 1) * 4 * SUB, :] * same
            res = dot_nn(band, v_ref[pl.ds(start, GROUP), cols])
            sum_s[sub * SUB : (sub + 1) * SUB, cols] = gathered(res)
    probs_ref[...] = jnp.zeros(probs_ref.shape, BF)
    for doc in range(docs):
        low, high = bounds[doc], bounds[docs + doc]
        rows = slice(doc * LAND, (doc + 1) * LAND)

        @pl.when((high > first) & (low < first + BLOCK))
        def _():
            place = iota((1, BLOCK), 1) + first
            valid = (place >= low) & (place < high)
            for g in range(groups):
                cols = slice(g * GROUP, (g + 1) * GROUP)
                scores = dot_nt(spread(mk_ref[rows, cols]), q_ref[:, cols]) * scale
                scores = scores.reshape(4, LAND, BLOCK)
                weights = jnp.exp(scores - jnp.max(scores, axis=1, keepdims=True))
                probs = weights / jnp.sum(weights, axis=1, keepdims=True)
                probs = jnp.where(valid, probs.reshape(GROUP, BLOCK), 0.0).astype(BF)
                probs_ref[cols, :] = probs_ref[cols, :] + probs
                sum_s[:, cols] = sum_s[:, cols] + dot_tn(probs, spread(mix_ref[rows, cols]))

    mixed_ref[...] = sum_s[...].astype(BF)


def token_back_kernel(
    docs, scale, bounds, q_ref, gm_ref, probs_ref, mk_ref, mix_ref, gq_ref, gmix_ref, gmk_ref, gq_s
):
    width = q_ref.shape[1]
    groups = width // GROUP
    first = pl.program_id(0) * BLOCK

    @pl.when(pl.program_id(0) == 0)
    def _():
        gmix_ref[...] = jnp.zeros(gmix_ref.shape, F32)
        gmk_ref[...] = jnp.zeros(gmk_ref.shape, F32)

    gq_s[...] = jnp.zeros(gq_s.shape, F32)
    for doc in range(docs):
        low, high = bounds[doc], bounds[docs + doc]
        rows = slice(doc * LAND, (doc + 1) * LAND)

        @pl.when((high > first) & (low < first + BLOCK))
        def _():
            place = iota((1, BLOCK), 1) + first
            valid = (place >= low) & (place < high)
            for g in range(groups):
                cols = slice(g * GROUP, (g + 1) * GROUP)
                probs = jnp.where(valid, probs_ref[cols, :].astype(F32), 0.0)
                gmix_ref[rows, cols] += gathered(dot_nn(probs.astype(BF), gm_ref[:, cols]))
                grad = dot_nt(spread(mix_ref[rows, cols]), gm_ref[:, cols])
                heavy = (probs * grad).reshape(4, LAND, BLOCK)
                shared = probs.reshape(4, LAND, BLOCK) * jnp.sum(heavy, axis=1, keepdims=True)
                grad = ((heavy - shared).reshape(GROUP, BLOCK) * scale).astype(BF)
                gmk_ref[rows, cols] += gathered(dot_nn(grad, q_ref[:, cols]))
                gq_s[:, cols] += dot_tn(grad, spread(mk_ref[rows, cols]))

    gq_ref[...] = gq_s[...].astype(BF)


def conv_back_kernel(docs, bounds, gm_ref, v_ref, taps_ref, out_ref, sum_ref, band_s, prod_s):
    width = gm_ref.shape[1]
    groups = width // GROUP
    radius = (TAPS - 1) // 2
    first = pl.program_id(0) * BLOCK

    @pl.when(pl.program_id(0) == 0)
    def _():
        make_band(taps_ref, band_s)
        prod_s[...] = jnp.zeros(prod_s.shape, F32)

    for sub in range(BLOCK // SUB):
        start = pl.multiple_of(first + sub * SUB, SUB)
        same = same_doc(start, bounds, docs, radius)
        same = jnp.where(jnp.concatenate([same] * 4, axis=0), 1.0, 0.0)
        for g in range(groups):
            cols = slice(g * GROUP, (g + 1) * GROUP)
            tall = slice(g * 4 * SUB, (g + 1) * 4 * SUB)
            band = band_s[tall, :] * same.astype(BF)
            res = dot_nn(band, gm_ref[pl.ds(start, GROUP), cols])
            out_ref[sub * SUB : (sub + 1) * SUB, cols] = gathered(res)
            own = gm_ref[pl.ds(pl.multiple_of(start + radius, 16), SUB), cols]
            product = dot_nt(spread(own), v_ref[pl.ds(start, GROUP), cols])
            prod_s[tall, :] += product * same

    @pl.when(pl.program_id(0) == pl.num_programs(0) - 1)
    def _():
        flip = (iota((SUB, SUB), 0) + iota((SUB, SUB), 1) == SUB - 1).astype(F32).astype(BF)
        sum_ref[...] = jnp.zeros(sum_ref.shape, F32)
        for head in range(taps_ref.shape[0]):
            product = prod_s[head * SUB : (head + 1) * SUB, :]
            high = product.astype(BF)
            low = (product - high.astype(F32)).astype(BF)
            turned = pltpu.roll(dot_nn(flip, high) + dot_nn(flip, low), 0, 1, stride=1, stride_axis=0)
            sum_ref[head : head + 1, :] = jnp.sum(turned, axis=0, keepdims=True)


def ffn_kernel(
    x_ref, mixed_ref, cot_ref, w_out_ref, w_up_ref, w_down_ref, rows_ref, bias_up_ref,
    result_ref, grad_one_ref, active_ref, grad_up_ref, low_ref, low_two_ref, low_one_ref,
    grad_mixed_ref, sums_ref, sum_up_ref, slope_s,
):
    width = x_ref.shape[1]
    hidden = w_up_ref.shape[1]
    chunks = [slice(at, at + width) for at in range(0, hidden, width)]

    def row(i):
        return rows_ref[i : i + 1, :]

    @pl.when(pl.program_id(0) == 0)
    def _():
        sums_ref[...] = jnp.zeros(sums_ref.shape, F32)
        sum_up_ref[...] = jnp.zeros(sum_up_ref.shape, F32)

    def add_sum(i, cells):
        sums_ref[i : i + 1, :] += jnp.sum(cells, axis=0, keepdims=True)

    attended = dot_nn(mixed_ref[...], w_out_ref[...]) + row(0)
    norm_one, inverse_one = normalize(x_ref[...].astype(F32) + attended)
    hidden_one = norm_one * row(1) + row(2)
    hidden_low = hidden_one.astype(BF)
    low_ref[...] = hidden_low
    lowered = hidden_one + row(3)
    for cols in chunks:
        upper = dot_nn(hidden_low, w_up_ref[:, cols]) + bias_up_ref[:1, cols]
        active, slope = gelu_both(upper)
        active = active.astype(BF)
        active_ref[:, cols] = active
        slope_s[:, cols] = slope.astype(BF)
        lowered = lowered + dot_nn(active, w_down_ref[cols, :])
    norm_two, inverse_two = normalize(lowered)
    result_ref[...] = norm_two * row(4) + row(5)
    upstream = cot_ref[...].astype(F32)
    add_sum(0, upstream * norm_two)
    add_sum(1, upstream)
    grad_two = norm_back(upstream * row(4), norm_two, inverse_two)
    low_two = grad_two.astype(BF)
    low_two_ref[...] = low_two
    add_sum(2, low_two.astype(F32))
    grad_hidden = grad_two
    for cols in chunks:
        grad_up = dot_nt(low_two, w_down_ref[cols, :]) * slope_s[:, cols].astype(F32)
        grad_up = grad_up.astype(BF)
        grad_up_ref[:, cols] = grad_up
        sum_up_ref[:1, cols] += jnp.sum(grad_up.astype(F32), axis=0, keepdims=True)
        grad_hidden = grad_hidden + dot_nt(grad_up, w_up_ref[:, cols])
    add_sum(3, grad_hidden * norm_one)
    add_sum(4, grad_hidden)
    grad_one = norm_back(grad_hidden * row(1), norm_one, inverse_one)
    grad_one_ref[...] = grad_one
    low_one = grad_one.astype(BF)
    low_one_ref[...] = low_one
    add_sum(5, low_one.astype(F32))
    grad_mixed_ref[...] = dot_nt(low_one, w_out_ref[...]).astype(BF)


def landmark_back_kernel(
    docs, scale, bounds, k_ref, v_ref, conv_ref, mq_ref, grad_ref, level_ref, dots_ref,
    gk_ref, gv_ref, gmq_ref, gk_s, gv_s,
):
    width = k_ref.shape[1]
    groups = width // GROUP
    first = pl.program_id(0) * BLOCK

    @pl.when(pl.program_id(0) == 0)
    def _():
        gmq_ref[...] = jnp.zeros(gmq_ref.shape, F32)

    gk_s[...] = jnp.zeros(gk_s.shape, F32)
    gv_s[...] = conv_ref[...]
    for doc in range(docs):
        low, high = bounds[doc], bounds[docs + doc]
        rows = slice(doc * LAND, (doc + 1) * LAND)

        @pl.when((high > first) & (low < first + BLOCK))
        def _():
            place = iota((1, BLOCK), 1) + first
            valid = (place >= low) & (place < high)

            level, dots = merge_three(level_ref[rows, :]), merge_three(dots_ref[rows, :])

            def column(lanes, g):
                return jnp.concatenate(
                    [lanes[:, 4 * g + h : 4 * g + h + 1] for h in range(4)], axis=0
                )

            for g in range(groups):
                cols = slice(g * GROUP, (g + 1) * GROUP)
                wide_q, wide_g = spread(mq_ref[rows, cols]), spread(grad_ref[rows, cols])
                scores = dot_nt(wide_q, k_ref[:, cols]) * scale - column(level, g)
                probs = jnp.exp(jnp.where(valid, scores, NEGATIVE))
                grad = dot_nt(wide_g, v_ref[:, cols]) - column(dots, g)
                grad = (probs * grad * scale).astype(BF)
                gv_s[:, cols] += dot_tn(probs.astype(BF), wide_g)
                gk_s[:, cols] += dot_tn(grad, wide_q)
                gmq_ref[rows, cols] += gathered(dot_nn(grad, k_ref[:, cols]))

    gk_ref[...] = gk_s[...].astype(BF)
    gv_ref[...] = gv_s[...].astype(BF)


def gelu_both(upper):
    tangent = jnp.tanh(0.7978845608028654 * (upper + 0.044715 * upper * upper * upper))
    inner_slope = 0.7978845608028654 * (1.0 + 3.0 * 0.044715 * upper * upper)
    active = 0.5 * upper * (1.0 + tangent)
    slope = 0.5 * (1.0 + tangent) + 0.5 * upper * (1.0 - tangent * tangent) * inner_slope
    return active, slope


def normalize(residual):
    row_mean = jnp.mean(residual, axis=-1, keepdims=True)
    centered = residual - row_mean
    row_var = jnp.mean(centered * centered, axis=-1, keepdims=True)
    inverse_dev = lax.rsqrt(row_var + 1e-05)
    return (centered * inverse_dev, inverse_dev)


def norm_back(grad_normed, normed, inverse_dev):
    return inverse_dev * (
        grad_normed
        - jnp.mean(grad_normed, axis=-1, keepdims=True)
        - normed * jnp.mean(grad_normed * normed, axis=-1, keepdims=True)
    )


def dot_high(a, b, dims):
    return lax.dot_general(
        a, b, (dims, ((), ())), precision=HIGH, preferred_element_type=F32
    )


NN, NT, TN = ((1,), (0,)), ((1,), (1,)), ((0,), (0,))


def pinv_kernel(scale, q_ref, k_ref, inverse_ref, kernel_ref, saved_ref):
    count = q_ref.shape[0]
    eye = (iota((LAND, LAND), 0) == iota((LAND, LAND), 1)).astype(F32)
    kernels, inverses = [], []
    for p in range(count):
        scores = dot_high(q_ref[p], k_ref[p], NT) * scale
        weights = jnp.exp(scores - jnp.max(scores, axis=1, keepdims=True))
        kernel = weights / jnp.sum(weights, axis=1, keepdims=True)
        kernel_ref[p] = kernel
        kernels.append(kernel)
        largest = jnp.max(jnp.sum(kernel, axis=0, keepdims=True), axis=1, keepdims=True)
        inverses.append(kernel.T / largest)
    for sweep in range(NS_ITERS):
        products = [dot_high(kernels[p], inverses[p], NN) for p in range(count)]
        second = [
            15.0 * eye - dot_high(products[p], 7.0 * eye - products[p], NN) for p in range(count)
        ]
        third = [13.0 * eye - dot_high(products[p], second[p], NN) for p in range(count)]
        for p in range(count):
            at = (sweep * count + p) * 4
            saved_ref[at], saved_ref[at + 1] = inverses[p], products[p]
            saved_ref[at + 2], saved_ref[at + 3] = second[p], third[p]
        inverses = [0.25 * dot_high(inverses[p], third[p], NN) for p in range(count)]
    for p in range(count):
        inverse_ref[p] = inverses[p]


def pinv_back_kernel(scale, q_ref, k_ref, kernel_ref, saved_ref, grad_ref, avg_ref, gq_ref, gk_ref):
    count = q_ref.shape[0]
    each = range(count)
    eye = (iota((LAND, LAND), 0) == iota((LAND, LAND), 1)).astype(F32)
    grads = [dot_nt(grad_ref[p], avg_ref[p]) for p in each]
    kernels = [kernel_ref[p] for p in each]
    totals = [jnp.zeros((LAND, LAND), F32) for p in each]
    for sweep in reversed(range(NS_ITERS)):
        first = [(sweep * count + p) * 4 for p in each]
        inverses, products = [saved_ref[a] for a in first], [saved_ref[a + 1] for a in first]
        grad_third = [0.25 * dot_high(inverses[p], grads[p], TN) for p in each]
        nexts = [0.25 * dot_high(grads[p], saved_ref[first[p] + 3], NT) for p in each]
        grad_second = [-dot_high(products[p], grad_third[p], TN) for p in each]
        grad_product = [-dot_high(grad_third[p], saved_ref[first[p] + 2], NT) for p in each]
        grad_first = [-dot_high(products[p], grad_second[p], TN) for p in each]
        grad_product = [
            grad_product[p]
            - dot_high(grad_second[p], 7.0 * eye - products[p], NT)
            - grad_first[p]
            for p in each
        ]
        totals = [totals[p] + dot_high(grad_product[p], inverses[p], NT) for p in each]
        grads = [nexts[p] + dot_high(kernels[p], grad_product[p], TN) for p in each]
    for p in each:
        kernel = kernels[p]
        sums = jnp.sum(kernel, axis=0, keepdims=True)
        largest = jnp.max(sums, axis=1, keepdims=True)
        flipped = grads[p].T
        loss = jnp.sum(jnp.sum(flipped * kernel, axis=1, keepdims=True), axis=0, keepdims=True)
        at_top = (sums == largest).astype(F32)
        at_top = at_top / jnp.sum(at_top, axis=1, keepdims=True)
        grad = totals[p] + flipped / largest - at_top * (loss / (largest * largest))
        grad = kernel * (grad - jnp.sum(grad * kernel, axis=1, keepdims=True)) * scale
        gq_ref[p] = dot_high(grad, k_ref[p], NN)
        gk_ref[p] = dot_high(grad, q_ref[p], TN)


def settle_qkv_kernel(side_ref, late_ref, late_other_ref, early_ref, early_other_ref, out_ref):
    part = pl.program_id(0)
    own = jnp.where(part == 2, pl.program_id(1), part) == side_ref[0]
    choices = [
        (late_ref, own & (part < 2)),
        (late_other_ref, jnp.logical_not(own) & (part < 2)),
        (early_ref, own & (part == 2)),
        (early_other_ref, jnp.logical_not(own) & (part == 2)),
    ]
    for ref, chosen in choices:

        @pl.when(chosen)
        def _():
            out_ref[...] = ref[...].astype(F32)


def settle_qkv(late, late_other, early, early_other, width):
    side = (lax.axis_index("seq") % 2).astype(jnp.int32).reshape(1)
    rows = width // 2

    def spec(used):
        return pl.BlockSpec((rows, width), lambda j, i, s: (jnp.where(used(j), i, 0), 0))

    return pl.pallas_call(
        settle_qkv_kernel,
        grid_spec=pltpu.PrefetchScalarGridSpec(
            num_scalar_prefetch=1,
            grid=(3, 2),
            in_specs=[spec(lambda j: j < 2)] * 2 + [spec(lambda j: j < 0)] * 2,
            out_specs=pl.BlockSpec((rows, width), lambda j, i, s: (i, j)),
        ),
        out_shape=jax.ShapeDtypeStruct((width, 3 * width), F32),
        name="settle_qkv",
    )(side, late, late_other, early, early_other)


def per_device(
    inputs, doc_lengths, w_qkv, bias_q, bias_v, conv_taps, w_out, bias_out, norm1_gain,
    norm1_bias, w_up, bias_up, w_down, bias_down, norm2_gain, norm2_bias, cotangent,
):
    tokens = inputs[0]
    tok_count, width = tokens.shape
    heads, tap_count = conv_taps.shape
    size = width // heads
    radius = (tap_count - 1) // 2
    lengths = doc_lengths[0]
    docs = lengths.shape[0]
    mark_count = docs * LAND
    scale = 1.0 / math.sqrt(size)
    seq_count = lax.axis_size("seq")
    me = lax.axis_index("seq")
    row_first = me * tok_count
    ends = jnp.cumsum(lengths)
    starts = ends - lengths
    bounds = (jnp.concatenate([starts, ends]) - row_first).astype(jnp.int32)
    within = jnp.arange(LAND + 1, dtype=jnp.int32)
    edges = starts[:, None] + (within[None, :] * lengths[:, None] + LAND - 1) // LAND
    mark_low = edges[:, :-1].reshape(mark_count, 1)
    mark_high = edges[:, 1:].reshape(mark_count, 1)
    counts = (mark_high - mark_low).astype(F32)
    places = row_first + jnp.arange(tok_count, dtype=jnp.int32)[None, :]
    onehot = ((places >= mark_low) & (places < mark_high)).astype(BF)
    rows_in = (((0,), (0,)), ((), ()))
    cols_in = (((1,), (1,)), ((), ()))
    blocks = tok_count // BLOCK
    window_rows = tok_count + GROUP - SUB
    smem = pl.BlockSpec(memory_space=pltpu.SMEM)
    params = pltpu.CompilerParams(vmem_limit_bytes=40 * 1024 * 1024)
    tok_spec = pl.BlockSpec((BLOCK, width), lambda i: (i, 0))

    def part(col):
        return pl.BlockSpec((BLOCK, width), lambda i: (i, col))

    def fixed(*shape):
        return pl.BlockSpec(shape, lambda i: (0,) * len(shape))

    def shaped(shape, dtype):
        return jax.ShapeDtypeStruct(shape, dtype)

    means = jnp.dot(onehot, tokens, preferred_element_type=F32) / counts
    mean_in = seq_whole(seq_quarter(means.astype(BF), add_join))
    marks = jnp.dot(mean_in, w_qkv[:, : 2 * width], preferred_element_type=F32)
    mark_q = (marks[:, :width] + bias_q).astype(BF)
    mark_k = marks[:, width:].astype(BF)

    bias = jnp.concatenate([bias_q, jnp.zeros_like(bias_q), bias_v])
    qkv = (jnp.dot(tokens, w_qkv, preferred_element_type=F32) + bias).astype(BF)
    value_ext = extended(qkv[:, 2 * width :], radius, window_rows)
    value_ext, mark_q, mark_k = lax.optimization_barrier((value_ext, mark_q, mark_k))

    def one_col(col):
        return pl.BlockSpec((tok_count, width), lambda i: (0, col))

    stats = pl.pallas_call(
        lambda *refs: landmark_kernel(docs, scale, *refs),
        grid=(1,),
        in_specs=[smem, fixed(mark_count, width), one_col(1), one_col(2)],
        out_specs=fixed(mark_count, width + 128),
        out_shape=shaped((mark_count, width + 128), BF),
        scratch_shapes=[
            pltpu.VMEM((width, 128), F32), pltpu.VMEM((width, 128), F32),
            pltpu.VMEM((width, GROUP), F32),
        ],
        compiler_params=params,
        name="landmark",
    )(bounds, mark_q, qkv, qkv)
    far_count = seq_count // 4
    own_count = -(-heads // far_count)
    own_doc = (me % 2) * 2 + (me // 2) % 2
    own_at = (me // 4) * own_count * size
    spare = far_count * own_count * size - width

    def own_heads(array):
        array = jnp.pad(array, ((0, 0), (0, spare)))
        array = lax.dynamic_slice_in_dim(array, own_at, own_count * size, 1)
        return array.reshape(LAND, own_count, size).transpose(1, 0, 2)

    def of_doc(array):
        return lax.dynamic_slice_in_dim(array, own_doc * LAND, LAND, 0)

    mine, other = halves(stats, 1)
    stats = join(mine, swap(other, "seq", 1))
    stats, later_q, later_k = lax.optimization_barrier((stats, mark_q, mark_k))
    own_q = own_heads(of_doc(later_q)).astype(F32)
    own_k = own_heads(of_doc(later_k)).astype(F32)
    square = (own_count, LAND, LAND)
    own_inverse, kernel, saved = pl.pallas_call(
        lambda *refs: pinv_kernel(scale, *refs),
        out_shape=(
            shaped(square, F32), shaped(square, F32),
            shaped((4 * NS_ITERS * own_count, LAND, LAND), F32),
        ),
        name="pinv",
    )(own_q, own_k)
    inverse = own_inverse.transpose(1, 0, 2).reshape(LAND, own_count * size).astype(BF)
    mine, other = halves(stats, 2)
    stats = join(mine, swap(other, "seq", 2))
    for i in range(2, seq_count.bit_length() - 1):
        other = swap(jnp.concatenate([stats, inverse], 1), "seq", 1 << i)
        stats = join(stats, other[:, : width + 128])
        other = other[:, width + 128 :]
        inverse = jnp.where(
            (me >> i) % 2 == 0,
            jnp.concatenate([inverse, other], 1),
            jnp.concatenate([other, inverse], 1),
        )
    inverse = inverse[:, :width]
    mix = pl.pallas_call(
        mix_kernel, out_shape=shaped((LAND, width + 128), BF), name="mix"
    )(inverse, stats)
    mix = seq_whole(mix)

    taps = jnp.pad(conv_taps, ((0, 0), (0, GROUP - tap_count)))
    mark_spec = fixed(mark_count, width)
    mixed, probs = pl.pallas_call(
        lambda *refs: token_kernel(docs, scale, *refs),
        grid=(blocks,),
        in_specs=[
            smem, part(0), fixed(window_rows, width), mark_spec, mark_spec, fixed(heads, GROUP)
        ],
        out_specs=(tok_spec, pl.BlockSpec((width, BLOCK), lambda i: (0, i))),
        out_shape=(shaped((tok_count, width), BF), shaped((width, tok_count), BF)),
        scratch_shapes=[pltpu.VMEM((heads * SUB, GROUP), BF), pltpu.VMEM((BLOCK, width), F32)],
        compiler_params=params,
        name="token",
    )(bounds, qkv, value_ext, mark_k, mix, taps)

    hidden = w_up.shape[1]
    vectors = jnp.stack([bias_out, norm1_gain, norm1_bias, bias_down, norm2_gain, norm2_bias])
    vectors = jnp.pad(vectors, ((0, 2), (0, 0)))
    wide_spec = pl.BlockSpec((FFN_BLOCK, hidden), lambda i: (i, 0))
    ffn_spec = pl.BlockSpec((FFN_BLOCK, width), lambda i: (i, 0))
    narrow = shaped((tok_count, width), BF)
    (
        result, grad_one, active, grad_upper, hidden_low, grad_low_two, grad_low_one,
        grad_mixed, sums, sum_up,
    ) = pl.pallas_call(
        ffn_kernel,
        grid=(tok_count // FFN_BLOCK,),
        in_specs=[
            ffn_spec, ffn_spec, ffn_spec, fixed(width, width), fixed(width, hidden),
            fixed(hidden, width), fixed(8, width), fixed(8, hidden),
        ],
        out_specs=(
            ffn_spec, ffn_spec, wide_spec, wide_spec, ffn_spec, ffn_spec, ffn_spec, ffn_spec,
            fixed(8, width), fixed(8, hidden),
        ),
        out_shape=(
            shaped((tok_count, width), F32), shaped((tok_count, width), F32),
            shaped((tok_count, hidden), BF), shaped((tok_count, hidden), BF),
            narrow, narrow, narrow, narrow, shaped((8, width), F32), shaped((8, hidden), F32),
        ),
        scratch_shapes=[pltpu.VMEM((FFN_BLOCK, hidden), BF)],
        compiler_params=pltpu.CompilerParams(vmem_limit_bytes=58 * 1024 * 1024),
        name="ffn",
    )(
        tokens, mixed, cotangent[0], w_out, w_up, w_down, vectors,
        jnp.broadcast_to(bias_up[None, :], (8, hidden)),
    )

    grad_queries, grad_mix, grad_mk = pl.pallas_call(
        lambda *refs: token_back_kernel(docs, scale, *refs),
        grid=(blocks,),
        in_specs=[
            smem, part(0), tok_spec, pl.BlockSpec((width, BLOCK), lambda i: (0, i)), mark_spec,
            mark_spec,
        ],
        out_specs=(tok_spec, mark_spec, mark_spec),
        out_shape=(
            shaped((tok_count, width), BF), shaped((mark_count, width), F32),
            shaped((mark_count, width), F32),
        ),
        scratch_shapes=[pltpu.VMEM((BLOCK, width), F32)],
        compiler_params=params,
        name="token_back",
    )(bounds, qkv, grad_mixed, probs, mark_k, mix)
    grad_w_down = lax.dot_general(active, grad_low_two, rows_in, preferred_element_type=F32)
    grad_w_up = lax.dot_general(hidden_low, grad_upper, rows_in, preferred_element_type=F32)
    grad_w_out = lax.dot_general(mixed, grad_low_one, rows_in, preferred_element_type=F32)
    grad_mix, grad_w_down, grad_w_up, grad_w_out = lax.optimization_barrier(
        (grad_mix.astype(BF), grad_w_down.astype(BF), grad_w_up.astype(BF), grad_w_out.astype(BF))
    )
    sum_w_down, sum_w_up, sum_w_out = lax.psum(
        (grad_w_down, grad_w_up, grad_w_out), ("row", "seq")
    )

    def remaining(grad_mix, grad_mk, stats, mix):
        grad_mix = seq_quarter(grad_mix.astype(BF), add_join)

        grad_ext = extended(grad_mixed, radius, window_rows)
        grad_conv, products = pl.pallas_call(
            lambda *refs: conv_back_kernel(docs, *refs),
            grid=(blocks,),
            in_specs=[
                smem, fixed(window_rows, width), fixed(window_rows, width), fixed(heads, GROUP)
            ],
            out_specs=(tok_spec, fixed(16, GROUP)),
            out_shape=(shaped((tok_count, width), F32), shaped((16, GROUP), F32)),
            scratch_shapes=[
                pltpu.VMEM((heads * SUB, GROUP), BF), pltpu.VMEM((heads * SUB, GROUP), F32)
            ],
            compiler_params=params,
            name="conv_back",
        )(bounds, grad_ext, value_ext, jnp.pad(conv_taps[:, ::-1], ((0, 0), (0, GROUP - tap_count))))
        grad_conv_taps = products[:heads, SUB - 1 : SUB - 1 + tap_count]
        grad_mix, grad_conv, grad_conv_taps = lax.optimization_barrier(
            (grad_mix, grad_conv, grad_conv_taps)
        )

        grad_avg = pl.pallas_call(
            mix_back_kernel, out_shape=shaped((LAND, width + 128), BF), name="mix_back"
        )(inverse, stats, grad_mix)
        grad_avg = seq_whole(grad_avg)
        lane_spec = pl.BlockSpec((mark_count, 128), lambda i: (0, width // 128))
        grad_keys, grad_values, grad_mq = pl.pallas_call(
            lambda *refs: landmark_back_kernel(docs, scale, *refs),
            grid=(blocks,),
            in_specs=[
                smem, part(1), part(2), tok_spec, mark_spec, mark_spec, lane_spec, lane_spec
            ],
            out_specs=(tok_spec, tok_spec, mark_spec),
            out_shape=(
                shaped((tok_count, width), BF), shaped((tok_count, width), BF),
                shaped((mark_count, width), F32),
            ),
            scratch_shapes=[pltpu.VMEM((BLOCK, width), F32), pltpu.VMEM((BLOCK, width), F32)],
            compiler_params=params,
            name="landmark_back",
        )(bounds, qkv, qkv, grad_conv, mark_q, grad_avg, mix, grad_avg)


        def weight_grad(grads):
            return lax.dot_general(tokens, grads, rows_in, preferred_element_type=F32)

        early = weight_grad(grad_values).astype(BF)
        grad_mix, early = lax.optimization_barrier((grad_mix, early))
        early = advance(begin(early, ORDER, ORDER), 1)
        grad_mq_small, grad_mk_small = pl.pallas_call(
            lambda *refs: pinv_back_kernel(scale, *refs),
            out_shape=(shaped(square, F32), shaped(square, F32)),
            name="pinv_back",
        )(own_q, own_k, kernel, saved, own_heads(grad_mix), own_heads(stats[:, :width]))

        grad_mq_small, (early,) = tied(grad_mq_small, [early])
        early = advance(early, 1)

        def with_small(array, small):
            small = small.transpose(1, 0, 2).reshape(LAND, own_count * size)
            small = lax.dynamic_update_slice_in_dim(
                jnp.zeros((LAND, width + spare), F32), small, own_at, 1
            )[:, :width]
            first = own_doc * LAND
            rows = lax.dynamic_slice_in_dim(array, first, LAND, 0) + small
            return lax.dynamic_update_slice_in_dim(array, rows, first, 0)

        grad_mq = with_small(grad_mq, grad_mq_small)
        grad_mk = with_small(grad_mk, grad_mk_small)
        grad_marks = jnp.concatenate([grad_mq, grad_mk], axis=1).astype(BF)
        mark_back = lax.dot_general(
            grad_marks, w_qkv[:, : 2 * width], cols_in, preferred_element_type=F32
        ) / counts
        mark_back = mark_back.astype(BF)

        grad_bias_q = jnp.sum(grad_queries.astype(F32), axis=0) + jnp.sum(grad_mq, axis=0)
        grad_bias_v = jnp.sum(grad_values.astype(F32), axis=0)
        mark_grad_q = lax.dot_general(
            mean_in, grad_marks[:, :width], rows_in, preferred_element_type=F32
        )
        mark_grad_k = lax.dot_general(
            mean_in, grad_marks[:, width:], rows_in, preferred_element_type=F32
        )
        others = jnp.concatenate(
            [
                sum_up[0].reshape(hidden // width, width),
                grad_bias_q[None],
                grad_bias_v[None],
                jnp.pad(grad_conv_taps.reshape(1, -1), ((0, 0), (0, width - heads * tap_count))),
                jnp.zeros((4 - hidden // width + 1, width), F32),
            ],
            0,
        )
        spare_rows = width // 6
        small = jnp.concatenate([sums, others], 0).astype(BF)
        below = width + 2 * spare_rows - small.shape[0]
        late = jnp.pad(small, ((width, below), (0, 0)))
        late = lax.dynamic_update_slice_in_dim(
            late, (weight_grad(grad_queries) + mark_grad_q).astype(BF), 0, 0
        )
        late = lax.dynamic_update_slice_in_dim(
            late, (weight_grad(grad_keys) + mark_grad_k).astype(BF), width + spare_rows, 0
        )
        late = begin(late, ORDER, ORDER)
        grad_projected = jnp.concatenate([grad_queries, grad_keys, grad_values], axis=1)
        grad_input = grad_one + lax.dot_general(
            grad_projected, w_qkv, cols_in, preferred_element_type=F32
        )
        for step in seq_steps():
            mark_back = step(mark_back)
            early, late = advance(early, 1), advance(late, 1)
            (mark_back, grad_input), (early, late) = tied((mark_back, grad_input), [early, late])
        return early[0], late[0], mark_back, grad_input

    plan = stages(ORDER)
    sent = len(seq_steps())

    def rows_left(rows, done):
        return rows >> min(done, 2 * len(plan) - done)

    early_rows = rows_left(width, sent + 2)
    late_rows = rows_left(2 * width + width // 3, sent)

    def nothing(*unused):
        return tuple(
            jnp.zeros((rows, width), BF) for rows in (early_rows, late_rows, mark_count)
        ) + (jnp.zeros((tok_count, width), F32),)

    early, late, mark_back, grad_input = lax.cond(
        lengths[0] > 0, remaining, nothing, grad_mix, grad_mk, stats, mix
    )
    early, late = (early, plan, plan, sent + 2), (late, plan, plan, sent)
    last = 2 * len(plan) - 1
    late = advance(late, 2)
    (sum_w_down, sum_w_up, sum_w_out), (late,) = tied(
        (sum_w_down.astype(F32), sum_w_up.astype(F32), sum_w_out.astype(F32)), [late]
    )
    early, late = advance(early, last - early[3]), advance(late, last - late[3])
    grad_input = grad_input + lax.dot_general(
        onehot, mark_back, rows_in, preferred_element_type=F32
    )
    grad_input, (early, late) = tied(grad_input, [early, late])
    early, early_other = last_swap(early)[:2]
    late, late_other = last_swap(late)[:2]
    sum_w_qkv = settle_qkv(late, late_other, early, early_other, width)
    first_core = me % 2 == 0
    flat = jnp.where(first_core, late[width:], late_other[width:])[:16].astype(F32)
    at = sums.shape[0] + hidden // width
    pieces = [
        flat[at], flat[at + 1], flat[at + 2, : heads * tap_count], flat[5], flat[3], flat[4],
        flat[sums.shape[0] : at].reshape(hidden), flat[2], flat[0], flat[1],
    ]
    return (
        result[None], grad_input[None], sum_w_qkv, pieces[0], pieces[1],
        pieces[2].reshape(heads, tap_count), sum_w_out, pieces[3], pieces[4], pieces[5],
        sum_w_up, pieces[6], sum_w_down, pieces[7], pieces[8], pieces[9],
    )


def solution(mesh):
    whole, tokens = P(), P("row", "seq", None)
    return jax.shard_map(
        per_device,
        mesh=mesh,
        in_specs=(tokens, P("row", None)) + (whole,) * 14 + (tokens,),
        out_specs=(tokens, tokens) + (whole,) * 14,
        check_vma=False,
    )
```

```python
import math

import jax
import jax.numpy as jnp
from jax import lax
from jax.experimental import pallas as pl
from jax.experimental.pallas import tpu as pltpu
from jax.sharding import PartitionSpec as P

LAND = 64
NS_ITERS = 6
HIGH = lax.Precision.HIGHEST
NEGATIVE = -1e30
BF = jnp.bfloat16
F32 = jnp.float32

BLOCK = 256
GROUP = 256
SUB = 128
TAPS = 33
FFN_BLOCK = 256
ORDER = ("row", "near", "far")


def swap(array, axis, bit):
    count = lax.axis_size(axis)
    return lax.ppermute(array, axis, [(i, i ^ bit) for i in range(count)])


def add_parts(parts):
    total = parts[0].astype(F32)
    for part in parts[1:]:
        total = total + part.astype(F32)
    return total


def halves(array, bit):
    rows = array.shape[0] // 2
    side = (lax.axis_index("seq") // bit) % 2
    mine = lax.dynamic_slice_in_dim(array, side * rows, rows, 0)
    other = lax.dynamic_slice_in_dim(array, (1 - side) * rows, rows, 0)
    return mine, other


def seq_quarter(array, join):
    bits = [1 << i for i in range(lax.axis_size("seq").bit_length() - 1)]
    for bit in bits[:2]:
        mine, other = halves(array, bit)
        array = join(mine, swap(other, "seq", bit))
    for bit in bits[2:]:
        array = join(array, swap(array, "seq", bit))
    return array


def paired(array, axis, bit, dim):
    other = swap(array, axis, bit)
    side = (lax.axis_index(axis) // bit) % 2
    return jnp.where(
        side == 0,
        jnp.concatenate([array, other], dim),
        jnp.concatenate([other, array], dim),
    )


def seq_whole(array):
    return paired(paired(array, "seq", 2, 0), "seq", 1, 0)


def seq_steps():
    bits = [1 << i for i in range(lax.axis_size("seq").bit_length() - 1)]

    def halve(bit):
        def step(array):
            mine, other = halves(array, bit)
            return add_join(mine, swap(other, "seq", bit))

        return step

    def whole(bit):
        return lambda array: add_join(array, swap(array, "seq", bit))

    def double(bit):
        return lambda array: paired(array, "seq", bit, 0)

    return (
        [halve(bit) for bit in bits[:2]]
        + [whole(bit) for bit in bits[2:]]
        + [double(bit) for bit in reversed(bits[:2])]
    )


def add_join(first, second):
    return (first.astype(F32) + second.astype(F32)).astype(BF)


def stages(order):
    row = [("row", 1 << i) for i in range(lax.axis_size("row").bit_length() - 1)]
    seq = [[("seq", 1 << i)] for i in range(lax.axis_size("seq").bit_length() - 1)]
    named = {"core": seq[0], "row": row, "near": seq[1], "far": seq[2], "rest": sum(seq[3:], [])}
    return sum([named[name] for name in ("core",) + order + ("rest",)], [])


def begin(array, down, back):
    return array, stages(down), stages(back), 0


def advance(state, steps):
    held, down, back, done = state
    for step in range(done, min(done + steps, 2 * len(down))):
        if step < len(down):
            axis, bit = down[step]
            half = held.shape[0] // 2
            side = (lax.axis_index(axis) // bit) % 2
            mine = lax.dynamic_slice_in_dim(held, side * half, half, 0)
            other = lax.dynamic_slice_in_dim(held, (1 - side) * half, half, 0)
            held = mine.astype(F32) + swap(other, axis, bit).astype(F32)
            held = held.astype(BF)
        else:
            axis, bit = back[2 * len(down) - 1 - step]
            held = paired(held, axis, bit, 0)
    return held, down, back, min(done + steps, 2 * len(down))


def double_beside(state, values):
    held, down, back, done = state
    axis, bit = back[2 * len(down) - 1 - done]
    other, values = lax.optimization_barrier((swap(held, axis, bit), values))
    side = (lax.axis_index(axis) // bit) % 2
    held = jnp.where(
        side == 0,
        jnp.concatenate([held, other], 0),
        jnp.concatenate([other, held], 0),
    )
    return (held, down, back, done + 1), values


def last_swap(state):
    down, back = state[1], state[2]
    held = advance(state, 2 * len(down) - 1 - state[3])[0]
    return held, swap(held, *down[0]), down, back


def tied(values, states):
    values, helds = lax.optimization_barrier((values, [state[0] for state in states]))
    return values, [(held,) + state[1:] for held, state in zip(helds, states)]


def extended(cells, width, rows):
    count = lax.axis_size("seq")
    head = cells[:width]
    tail = cells[-width:]
    return jnp.concatenate(
        [
            lax.ppermute(tail, "seq", [(i, i + 1) for i in range(count - 1)]),
            cells,
            lax.ppermute(head, "seq", [(i + 1, i) for i in range(count - 1)]),
            jnp.zeros((rows - cells.shape[0] - 2 * width, cells.shape[1]), cells.dtype),
        ],
        axis=0,
    )


def dot_nn(a, b):
    return jnp.dot(a, b, preferred_element_type=F32)


def dot_nt(a, b):
    return lax.dot_general(a, b, (((1,), (1,)), ((), ())), preferred_element_type=F32)


def dot_tn(a, b):
    return lax.dot_general(a, b, (((0,), (0,)), ((), ())), preferred_element_type=F32)


def iota(shape, dim):
    return lax.broadcasted_iota(jnp.int32, shape, dim)


def spread(block):
    rows = block.shape[0]
    tall = jnp.concatenate([block] * 4, axis=0).astype(F32)
    shape = (4 * rows, GROUP)
    keep = iota(shape, 0) // rows == iota(shape, 1) // LAND
    return jnp.where(keep, tall, 0.0).astype(BF)


def gathered(square):
    rows = square.shape[0] // 4
    lane = iota((rows, GROUP), 1) // LAND
    out = square[:rows]
    for head in range(1, 4):
        out = jnp.where(lane == head, square[head * rows : (head + 1) * rows], out)
    return out


def by_head(columns, first, shape):
    lane = iota(shape, 1)
    out = jnp.zeros(shape, F32)
    for head, column in enumerate(columns):
        out = jnp.where((lane % 16 == first + head) & (lane < 48), column, out)
    return out


def split_three(cells):
    lane = iota(cells.shape, 1)
    high = cells.astype(BF).astype(F32)
    mid = (cells - high).astype(BF).astype(F32)
    low = cells - high - mid
    return jnp.where(lane < 16, high, jnp.where(lane < 32, mid, low)).astype(BF)


def merge_three(cells):
    cells = cells.astype(F32)
    return cells + pltpu.roll(cells, 112, 1) + pltpu.roll(cells, 96, 1)


def head_lanes(heads, width):
    return (iota((128, width), 0) == iota((128, width), 1) // LAND).astype(F32)


def doc_of(places, bounds, docs):
    out = (places >= bounds[2 * docs - 1]).astype(jnp.int32)
    for doc in range(docs):
        out = out + (places >= bounds[doc]).astype(jnp.int32)
    return out


def landmark_kernel(docs, scale, bounds, mq_ref, k_ref, v_ref, out_ref, max_s, sum_s, acc_s):
    tokens, width = k_ref.shape
    groups = width // GROUP
    heads = width // LAND
    out_ref[:, :width] = jnp.zeros((docs * LAND, width), BF)
    empty = jnp.full((docs * LAND, 128), NEGATIVE, F32)
    out_ref[:, width:] = jnp.where(iota(empty.shape, 1) < 48, split_three(empty).astype(F32), 0.0).astype(BF)
    for doc in range(docs):
        low = jnp.clip(bounds[doc], 0, tokens)
        high = jnp.clip(bounds[docs + doc], 0, tokens)
        rows = slice(doc * LAND, (doc + 1) * LAND)

        @pl.when(high > low)
        def _():
            max_s[...] = jnp.full(max_s.shape, NEGATIVE, F32)
            sum_s[...] = jnp.zeros(sum_s.shape, F32)
            acc_s[...] = jnp.zeros(acc_s.shape, F32)
            wide = [
                spread(mq_ref[rows, g * GROUP : (g + 1) * GROUP]) for g in range(groups)
            ]

            ones = jnp.ones((BLOCK, 128), BF)

            def step(block, carry):
                first = pl.multiple_of(block * BLOCK, BLOCK)
                at = pl.ds(first, BLOCK)
                place = iota((1, BLOCK), 1) + first
                valid = (place >= low) & (place < high)
                for g in range(groups):
                    cols = slice(g * GROUP, (g + 1) * GROUP)
                    scores = dot_nt(wide[g], k_ref[at, cols]) * scale
                    scores = jnp.where(valid, scores, NEGATIVE)
                    old = max_s[cols, :]
                    top = jnp.maximum(old, jnp.max(scores, axis=1, keepdims=True))
                    weights = jnp.exp(scores - twice(top)).astype(BF)
                    shrink = jnp.exp(old - top)
                    max_s[cols, :] = top
                    sum_s[cols, :] = sum_s[cols, :] * shrink + dot_nn(weights, ones)
                    acc_s[cols, :] = acc_s[cols, :] * twice(shrink) + dot_nn(weights, v_ref[at, cols])
                return carry

            lax.fori_loop(low // BLOCK, (high + BLOCK - 1) // BLOCK, step, 0)
            columns = []
            for g in range(groups):
                cols = slice(g * GROUP, (g + 1) * GROUP)
                sums = sum_s[cols, :]
                out_ref[rows, cols] = gathered(acc_s[cols, :] / twice(sums)).astype(BF)
                level = max_s[cols, :] + jnp.log(sums)
                columns += [level[h * LAND : (h + 1) * LAND] for h in range(4)]
            out_ref[rows, width:] = split_three(by_head(columns, 0, (LAND, 128)))


def twice(cells):
    return jnp.concatenate([cells, cells], axis=1)


def join_kernel(a_ref, b_ref, out_ref):
    width = a_ref.shape[1] - 128
    heads = width // LAND
    first, second = merge_three(a_ref[:, width:]), merge_three(b_ref[:, width:])
    lane = iota(first.shape, 1)
    first = jnp.where(lane < heads, first, 0.0)
    second = jnp.where(lane < heads, second, 0.0)
    top = jnp.maximum(first, second)
    exp_a, exp_b = jnp.exp(first - top), jnp.exp(second - top)
    both = exp_a + exp_b
    level = top + jnp.log(both)
    pick = head_lanes(heads, width).astype(BF)
    share = exp_b / both
    high = share.astype(BF)
    low = (share - high.astype(F32)).astype(BF)
    share = dot_nn(jnp.concatenate([high, low], 1), jnp.concatenate([pick, pick], 0))
    from_a, from_b = a_ref[:, :width].astype(F32), b_ref[:, :width].astype(F32)
    out_ref[:, :width] = (from_a + share * (from_b - from_a)).astype(BF)
    level = jnp.where(lane < heads, level, 0.0)
    level = level + pltpu.roll(level, 16, 1) + pltpu.roll(level, 32, 1)
    out_ref[:, width:] = split_three(level)


def join(first, second):
    return pl.pallas_call(
        join_kernel, out_shape=jax.ShapeDtypeStruct(first.shape, BF), name="join"
    )(first, second)


def mix_kernel(inv_ref, stat_ref, mix_ref):
    width = stat_ref.shape[1] - 128
    for g in range(width // GROUP):
        cols = slice(g * GROUP, (g + 1) * GROUP)
        mix_ref[:, cols] = dot_nn(inv_ref[:, cols], spread(stat_ref[:, cols])).astype(BF)
    mix_ref[:, width:] = stat_ref[:, width:]


def mix_back_kernel(inv_ref, stat_ref, grad_ref, out_ref):
    width = stat_ref.shape[1] - 128
    columns = []
    for g in range(width // GROUP):
        cols = slice(g * GROUP, (g + 1) * GROUP)
        grad = gathered(dot_tn(inv_ref[:, cols], grad_ref[:, cols]))
        out_ref[:, cols] = grad.astype(BF)
        product = grad * stat_ref[:, cols].astype(F32)
        lane = iota(product.shape, 1) // LAND
        for h in range(4):
            columns.append(jnp.sum(jnp.where(lane == h, product, 0.0), axis=1, keepdims=True))
    out_ref[:, width:] = split_three(by_head(columns, 0, (LAND, 128)))


def make_band(taps_ref, band_s):
    for head in range(taps_ref.shape[0]):
        row = jnp.broadcast_to(taps_ref[head : head + 1, :], (SUB, GROUP))
        band_s[head * SUB : (head + 1) * SUB, :] = pltpu.roll(row, 0, 1, stride=1, stride_axis=0).astype(BF)


def same_doc(first, bounds, docs, radius):
    rows = iota((SUB, GROUP), 0) + first
    cols = iota((SUB, GROUP), 1) + (first - radius)
    return doc_of(rows, bounds, docs) == doc_of(cols, bounds, docs)


def token_kernel(
    docs, scale, bounds, q_ref, v_ref, mk_ref, mix_ref, taps_ref, mixed_ref, probs_ref, band_s, sum_s
):
    width = q_ref.shape[1]
    groups = width // GROUP
    radius = (TAPS - 1) // 2
    first = pl.program_id(0) * BLOCK

    @pl.when(pl.program_id(0) == 0)
    def _():
        make_band(taps_ref, band_s)

    for sub in range(BLOCK // SUB):
        start = pl.multiple_of(first + sub * SUB, SUB)
        same = same_doc(start, bounds, docs, radius)
        same = jnp.where(jnp.concatenate([same] * 4, axis=0), 1.0, 0.0).astype(BF)
        for g in range(groups):
            cols = slice(g * GROUP, (g + 1) * GROUP)
            band = band_s[g * 4 * SUB : (g + 1) * 4 * SUB, :] * same
            res = dot_nn(band, v_ref[pl.ds(start, GROUP), cols])
            sum_s[sub * SUB : (sub + 1) * SUB, cols] = gathered(res)
    probs_ref[...] = jnp.zeros(probs_ref.shape, BF)
    for doc in range(docs):
        low, high = bounds[doc], bounds[docs + doc]
        rows = slice(doc * LAND, (doc + 1) * LAND)

        @pl.when((high > first) & (low < first + BLOCK))
        def _():
            place = iota((1, BLOCK), 1) + first
            valid = (place >= low) & (place < high)
            for g in range(groups):
                cols = slice(g * GROUP, (g + 1) * GROUP)
                scores = dot_nt(spread(mk_ref[rows, cols]), q_ref[:, cols]) * scale
                scores = scores.reshape(4, LAND, BLOCK)
                weights = jnp.exp(scores - jnp.max(scores, axis=1, keepdims=True))
                probs = weights / jnp.sum(weights, axis=1, keepdims=True)
                probs = jnp.where(valid, probs.reshape(GROUP, BLOCK), 0.0).astype(BF)
                probs_ref[cols, :] = probs_ref[cols, :] + probs
                sum_s[:, cols] = sum_s[:, cols] + dot_tn(probs, spread(mix_ref[rows, cols]))

    mixed_ref[...] = sum_s[...].astype(BF)


def token_back_kernel(
    docs, scale, bounds, q_ref, gm_ref, probs_ref, mk_ref, mix_ref, gq_ref, gmix_ref, gmk_ref, gq_s
):
    width = q_ref.shape[1]
    groups = width // GROUP
    first = pl.program_id(0) * BLOCK

    @pl.when(pl.program_id(0) == 0)
    def _():
        gmix_ref[...] = jnp.zeros(gmix_ref.shape, F32)
        gmk_ref[...] = jnp.zeros(gmk_ref.shape, F32)

    gq_s[...] = jnp.zeros(gq_s.shape, F32)
    for doc in range(docs):
        low, high = bounds[doc], bounds[docs + doc]
        rows = slice(doc * LAND, (doc + 1) * LAND)

        @pl.when((high > first) & (low < first + BLOCK))
        def _():
            place = iota((1, BLOCK), 1) + first
            valid = (place >= low) & (place < high)
            for g in range(groups):
                cols = slice(g * GROUP, (g + 1) * GROUP)
                probs = jnp.where(valid, probs_ref[cols, :].astype(F32), 0.0)
                gmix_ref[rows, cols] += gathered(dot_nn(probs.astype(BF), gm_ref[:, cols]))
                grad = dot_nt(spread(mix_ref[rows, cols]), gm_ref[:, cols])
                heavy = (probs * grad).reshape(4, LAND, BLOCK)
                shared = probs.reshape(4, LAND, BLOCK) * jnp.sum(heavy, axis=1, keepdims=True)
                grad = ((heavy - shared).reshape(GROUP, BLOCK) * scale).astype(BF)
                gmk_ref[rows, cols] += gathered(dot_nn(grad, q_ref[:, cols]))
                gq_s[:, cols] += dot_tn(grad, spread(mk_ref[rows, cols]))

    gq_ref[...] = gq_s[...].astype(BF)


def conv_back_kernel(docs, bounds, gm_ref, v_ref, taps_ref, out_ref, sum_ref, band_s, prod_s):
    width = gm_ref.shape[1]
    groups = width // GROUP
    radius = (TAPS - 1) // 2
    first = pl.program_id(0) * BLOCK

    @pl.when(pl.program_id(0) == 0)
    def _():
        make_band(taps_ref, band_s)
        prod_s[...] = jnp.zeros(prod_s.shape, F32)

    for sub in range(BLOCK // SUB):
        start = pl.multiple_of(first + sub * SUB, SUB)
        same = same_doc(start, bounds, docs, radius)
        same = jnp.where(jnp.concatenate([same] * 4, axis=0), 1.0, 0.0)
        for g in range(groups):
            cols = slice(g * GROUP, (g + 1) * GROUP)
            tall = slice(g * 4 * SUB, (g + 1) * 4 * SUB)
            band = band_s[tall, :] * same.astype(BF)
            res = dot_nn(band, gm_ref[pl.ds(start, GROUP), cols])
            out_ref[sub * SUB : (sub + 1) * SUB, cols] = gathered(res)
            own = gm_ref[pl.ds(pl.multiple_of(start + radius, 16), SUB), cols]
            product = dot_nt(spread(own), v_ref[pl.ds(start, GROUP), cols])
            prod_s[tall, :] += product * same

    @pl.when(pl.program_id(0) == pl.num_programs(0) - 1)
    def _():
        flip = (iota((SUB, SUB), 0) + iota((SUB, SUB), 1) == SUB - 1).astype(F32).astype(BF)
        sum_ref[...] = jnp.zeros(sum_ref.shape, F32)
        for head in range(taps_ref.shape[0]):
            product = prod_s[head * SUB : (head + 1) * SUB, :]
            high = product.astype(BF)
            low = (product - high.astype(F32)).astype(BF)
            turned = pltpu.roll(dot_nn(flip, high) + dot_nn(flip, low), 0, 1, stride=1, stride_axis=0)
            sum_ref[head : head + 1, :] = jnp.sum(turned, axis=0, keepdims=True)


def ffn_kernel(
    x_ref, mixed_ref, cot_ref, w_out_ref, w_up_ref, w_down_ref, rows_ref, bias_up_ref,
    result_ref, grad_one_ref, active_ref, grad_up_ref, low_ref, low_two_ref, low_one_ref,
    grad_mixed_ref, sums_ref, sum_up_ref, slope_s,
):
    width = x_ref.shape[1]
    hidden = w_up_ref.shape[1]
    chunks = [slice(at, at + width) for at in range(0, hidden, width)]

    def row(i):
        return rows_ref[i : i + 1, :]

    @pl.when(pl.program_id(0) == 0)
    def _():
        sums_ref[...] = jnp.zeros(sums_ref.shape, F32)
        sum_up_ref[...] = jnp.zeros(sum_up_ref.shape, F32)

    def add_sum(i, cells):
        sums_ref[i : i + 1, :] += jnp.sum(cells, axis=0, keepdims=True)

    attended = dot_nn(mixed_ref[...], w_out_ref[...]) + row(0)
    norm_one, inverse_one = normalize(x_ref[...].astype(F32) + attended)
    hidden_one = norm_one * row(1) + row(2)
    hidden_low = hidden_one.astype(BF)
    low_ref[...] = hidden_low
    lowered = hidden_one + row(3)
    for cols in chunks:
        upper = dot_nn(hidden_low, w_up_ref[:, cols]) + bias_up_ref[:1, cols]
        active, slope = gelu_both(upper)
        active = active.astype(BF)
        active_ref[:, cols] = active
        slope_s[:, cols] = slope.astype(BF)
        lowered = lowered + dot_nn(active, w_down_ref[cols, :])
    norm_two, inverse_two = normalize(lowered)
    result_ref[...] = norm_two * row(4) + row(5)
    upstream = cot_ref[...].astype(F32)
    add_sum(0, upstream * norm_two)
    add_sum(1, upstream)
    grad_two = norm_back(upstream * row(4), norm_two, inverse_two)
    low_two = grad_two.astype(BF)
    low_two_ref[...] = low_two
    add_sum(2, low_two.astype(F32))
    grad_hidden = grad_two
    for cols in chunks:
        grad_up = dot_nt(low_two, w_down_ref[cols, :]) * slope_s[:, cols].astype(F32)
        grad_up = grad_up.astype(BF)
        grad_up_ref[:, cols] = grad_up
        sum_up_ref[:1, cols] += jnp.sum(grad_up.astype(F32), axis=0, keepdims=True)
        grad_hidden = grad_hidden + dot_nt(grad_up, w_up_ref[:, cols])
    add_sum(3, grad_hidden * norm_one)
    add_sum(4, grad_hidden)
    grad_one = norm_back(grad_hidden * row(1), norm_one, inverse_one)
    grad_one_ref[...] = grad_one
    low_one = grad_one.astype(BF)
    low_one_ref[...] = low_one
    add_sum(5, low_one.astype(F32))
    grad_mixed_ref[...] = dot_nt(low_one, w_out_ref[...]).astype(BF)


def landmark_back_kernel(
    docs, scale, bounds, k_ref, v_ref, conv_ref, mq_ref, grad_ref, level_ref, dots_ref,
    gk_ref, gv_ref, gmq_ref, gk_s, gv_s,
):
    width = k_ref.shape[1]
    groups = width // GROUP
    first = pl.program_id(0) * BLOCK

    @pl.when(pl.program_id(0) == 0)
    def _():
        gmq_ref[...] = jnp.zeros(gmq_ref.shape, F32)

    gk_s[...] = jnp.zeros(gk_s.shape, F32)
    gv_s[...] = conv_ref[...]
    for doc in range(docs):
        low, high = bounds[doc], bounds[docs + doc]
        rows = slice(doc * LAND, (doc + 1) * LAND)

        @pl.when((high > first) & (low < first + BLOCK))
        def _():
            place = iota((1, BLOCK), 1) + first
            valid = (place >= low) & (place < high)

            level, dots = merge_three(level_ref[rows, :]), merge_three(dots_ref[rows, :])

            def column(lanes, g):
                return jnp.concatenate(
                    [lanes[:, 4 * g + h : 4 * g + h + 1] for h in range(4)], axis=0
                )

            for g in range(groups):
                cols = slice(g * GROUP, (g + 1) * GROUP)
                wide_q, wide_g = spread(mq_ref[rows, cols]), spread(grad_ref[rows, cols])
                scores = dot_nt(wide_q, k_ref[:, cols]) * scale - column(level, g)
                probs = jnp.exp(jnp.where(valid, scores, NEGATIVE))
                grad = dot_nt(wide_g, v_ref[:, cols]) - column(dots, g)
                grad = (probs * grad * scale).astype(BF)
                gv_s[:, cols] += dot_tn(probs.astype(BF), wide_g)
                gk_s[:, cols] += dot_tn(grad, wide_q)
                gmq_ref[rows, cols] += gathered(dot_nn(grad, k_ref[:, cols]))

    gk_ref[...] = gk_s[...].astype(BF)
    gv_ref[...] = gv_s[...].astype(BF)


def gelu_both(upper):
    tangent = jnp.tanh(0.7978845608028654 * (upper + 0.044715 * upper * upper * upper))
    inner_slope = 0.7978845608028654 * (1.0 + 3.0 * 0.044715 * upper * upper)
    active = 0.5 * upper * (1.0 + tangent)
    slope = 0.5 * (1.0 + tangent) + 0.5 * upper * (1.0 - tangent * tangent) * inner_slope
    return active, slope


def normalize(residual):
    row_mean = jnp.mean(residual, axis=-1, keepdims=True)
    centered = residual - row_mean
    row_var = jnp.mean(centered * centered, axis=-1, keepdims=True)
    inverse_dev = lax.rsqrt(row_var + 1e-05)
    return (centered * inverse_dev, inverse_dev)


def norm_back(grad_normed, normed, inverse_dev):
    return inverse_dev * (
        grad_normed
        - jnp.mean(grad_normed, axis=-1, keepdims=True)
        - normed * jnp.mean(grad_normed * normed, axis=-1, keepdims=True)
    )


def dot_high(a, b, dims):
    return lax.dot_general(
        a, b, (dims, ((), ())), precision=HIGH, preferred_element_type=F32
    )


NN, NT, TN = ((1,), (0,)), ((1,), (1,)), ((0,), (0,))


def pinv_kernel(scale, q_ref, k_ref, inverse_ref, kernel_ref, saved_ref):
    count = q_ref.shape[0]
    eye = (iota((LAND, LAND), 0) == iota((LAND, LAND), 1)).astype(F32)
    kernels, inverses = [], []
    for p in range(count):
        scores = dot_high(q_ref[p], k_ref[p], NT) * scale
        weights = jnp.exp(scores - jnp.max(scores, axis=1, keepdims=True))
        kernel = weights / jnp.sum(weights, axis=1, keepdims=True)
        kernel_ref[p] = kernel
        kernels.append(kernel)
        largest = jnp.max(jnp.sum(kernel, axis=0, keepdims=True), axis=1, keepdims=True)
        inverses.append(kernel.T / largest)
    for sweep in range(NS_ITERS):
        products = [dot_high(kernels[p], inverses[p], NN) for p in range(count)]
        second = [
            15.0 * eye - dot_high(products[p], 7.0 * eye - products[p], NN) for p in range(count)
        ]
        third = [13.0 * eye - dot_high(products[p], second[p], NN) for p in range(count)]
        for p in range(count):
            at = (sweep * count + p) * 4
            saved_ref[at], saved_ref[at + 1] = inverses[p], products[p]
            saved_ref[at + 2], saved_ref[at + 3] = second[p], third[p]
        inverses = [0.25 * dot_high(inverses[p], third[p], NN) for p in range(count)]
    for p in range(count):
        inverse_ref[p] = inverses[p]


def pinv_back_kernel(scale, q_ref, k_ref, kernel_ref, saved_ref, grad_ref, avg_ref, gq_ref, gk_ref):
    count = q_ref.shape[0]
    each = range(count)
    eye = (iota((LAND, LAND), 0) == iota((LAND, LAND), 1)).astype(F32)
    grads = [dot_nt(grad_ref[p], avg_ref[p]) for p in each]
    kernels = [kernel_ref[p] for p in each]
    totals = [jnp.zeros((LAND, LAND), F32) for p in each]
    for sweep in reversed(range(NS_ITERS)):
        first = [(sweep * count + p) * 4 for p in each]
        inverses, products = [saved_ref[a] for a in first], [saved_ref[a + 1] for a in first]
        grad_third = [0.25 * dot_high(inverses[p], grads[p], TN) for p in each]
        nexts = [0.25 * dot_high(grads[p], saved_ref[first[p] + 3], NT) for p in each]
        grad_second = [-dot_high(products[p], grad_third[p], TN) for p in each]
        grad_product = [-dot_high(grad_third[p], saved_ref[first[p] + 2], NT) for p in each]
        grad_first = [-dot_high(products[p], grad_second[p], TN) for p in each]
        grad_product = [
            grad_product[p]
            - dot_high(grad_second[p], 7.0 * eye - products[p], NT)
            - grad_first[p]
            for p in each
        ]
        totals = [totals[p] + dot_high(grad_product[p], inverses[p], NT) for p in each]
        grads = [nexts[p] + dot_high(kernels[p], grad_product[p], TN) for p in each]
    for p in each:
        kernel = kernels[p]
        sums = jnp.sum(kernel, axis=0, keepdims=True)
        largest = jnp.max(sums, axis=1, keepdims=True)
        flipped = grads[p].T
        loss = jnp.sum(jnp.sum(flipped * kernel, axis=1, keepdims=True), axis=0, keepdims=True)
        at_top = (sums == largest).astype(F32)
        at_top = at_top / jnp.sum(at_top, axis=1, keepdims=True)
        grad = totals[p] + flipped / largest - at_top * (loss / (largest * largest))
        grad = kernel * (grad - jnp.sum(grad * kernel, axis=1, keepdims=True)) * scale
        gq_ref[p] = dot_high(grad, k_ref[p], NN)
        gk_ref[p] = dot_high(grad, q_ref[p], TN)


def settle_qkv_kernel(side_ref, late_ref, late_other_ref, early_ref, early_other_ref, out_ref):
    part = pl.program_id(0)
    own = jnp.where(part == 0, 0, 1) == side_ref[0]
    choices = [
        (late_ref, own & (part < 2)),
        (late_other_ref, jnp.logical_not(own) & (part < 2)),
        (early_ref, own & (part == 2)),
        (early_other_ref, jnp.logical_not(own) & (part == 2)),
    ]
    for ref, chosen in choices:

        @pl.when(chosen)
        def _():
            out_ref[...] = ref[...].astype(F32)


def settle_qkv(late, late_other, early, early_other, width):
    side = (lax.axis_index("seq") % 2).astype(jnp.int32).reshape(1)
    rows = width // 2

    def spec(used):
        return pl.BlockSpec((rows, width), lambda j, i, s: (jnp.where(used(j), i, 0), 0))

    return pl.pallas_call(
        settle_qkv_kernel,
        grid_spec=pltpu.PrefetchScalarGridSpec(
            num_scalar_prefetch=1,
            grid=(3, 2),
            in_specs=[spec(lambda j: j < 2), spec(lambda j: j < 2)] + [spec(lambda j: j == 2)] * 2,
            out_specs=pl.BlockSpec((rows, width), lambda j, i, s: (i, j)),
        ),
        out_shape=jax.ShapeDtypeStruct((width, 3 * width), F32),
        name="settle_qkv",
    )(side, late, late_other, early, early_other)


def per_device(
    inputs, doc_lengths, w_qkv, bias_q, bias_v, conv_taps, w_out, bias_out, norm1_gain,
    norm1_bias, w_up, bias_up, w_down, bias_down, norm2_gain, norm2_bias, cotangent,
):
    tokens = inputs[0]
    tok_count, width = tokens.shape
    heads, tap_count = conv_taps.shape
    size = width // heads
    radius = (tap_count - 1) // 2
    lengths = doc_lengths[0]
    docs = lengths.shape[0]
    mark_count = docs * LAND
    scale = 1.0 / math.sqrt(size)
    seq_count = lax.axis_size("seq")
    me = lax.axis_index("seq")
    row_first = me * tok_count
    ends = jnp.cumsum(lengths)
    starts = ends - lengths
    bounds = (jnp.concatenate([starts, ends]) - row_first).astype(jnp.int32)
    within = jnp.arange(LAND + 1, dtype=jnp.int32)
    edges = starts[:, None] + (within[None, :] * lengths[:, None] + LAND - 1) // LAND
    mark_low = edges[:, :-1].reshape(mark_count, 1)
    mark_high = edges[:, 1:].reshape(mark_count, 1)
    counts = (mark_high - mark_low).astype(F32)
    places = row_first + jnp.arange(tok_count, dtype=jnp.int32)[None, :]
    onehot = ((places >= mark_low) & (places < mark_high)).astype(BF)
    rows_in = (((0,), (0,)), ((), ()))
    cols_in = (((1,), (1,)), ((), ()))
    blocks = tok_count // BLOCK
    window_rows = tok_count + GROUP - SUB
    smem = pl.BlockSpec(memory_space=pltpu.SMEM)
    params = pltpu.CompilerParams(vmem_limit_bytes=40 * 1024 * 1024)
    tok_spec = pl.BlockSpec((BLOCK, width), lambda i: (i, 0))

    def part(col):
        return pl.BlockSpec((BLOCK, width), lambda i: (i, col))

    def fixed(*shape):
        return pl.BlockSpec(shape, lambda i: (0,) * len(shape))

    def shaped(shape, dtype):
        return jax.ShapeDtypeStruct(shape, dtype)

    means = jnp.dot(onehot, tokens, preferred_element_type=F32) / counts
    mean_in = seq_whole(seq_quarter(means.astype(BF), add_join))
    marks = jnp.dot(mean_in, w_qkv[:, : 2 * width], preferred_element_type=F32)
    mark_q = (marks[:, :width] + bias_q).astype(BF)
    mark_k = marks[:, width:].astype(BF)

    bias = jnp.concatenate([bias_q, jnp.zeros_like(bias_q), bias_v])
    qkv = (jnp.dot(tokens, w_qkv, preferred_element_type=F32) + bias).astype(BF)
    value_ext = extended(qkv[:, 2 * width :], radius, window_rows)
    value_ext, mark_q, mark_k = lax.optimization_barrier((value_ext, mark_q, mark_k))

    def one_col(col):
        return pl.BlockSpec((tok_count, width), lambda i: (0, col))

    stats = pl.pallas_call(
        lambda *refs: landmark_kernel(docs, scale, *refs),
        grid=(1,),
        in_specs=[smem, fixed(mark_count, width), one_col(1), one_col(2)],
        out_specs=fixed(mark_count, width + 128),
        out_shape=shaped((mark_count, width + 128), BF),
        scratch_shapes=[
            pltpu.VMEM((width, 128), F32), pltpu.VMEM((width, 128), F32),
            pltpu.VMEM((width, GROUP), F32),
        ],
        compiler_params=params,
        name="landmark",
    )(bounds, mark_q, qkv, qkv)
    far_count = seq_count // 4
    own_count = -(-heads // far_count)
    own_doc = (me % 2) * 2 + (me // 2) % 2
    own_at = (me // 4) * own_count * size
    spare = far_count * own_count * size - width

    def own_heads(array):
        array = jnp.pad(array, ((0, 0), (0, spare)))
        array = lax.dynamic_slice_in_dim(array, own_at, own_count * size, 1)
        return array.reshape(LAND, own_count, size).transpose(1, 0, 2)

    def of_doc(array):
        return lax.dynamic_slice_in_dim(array, own_doc * LAND, LAND, 0)

    mine, other = halves(stats, 1)
    stats = join(mine, swap(other, "seq", 1))
    stats, later_q, later_k = lax.optimization_barrier((stats, mark_q, mark_k))
    own_q = own_heads(of_doc(later_q)).astype(F32)
    own_k = own_heads(of_doc(later_k)).astype(F32)
    square = (own_count, LAND, LAND)
    own_inverse, kernel, saved = pl.pallas_call(
        lambda *refs: pinv_kernel(scale, *refs),
        out_shape=(
            shaped(square, F32), shaped(square, F32),
            shaped((4 * NS_ITERS * own_count, LAND, LAND), F32),
        ),
        name="pinv",
    )(own_q, own_k)
    inverse = own_inverse.transpose(1, 0, 2).reshape(LAND, own_count * size).astype(BF)
    mine, other = halves(stats, 2)
    stats = join(mine, swap(other, "seq", 2))
    for i in range(2, seq_count.bit_length() - 1):
        other = swap(jnp.concatenate([stats, inverse], 1), "seq", 1 << i)
        stats = join(stats, other[:, : width + 128])
        other = other[:, width + 128 :]
        inverse = jnp.where(
            (me >> i) % 2 == 0,
            jnp.concatenate([inverse, other], 1),
            jnp.concatenate([other, inverse], 1),
        )
    inverse = inverse[:, :width]
    mix = pl.pallas_call(
        mix_kernel, out_shape=shaped((LAND, width + 128), BF), name="mix"
    )(inverse, stats)
    mix = seq_whole(mix)

    taps = jnp.pad(conv_taps, ((0, 0), (0, GROUP - tap_count)))
    mark_spec = fixed(mark_count, width)
    mixed, probs = pl.pallas_call(
        lambda *refs: token_kernel(docs, scale, *refs),
        grid=(blocks,),
        in_specs=[
            smem, part(0), fixed(window_rows, width), mark_spec, mark_spec, fixed(heads, GROUP)
        ],
        out_specs=(tok_spec, pl.BlockSpec((width, BLOCK), lambda i: (0, i))),
        out_shape=(shaped((tok_count, width), BF), shaped((width, tok_count), BF)),
        scratch_shapes=[pltpu.VMEM((heads * SUB, GROUP), BF), pltpu.VMEM((BLOCK, width), F32)],
        compiler_params=params,
        name="token",
    )(bounds, qkv, value_ext, mark_k, mix, taps)

    hidden = w_up.shape[1]
    vectors = jnp.stack([bias_out, norm1_gain, norm1_bias, bias_down, norm2_gain, norm2_bias])
    vectors = jnp.pad(vectors, ((0, 2), (0, 0)))
    wide_spec = pl.BlockSpec((FFN_BLOCK, hidden), lambda i: (i, 0))
    ffn_spec = pl.BlockSpec((FFN_BLOCK, width), lambda i: (i, 0))
    narrow = shaped((tok_count, width), BF)
    (
        result, grad_one, active, grad_upper, hidden_low, grad_low_two, grad_low_one,
        grad_mixed, sums, sum_up,
    ) = pl.pallas_call(
        ffn_kernel,
        grid=(tok_count // FFN_BLOCK,),
        in_specs=[
            ffn_spec, ffn_spec, ffn_spec, fixed(width, width), fixed(width, hidden),
            fixed(hidden, width), fixed(8, width), fixed(8, hidden),
        ],
        out_specs=(
            ffn_spec, ffn_spec, wide_spec, wide_spec, ffn_spec, ffn_spec, ffn_spec, ffn_spec,
            fixed(8, width), fixed(8, hidden),
        ),
        out_shape=(
            shaped((tok_count, width), F32), shaped((tok_count, width), F32),
            shaped((tok_count, hidden), BF), shaped((tok_count, hidden), BF),
            narrow, narrow, narrow, narrow, shaped((8, width), F32), shaped((8, hidden), F32),
        ),
        scratch_shapes=[pltpu.VMEM((FFN_BLOCK, hidden), BF)],
        compiler_params=pltpu.CompilerParams(vmem_limit_bytes=58 * 1024 * 1024),
        name="ffn",
    )(
        tokens, mixed, cotangent[0], w_out, w_up, w_down, vectors,
        jnp.broadcast_to(bias_up[None, :], (8, hidden)),
    )

    grad_queries, grad_mix, grad_mk = pl.pallas_call(
        lambda *refs: token_back_kernel(docs, scale, *refs),
        grid=(blocks,),
        in_specs=[
            smem, part(0), tok_spec, pl.BlockSpec((width, BLOCK), lambda i: (0, i)), mark_spec,
            mark_spec,
        ],
        out_specs=(tok_spec, mark_spec, mark_spec),
        out_shape=(
            shaped((tok_count, width), BF), shaped((mark_count, width), F32),
            shaped((mark_count, width), F32),
        ),
        scratch_shapes=[pltpu.VMEM((BLOCK, width), F32)],
        compiler_params=params,
        name="token_back",
    )(bounds, qkv, grad_mixed, probs, mark_k, mix)
    grad_w_down = lax.dot_general(active, grad_low_two, rows_in, preferred_element_type=F32)
    grad_w_up = lax.dot_general(hidden_low, grad_upper, rows_in, preferred_element_type=F32)
    grad_mix, grad_w_down, grad_w_up = lax.optimization_barrier(
        (grad_mix.astype(BF), grad_w_down.astype(BF), grad_w_up.astype(BF))
    )
    sum_w_down, sum_w_up = lax.psum((grad_w_down, grad_w_up), ("row", "seq"))

    def remaining(grad_mix, grad_mk, stats, mix):
        grad_mix = seq_quarter(grad_mix.astype(BF), add_join)
        grad_w_out = lax.dot_general(mixed, grad_low_one, rows_in, preferred_element_type=F32)

        grad_ext = extended(grad_mixed, radius, window_rows)
        grad_conv, products = pl.pallas_call(
            lambda *refs: conv_back_kernel(docs, *refs),
            grid=(blocks,),
            in_specs=[
                smem, fixed(window_rows, width), fixed(window_rows, width), fixed(heads, GROUP)
            ],
            out_specs=(tok_spec, fixed(16, GROUP)),
            out_shape=(shaped((tok_count, width), F32), shaped((16, GROUP), F32)),
            scratch_shapes=[
                pltpu.VMEM((heads * SUB, GROUP), BF), pltpu.VMEM((heads * SUB, GROUP), F32)
            ],
            compiler_params=params,
            name="conv_back",
        )(bounds, grad_ext, value_ext, jnp.pad(conv_taps[:, ::-1], ((0, 0), (0, GROUP - tap_count))))
        grad_conv_taps = products[:heads, SUB - 1 : SUB - 1 + tap_count]
        grad_mix, grad_conv, grad_conv_taps = lax.optimization_barrier(
            (grad_mix, grad_conv, grad_conv_taps)
        )

        grad_avg = pl.pallas_call(
            mix_back_kernel, out_shape=shaped((LAND, width + 128), BF), name="mix_back"
        )(inverse, stats, grad_mix)
        grad_avg = seq_whole(grad_avg)
        lane_spec = pl.BlockSpec((mark_count, 128), lambda i: (0, width // 128))
        grad_keys, grad_values, grad_mq = pl.pallas_call(
            lambda *refs: landmark_back_kernel(docs, scale, *refs),
            grid=(blocks,),
            in_specs=[
                smem, part(1), part(2), tok_spec, mark_spec, mark_spec, lane_spec, lane_spec
            ],
            out_specs=(tok_spec, tok_spec, mark_spec),
            out_shape=(
                shaped((tok_count, width), BF), shaped((tok_count, width), BF),
                shaped((mark_count, width), F32),
            ),
            scratch_shapes=[pltpu.VMEM((BLOCK, width), F32), pltpu.VMEM((BLOCK, width), F32)],
            compiler_params=params,
            name="landmark_back",
        )(bounds, qkv, qkv, grad_conv, mark_q, grad_avg, mix, grad_avg)


        def weight_grad(grads):
            return lax.dot_general(tokens, grads, rows_in, preferred_element_type=F32)

        early = jnp.pad(grad_w_out.astype(BF), ((0, width), (0, 0)))
        early = lax.dynamic_update_slice_in_dim(
            early, weight_grad(grad_values).astype(BF), width, 0
        )
        grad_mix, early = lax.optimization_barrier((grad_mix, early))
        early = advance(begin(early, ORDER, ORDER), 1)
        grad_mq_small, grad_mk_small = pl.pallas_call(
            lambda *refs: pinv_back_kernel(scale, *refs),
            out_shape=(shaped(square, F32), shaped(square, F32)),
            name="pinv_back",
        )(own_q, own_k, kernel, saved, own_heads(grad_mix), own_heads(stats[:, :width]))

        grad_mq_small, (early,) = tied(grad_mq_small, [early])
        early = advance(early, 1)

        def with_small(array, small):
            small = small.transpose(1, 0, 2).reshape(LAND, own_count * size)
            small = lax.dynamic_update_slice_in_dim(
                jnp.zeros((LAND, width + spare), F32), small, own_at, 1
            )[:, :width]
            first = own_doc * LAND
            rows = lax.dynamic_slice_in_dim(array, first, LAND, 0) + small
            return lax.dynamic_update_slice_in_dim(array, rows, first, 0)

        grad_mq = with_small(grad_mq, grad_mq_small)
        grad_mk = with_small(grad_mk, grad_mk_small)
        grad_marks = jnp.concatenate([grad_mq, grad_mk], axis=1).astype(BF)
        mark_back = lax.dot_general(
            grad_marks, w_qkv[:, : 2 * width], cols_in, preferred_element_type=F32
        ) / counts
        mark_back = mark_back.astype(BF)

        grad_bias_q = jnp.sum(grad_queries.astype(F32), axis=0) + jnp.sum(grad_mq, axis=0)
        grad_bias_v = jnp.sum(grad_values.astype(F32), axis=0)
        mark_grad_q = lax.dot_general(
            mean_in, grad_marks[:, :width], rows_in, preferred_element_type=F32
        )
        mark_grad_k = lax.dot_general(
            mean_in, grad_marks[:, width:], rows_in, preferred_element_type=F32
        )
        others = jnp.concatenate(
            [
                sum_up[0].reshape(hidden // width, width),
                grad_bias_q[None],
                grad_bias_v[None],
                jnp.pad(grad_conv_taps.reshape(1, -1), ((0, 0), (0, width - heads * tap_count))),
                jnp.zeros((4 - hidden // width + 1, width), F32),
            ],
            0,
        )
        spare_rows = width // 6
        small = jnp.concatenate([sums, others], 0).astype(BF)
        below = width + 2 * spare_rows - small.shape[0]
        late = jnp.pad(small, ((width, below), (0, 0)))
        late = lax.dynamic_update_slice_in_dim(
            late, (weight_grad(grad_queries) + mark_grad_q).astype(BF), 0, 0
        )
        late = lax.dynamic_update_slice_in_dim(
            late, (weight_grad(grad_keys) + mark_grad_k).astype(BF), width + spare_rows, 0
        )
        late, (early,) = tied(late, [early])
        late = begin(late, ORDER, ORDER)
        grad_projected = jnp.concatenate([grad_queries, grad_keys, grad_values], axis=1)
        grad_input = grad_one + lax.dot_general(
            grad_projected, w_qkv, cols_in, preferred_element_type=F32
        )
        for step in seq_steps():
            mark_back = step(mark_back)
            early, late = advance(early, 1), advance(late, 1)
            (mark_back, grad_input), (early, late) = tied((mark_back, grad_input), [early, late])
        return early[0], late[0], mark_back, grad_input

    plan = stages(ORDER)
    sent = len(seq_steps())

    def rows_left(rows, done):
        return rows >> min(done, 2 * len(plan) - done)

    early_rows = rows_left(2 * width, sent + 2)
    late_rows = rows_left(2 * width + width // 3, sent)

    def nothing(*unused):
        return tuple(
            jnp.zeros((rows, width), BF) for rows in (early_rows, late_rows, mark_count)
        ) + (jnp.zeros((tok_count, width), F32),)

    early, late, mark_back, grad_input = lax.cond(
        lengths[0] > 0, remaining, nothing, grad_mix, grad_mk, stats, mix
    )
    early, late = (early, plan, plan, sent + 2), (late, plan, plan, sent)
    last = 2 * len(plan) - 1
    early, late = advance(early, last - early[3]), advance(late, last - 1 - late[3])
    late, (sum_w_down, sum_w_up) = double_beside(
        late, (sum_w_down.astype(F32), sum_w_up.astype(F32))
    )
    grad_input = grad_input + lax.dot_general(
        onehot, mark_back, rows_in, preferred_element_type=F32
    )
    grad_input, (early, late) = tied(grad_input, [early, late])
    early, early_other = last_swap(early)[:2]
    late, late_other = last_swap(late)[:2]
    sum_w_qkv = settle_qkv(late, late_other, early, early_other, width)
    first_core = me % 2 == 0
    sum_w_out = jnp.where(first_core, early, early_other).astype(F32)
    flat = jnp.where(first_core, late[width:], late_other[width:])[:16].astype(F32)
    at = sums.shape[0] + hidden // width
    pieces = [
        flat[at], flat[at + 1], flat[at + 2, : heads * tap_count], flat[5], flat[3], flat[4],
        flat[sums.shape[0] : at].reshape(hidden), flat[2], flat[0], flat[1],
    ]
    return (
        result[None], grad_input[None], sum_w_qkv, pieces[0], pieces[1],
        pieces[2].reshape(heads, tap_count), sum_w_out, pieces[3], pieces[4], pieces[5],
        sum_w_up, pieces[6], sum_w_down, pieces[7], pieces[8], pieces[9],
    )


def solution(mesh):
    whole, tokens = P(), P("row", "seq", None)
    return jax.shard_map(
        per_device,
        mesh=mesh,
        in_specs=(tokens, P("row", None)) + (whole,) * 14 + (tokens,),
        out_specs=(tokens, tokens) + (whole,) * 14,
        check_vma=False,
    )
```

```python
import math

import jax
import jax.numpy as jnp
from jax import lax
from jax.experimental import pallas as pl
from jax.experimental.pallas import tpu as pltpu
from jax.sharding import PartitionSpec as P

LAND = 64
NS_ITERS = 6
HIGH = lax.Precision.HIGHEST
NEGATIVE = -1e30
BF = jnp.bfloat16
F32 = jnp.float32

BLOCK = 256
GROUP = 256
SUB = 128
TAPS = 33
FFN_BLOCK = 256
ORDER = ("row", "near", "far")


def swap(array, axis, bit):
    count = lax.axis_size(axis)
    return lax.ppermute(array, axis, [(i, i ^ bit) for i in range(count)])


def add_parts(parts):
    total = parts[0].astype(F32)
    for part in parts[1:]:
        total = total + part.astype(F32)
    return total


def halves(array, bit):
    rows = array.shape[0] // 2
    side = (lax.axis_index("seq") // bit) % 2
    mine = lax.dynamic_slice_in_dim(array, side * rows, rows, 0)
    other = lax.dynamic_slice_in_dim(array, (1 - side) * rows, rows, 0)
    return mine, other


def seq_quarter(array, join):
    bits = [1 << i for i in range(lax.axis_size("seq").bit_length() - 1)]
    for bit in bits[:2]:
        mine, other = halves(array, bit)
        array = join(mine, swap(other, "seq", bit))
    for bit in bits[2:]:
        array = join(array, swap(array, "seq", bit))
    return array


def paired(array, axis, bit, dim):
    other = swap(array, axis, bit)
    side = (lax.axis_index(axis) // bit) % 2
    return jnp.where(
        side == 0,
        jnp.concatenate([array, other], dim),
        jnp.concatenate([other, array], dim),
    )


def seq_whole(array):
    return paired(paired(array, "seq", 2, 0), "seq", 1, 0)


def seq_steps():
    bits = [1 << i for i in range(lax.axis_size("seq").bit_length() - 1)]

    def halve(bit):
        def step(array):
            mine, other = halves(array, bit)
            return add_join(mine, swap(other, "seq", bit))

        return step

    def whole(bit):
        return lambda array: add_join(array, swap(array, "seq", bit))

    def double(bit):
        return lambda array: paired(array, "seq", bit, 0)

    return (
        [halve(bit) for bit in bits[:2]]
        + [whole(bit) for bit in bits[2:]]
        + [double(bit) for bit in reversed(bits[:2])]
    )


def add_join(first, second):
    return (first.astype(F32) + second.astype(F32)).astype(BF)


def stages(order):
    row = [("row", 1 << i) for i in range(lax.axis_size("row").bit_length() - 1)]
    seq = [[("seq", 1 << i)] for i in range(lax.axis_size("seq").bit_length() - 1)]
    named = {"core": seq[0], "row": row, "near": seq[1], "far": seq[2], "rest": sum(seq[3:], [])}
    return sum([named[name] for name in ("core",) + order + ("rest",)], [])


def begin(array, down, back):
    return array, stages(down), stages(back), 0


def advance(state, steps):
    held, down, back, done = state
    for step in range(done, min(done + steps, 2 * len(down))):
        if step < len(down):
            axis, bit = down[step]
            half = held.shape[0] // 2
            side = (lax.axis_index(axis) // bit) % 2
            mine = lax.dynamic_slice_in_dim(held, side * half, half, 0)
            other = lax.dynamic_slice_in_dim(held, (1 - side) * half, half, 0)
            held = mine.astype(F32) + swap(other, axis, bit).astype(F32)
            held = held.astype(BF)
        else:
            axis, bit = back[2 * len(down) - 1 - step]
            held = paired(held, axis, bit, 0)
    return held, down, back, min(done + steps, 2 * len(down))


def double_beside(state, values):
    held, down, back, done = state
    axis, bit = back[2 * len(down) - 1 - done]
    other, values = lax.optimization_barrier((swap(held, axis, bit), values))
    side = (lax.axis_index(axis) // bit) % 2
    held = jnp.where(
        side == 0,
        jnp.concatenate([held, other], 0),
        jnp.concatenate([other, held], 0),
    )
    return (held, down, back, done + 1), values


def last_swap(state):
    down, back = state[1], state[2]
    held = advance(state, 2 * len(down) - 1 - state[3])[0]
    return held, swap(held, *down[0]), down, back


def tied(values, states):
    values, helds = lax.optimization_barrier((values, [state[0] for state in states]))
    return values, [(held,) + state[1:] for held, state in zip(helds, states)]


def extended(cells, width, rows):
    count = lax.axis_size("seq")
    head = cells[:width]
    tail = cells[-width:]
    return jnp.concatenate(
        [
            lax.ppermute(tail, "seq", [(i, i + 1) for i in range(count - 1)]),
            cells,
            lax.ppermute(head, "seq", [(i + 1, i) for i in range(count - 1)]),
            jnp.zeros((rows - cells.shape[0] - 2 * width, cells.shape[1]), cells.dtype),
        ],
        axis=0,
    )


def dot_nn(a, b):
    return jnp.dot(a, b, preferred_element_type=F32)


def dot_nt(a, b):
    return lax.dot_general(a, b, (((1,), (1,)), ((), ())), preferred_element_type=F32)


def dot_tn(a, b):
    return lax.dot_general(a, b, (((0,), (0,)), ((), ())), preferred_element_type=F32)


def iota(shape, dim):
    return lax.broadcasted_iota(jnp.int32, shape, dim)


def spread(block):
    rows = block.shape[0]
    tall = jnp.concatenate([block] * 4, axis=0).astype(F32)
    shape = (4 * rows, GROUP)
    keep = iota(shape, 0) // rows == iota(shape, 1) // LAND
    return jnp.where(keep, tall, 0.0).astype(BF)


def gathered(square):
    rows = square.shape[0] // 4
    lane = iota((rows, GROUP), 1) // LAND
    out = square[:rows]
    for head in range(1, 4):
        out = jnp.where(lane == head, square[head * rows : (head + 1) * rows], out)
    return out


def by_head(columns, first, shape):
    lane = iota(shape, 1)
    out = jnp.zeros(shape, F32)
    for head, column in enumerate(columns):
        out = jnp.where((lane % 16 == first + head) & (lane < 48), column, out)
    return out


def split_three(cells):
    lane = iota(cells.shape, 1)
    high = cells.astype(BF).astype(F32)
    mid = (cells - high).astype(BF).astype(F32)
    low = cells - high - mid
    return jnp.where(lane < 16, high, jnp.where(lane < 32, mid, low)).astype(BF)


def merge_three(cells):
    cells = cells.astype(F32)
    return cells + pltpu.roll(cells, 112, 1) + pltpu.roll(cells, 96, 1)


def head_lanes(heads, width):
    return (iota((128, width), 0) == iota((128, width), 1) // LAND).astype(F32)


def doc_of(places, bounds, docs):
    out = (places >= bounds[2 * docs - 1]).astype(jnp.int32)
    for doc in range(docs):
        out = out + (places >= bounds[doc]).astype(jnp.int32)
    return out


def landmark_kernel(docs, scale, bounds, mq_ref, k_ref, v_ref, out_ref, max_s, sum_s, acc_s):
    tokens, width = k_ref.shape
    groups = width // GROUP
    heads = width // LAND
    out_ref[:, :width] = jnp.zeros((docs * LAND, width), BF)
    empty = jnp.full((docs * LAND, 128), NEGATIVE, F32)
    out_ref[:, width:] = jnp.where(iota(empty.shape, 1) < 48, split_three(empty).astype(F32), 0.0).astype(BF)
    for doc in range(docs):
        low = jnp.clip(bounds[doc], 0, tokens)
        high = jnp.clip(bounds[docs + doc], 0, tokens)
        rows = slice(doc * LAND, (doc + 1) * LAND)

        @pl.when(high > low)
        def _():
            max_s[...] = jnp.full(max_s.shape, NEGATIVE, F32)
            sum_s[...] = jnp.zeros(sum_s.shape, F32)
            acc_s[...] = jnp.zeros(acc_s.shape, F32)
            wide = [
                spread(mq_ref[rows, g * GROUP : (g + 1) * GROUP]) for g in range(groups)
            ]

            ones = jnp.ones((BLOCK, 128), BF)

            def step(block, carry):
                first = pl.multiple_of(block * BLOCK, BLOCK)
                at = pl.ds(first, BLOCK)
                place = iota((1, BLOCK), 1) + first
                valid = (place >= low) & (place < high)
                for g in range(groups):
                    cols = slice(g * GROUP, (g + 1) * GROUP)
                    scores = dot_nt(wide[g], k_ref[at, cols]) * scale
                    scores = jnp.where(valid, scores, NEGATIVE)
                    old = max_s[cols, :]
                    top = jnp.maximum(old, jnp.max(scores, axis=1, keepdims=True))
                    weights = jnp.exp(scores - twice(top)).astype(BF)
                    shrink = jnp.exp(old - top)
                    max_s[cols, :] = top
                    sum_s[cols, :] = sum_s[cols, :] * shrink + dot_nn(weights, ones)
                    acc_s[cols, :] = acc_s[cols, :] * twice(shrink) + dot_nn(weights, v_ref[at, cols])
                return carry

            lax.fori_loop(low // BLOCK, (high + BLOCK - 1) // BLOCK, step, 0)
            columns = []
            for g in range(groups):
                cols = slice(g * GROUP, (g + 1) * GROUP)
                sums = sum_s[cols, :]
                out_ref[rows, cols] = gathered(acc_s[cols, :] / twice(sums)).astype(BF)
                level = max_s[cols, :] + jnp.log(sums)
                columns += [level[h * LAND : (h + 1) * LAND] for h in range(4)]
            out_ref[rows, width:] = split_three(by_head(columns, 0, (LAND, 128)))


def twice(cells):
    return jnp.concatenate([cells, cells], axis=1)


def join_kernel(a_ref, b_ref, out_ref):
    width = a_ref.shape[1] - 128
    heads = width // LAND
    first, second = merge_three(a_ref[:, width:]), merge_three(b_ref[:, width:])
    lane = iota(first.shape, 1)
    first = jnp.where(lane < heads, first, 0.0)
    second = jnp.where(lane < heads, second, 0.0)
    top = jnp.maximum(first, second)
    exp_a, exp_b = jnp.exp(first - top), jnp.exp(second - top)
    both = exp_a + exp_b
    level = top + jnp.log(both)
    pick = head_lanes(heads, width).astype(BF)
    share = exp_b / both
    high = share.astype(BF)
    low = (share - high.astype(F32)).astype(BF)
    share = dot_nn(jnp.concatenate([high, low], 1), jnp.concatenate([pick, pick], 0))
    from_a, from_b = a_ref[:, :width].astype(F32), b_ref[:, :width].astype(F32)
    out_ref[:, :width] = (from_a + share * (from_b - from_a)).astype(BF)
    level = jnp.where(lane < heads, level, 0.0)
    level = level + pltpu.roll(level, 16, 1) + pltpu.roll(level, 32, 1)
    out_ref[:, width:] = split_three(level)


def join(first, second):
    return pl.pallas_call(
        join_kernel, out_shape=jax.ShapeDtypeStruct(first.shape, BF), name="join"
    )(first, second)


def mix_kernel(inv_ref, stat_ref, mix_ref):
    width = stat_ref.shape[1] - 128
    for g in range(width // GROUP):
        cols = slice(g * GROUP, (g + 1) * GROUP)
        mix_ref[:, cols] = dot_nn(inv_ref[:, cols], spread(stat_ref[:, cols])).astype(BF)
    mix_ref[:, width:] = stat_ref[:, width:]


def mix_back_kernel(inv_ref, stat_ref, grad_ref, out_ref):
    width = stat_ref.shape[1] - 128
    columns = []
    for g in range(width // GROUP):
        cols = slice(g * GROUP, (g + 1) * GROUP)
        grad = gathered(dot_tn(inv_ref[:, cols], grad_ref[:, cols]))
        out_ref[:, cols] = grad.astype(BF)
        product = grad * stat_ref[:, cols].astype(F32)
        lane = iota(product.shape, 1) // LAND
        for h in range(4):
            columns.append(jnp.sum(jnp.where(lane == h, product, 0.0), axis=1, keepdims=True))
    out_ref[:, width:] = split_three(by_head(columns, 0, (LAND, 128)))


def make_band(taps_ref, band_s):
    for head in range(taps_ref.shape[0]):
        row = jnp.broadcast_to(taps_ref[head : head + 1, :], (SUB, GROUP))
        band_s[head * SUB : (head + 1) * SUB, :] = pltpu.roll(row, 0, 1, stride=1, stride_axis=0).astype(BF)


def same_doc(first, bounds, docs, radius):
    rows = iota((SUB, GROUP), 0) + first
    cols = iota((SUB, GROUP), 1) + (first - radius)
    return doc_of(rows, bounds, docs) == doc_of(cols, bounds, docs)


def token_kernel(
    docs, scale, bounds, q_ref, v_ref, mk_ref, mix_ref, taps_ref, mixed_ref, probs_ref, band_s, sum_s
):
    width = q_ref.shape[1]
    groups = width // GROUP
    radius = (TAPS - 1) // 2
    first = pl.program_id(0) * BLOCK

    @pl.when(pl.program_id(0) == 0)
    def _():
        make_band(taps_ref, band_s)

    for sub in range(BLOCK // SUB):
        start = pl.multiple_of(first + sub * SUB, SUB)
        same = same_doc(start, bounds, docs, radius)
        same = jnp.where(jnp.concatenate([same] * 4, axis=0), 1.0, 0.0).astype(BF)
        for g in range(groups):
            cols = slice(g * GROUP, (g + 1) * GROUP)
            band = band_s[g * 4 * SUB : (g + 1) * 4 * SUB, :] * same
            res = dot_nn(band, v_ref[pl.ds(start, GROUP), cols])
            sum_s[sub * SUB : (sub + 1) * SUB, cols] = gathered(res)
    probs_ref[...] = jnp.zeros(probs_ref.shape, BF)
    for doc in range(docs):
        low, high = bounds[doc], bounds[docs + doc]
        rows = slice(doc * LAND, (doc + 1) * LAND)

        @pl.when((high > first) & (low < first + BLOCK))
        def _():
            place = iota((1, BLOCK), 1) + first
            valid = (place >= low) & (place < high)
            for g in range(groups):
                cols = slice(g * GROUP, (g + 1) * GROUP)
                scores = dot_nt(spread(mk_ref[rows, cols]), q_ref[:, cols]) * scale
                scores = scores.reshape(4, LAND, BLOCK)
                weights = jnp.exp(scores - jnp.max(scores, axis=1, keepdims=True))
                probs = weights / jnp.sum(weights, axis=1, keepdims=True)
                probs = jnp.where(valid, probs.reshape(GROUP, BLOCK), 0.0).astype(BF)
                probs_ref[cols, :] = probs_ref[cols, :] + probs
                sum_s[:, cols] = sum_s[:, cols] + dot_tn(probs, spread(mix_ref[rows, cols]))

    mixed_ref[...] = sum_s[...].astype(BF)


def token_back_kernel(
    docs, scale, bounds, q_ref, gm_ref, probs_ref, mk_ref, mix_ref, gq_ref, gmix_ref, gmk_ref, gq_s
):
    width = q_ref.shape[1]
    groups = width // GROUP
    first = pl.program_id(0) * BLOCK

    @pl.when(pl.program_id(0) == 0)
    def _():
        gmix_ref[...] = jnp.zeros(gmix_ref.shape, F32)
        gmk_ref[...] = jnp.zeros(gmk_ref.shape, F32)

    gq_s[...] = jnp.zeros(gq_s.shape, F32)
    for doc in range(docs):
        low, high = bounds[doc], bounds[docs + doc]
        rows = slice(doc * LAND, (doc + 1) * LAND)

        @pl.when((high > first) & (low < first + BLOCK))
        def _():
            place = iota((1, BLOCK), 1) + first
            valid = (place >= low) & (place < high)
            for g in range(groups):
                cols = slice(g * GROUP, (g + 1) * GROUP)
                probs = jnp.where(valid, probs_ref[cols, :].astype(F32), 0.0)
                gmix_ref[rows, cols] += gathered(dot_nn(probs.astype(BF), gm_ref[:, cols]))
                grad = dot_nt(spread(mix_ref[rows, cols]), gm_ref[:, cols])
                heavy = (probs * grad).reshape(4, LAND, BLOCK)
                shared = probs.reshape(4, LAND, BLOCK) * jnp.sum(heavy, axis=1, keepdims=True)
                grad = ((heavy - shared).reshape(GROUP, BLOCK) * scale).astype(BF)
                gmk_ref[rows, cols] += gathered(dot_nn(grad, q_ref[:, cols]))
                gq_s[:, cols] += dot_tn(grad, spread(mk_ref[rows, cols]))

    gq_ref[...] = gq_s[...].astype(BF)


def conv_back_kernel(docs, bounds, gm_ref, v_ref, taps_ref, out_ref, sum_ref, band_s, prod_s):
    width = gm_ref.shape[1]
    groups = width // GROUP
    radius = (TAPS - 1) // 2
    first = pl.program_id(0) * BLOCK

    @pl.when(pl.program_id(0) == 0)
    def _():
        make_band(taps_ref, band_s)
        prod_s[...] = jnp.zeros(prod_s.shape, F32)

    for sub in range(BLOCK // SUB):
        start = pl.multiple_of(first + sub * SUB, SUB)
        same = same_doc(start, bounds, docs, radius)
        same = jnp.where(jnp.concatenate([same] * 4, axis=0), 1.0, 0.0)
        for g in range(groups):
            cols = slice(g * GROUP, (g + 1) * GROUP)
            tall = slice(g * 4 * SUB, (g + 1) * 4 * SUB)
            band = band_s[tall, :] * same.astype(BF)
            res = dot_nn(band, gm_ref[pl.ds(start, GROUP), cols])
            out_ref[sub * SUB : (sub + 1) * SUB, cols] = gathered(res)
            own = gm_ref[pl.ds(pl.multiple_of(start + radius, 16), SUB), cols]
            product = dot_nt(spread(own), v_ref[pl.ds(start, GROUP), cols])
            prod_s[tall, :] += product * same

    @pl.when(pl.program_id(0) == pl.num_programs(0) - 1)
    def _():
        flip = (iota((SUB, SUB), 0) + iota((SUB, SUB), 1) == SUB - 1).astype(F32).astype(BF)
        sum_ref[...] = jnp.zeros(sum_ref.shape, F32)
        for head in range(taps_ref.shape[0]):
            product = prod_s[head * SUB : (head + 1) * SUB, :]
            high = product.astype(BF)
            low = (product - high.astype(F32)).astype(BF)
            turned = pltpu.roll(dot_nn(flip, high) + dot_nn(flip, low), 0, 1, stride=1, stride_axis=0)
            sum_ref[head : head + 1, :] = jnp.sum(turned, axis=0, keepdims=True)


def ffn_kernel(
    x_ref, mixed_ref, cot_ref, w_out_ref, w_up_ref, w_down_ref, rows_ref, bias_up_ref,
    result_ref, grad_one_ref, active_ref, grad_up_ref, low_ref, low_two_ref, low_one_ref,
    grad_mixed_ref, sums_ref, sum_up_ref, slope_s,
):
    width = x_ref.shape[1]
    hidden = w_up_ref.shape[1]
    chunks = [slice(at, at + width) for at in range(0, hidden, width)]

    def row(i):
        return rows_ref[i : i + 1, :]

    @pl.when(pl.program_id(0) == 0)
    def _():
        sums_ref[...] = jnp.zeros(sums_ref.shape, F32)
        sum_up_ref[...] = jnp.zeros(sum_up_ref.shape, F32)

    def add_sum(i, cells):
        sums_ref[i : i + 1, :] += jnp.sum(cells, axis=0, keepdims=True)

    attended = dot_nn(mixed_ref[...], w_out_ref[...]) + row(0)
    norm_one, inverse_one = normalize(x_ref[...].astype(F32) + attended)
    hidden_one = norm_one * row(1) + row(2)
    hidden_low = hidden_one.astype(BF)
    low_ref[...] = hidden_low
    lowered = hidden_one + row(3)
    for cols in chunks:
        upper = dot_nn(hidden_low, w_up_ref[:, cols]) + bias_up_ref[:1, cols]
        active, slope = gelu_both(upper)
        active = active.astype(BF)
        active_ref[:, cols] = active
        slope_s[:, cols] = slope.astype(BF)
        lowered = lowered + dot_nn(active, w_down_ref[cols, :])
    norm_two, inverse_two = normalize(lowered)
    result_ref[...] = norm_two * row(4) + row(5)
    upstream = cot_ref[...].astype(F32)
    add_sum(0, upstream * norm_two)
    add_sum(1, upstream)
    grad_two = norm_back(upstream * row(4), norm_two, inverse_two)
    low_two = grad_two.astype(BF)
    low_two_ref[...] = low_two
    add_sum(2, low_two.astype(F32))
    grad_hidden = grad_two
    for cols in chunks:
        grad_up = dot_nt(low_two, w_down_ref[cols, :]) * slope_s[:, cols].astype(F32)
        grad_up = grad_up.astype(BF)
        grad_up_ref[:, cols] = grad_up
        sum_up_ref[:1, cols] += jnp.sum(grad_up.astype(F32), axis=0, keepdims=True)
        grad_hidden = grad_hidden + dot_nt(grad_up, w_up_ref[:, cols])
    add_sum(3, grad_hidden * norm_one)
    add_sum(4, grad_hidden)
    grad_one = norm_back(grad_hidden * row(1), norm_one, inverse_one)
    grad_one_ref[...] = grad_one
    low_one = grad_one.astype(BF)
    low_one_ref[...] = low_one
    add_sum(5, low_one.astype(F32))
    grad_mixed_ref[...] = dot_nt(low_one, w_out_ref[...]).astype(BF)


def landmark_back_kernel(
    docs, scale, bounds, k_ref, v_ref, conv_ref, mq_ref, grad_ref, level_ref, dots_ref,
    gk_ref, gv_ref, gmq_ref, gk_s, gv_s,
):
    width = k_ref.shape[1]
    groups = width // GROUP
    first = pl.program_id(0) * BLOCK

    @pl.when(pl.program_id(0) == 0)
    def _():
        gmq_ref[...] = jnp.zeros(gmq_ref.shape, F32)

    gk_s[...] = jnp.zeros(gk_s.shape, F32)
    gv_s[...] = conv_ref[...]
    for doc in range(docs):
        low, high = bounds[doc], bounds[docs + doc]
        rows = slice(doc * LAND, (doc + 1) * LAND)

        @pl.when((high > first) & (low < first + BLOCK))
        def _():
            place = iota((1, BLOCK), 1) + first
            valid = (place >= low) & (place < high)

            level, dots = merge_three(level_ref[rows, :]), merge_three(dots_ref[rows, :])

            def column(lanes, g):
                return jnp.concatenate(
                    [lanes[:, 4 * g + h : 4 * g + h + 1] for h in range(4)], axis=0
                )

            for g in range(groups):
                cols = slice(g * GROUP, (g + 1) * GROUP)
                wide_q, wide_g = spread(mq_ref[rows, cols]), spread(grad_ref[rows, cols])
                scores = dot_nt(wide_q, k_ref[:, cols]) * scale - column(level, g)
                probs = jnp.exp(jnp.where(valid, scores, NEGATIVE))
                grad = dot_nt(wide_g, v_ref[:, cols]) - column(dots, g)
                grad = (probs * grad * scale).astype(BF)
                gv_s[:, cols] += dot_tn(probs.astype(BF), wide_g)
                gk_s[:, cols] += dot_tn(grad, wide_q)
                gmq_ref[rows, cols] += gathered(dot_nn(grad, k_ref[:, cols]))

    gk_ref[...] = gk_s[...].astype(BF)
    gv_ref[...] = gv_s[...].astype(BF)


def gelu_both(upper):
    tangent = jnp.tanh(0.7978845608028654 * (upper + 0.044715 * upper * upper * upper))
    inner_slope = 0.7978845608028654 * (1.0 + 3.0 * 0.044715 * upper * upper)
    active = 0.5 * upper * (1.0 + tangent)
    slope = 0.5 * (1.0 + tangent) + 0.5 * upper * (1.0 - tangent * tangent) * inner_slope
    return active, slope


def normalize(residual):
    row_mean = jnp.mean(residual, axis=-1, keepdims=True)
    centered = residual - row_mean
    row_var = jnp.mean(centered * centered, axis=-1, keepdims=True)
    inverse_dev = lax.rsqrt(row_var + 1e-05)
    return (centered * inverse_dev, inverse_dev)


def norm_back(grad_normed, normed, inverse_dev):
    return inverse_dev * (
        grad_normed
        - jnp.mean(grad_normed, axis=-1, keepdims=True)
        - normed * jnp.mean(grad_normed * normed, axis=-1, keepdims=True)
    )


def dot_high(a, b, dims):
    return lax.dot_general(
        a, b, (dims, ((), ())), precision=HIGH, preferred_element_type=F32
    )


NN, NT, TN = ((1,), (0,)), ((1,), (1,)), ((0,), (0,))


def pinv_kernel(scale, q_ref, k_ref, inverse_ref, kernel_ref, saved_ref):
    count = q_ref.shape[0]
    eye = (iota((LAND, LAND), 0) == iota((LAND, LAND), 1)).astype(F32)
    kernels, inverses = [], []
    for p in range(count):
        scores = dot_high(q_ref[p], k_ref[p], NT) * scale
        weights = jnp.exp(scores - jnp.max(scores, axis=1, keepdims=True))
        kernel = weights / jnp.sum(weights, axis=1, keepdims=True)
        kernel_ref[p] = kernel
        kernels.append(kernel)
        largest = jnp.max(jnp.sum(kernel, axis=0, keepdims=True), axis=1, keepdims=True)
        inverses.append(kernel.T / largest)
    for sweep in range(NS_ITERS):
        products = [dot_high(kernels[p], inverses[p], NN) for p in range(count)]
        second = [
            15.0 * eye - dot_high(products[p], 7.0 * eye - products[p], NN) for p in range(count)
        ]
        third = [13.0 * eye - dot_high(products[p], second[p], NN) for p in range(count)]
        for p in range(count):
            at = (sweep * count + p) * 4
            saved_ref[at], saved_ref[at + 1] = inverses[p], products[p]
            saved_ref[at + 2], saved_ref[at + 3] = second[p], third[p]
        inverses = [0.25 * dot_high(inverses[p], third[p], NN) for p in range(count)]
    for p in range(count):
        inverse_ref[p] = inverses[p]


def pinv_back_kernel(scale, q_ref, k_ref, kernel_ref, saved_ref, grad_ref, avg_ref, gq_ref, gk_ref):
    count = q_ref.shape[0]
    each = range(count)
    eye = (iota((LAND, LAND), 0) == iota((LAND, LAND), 1)).astype(F32)
    grads = [dot_nt(grad_ref[p], avg_ref[p]) for p in each]
    kernels = [kernel_ref[p] for p in each]
    totals = [jnp.zeros((LAND, LAND), F32) for p in each]
    for sweep in reversed(range(NS_ITERS)):
        first = [(sweep * count + p) * 4 for p in each]
        inverses, products = [saved_ref[a] for a in first], [saved_ref[a + 1] for a in first]
        grad_third = [0.25 * dot_high(inverses[p], grads[p], TN) for p in each]
        nexts = [0.25 * dot_high(grads[p], saved_ref[first[p] + 3], NT) for p in each]
        grad_second = [-dot_high(products[p], grad_third[p], TN) for p in each]
        grad_product = [-dot_high(grad_third[p], saved_ref[first[p] + 2], NT) for p in each]
        grad_first = [-dot_high(products[p], grad_second[p], TN) for p in each]
        grad_product = [
            grad_product[p]
            - dot_high(grad_second[p], 7.0 * eye - products[p], NT)
            - grad_first[p]
            for p in each
        ]
        totals = [totals[p] + dot_high(grad_product[p], inverses[p], NT) for p in each]
        grads = [nexts[p] + dot_high(kernels[p], grad_product[p], TN) for p in each]
    for p in each:
        kernel = kernels[p]
        sums = jnp.sum(kernel, axis=0, keepdims=True)
        largest = jnp.max(sums, axis=1, keepdims=True)
        flipped = grads[p].T
        loss = jnp.sum(jnp.sum(flipped * kernel, axis=1, keepdims=True), axis=0, keepdims=True)
        at_top = (sums == largest).astype(F32)
        at_top = at_top / jnp.sum(at_top, axis=1, keepdims=True)
        grad = totals[p] + flipped / largest - at_top * (loss / (largest * largest))
        grad = kernel * (grad - jnp.sum(grad * kernel, axis=1, keepdims=True)) * scale
        gq_ref[p] = dot_high(grad, k_ref[p], NN)
        gk_ref[p] = dot_high(grad, q_ref[p], TN)


def settle_qkv_kernel(side_ref, late_ref, late_other_ref, early_ref, early_other_ref, out_ref):
    part = pl.program_id(0)
    own = jnp.where(part == 0, 0, 1) == side_ref[0]
    choices = [
        (late_ref, own & (part < 2)),
        (late_other_ref, jnp.logical_not(own) & (part < 2)),
        (early_ref, own & (part == 2)),
        (early_other_ref, jnp.logical_not(own) & (part == 2)),
    ]
    for ref, chosen in choices:

        @pl.when(chosen)
        def _():
            out_ref[...] = ref[...].astype(F32)


def settle_qkv(late, late_other, early, early_other, width):
    side = (lax.axis_index("seq") % 2).astype(jnp.int32).reshape(1)
    rows = width // 2

    def spec(used):
        return pl.BlockSpec((rows, width), lambda j, i, s: (jnp.where(used(j), i, 0), 0))

    return pl.pallas_call(
        settle_qkv_kernel,
        grid_spec=pltpu.PrefetchScalarGridSpec(
            num_scalar_prefetch=1,
            grid=(3, 2),
            in_specs=[spec(lambda j: j < 2), spec(lambda j: j < 2)] + [spec(lambda j: j == 2)] * 2,
            out_specs=pl.BlockSpec((rows, width), lambda j, i, s: (i, j)),
        ),
        out_shape=jax.ShapeDtypeStruct((width, 3 * width), F32),
        name="settle_qkv",
    )(side, late, late_other, early, early_other)


def per_device(
    inputs, doc_lengths, w_qkv, bias_q, bias_v, conv_taps, w_out, bias_out, norm1_gain,
    norm1_bias, w_up, bias_up, w_down, bias_down, norm2_gain, norm2_bias, cotangent,
):
    tokens = inputs[0]
    tok_count, width = tokens.shape
    heads, tap_count = conv_taps.shape
    size = width // heads
    radius = (tap_count - 1) // 2
    lengths = doc_lengths[0]
    docs = lengths.shape[0]
    mark_count = docs * LAND
    scale = 1.0 / math.sqrt(size)
    seq_count = lax.axis_size("seq")
    me = lax.axis_index("seq")
    row_first = me * tok_count
    ends = jnp.cumsum(lengths)
    starts = ends - lengths
    bounds = (jnp.concatenate([starts, ends]) - row_first).astype(jnp.int32)
    within = jnp.arange(LAND + 1, dtype=jnp.int32)
    edges = starts[:, None] + (within[None, :] * lengths[:, None] + LAND - 1) // LAND
    mark_low = edges[:, :-1].reshape(mark_count, 1)
    mark_high = edges[:, 1:].reshape(mark_count, 1)
    counts = (mark_high - mark_low).astype(F32)
    places = row_first + jnp.arange(tok_count, dtype=jnp.int32)[None, :]
    onehot = ((places >= mark_low) & (places < mark_high)).astype(BF)
    rows_in = (((0,), (0,)), ((), ()))
    cols_in = (((1,), (1,)), ((), ()))
    blocks = tok_count // BLOCK
    window_rows = tok_count + GROUP - SUB
    smem = pl.BlockSpec(memory_space=pltpu.SMEM)
    params = pltpu.CompilerParams(vmem_limit_bytes=40 * 1024 * 1024)
    tok_spec = pl.BlockSpec((BLOCK, width), lambda i: (i, 0))

    def part(col):
        return pl.BlockSpec((BLOCK, width), lambda i: (i, col))

    def fixed(*shape):
        return pl.BlockSpec(shape, lambda i: (0,) * len(shape))

    def shaped(shape, dtype):
        return jax.ShapeDtypeStruct(shape, dtype)

    means = jnp.dot(onehot, tokens, preferred_element_type=F32) / counts
    mean_in = seq_whole(seq_quarter(means.astype(BF), add_join))
    marks = jnp.dot(mean_in, w_qkv[:, : 2 * width], preferred_element_type=F32)
    mark_q = (marks[:, :width] + bias_q).astype(BF)
    mark_k = marks[:, width:].astype(BF)

    bias = jnp.concatenate([bias_q, jnp.zeros_like(bias_q), bias_v])
    qkv = (jnp.dot(tokens, w_qkv, preferred_element_type=F32) + bias).astype(BF)
    value_ext = extended(qkv[:, 2 * width :], radius, window_rows)
    value_ext, mark_q, mark_k = lax.optimization_barrier((value_ext, mark_q, mark_k))

    def one_col(col):
        return pl.BlockSpec((tok_count, width), lambda i: (0, col))

    stats = pl.pallas_call(
        lambda *refs: landmark_kernel(docs, scale, *refs),
        grid=(1,),
        in_specs=[smem, fixed(mark_count, width), one_col(1), one_col(2)],
        out_specs=fixed(mark_count, width + 128),
        out_shape=shaped((mark_count, width + 128), BF),
        scratch_shapes=[
            pltpu.VMEM((width, 128), F32), pltpu.VMEM((width, 128), F32),
            pltpu.VMEM((width, GROUP), F32),
        ],
        compiler_params=params,
        name="landmark",
    )(bounds, mark_q, qkv, qkv)
    far_count = seq_count // 4
    own_count = -(-heads // far_count)
    own_doc = (me % 2) * 2 + (me // 2) % 2
    own_at = (me // 4) * own_count * size
    spare = far_count * own_count * size - width

    def own_heads(array):
        array = jnp.pad(array, ((0, 0), (0, spare)))
        array = lax.dynamic_slice_in_dim(array, own_at, own_count * size, 1)
        return array.reshape(LAND, own_count, size).transpose(1, 0, 2)

    def of_doc(array):
        return lax.dynamic_slice_in_dim(array, own_doc * LAND, LAND, 0)

    mine, other = halves(stats, 1)
    stats = join(mine, swap(other, "seq", 1))
    stats, later_q, later_k = lax.optimization_barrier((stats, mark_q, mark_k))
    own_q = own_heads(of_doc(later_q)).astype(F32)
    own_k = own_heads(of_doc(later_k)).astype(F32)
    square = (own_count, LAND, LAND)
    own_inverse, kernel, saved = pl.pallas_call(
        lambda *refs: pinv_kernel(scale, *refs),
        out_shape=(
            shaped(square, F32), shaped(square, F32),
            shaped((4 * NS_ITERS * own_count, LAND, LAND), F32),
        ),
        name="pinv",
    )(own_q, own_k)
    inverse = own_inverse.transpose(1, 0, 2).reshape(LAND, own_count * size).astype(BF)
    mine, other = halves(stats, 2)
    stats = join(mine, swap(other, "seq", 2))
    for i in range(2, seq_count.bit_length() - 1):
        other = swap(jnp.concatenate([stats, inverse], 1), "seq", 1 << i)
        stats = join(stats, other[:, : width + 128])
        other = other[:, width + 128 :]
        inverse = jnp.where(
            (me >> i) % 2 == 0,
            jnp.concatenate([inverse, other], 1),
            jnp.concatenate([other, inverse], 1),
        )
    inverse = inverse[:, :width]
    mix = pl.pallas_call(
        mix_kernel, out_shape=shaped((LAND, width + 128), BF), name="mix"
    )(inverse, stats)
    mix = seq_whole(mix)

    taps = jnp.pad(conv_taps, ((0, 0), (0, GROUP - tap_count)))
    mark_spec = fixed(mark_count, width)
    mixed, probs = pl.pallas_call(
        lambda *refs: token_kernel(docs, scale, *refs),
        grid=(blocks,),
        in_specs=[
            smem, part(0), fixed(window_rows, width), mark_spec, mark_spec, fixed(heads, GROUP)
        ],
        out_specs=(tok_spec, pl.BlockSpec((width, BLOCK), lambda i: (0, i))),
        out_shape=(shaped((tok_count, width), BF), shaped((width, tok_count), BF)),
        scratch_shapes=[pltpu.VMEM((heads * SUB, GROUP), BF), pltpu.VMEM((BLOCK, width), F32)],
        compiler_params=params,
        name="token",
    )(bounds, qkv, value_ext, mark_k, mix, taps)

    hidden = w_up.shape[1]
    vectors = jnp.stack([bias_out, norm1_gain, norm1_bias, bias_down, norm2_gain, norm2_bias])
    vectors = jnp.pad(vectors, ((0, 2), (0, 0)))
    wide_spec = pl.BlockSpec((FFN_BLOCK, hidden), lambda i: (i, 0))
    ffn_spec = pl.BlockSpec((FFN_BLOCK, width), lambda i: (i, 0))
    narrow = shaped((tok_count, width), BF)
    (
        result, grad_one, active, grad_upper, hidden_low, grad_low_two, grad_low_one,
        grad_mixed, sums, sum_up,
    ) = pl.pallas_call(
        ffn_kernel,
        grid=(tok_count // FFN_BLOCK,),
        in_specs=[
            ffn_spec, ffn_spec, ffn_spec, fixed(width, width), fixed(width, hidden),
            fixed(hidden, width), fixed(8, width), fixed(8, hidden),
        ],
        out_specs=(
            ffn_spec, ffn_spec, wide_spec, wide_spec, ffn_spec, ffn_spec, ffn_spec, ffn_spec,
            fixed(8, width), fixed(8, hidden),
        ),
        out_shape=(
            shaped((tok_count, width), F32), shaped((tok_count, width), F32),
            shaped((tok_count, hidden), BF), shaped((tok_count, hidden), BF),
            narrow, narrow, narrow, narrow, shaped((8, width), F32), shaped((8, hidden), F32),
        ),
        scratch_shapes=[pltpu.VMEM((FFN_BLOCK, hidden), BF)],
        compiler_params=pltpu.CompilerParams(vmem_limit_bytes=58 * 1024 * 1024),
        name="ffn",
    )(
        tokens, mixed, cotangent[0], w_out, w_up, w_down, vectors,
        jnp.broadcast_to(bias_up[None, :], (8, hidden)),
    )

    grad_queries, grad_mix, grad_mk = pl.pallas_call(
        lambda *refs: token_back_kernel(docs, scale, *refs),
        grid=(blocks,),
        in_specs=[
            smem, part(0), tok_spec, pl.BlockSpec((width, BLOCK), lambda i: (0, i)), mark_spec,
            mark_spec,
        ],
        out_specs=(tok_spec, mark_spec, mark_spec),
        out_shape=(
            shaped((tok_count, width), BF), shaped((mark_count, width), F32),
            shaped((mark_count, width), F32),
        ),
        scratch_shapes=[pltpu.VMEM((BLOCK, width), F32)],
        compiler_params=params,
        name="token_back",
    )(bounds, qkv, grad_mixed, probs, mark_k, mix)
    grad_w_down = lax.dot_general(active, grad_low_two, rows_in, preferred_element_type=F32)
    grad_w_up = lax.dot_general(hidden_low, grad_upper, rows_in, preferred_element_type=F32)
    grad_mix, grad_w_down, grad_w_up = lax.optimization_barrier(
        (grad_mix.astype(BF), grad_w_down.astype(BF), grad_w_up.astype(BF))
    )
    sum_w_down, sum_w_up = lax.psum((grad_w_down, grad_w_up), ("row", "seq"))

    def remaining(grad_mix, grad_mk, stats, mix):
        grad_mix = seq_quarter(grad_mix.astype(BF), add_join)
        grad_w_out = lax.dot_general(mixed, grad_low_one, rows_in, preferred_element_type=F32)

        grad_ext = extended(grad_mixed, radius, window_rows)
        grad_conv, products = pl.pallas_call(
            lambda *refs: conv_back_kernel(docs, *refs),
            grid=(blocks,),
            in_specs=[
                smem, fixed(window_rows, width), fixed(window_rows, width), fixed(heads, GROUP)
            ],
            out_specs=(tok_spec, fixed(16, GROUP)),
            out_shape=(shaped((tok_count, width), F32), shaped((16, GROUP), F32)),
            scratch_shapes=[
                pltpu.VMEM((heads * SUB, GROUP), BF), pltpu.VMEM((heads * SUB, GROUP), F32)
            ],
            compiler_params=params,
            name="conv_back",
        )(bounds, grad_ext, value_ext, jnp.pad(conv_taps[:, ::-1], ((0, 0), (0, GROUP - tap_count))))
        grad_conv_taps = products[:heads, SUB - 1 : SUB - 1 + tap_count]
        grad_mix, grad_conv, grad_conv_taps = lax.optimization_barrier(
            (grad_mix, grad_conv, grad_conv_taps)
        )

        grad_avg = pl.pallas_call(
            mix_back_kernel, out_shape=shaped((LAND, width + 128), BF), name="mix_back"
        )(inverse, stats, grad_mix)
        grad_avg = seq_whole(grad_avg)
        lane_spec = pl.BlockSpec((mark_count, 128), lambda i: (0, width // 128))
        grad_keys, grad_values, grad_mq = pl.pallas_call(
            lambda *refs: landmark_back_kernel(docs, scale, *refs),
            grid=(blocks,),
            in_specs=[
                smem, part(1), part(2), tok_spec, mark_spec, mark_spec, lane_spec, lane_spec
            ],
            out_specs=(tok_spec, tok_spec, mark_spec),
            out_shape=(
                shaped((tok_count, width), BF), shaped((tok_count, width), BF),
                shaped((mark_count, width), F32),
            ),
            scratch_shapes=[pltpu.VMEM((BLOCK, width), F32), pltpu.VMEM((BLOCK, width), F32)],
            compiler_params=params,
            name="landmark_back",
        )(bounds, qkv, qkv, grad_conv, mark_q, grad_avg, mix, grad_avg)


        def weight_grad(grads):
            return lax.dot_general(tokens, grads, rows_in, preferred_element_type=F32)

        early = jnp.pad(grad_w_out.astype(BF), ((0, width), (0, 0)))
        early = lax.dynamic_update_slice_in_dim(
            early, weight_grad(grad_values).astype(BF), width, 0
        )
        early = advance(begin(early, ORDER, ORDER), 1)
        grad_mix, (early,) = tied(grad_mix, [early])
        early = advance(early, 1)
        grad_mq_small, grad_mk_small = pl.pallas_call(
            lambda *refs: pinv_back_kernel(scale, *refs),
            out_shape=(shaped(square, F32), shaped(square, F32)),
            name="pinv_back",
        )(own_q, own_k, kernel, saved, own_heads(grad_mix), own_heads(stats[:, :width]))

        grad_mq_small, (early,) = tied(grad_mq_small, [early])

        def with_small(array, small):
            small = small.transpose(1, 0, 2).reshape(LAND, own_count * size)
            small = lax.dynamic_update_slice_in_dim(
                jnp.zeros((LAND, width + spare), F32), small, own_at, 1
            )[:, :width]
            first = own_doc * LAND
            rows = lax.dynamic_slice_in_dim(array, first, LAND, 0) + small
            return lax.dynamic_update_slice_in_dim(array, rows, first, 0)

        grad_mq = with_small(grad_mq, grad_mq_small)
        grad_mk = with_small(grad_mk, grad_mk_small)
        grad_marks = jnp.concatenate([grad_mq, grad_mk], axis=1).astype(BF)
        mark_back = lax.dot_general(
            grad_marks, w_qkv[:, : 2 * width], cols_in, preferred_element_type=F32
        ) / counts
        mark_back = mark_back.astype(BF)

        grad_bias_q = jnp.sum(grad_queries.astype(F32), axis=0) + jnp.sum(grad_mq, axis=0)
        grad_bias_v = jnp.sum(grad_values.astype(F32), axis=0)
        mark_grad_q = lax.dot_general(
            mean_in, grad_marks[:, :width], rows_in, preferred_element_type=F32
        )
        mark_grad_k = lax.dot_general(
            mean_in, grad_marks[:, width:], rows_in, preferred_element_type=F32
        )
        others = jnp.concatenate(
            [
                sum_up[0].reshape(hidden // width, width),
                grad_bias_q[None],
                grad_bias_v[None],
                jnp.pad(grad_conv_taps.reshape(1, -1), ((0, 0), (0, width - heads * tap_count))),
                jnp.zeros((4 - hidden // width + 1, width), F32),
            ],
            0,
        )
        spare_rows = width // 6
        small = jnp.concatenate([sums, others], 0).astype(BF)
        below = width + 2 * spare_rows - small.shape[0]
        late = jnp.pad(small, ((width, below), (0, 0)))
        late = lax.dynamic_update_slice_in_dim(
            late, (weight_grad(grad_queries) + mark_grad_q).astype(BF), 0, 0
        )
        late = lax.dynamic_update_slice_in_dim(
            late, (weight_grad(grad_keys) + mark_grad_k).astype(BF), width + spare_rows, 0
        )
        late = begin(late, ORDER, ORDER)
        grad_projected = jnp.concatenate([grad_queries, grad_keys, grad_values], axis=1)
        grad_input = grad_one + lax.dot_general(
            grad_projected, w_qkv, cols_in, preferred_element_type=F32
        )
        for step in seq_steps():
            mark_back = step(mark_back)
            early, late = advance(early, 1), advance(late, 1)
            (mark_back, grad_input), (early, late) = tied((mark_back, grad_input), [early, late])
        return early[0], late[0], mark_back, grad_input

    plan = stages(ORDER)
    sent = len(seq_steps())

    def rows_left(rows, done):
        return rows >> min(done, 2 * len(plan) - done)

    early_rows = rows_left(2 * width, sent + 2)
    late_rows = rows_left(2 * width + width // 3, sent)

    def nothing(*unused):
        return tuple(
            jnp.zeros((rows, width), BF) for rows in (early_rows, late_rows, mark_count)
        ) + (jnp.zeros((tok_count, width), F32),)

    early, late, mark_back, grad_input = lax.cond(
        lengths[0] > 0, remaining, nothing, grad_mix, grad_mk, stats, mix
    )
    early, late = (early, plan, plan, sent + 2), (late, plan, plan, sent)
    last = 2 * len(plan) - 1
    early, late = advance(early, last - early[3]), advance(late, last - 1 - late[3])
    late, (sum_w_down, sum_w_up) = double_beside(
        late, (sum_w_down.astype(F32), sum_w_up.astype(F32))
    )
    grad_input = grad_input + lax.dot_general(
        onehot, mark_back, rows_in, preferred_element_type=F32
    )
    grad_input, (early, late) = tied(grad_input, [early, late])
    early, early_other = last_swap(early)[:2]
    late, late_other = last_swap(late)[:2]
    sum_w_qkv = settle_qkv(late, late_other, early, early_other, width)
    first_core = me % 2 == 0
    sum_w_out = jnp.where(first_core, early, early_other).astype(F32)
    flat = jnp.where(first_core, late[width:], late_other[width:])[:16].astype(F32)
    at = sums.shape[0] + hidden // width
    pieces = [
        flat[at], flat[at + 1], flat[at + 2, : heads * tap_count], flat[5], flat[3], flat[4],
        flat[sums.shape[0] : at].reshape(hidden), flat[2], flat[0], flat[1],
    ]
    return (
        result[None], grad_input[None], sum_w_qkv, pieces[0], pieces[1],
        pieces[2].reshape(heads, tap_count), sum_w_out, pieces[3], pieces[4], pieces[5],
        sum_w_up, pieces[6], sum_w_down, pieces[7], pieces[8], pieces[9],
    )


def solution(mesh):
    whole, tokens = P(), P("row", "seq", None)
    return jax.shard_map(
        per_device,
        mesh=mesh,
        in_specs=(tokens, P("row", None)) + (whole,) * 14 + (tokens,),
        out_specs=(tokens, tokens) + (whole,) * 14,
        check_vma=False,
    )
```

```python
import math

import jax
import jax.numpy as jnp
from jax import lax
from jax.experimental import pallas as pl
from jax.experimental.pallas import tpu as pltpu
from jax.sharding import PartitionSpec as P

LAND = 64
NS_ITERS = 6
HIGH = lax.Precision.HIGHEST
NEGATIVE = -1e30
BF = jnp.bfloat16
F32 = jnp.float32

BLOCK = 256
GROUP = 256
SUB = 128
TAPS = 33
FFN_BLOCK = 256
ORDER = ("row", "near", "far")


def swap(array, axis, bit):
    count = lax.axis_size(axis)
    return lax.ppermute(array, axis, [(i, i ^ bit) for i in range(count)])


def add_parts(parts):
    total = parts[0].astype(F32)
    for part in parts[1:]:
        total = total + part.astype(F32)
    return total


def halves(array, bit):
    rows = array.shape[0] // 2
    side = (lax.axis_index("seq") // bit) % 2
    mine = lax.dynamic_slice_in_dim(array, side * rows, rows, 0)
    other = lax.dynamic_slice_in_dim(array, (1 - side) * rows, rows, 0)
    return mine, other


def seq_quarter(array, join):
    bits = [1 << i for i in range(lax.axis_size("seq").bit_length() - 1)]
    for bit in bits[:2]:
        mine, other = halves(array, bit)
        array = join(mine, swap(other, "seq", bit))
    for bit in bits[2:]:
        array = join(array, swap(array, "seq", bit))
    return array


def paired(array, axis, bit, dim):
    other = swap(array, axis, bit)
    side = (lax.axis_index(axis) // bit) % 2
    return jnp.where(
        side == 0,
        jnp.concatenate([array, other], dim),
        jnp.concatenate([other, array], dim),
    )


def seq_whole(array):
    return paired(paired(array, "seq", 2, 0), "seq", 1, 0)


def seq_steps():
    bits = [1 << i for i in range(lax.axis_size("seq").bit_length() - 1)]

    def halve(bit):
        def step(array):
            mine, other = halves(array, bit)
            return add_join(mine, swap(other, "seq", bit))

        return step

    def whole(bit):
        return lambda array: add_join(array, swap(array, "seq", bit))

    def double(bit):
        return lambda array: paired(array, "seq", bit, 0)

    return (
        [halve(bit) for bit in bits[:2]]
        + [whole(bit) for bit in bits[2:]]
        + [double(bit) for bit in reversed(bits[:2])]
    )


def add_join(first, second):
    return (first.astype(F32) + second.astype(F32)).astype(BF)


def stages(order):
    row = [("row", 1 << i) for i in range(lax.axis_size("row").bit_length() - 1)]
    seq = [[("seq", 1 << i)] for i in range(lax.axis_size("seq").bit_length() - 1)]
    named = {"core": seq[0], "row": row, "near": seq[1], "far": seq[2], "rest": sum(seq[3:], [])}
    return sum([named[name] for name in ("core",) + order + ("rest",)], [])


def begin(array, down, back):
    return array, stages(down), stages(back), 0


def advance(state, steps):
    held, down, back, done = state
    for step in range(done, min(done + steps, 2 * len(down))):
        if step < len(down):
            axis, bit = down[step]
            half = held.shape[0] // 2
            side = (lax.axis_index(axis) // bit) % 2
            mine = lax.dynamic_slice_in_dim(held, side * half, half, 0)
            other = lax.dynamic_slice_in_dim(held, (1 - side) * half, half, 0)
            held = mine.astype(F32) + swap(other, axis, bit).astype(F32)
            held = held.astype(BF)
        else:
            axis, bit = back[2 * len(down) - 1 - step]
            held = paired(held, axis, bit, 0)
    return held, down, back, min(done + steps, 2 * len(down))


def double_beside(state, values):
    held, down, back, done = state
    axis, bit = back[2 * len(down) - 1 - done]
    other, values = lax.optimization_barrier((swap(held, axis, bit), values))
    side = (lax.axis_index(axis) // bit) % 2
    held = jnp.where(
        side == 0,
        jnp.concatenate([held, other], 0),
        jnp.concatenate([other, held], 0),
    )
    return (held, down, back, done + 1), values


def last_swap(state):
    down, back = state[1], state[2]
    held = advance(state, 2 * len(down) - 1 - state[3])[0]
    return held, swap(held, *down[0]), down, back


def tied(values, states):
    values, helds = lax.optimization_barrier((values, [state[0] for state in states]))
    return values, [(held,) + state[1:] for held, state in zip(helds, states)]


def extended(cells, width, rows):
    count = lax.axis_size("seq")
    head = cells[:width]
    tail = cells[-width:]
    return jnp.concatenate(
        [
            lax.ppermute(tail, "seq", [(i, i + 1) for i in range(count - 1)]),
            cells,
            lax.ppermute(head, "seq", [(i + 1, i) for i in range(count - 1)]),
            jnp.zeros((rows - cells.shape[0] - 2 * width, cells.shape[1]), cells.dtype),
        ],
        axis=0,
    )


def dot_nn(a, b):
    return jnp.dot(a, b, preferred_element_type=F32)


def dot_nt(a, b):
    return lax.dot_general(a, b, (((1,), (1,)), ((), ())), preferred_element_type=F32)


def dot_tn(a, b):
    return lax.dot_general(a, b, (((0,), (0,)), ((), ())), preferred_element_type=F32)


def iota(shape, dim):
    return lax.broadcasted_iota(jnp.int32, shape, dim)


def spread(block):
    rows = block.shape[0]
    tall = jnp.concatenate([block] * 4, axis=0).astype(F32)
    shape = (4 * rows, GROUP)
    keep = iota(shape, 0) // rows == iota(shape, 1) // LAND
    return jnp.where(keep, tall, 0.0).astype(BF)


def gathered(square):
    rows = square.shape[0] // 4
    lane = iota((rows, GROUP), 1) // LAND
    out = square[:rows]
    for head in range(1, 4):
        out = jnp.where(lane == head, square[head * rows : (head + 1) * rows], out)
    return out


def by_head(columns, first, shape):
    lane = iota(shape, 1)
    out = jnp.zeros(shape, F32)
    for head, column in enumerate(columns):
        out = jnp.where((lane % 16 == first + head) & (lane < 48), column, out)
    return out


def split_three(cells):
    lane = iota(cells.shape, 1)
    high = cells.astype(BF).astype(F32)
    mid = (cells - high).astype(BF).astype(F32)
    low = cells - high - mid
    return jnp.where(lane < 16, high, jnp.where(lane < 32, mid, low)).astype(BF)


def merge_three(cells):
    cells = cells.astype(F32)
    return cells + pltpu.roll(cells, 112, 1) + pltpu.roll(cells, 96, 1)


def head_lanes(heads, width):
    return (iota((128, width), 0) == iota((128, width), 1) // LAND).astype(F32)


def doc_of(places, bounds, docs):
    out = (places >= bounds[2 * docs - 1]).astype(jnp.int32)
    for doc in range(docs):
        out = out + (places >= bounds[doc]).astype(jnp.int32)
    return out


def landmark_kernel(docs, scale, bounds, mq_ref, k_ref, v_ref, out_ref, max_s, sum_s, acc_s):
    tokens, width = k_ref.shape
    groups = width // GROUP
    heads = width // LAND
    out_ref[:, :width] = jnp.zeros((docs * LAND, width), BF)
    empty = jnp.full((docs * LAND, 128), NEGATIVE, F32)
    out_ref[:, width:] = jnp.where(iota(empty.shape, 1) < 48, split_three(empty).astype(F32), 0.0).astype(BF)
    for doc in range(docs):
        low = jnp.clip(bounds[doc], 0, tokens)
        high = jnp.clip(bounds[docs + doc], 0, tokens)
        rows = slice(doc * LAND, (doc + 1) * LAND)

        @pl.when(high > low)
        def _():
            max_s[...] = jnp.full(max_s.shape, NEGATIVE, F32)
            sum_s[...] = jnp.zeros(sum_s.shape, F32)
            acc_s[...] = jnp.zeros(acc_s.shape, F32)
            wide = [
                spread(mq_ref[rows, g * GROUP : (g + 1) * GROUP]) for g in range(groups)
            ]

            ones = jnp.ones((BLOCK, 128), BF)

            def step(block, carry):
                first = pl.multiple_of(block * BLOCK, BLOCK)
                at = pl.ds(first, BLOCK)
                place = iota((1, BLOCK), 1) + first
                valid = (place >= low) & (place < high)
                for g in range(groups):
                    cols = slice(g * GROUP, (g + 1) * GROUP)
                    scores = dot_nt(wide[g], k_ref[at, cols]) * scale
                    scores = jnp.where(valid, scores, NEGATIVE)
                    old = max_s[cols, :]
                    top = jnp.maximum(old, jnp.max(scores, axis=1, keepdims=True))
                    weights = jnp.exp(scores - twice(top)).astype(BF)
                    shrink = jnp.exp(old - top)
                    max_s[cols, :] = top
                    sum_s[cols, :] = sum_s[cols, :] * shrink + dot_nn(weights, ones)
                    acc_s[cols, :] = acc_s[cols, :] * twice(shrink) + dot_nn(weights, v_ref[at, cols])
                return carry

            lax.fori_loop(low // BLOCK, (high + BLOCK - 1) // BLOCK, step, 0)
            columns = []
            for g in range(groups):
                cols = slice(g * GROUP, (g + 1) * GROUP)
                sums = sum_s[cols, :]
                out_ref[rows, cols] = gathered(acc_s[cols, :] / twice(sums)).astype(BF)
                level = max_s[cols, :] + jnp.log(sums)
                columns += [level[h * LAND : (h + 1) * LAND] for h in range(4)]
            out_ref[rows, width:] = split_three(by_head(columns, 0, (LAND, 128)))


def twice(cells):
    return jnp.concatenate([cells, cells], axis=1)


def join_kernel(a_ref, b_ref, out_ref):
    width = a_ref.shape[1] - 128
    heads = width // LAND
    first, second = merge_three(a_ref[:, width:]), merge_three(b_ref[:, width:])
    lane = iota(first.shape, 1)
    first = jnp.where(lane < heads, first, 0.0)
    second = jnp.where(lane < heads, second, 0.0)
    top = jnp.maximum(first, second)
    exp_a, exp_b = jnp.exp(first - top), jnp.exp(second - top)
    both = exp_a + exp_b
    level = top + jnp.log(both)
    pick = head_lanes(heads, width).astype(BF)
    share = exp_b / both
    high = share.astype(BF)
    low = (share - high.astype(F32)).astype(BF)
    share = dot_nn(jnp.concatenate([high, low], 1), jnp.concatenate([pick, pick], 0))
    from_a, from_b = a_ref[:, :width].astype(F32), b_ref[:, :width].astype(F32)
    out_ref[:, :width] = (from_a + share * (from_b - from_a)).astype(BF)
    level = jnp.where(lane < heads, level, 0.0)
    level = level + pltpu.roll(level, 16, 1) + pltpu.roll(level, 32, 1)
    out_ref[:, width:] = split_three(level)


def join(first, second):
    return pl.pallas_call(
        join_kernel, out_shape=jax.ShapeDtypeStruct(first.shape, BF), name="join"
    )(first, second)


def mix_kernel(inv_ref, stat_ref, mix_ref):
    width = stat_ref.shape[1] - 128
    for g in range(width // GROUP):
        cols = slice(g * GROUP, (g + 1) * GROUP)
        mix_ref[:, cols] = dot_nn(inv_ref[:, cols], spread(stat_ref[:, cols])).astype(BF)
    mix_ref[:, width:] = stat_ref[:, width:]


def mix_back_kernel(inv_ref, stat_ref, grad_ref, out_ref):
    width = stat_ref.shape[1] - 128
    columns = []
    for g in range(width // GROUP):
        cols = slice(g * GROUP, (g + 1) * GROUP)
        grad = gathered(dot_tn(inv_ref[:, cols], grad_ref[:, cols]))
        out_ref[:, cols] = grad.astype(BF)
        product = grad * stat_ref[:, cols].astype(F32)
        lane = iota(product.shape, 1) // LAND
        for h in range(4):
            columns.append(jnp.sum(jnp.where(lane == h, product, 0.0), axis=1, keepdims=True))
    out_ref[:, width:] = split_three(by_head(columns, 0, (LAND, 128)))


def make_band(taps_ref, band_s):
    for head in range(taps_ref.shape[0]):
        row = jnp.broadcast_to(taps_ref[head : head + 1, :], (SUB, GROUP))
        band_s[head * SUB : (head + 1) * SUB, :] = pltpu.roll(row, 0, 1, stride=1, stride_axis=0).astype(BF)


def same_doc(first, bounds, docs, radius):
    rows = iota((SUB, GROUP), 0) + first
    cols = iota((SUB, GROUP), 1) + (first - radius)
    return doc_of(rows, bounds, docs) == doc_of(cols, bounds, docs)


def token_kernel(
    docs, scale, bounds, q_ref, v_ref, mk_ref, mix_ref, taps_ref, mixed_ref, probs_ref, band_s, sum_s
):
    width = q_ref.shape[1]
    groups = width // GROUP
    radius = (TAPS - 1) // 2
    first = pl.program_id(0) * BLOCK

    @pl.when(pl.program_id(0) == 0)
    def _():
        make_band(taps_ref, band_s)

    for sub in range(BLOCK // SUB):
        start = pl.multiple_of(first + sub * SUB, SUB)
        same = same_doc(start, bounds, docs, radius)
        same = jnp.where(jnp.concatenate([same] * 4, axis=0), 1.0, 0.0).astype(BF)
        for g in range(groups):
            cols = slice(g * GROUP, (g + 1) * GROUP)
            band = band_s[g * 4 * SUB : (g + 1) * 4 * SUB, :] * same
            res = dot_nn(band, v_ref[pl.ds(start, GROUP), cols])
            sum_s[sub * SUB : (sub + 1) * SUB, cols] = gathered(res)
    probs_ref[...] = jnp.zeros(probs_ref.shape, BF)
    for doc in range(docs):
        low, high = bounds[doc], bounds[docs + doc]
        rows = slice(doc * LAND, (doc + 1) * LAND)

        @pl.when((high > first) & (low < first + BLOCK))
        def _():
            place = iota((1, BLOCK), 1) + first
            valid = (place >= low) & (place < high)
            for g in range(groups):
                cols = slice(g * GROUP, (g + 1) * GROUP)
                scores = dot_nt(spread(mk_ref[rows, cols]), q_ref[:, cols]) * scale
                scores = scores.reshape(4, LAND, BLOCK)
                weights = jnp.exp(scores - jnp.max(scores, axis=1, keepdims=True))
                probs = weights / jnp.sum(weights, axis=1, keepdims=True)
                probs = jnp.where(valid, probs.reshape(GROUP, BLOCK), 0.0).astype(BF)
                probs_ref[cols, :] = probs_ref[cols, :] + probs
                sum_s[:, cols] = sum_s[:, cols] + dot_tn(probs, spread(mix_ref[rows, cols]))

    mixed_ref[...] = sum_s[...].astype(BF)


def token_back_kernel(
    docs, scale, bounds, q_ref, gm_ref, probs_ref, mk_ref, mix_ref, gq_ref, gmix_ref, gmk_ref, gq_s
):
    width = q_ref.shape[1]
    groups = width // GROUP
    first = pl.program_id(0) * BLOCK

    @pl.when(pl.program_id(0) == 0)
    def _():
        gmix_ref[...] = jnp.zeros(gmix_ref.shape, F32)
        gmk_ref[...] = jnp.zeros(gmk_ref.shape, F32)

    gq_s[...] = jnp.zeros(gq_s.shape, F32)
    for doc in range(docs):
        low, high = bounds[doc], bounds[docs + doc]
        rows = slice(doc * LAND, (doc + 1) * LAND)

        @pl.when((high > first) & (low < first + BLOCK))
        def _():
            place = iota((1, BLOCK), 1) + first
            valid = (place >= low) & (place < high)
            for g in range(groups):
                cols = slice(g * GROUP, (g + 1) * GROUP)
                probs = jnp.where(valid, probs_ref[cols, :].astype(F32), 0.0)
                gmix_ref[rows, cols] += gathered(dot_nn(probs.astype(BF), gm_ref[:, cols]))
                grad = dot_nt(spread(mix_ref[rows, cols]), gm_ref[:, cols])
                heavy = (probs * grad).reshape(4, LAND, BLOCK)
                shared = probs.reshape(4, LAND, BLOCK) * jnp.sum(heavy, axis=1, keepdims=True)
                grad = ((heavy - shared).reshape(GROUP, BLOCK) * scale).astype(BF)
                gmk_ref[rows, cols] += gathered(dot_nn(grad, q_ref[:, cols]))
                gq_s[:, cols] += dot_tn(grad, spread(mk_ref[rows, cols]))

    gq_ref[...] = gq_s[...].astype(BF)


def conv_back_kernel(docs, bounds, gm_ref, v_ref, taps_ref, out_ref, sum_ref, band_s, prod_s):
    width = gm_ref.shape[1]
    groups = width // GROUP
    radius = (TAPS - 1) // 2
    first = pl.program_id(0) * BLOCK

    @pl.when(pl.program_id(0) == 0)
    def _():
        make_band(taps_ref, band_s)
        prod_s[...] = jnp.zeros(prod_s.shape, F32)

    for sub in range(BLOCK // SUB):
        start = pl.multiple_of(first + sub * SUB, SUB)
        same = same_doc(start, bounds, docs, radius)
        same = jnp.where(jnp.concatenate([same] * 4, axis=0), 1.0, 0.0)
        for g in range(groups):
            cols = slice(g * GROUP, (g + 1) * GROUP)
            tall = slice(g * 4 * SUB, (g + 1) * 4 * SUB)
            band = band_s[tall, :] * same.astype(BF)
            res = dot_nn(band, gm_ref[pl.ds(start, GROUP), cols])
            out_ref[sub * SUB : (sub + 1) * SUB, cols] = gathered(res)
            own = gm_ref[pl.ds(pl.multiple_of(start + radius, 16), SUB), cols]
            product = dot_nt(spread(own), v_ref[pl.ds(start, GROUP), cols])
            prod_s[tall, :] += product * same

    @pl.when(pl.program_id(0) == pl.num_programs(0) - 1)
    def _():
        flip = (iota((SUB, SUB), 0) + iota((SUB, SUB), 1) == SUB - 1).astype(F32).astype(BF)
        sum_ref[...] = jnp.zeros(sum_ref.shape, F32)
        for head in range(taps_ref.shape[0]):
            product = prod_s[head * SUB : (head + 1) * SUB, :]
            high = product.astype(BF)
            low = (product - high.astype(F32)).astype(BF)
            turned = pltpu.roll(dot_nn(flip, high) + dot_nn(flip, low), 0, 1, stride=1, stride_axis=0)
            sum_ref[head : head + 1, :] = jnp.sum(turned, axis=0, keepdims=True)


def ffn_kernel(
    x_ref, mixed_ref, cot_ref, w_out_ref, w_up_ref, w_down_ref, rows_ref, bias_up_ref,
    result_ref, grad_one_ref, active_ref, grad_up_ref, low_ref, low_two_ref, low_one_ref,
    grad_mixed_ref, sums_ref, sum_up_ref, slope_s,
):
    width = x_ref.shape[1]
    hidden = w_up_ref.shape[1]
    chunks = [slice(at, at + width) for at in range(0, hidden, width)]

    def row(i):
        return rows_ref[i : i + 1, :]

    @pl.when(pl.program_id(0) == 0)
    def _():
        sums_ref[...] = jnp.zeros(sums_ref.shape, F32)
        sum_up_ref[...] = jnp.zeros(sum_up_ref.shape, F32)

    def add_sum(i, cells):
        sums_ref[i : i + 1, :] += jnp.sum(cells, axis=0, keepdims=True)

    attended = dot_nn(mixed_ref[...], w_out_ref[...]) + row(0)
    norm_one, inverse_one = normalize(x_ref[...].astype(F32) + attended)
    hidden_one = norm_one * row(1) + row(2)
    hidden_low = hidden_one.astype(BF)
    low_ref[...] = hidden_low
    lowered = hidden_one + row(3)
    for cols in chunks:
        upper = dot_nn(hidden_low, w_up_ref[:, cols]) + bias_up_ref[:1, cols]
        active, slope = gelu_both(upper)
        active = active.astype(BF)
        active_ref[:, cols] = active
        slope_s[:, cols] = slope.astype(BF)
        lowered = lowered + dot_nn(active, w_down_ref[cols, :])
    norm_two, inverse_two = normalize(lowered)
    result_ref[...] = norm_two * row(4) + row(5)
    upstream = cot_ref[...].astype(F32)
    add_sum(0, upstream * norm_two)
    add_sum(1, upstream)
    grad_two = norm_back(upstream * row(4), norm_two, inverse_two)
    low_two = grad_two.astype(BF)
    low_two_ref[...] = low_two
    add_sum(2, low_two.astype(F32))
    grad_hidden = grad_two
    for cols in chunks:
        grad_up = dot_nt(low_two, w_down_ref[cols, :]) * slope_s[:, cols].astype(F32)
        grad_up = grad_up.astype(BF)
        grad_up_ref[:, cols] = grad_up
        sum_up_ref[:1, cols] += jnp.sum(grad_up.astype(F32), axis=0, keepdims=True)
        grad_hidden = grad_hidden + dot_nt(grad_up, w_up_ref[:, cols])
    add_sum(3, grad_hidden * norm_one)
    add_sum(4, grad_hidden)
    grad_one = norm_back(grad_hidden * row(1), norm_one, inverse_one)
    grad_one_ref[...] = grad_one
    low_one = grad_one.astype(BF)
    low_one_ref[...] = low_one
    add_sum(5, low_one.astype(F32))
    grad_mixed_ref[...] = dot_nt(low_one, w_out_ref[...]).astype(BF)


def landmark_back_kernel(
    docs, scale, bounds, k_ref, v_ref, conv_ref, mq_ref, grad_ref, level_ref, dots_ref,
    gk_ref, gv_ref, gmq_ref, gk_s, gv_s,
):
    width = k_ref.shape[1]
    groups = width // GROUP
    first = pl.program_id(0) * BLOCK

    @pl.when(pl.program_id(0) == 0)
    def _():
        gmq_ref[...] = jnp.zeros(gmq_ref.shape, F32)

    gk_s[...] = jnp.zeros(gk_s.shape, F32)
    gv_s[...] = conv_ref[...]
    for doc in range(docs):
        low, high = bounds[doc], bounds[docs + doc]
        rows = slice(doc * LAND, (doc + 1) * LAND)

        @pl.when((high > first) & (low < first + BLOCK))
        def _():
            place = iota((1, BLOCK), 1) + first
            valid = (place >= low) & (place < high)

            level, dots = merge_three(level_ref[rows, :]), merge_three(dots_ref[rows, :])

            def column(lanes, g):
                return jnp.concatenate(
                    [lanes[:, 4 * g + h : 4 * g + h + 1] for h in range(4)], axis=0
                )

            for g in range(groups):
                cols = slice(g * GROUP, (g + 1) * GROUP)
                wide_q, wide_g = spread(mq_ref[rows, cols]), spread(grad_ref[rows, cols])
                scores = dot_nt(wide_q, k_ref[:, cols]) * scale - column(level, g)
                probs = jnp.exp(jnp.where(valid, scores, NEGATIVE))
                grad = dot_nt(wide_g, v_ref[:, cols]) - column(dots, g)
                grad = (probs * grad * scale).astype(BF)
                gv_s[:, cols] += dot_tn(probs.astype(BF), wide_g)
                gk_s[:, cols] += dot_tn(grad, wide_q)
                gmq_ref[rows, cols] += gathered(dot_nn(grad, k_ref[:, cols]))

    gk_ref[...] = gk_s[...].astype(BF)
    gv_ref[...] = gv_s[...].astype(BF)


def gelu_both(upper):
    cubic = (0.7978845608028654 * 0.044715) * upper * upper
    tangent = jnp.tanh(upper * (0.7978845608028654 + cubic))
    gate = 0.5 + 0.5 * tangent
    active = upper * gate
    slope = gate + active * (1.0 - tangent) * (0.7978845608028654 + 3.0 * cubic)
    return active, slope


def normalize(residual):
    row_mean = jnp.mean(residual, axis=-1, keepdims=True)
    centered = residual - row_mean
    row_var = jnp.mean(centered * centered, axis=-1, keepdims=True)
    inverse_dev = lax.rsqrt(row_var + 1e-05)
    return (centered * inverse_dev, inverse_dev)


def norm_back(grad_normed, normed, inverse_dev):
    return inverse_dev * (
        grad_normed
        - jnp.mean(grad_normed, axis=-1, keepdims=True)
        - normed * jnp.mean(grad_normed * normed, axis=-1, keepdims=True)
    )


def dot_high(a, b, dims):
    return lax.dot_general(
        a, b, (dims, ((), ())), precision=HIGH, preferred_element_type=F32
    )


NN, NT, TN = ((1,), (0,)), ((1,), (1,)), ((0,), (0,))


def pinv_kernel(scale, q_ref, k_ref, inverse_ref, kernel_ref, saved_ref):
    count = q_ref.shape[0]
    eye = (iota((LAND, LAND), 0) == iota((LAND, LAND), 1)).astype(F32)
    kernels, inverses = [], []
    for p in range(count):
        scores = dot_high(q_ref[p], k_ref[p], NT) * scale
        weights = jnp.exp(scores - jnp.max(scores, axis=1, keepdims=True))
        kernel = weights / jnp.sum(weights, axis=1, keepdims=True)
        kernel_ref[p] = kernel
        kernels.append(kernel)
        largest = jnp.max(jnp.sum(kernel, axis=0, keepdims=True), axis=1, keepdims=True)
        inverses.append(kernel.T / largest)
    for sweep in range(NS_ITERS):
        products = [dot_high(kernels[p], inverses[p], NN) for p in range(count)]
        second = [
            15.0 * eye - dot_high(products[p], 7.0 * eye - products[p], NN) for p in range(count)
        ]
        third = [13.0 * eye - dot_high(products[p], second[p], NN) for p in range(count)]
        for p in range(count):
            at = (sweep * count + p) * 4
            saved_ref[at], saved_ref[at + 1] = inverses[p], products[p]
            saved_ref[at + 2], saved_ref[at + 3] = second[p], third[p]
        inverses = [0.25 * dot_high(inverses[p], third[p], NN) for p in range(count)]
    for p in range(count):
        inverse_ref[p] = inverses[p]


def pinv_back_kernel(scale, q_ref, k_ref, kernel_ref, saved_ref, grad_ref, avg_ref, gq_ref, gk_ref):
    count = q_ref.shape[0]
    each = range(count)
    eye = (iota((LAND, LAND), 0) == iota((LAND, LAND), 1)).astype(F32)
    grads = [dot_nt(grad_ref[p], avg_ref[p]) for p in each]
    kernels = [kernel_ref[p] for p in each]
    totals = [jnp.zeros((LAND, LAND), F32) for p in each]
    for sweep in reversed(range(NS_ITERS)):
        first = [(sweep * count + p) * 4 for p in each]
        inverses, products = [saved_ref[a] for a in first], [saved_ref[a + 1] for a in first]
        grad_third = [0.25 * dot_high(inverses[p], grads[p], TN) for p in each]
        nexts = [0.25 * dot_high(grads[p], saved_ref[first[p] + 3], NT) for p in each]
        grad_second = [-dot_high(products[p], grad_third[p], TN) for p in each]
        grad_product = [-dot_high(grad_third[p], saved_ref[first[p] + 2], NT) for p in each]
        grad_first = [-dot_high(products[p], grad_second[p], TN) for p in each]
        grad_product = [
            grad_product[p]
            - dot_high(grad_second[p], 7.0 * eye - products[p], NT)
            - grad_first[p]
            for p in each
        ]
        totals = [totals[p] + dot_high(grad_product[p], inverses[p], NT) for p in each]
        grads = [nexts[p] + dot_high(kernels[p], grad_product[p], TN) for p in each]
    for p in each:
        kernel = kernels[p]
        sums = jnp.sum(kernel, axis=0, keepdims=True)
        largest = jnp.max(sums, axis=1, keepdims=True)
        flipped = grads[p].T
        loss = jnp.sum(jnp.sum(flipped * kernel, axis=1, keepdims=True), axis=0, keepdims=True)
        at_top = (sums == largest).astype(F32)
        at_top = at_top / jnp.sum(at_top, axis=1, keepdims=True)
        grad = totals[p] + flipped / largest - at_top * (loss / (largest * largest))
        grad = kernel * (grad - jnp.sum(grad * kernel, axis=1, keepdims=True)) * scale
        gq_ref[p] = dot_high(grad, k_ref[p], NN)
        gk_ref[p] = dot_high(grad, q_ref[p], TN)


def settle_qkv_kernel(side_ref, late_ref, late_other_ref, early_ref, early_other_ref, out_ref):
    part = pl.program_id(0)
    own = jnp.where(part == 0, 0, 1) == side_ref[0]
    choices = [
        (late_ref, own & (part < 2)),
        (late_other_ref, jnp.logical_not(own) & (part < 2)),
        (early_ref, own & (part == 2)),
        (early_other_ref, jnp.logical_not(own) & (part == 2)),
    ]
    for ref, chosen in choices:

        @pl.when(chosen)
        def _():
            out_ref[...] = ref[...].astype(F32)


def settle_qkv(late, late_other, early, early_other, width):
    side = (lax.axis_index("seq") % 2).astype(jnp.int32).reshape(1)
    rows = width // 2

    def spec(used):
        return pl.BlockSpec((rows, width), lambda j, i, s: (jnp.where(used(j), i, 0), 0))

    return pl.pallas_call(
        settle_qkv_kernel,
        grid_spec=pltpu.PrefetchScalarGridSpec(
            num_scalar_prefetch=1,
            grid=(3, 2),
            in_specs=[spec(lambda j: j < 2), spec(lambda j: j < 2)] + [spec(lambda j: j == 2)] * 2,
            out_specs=pl.BlockSpec((rows, width), lambda j, i, s: (i, j)),
        ),
        out_shape=jax.ShapeDtypeStruct((width, 3 * width), F32),
        name="settle_qkv",
    )(side, late, late_other, early, early_other)


def per_device(
    inputs, doc_lengths, w_qkv, bias_q, bias_v, conv_taps, w_out, bias_out, norm1_gain,
    norm1_bias, w_up, bias_up, w_down, bias_down, norm2_gain, norm2_bias, cotangent,
):
    tokens = inputs[0]
    tok_count, width = tokens.shape
    heads, tap_count = conv_taps.shape
    size = width // heads
    radius = (tap_count - 1) // 2
    lengths = doc_lengths[0]
    docs = lengths.shape[0]
    mark_count = docs * LAND
    scale = 1.0 / math.sqrt(size)
    seq_count = lax.axis_size("seq")
    me = lax.axis_index("seq")
    row_first = me * tok_count
    ends = jnp.cumsum(lengths)
    starts = ends - lengths
    bounds = (jnp.concatenate([starts, ends]) - row_first).astype(jnp.int32)
    within = jnp.arange(LAND + 1, dtype=jnp.int32)
    edges = starts[:, None] + (within[None, :] * lengths[:, None] + LAND - 1) // LAND
    mark_low = edges[:, :-1].reshape(mark_count, 1)
    mark_high = edges[:, 1:].reshape(mark_count, 1)
    counts = (mark_high - mark_low).astype(F32)
    places = row_first + jnp.arange(tok_count, dtype=jnp.int32)[None, :]
    onehot = ((places >= mark_low) & (places < mark_high)).astype(BF)
    rows_in = (((0,), (0,)), ((), ()))
    cols_in = (((1,), (1,)), ((), ()))
    blocks = tok_count // BLOCK
    window_rows = tok_count + GROUP - SUB
    smem = pl.BlockSpec(memory_space=pltpu.SMEM)
    params = pltpu.CompilerParams(vmem_limit_bytes=40 * 1024 * 1024)
    tok_spec = pl.BlockSpec((BLOCK, width), lambda i: (i, 0))

    def part(col):
        return pl.BlockSpec((BLOCK, width), lambda i: (i, col))

    def fixed(*shape):
        return pl.BlockSpec(shape, lambda i: (0,) * len(shape))

    def shaped(shape, dtype):
        return jax.ShapeDtypeStruct(shape, dtype)

    means = jnp.dot(onehot, tokens, preferred_element_type=F32) / counts
    mean_in = seq_whole(seq_quarter(means.astype(BF), add_join))
    marks = jnp.dot(mean_in, w_qkv[:, : 2 * width], preferred_element_type=F32)
    mark_q = (marks[:, :width] + bias_q).astype(BF)
    mark_k = marks[:, width:].astype(BF)

    bias = jnp.concatenate([bias_q, jnp.zeros_like(bias_q), bias_v])
    qkv = (jnp.dot(tokens, w_qkv, preferred_element_type=F32) + bias).astype(BF)
    value_ext = extended(qkv[:, 2 * width :], radius, window_rows)
    value_ext, mark_q, mark_k = lax.optimization_barrier((value_ext, mark_q, mark_k))

    def one_col(col):
        return pl.BlockSpec((tok_count, width), lambda i: (0, col))

    stats = pl.pallas_call(
        lambda *refs: landmark_kernel(docs, scale, *refs),
        grid=(1,),
        in_specs=[smem, fixed(mark_count, width), one_col(1), one_col(2)],
        out_specs=fixed(mark_count, width + 128),
        out_shape=shaped((mark_count, width + 128), BF),
        scratch_shapes=[
            pltpu.VMEM((width, 128), F32), pltpu.VMEM((width, 128), F32),
            pltpu.VMEM((width, GROUP), F32),
        ],
        compiler_params=params,
        name="landmark",
    )(bounds, mark_q, qkv, qkv)
    far_count = seq_count // 4
    own_count = -(-heads // far_count)
    own_doc = (me % 2) * 2 + (me // 2) % 2
    own_at = (me // 4) * own_count * size
    spare = far_count * own_count * size - width

    def own_heads(array):
        array = jnp.pad(array, ((0, 0), (0, spare)))
        array = lax.dynamic_slice_in_dim(array, own_at, own_count * size, 1)
        return array.reshape(LAND, own_count, size).transpose(1, 0, 2)

    def of_doc(array):
        return lax.dynamic_slice_in_dim(array, own_doc * LAND, LAND, 0)

    mine, other = halves(stats, 1)
    stats = join(mine, swap(other, "seq", 1))
    stats, later_q, later_k = lax.optimization_barrier((stats, mark_q, mark_k))
    own_q = own_heads(of_doc(later_q)).astype(F32)
    own_k = own_heads(of_doc(later_k)).astype(F32)
    square = (own_count, LAND, LAND)
    own_inverse, kernel, saved = pl.pallas_call(
        lambda *refs: pinv_kernel(scale, *refs),
        out_shape=(
            shaped(square, F32), shaped(square, F32),
            shaped((4 * NS_ITERS * own_count, LAND, LAND), F32),
        ),
        name="pinv",
    )(own_q, own_k)
    inverse = own_inverse.transpose(1, 0, 2).reshape(LAND, own_count * size).astype(BF)
    mine, other = halves(stats, 2)
    stats = join(mine, swap(other, "seq", 2))
    for i in range(2, seq_count.bit_length() - 1):
        other = swap(jnp.concatenate([stats, inverse], 1), "seq", 1 << i)
        stats = join(stats, other[:, : width + 128])
        other = other[:, width + 128 :]
        inverse = jnp.where(
            (me >> i) % 2 == 0,
            jnp.concatenate([inverse, other], 1),
            jnp.concatenate([other, inverse], 1),
        )
    inverse = inverse[:, :width]
    mix = pl.pallas_call(
        mix_kernel, out_shape=shaped((LAND, width + 128), BF), name="mix"
    )(inverse, stats)
    mix = seq_whole(mix)

    taps = jnp.pad(conv_taps, ((0, 0), (0, GROUP - tap_count)))
    mark_spec = fixed(mark_count, width)
    mixed, probs = pl.pallas_call(
        lambda *refs: token_kernel(docs, scale, *refs),
        grid=(blocks,),
        in_specs=[
            smem, part(0), fixed(window_rows, width), mark_spec, mark_spec, fixed(heads, GROUP)
        ],
        out_specs=(tok_spec, pl.BlockSpec((width, BLOCK), lambda i: (0, i))),
        out_shape=(shaped((tok_count, width), BF), shaped((width, tok_count), BF)),
        scratch_shapes=[pltpu.VMEM((heads * SUB, GROUP), BF), pltpu.VMEM((BLOCK, width), F32)],
        compiler_params=params,
        name="token",
    )(bounds, qkv, value_ext, mark_k, mix, taps)

    hidden = w_up.shape[1]
    vectors = jnp.stack([bias_out, norm1_gain, norm1_bias, bias_down, norm2_gain, norm2_bias])
    vectors = jnp.pad(vectors, ((0, 2), (0, 0)))
    wide_spec = pl.BlockSpec((FFN_BLOCK, hidden), lambda i: (i, 0))
    ffn_spec = pl.BlockSpec((FFN_BLOCK, width), lambda i: (i, 0))
    narrow = shaped((tok_count, width), BF)
    (
        result, grad_one, active, grad_upper, hidden_low, grad_low_two, grad_low_one,
        grad_mixed, sums, sum_up,
    ) = pl.pallas_call(
        ffn_kernel,
        grid=(tok_count // FFN_BLOCK,),
        in_specs=[
            ffn_spec, ffn_spec, ffn_spec, fixed(width, width), fixed(width, hidden),
            fixed(hidden, width), fixed(8, width), fixed(8, hidden),
        ],
        out_specs=(
            ffn_spec, ffn_spec, wide_spec, wide_spec, ffn_spec, ffn_spec, ffn_spec, ffn_spec,
            fixed(8, width), fixed(8, hidden),
        ),
        out_shape=(
            shaped((tok_count, width), F32), shaped((tok_count, width), F32),
            shaped((tok_count, hidden), BF), shaped((tok_count, hidden), BF),
            narrow, narrow, narrow, narrow, shaped((8, width), F32), shaped((8, hidden), F32),
        ),
        scratch_shapes=[pltpu.VMEM((FFN_BLOCK, hidden), BF)],
        compiler_params=pltpu.CompilerParams(vmem_limit_bytes=58 * 1024 * 1024),
        name="ffn",
    )(
        tokens, mixed, cotangent[0], w_out, w_up, w_down, vectors,
        jnp.broadcast_to(bias_up[None, :], (8, hidden)),
    )

    grad_queries, grad_mix, grad_mk = pl.pallas_call(
        lambda *refs: token_back_kernel(docs, scale, *refs),
        grid=(blocks,),
        in_specs=[
            smem, part(0), tok_spec, pl.BlockSpec((width, BLOCK), lambda i: (0, i)), mark_spec,
            mark_spec,
        ],
        out_specs=(tok_spec, mark_spec, mark_spec),
        out_shape=(
            shaped((tok_count, width), BF), shaped((mark_count, width), F32),
            shaped((mark_count, width), F32),
        ),
        scratch_shapes=[pltpu.VMEM((BLOCK, width), F32)],
        compiler_params=params,
        name="token_back",
    )(bounds, qkv, grad_mixed, probs, mark_k, mix)
    grad_w_down = lax.dot_general(active, grad_low_two, rows_in, preferred_element_type=F32)
    grad_w_up = lax.dot_general(hidden_low, grad_upper, rows_in, preferred_element_type=F32)
    grad_mix, grad_w_down, grad_w_up = lax.optimization_barrier(
        (grad_mix.astype(BF), grad_w_down.astype(BF), grad_w_up.astype(BF))
    )
    sum_w_down, sum_w_up = lax.psum((grad_w_down, grad_w_up), ("row", "seq"))

    def remaining(grad_mix, grad_mk, stats, mix):
        grad_mix = seq_quarter(grad_mix.astype(BF), add_join)
        grad_w_out = lax.dot_general(mixed, grad_low_one, rows_in, preferred_element_type=F32)

        grad_ext = extended(grad_mixed, radius, window_rows)
        grad_conv, products = pl.pallas_call(
            lambda *refs: conv_back_kernel(docs, *refs),
            grid=(blocks,),
            in_specs=[
                smem, fixed(window_rows, width), fixed(window_rows, width), fixed(heads, GROUP)
            ],
            out_specs=(tok_spec, fixed(16, GROUP)),
            out_shape=(shaped((tok_count, width), F32), shaped((16, GROUP), F32)),
            scratch_shapes=[
                pltpu.VMEM((heads * SUB, GROUP), BF), pltpu.VMEM((heads * SUB, GROUP), F32)
            ],
            compiler_params=params,
            name="conv_back",
        )(bounds, grad_ext, value_ext, jnp.pad(conv_taps[:, ::-1], ((0, 0), (0, GROUP - tap_count))))
        grad_conv_taps = products[:heads, SUB - 1 : SUB - 1 + tap_count]
        grad_mix, grad_conv, grad_conv_taps = lax.optimization_barrier(
            (grad_mix, grad_conv, grad_conv_taps)
        )

        grad_avg = pl.pallas_call(
            mix_back_kernel, out_shape=shaped((LAND, width + 128), BF), name="mix_back"
        )(inverse, stats, grad_mix)
        grad_avg = seq_whole(grad_avg)
        lane_spec = pl.BlockSpec((mark_count, 128), lambda i: (0, width // 128))
        grad_keys, grad_values, grad_mq = pl.pallas_call(
            lambda *refs: landmark_back_kernel(docs, scale, *refs),
            grid=(blocks,),
            in_specs=[
                smem, part(1), part(2), tok_spec, mark_spec, mark_spec, lane_spec, lane_spec
            ],
            out_specs=(tok_spec, tok_spec, mark_spec),
            out_shape=(
                shaped((tok_count, width), BF), shaped((tok_count, width), BF),
                shaped((mark_count, width), F32),
            ),
            scratch_shapes=[pltpu.VMEM((BLOCK, width), F32), pltpu.VMEM((BLOCK, width), F32)],
            compiler_params=params,
            name="landmark_back",
        )(bounds, qkv, qkv, grad_conv, mark_q, grad_avg, mix, grad_avg)


        def weight_grad(grads):
            return lax.dot_general(tokens, grads, rows_in, preferred_element_type=F32)

        early = jnp.pad(grad_w_out.astype(BF), ((0, width), (0, 0)))
        early = lax.dynamic_update_slice_in_dim(
            early, weight_grad(grad_values).astype(BF), width, 0
        )
        early = advance(begin(early, ORDER, ORDER), 1)
        grad_mix, (early,) = tied(grad_mix, [early])
        early = advance(early, 1)
        grad_mq_small, grad_mk_small = pl.pallas_call(
            lambda *refs: pinv_back_kernel(scale, *refs),
            out_shape=(shaped(square, F32), shaped(square, F32)),
            name="pinv_back",
        )(own_q, own_k, kernel, saved, own_heads(grad_mix), own_heads(stats[:, :width]))

        grad_mq_small, (early,) = tied(grad_mq_small, [early])

        def with_small(array, small):
            small = small.transpose(1, 0, 2).reshape(LAND, own_count * size)
            small = lax.dynamic_update_slice_in_dim(
                jnp.zeros((LAND, width + spare), F32), small, own_at, 1
            )[:, :width]
            first = own_doc * LAND
            rows = lax.dynamic_slice_in_dim(array, first, LAND, 0) + small
            return lax.dynamic_update_slice_in_dim(array, rows, first, 0)

        grad_mq = with_small(grad_mq, grad_mq_small)
        grad_mk = with_small(grad_mk, grad_mk_small)
        grad_marks = jnp.concatenate([grad_mq, grad_mk], axis=1).astype(BF)
        mark_back = lax.dot_general(
            grad_marks, w_qkv[:, : 2 * width], cols_in, preferred_element_type=F32
        ) / counts
        mark_back = mark_back.astype(BF)

        grad_bias_q = jnp.sum(grad_queries.astype(F32), axis=0) + jnp.sum(grad_mq, axis=0)
        grad_bias_v = jnp.sum(grad_values.astype(F32), axis=0)
        mark_grad_q = lax.dot_general(
            mean_in, grad_marks[:, :width], rows_in, preferred_element_type=F32
        )
        mark_grad_k = lax.dot_general(
            mean_in, grad_marks[:, width:], rows_in, preferred_element_type=F32
        )
        others = jnp.concatenate(
            [
                sum_up[0].reshape(hidden // width, width),
                grad_bias_q[None],
                grad_bias_v[None],
                jnp.pad(grad_conv_taps.reshape(1, -1), ((0, 0), (0, width - heads * tap_count))),
                jnp.zeros((4 - hidden // width + 1, width), F32),
            ],
            0,
        )
        spare_rows = width // 6
        small = jnp.concatenate([sums, others], 0).astype(BF)
        below = width + 2 * spare_rows - small.shape[0]
        late = jnp.pad(small, ((width, below), (0, 0)))
        late = lax.dynamic_update_slice_in_dim(
            late, (weight_grad(grad_queries) + mark_grad_q).astype(BF), 0, 0
        )
        late = lax.dynamic_update_slice_in_dim(
            late, (weight_grad(grad_keys) + mark_grad_k).astype(BF), width + spare_rows, 0
        )
        late = begin(late, ORDER, ORDER)
        grad_projected = jnp.concatenate([grad_queries, grad_keys, grad_values], axis=1)
        grad_input = grad_one + lax.dot_general(
            grad_projected, w_qkv, cols_in, preferred_element_type=F32
        )
        for step in seq_steps():
            mark_back = step(mark_back)
            early, late = advance(early, 1), advance(late, 1)
            (mark_back, grad_input), (early, late) = tied((mark_back, grad_input), [early, late])
        return early[0], late[0], mark_back, grad_input

    plan = stages(ORDER)
    sent = len(seq_steps())

    def rows_left(rows, done):
        return rows >> min(done, 2 * len(plan) - done)

    early_rows = rows_left(2 * width, sent + 2)
    late_rows = rows_left(2 * width + width // 3, sent)

    def nothing(*unused):
        return tuple(
            jnp.zeros((rows, width), BF) for rows in (early_rows, late_rows, mark_count)
        ) + (jnp.zeros((tok_count, width), F32),)

    early, late, mark_back, grad_input = lax.cond(
        lengths[0] > 0, remaining, nothing, grad_mix, grad_mk, stats, mix
    )
    early, late = (early, plan, plan, sent + 2), (late, plan, plan, sent)
    last = 2 * len(plan) - 1
    early, late = advance(early, last - early[3]), advance(late, last - 1 - late[3])
    late, (sum_w_down, sum_w_up) = double_beside(
        late, (sum_w_down.astype(F32), sum_w_up.astype(F32))
    )
    grad_input = grad_input + lax.dot_general(
        onehot, mark_back, rows_in, preferred_element_type=F32
    )
    grad_input, (early, late) = tied(grad_input, [early, late])
    early, early_other = last_swap(early)[:2]
    late, late_other = last_swap(late)[:2]
    sum_w_qkv = settle_qkv(late, late_other, early, early_other, width)
    first_core = me % 2 == 0
    sum_w_out = jnp.where(first_core, early, early_other).astype(F32)
    flat = jnp.where(first_core, late[width:], late_other[width:])[:16].astype(F32)
    at = sums.shape[0] + hidden // width
    pieces = [
        flat[at], flat[at + 1], flat[at + 2, : heads * tap_count], flat[5], flat[3], flat[4],
        flat[sums.shape[0] : at].reshape(hidden), flat[2], flat[0], flat[1],
    ]
    return (
        result[None], grad_input[None], sum_w_qkv, pieces[0], pieces[1],
        pieces[2].reshape(heads, tap_count), sum_w_out, pieces[3], pieces[4], pieces[5],
        sum_w_up, pieces[6], sum_w_down, pieces[7], pieces[8], pieces[9],
    )


def solution(mesh):
    whole, tokens = P(), P("row", "seq", None)
    return jax.shard_map(
        per_device,
        mesh=mesh,
        in_specs=(tokens, P("row", None)) + (whole,) * 14 + (tokens,),
        out_specs=(tokens, tokens) + (whole,) * 14,
        check_vma=False,
    )
```
